32 devices in a mesh: groups: 2 (over x), tile: 16 (over z, y, core).
Axes of the slice: x: 2, y: 2, z: 4, core: 2. Of those that a mesh axis runs over, the one named last changes fastest.
Arguments:
- source: bfloat16 [512, 2, 69, 128], P('tile', 'groups'), parts along dimension 1, may hold values from -42 to 42
- weights: bfloat16 [1536, 128, 128], P('tile'), may hold values from -0.5 to 0.5
- block_source: int32 [1536], P('tile'), may hold values from 0 to 31
- block_target: int32 [1536], P('tile'), may hold values from 0 to 511, as said below
- edge_flip: int32 [16, 2], P('tile'), may hold values 0 or 1
- norm_gain: float32 [69], replicated, may hold values from 0.1 to 1.9
- first_kernel: bfloat16 [9, 69, 69], replicated, may hold values from -0.25 to 0.25
- second_kernel: bfloat16 [9, 69, 69], replicated, may hold values from -0.25 to 0.25
Outputs:
- gridded: bfloat16 [512, 2, 69, 128], P('tile', 'groups'), parts along dimension 1
- smoothed: bfloat16 [512, 2, 69, 128], P('tile', 'groups'), parts along dimension 1
The draws below stay inside these ranges and needn't reach their ends.
There are 2 independent parts, one for each index of `groups`. The reference program is written for one: setup_inputs(seed, part) draws one part's arguments, and reference() takes and returns one part's arrays. A program takes and returns all parts, laid end to end along the dimension named above; an argument that names none is the same for every part. Nothing has to cross between parts.
Inputs may be any that keep to these rules, and one draw needn't show every extreme that they name: `block_target`: band d lies at the latitude of tile position p = d mod 2, in column d // 2. Its entries name exactly 64 distinct target rows, all in tiles c * 2 + p or c * 2 + p + 1 (any column c, positions below 2). One band names at most 8 distinct rows of one tile, and every band at position 1 names exactly 8 rows of each tile at its own position.
All inputs are finite; a program needn't handle non-finite values. No bound on the sum of `edge_flip` on one device may be relied on, other than what follows from the above.
Results may differ from the reference program's by a relative error of at most 0.001.
The reference program's roundings to bfloat16 on the way count: a program that leaves them out, or rounds other values in their place, can miss the bound.
Values may be sent and summed in bfloat16 or wider, within the bound.
No kernel may reach another device: no remote copies, remote signals or barrier semaphores. Data moves between devices by JAX's collectives and lax.ppermute only.
A program may use at most 64 MiB of HBM per device.

```python
import math
import jax
import jax.numpy as jnp
from jax import lax

BLOCK = 128
CHANNELS = 69
TIMES = 1
ROWS = 32
TILE_COLS = 8
TILES = 16
TILE_ROWS = 2
ENTRIES = 96
LIVE = 64
CAP = 8
SLOTS = 128
SOURCE_BLOCKS = 512
TARGET_ROWS = 512
ALL_ENTRIES = 1536
N_TILE = 16


def draw_source(key, part):
    key = jax.random.fold_in(key, 11)
    subkeys = jax.random.split(key, 4)
    full_shape = (SOURCE_BLOCKS, TIMES, CHANNELS, BLOCK)
    channel_scale = jnp.exp(jax.random.uniform(subkeys[0], (1, 1, CHANNELS, 1), jnp.float32, math.log(0.32), math.log(3.2)))
    point_scale = jnp.exp(jax.random.uniform(subkeys[1], (SOURCE_BLOCKS, 1, 1, BLOCK), jnp.float32, math.log(0.32), math.log(3.2)))
    blended = jnp.clip(jax.random.normal(subkeys[3], full_shape, jnp.float32), -4.0, 4.0)
    return (blended * channel_scale * point_scale).astype(jnp.bfloat16)


def draw_block_target(key, part):
    key = jax.random.fold_in(key, 23)
    subkeys = jax.random.split(key, 3)
    column_rows = TILES // TILE_COLS
    group_count = 2 * TILE_COLS
    band_ids = jnp.arange(TILES, dtype=jnp.int32)
    position = band_ids % column_rows
    column = band_ids // column_rows
    polar_band = (position == column_rows - 1)[:, None]
    live_ids = jnp.arange(LIVE, dtype=jnp.int32)[None, :]
    half_cap = CAP // 2
    groups = jnp.where(polar_band, live_ids // CAP, live_ids // half_cap).astype(jnp.int32)
    within = jnp.where(polar_band, live_ids % CAP, live_ids % half_cap).astype(jnp.int32)
    row_offset = groups // TILE_COLS
    col_offset = groups % TILE_COLS
    tiles = (column[:, None] + col_offset) % TILE_COLS * column_rows + position[:, None] + row_offset
    shuffled = jax.vmap(lambda one_key: jax.random.permutation(one_key, ROWS))(jax.random.split(subkeys[0], TILES * group_count)).astype(jnp.int32)
    shuffled = shuffled.reshape(TILES, group_count * ROWS)
    rows = jnp.take_along_axis(shuffled, groups * ROWS + within, axis=1)
    live_targets = (tiles * ROWS + rows).astype(jnp.int32)
    extra_pick = jax.random.randint(subkeys[1], (TILES, ENTRIES - LIVE), 0, LIVE)
    targets = jnp.concatenate([live_targets, jnp.take_along_axis(live_targets, extra_pick, axis=1)], axis=1)
    mixing = jax.vmap(lambda one_key: jax.random.permutation(one_key, ENTRIES))(jax.random.split(subkeys[2], TILES))
    return jnp.take_along_axis(targets, mixing.astype(jnp.int32), axis=1).reshape(-1).astype(jnp.int32)


def plant(entries, rng, smallest, largest):
    longest = entries.shape.index(max(entries.shape))
    spots = []
    for shift in (0, 1):
        where = [jax.random.randint(jax.random.fold_in(rng, axis), (), 0, length) for axis, length in enumerate(entries.shape)]
        where[longest] = (where[longest] + shift) % entries.shape[longest]
        spots.append(tuple(where))
    return entries.at[spots[0]].set(smallest).at[spots[1]].set(largest)


def block_levels(own_key, dims, shards, smallest, largest):
    gain, own = 1.0, jax.random.fold_in(own_key, 6)
    for axis_at, blocks in shards:
        heights = jnp.exp(jax.random.uniform(jax.random.fold_in(own, axis_at), (blocks,), jnp.float32, smallest / len(shards), largest / len(shards)))
        gain = gain * jnp.repeat(heights, dims[axis_at] // blocks).reshape([-1 if axis == axis_at else 1 for axis in range(len(dims))])
    return gain


def centred(key, extent, scale, most, shards=(), kind=jnp.bfloat16):
    factor_of = block_levels(key, extent, shards, -0.22, 0.18) if shards else 1.0
    array = jax.random.normal(key, extent, jnp.float32) * scale * factor_of
    return jnp.minimum(jnp.maximum(array, -most), most).astype(kind)


def setup_inputs(seed: int = 0, part: int = 0) -> dict:
    seeds = jax.random.split(jax.random.key(seed), 9)
    part_keys = jax.random.split(jax.random.fold_in(seeds[8], part), 9)
    return {
        "source": draw_source(jax.random.fold_in(jax.random.fold_in(seeds[8], part), 71), part),
        "weights": centred(seeds[1], (ALL_ENTRIES, BLOCK, BLOCK), BLOCK ** -0.5, 0.5, ((0, 16),)),
        "block_source": plant(jax.random.randint(seeds[2], (ALL_ENTRIES,), 0, ROWS), jax.random.fold_in(seeds[2], 1), 0, ROWS - 1).astype(jnp.int32),
        "block_target": draw_block_target(jax.random.fold_in(seeds[8], 71), part),
        "edge_flip": plant((jax.random.randint(seeds[4], (TILES, 2), 0, 2) < 1).astype(jnp.int32), jax.random.fold_in(seeds[4], 1), 0, 1),
        "norm_gain": jnp.clip(1.0 + 0.18 * jax.random.normal(seeds[5], (CHANNELS,), jnp.float32), 0.1, 1.9),
        "first_kernel": centred(seeds[6], (9, CHANNELS, CHANNELS), (9 * CHANNELS) ** -0.5, 0.25),
        "second_kernel": centred(seeds[7], (9, CHANNELS, CHANNELS), (9 * CHANNELS) ** -0.5, 0.25),
    }


EPSILON = 1e-05

def slot_plan(targets, band_index, column_rows):
    entry_count = targets.shape[0]
    entry_order = jnp.arange(entry_count, dtype=jnp.int32)
    owners = (targets // ROWS).astype(jnp.int32)
    row_offset = owners % column_rows - band_index % column_rows
    col_offset = (owners // column_rows - band_index // column_rows) % TILE_COLS
    groups = (row_offset * TILE_COLS + col_offset).astype(jnp.int32)
    matching = targets[:, None] == targets[None, :]
    earliest = jnp.logical_not(jnp.any(matching & (entry_order[None, :] < entry_order[:, None]), axis=1))
    before_mine = earliest[None, :] & (groups[None, :] == groups[:, None]) & (targets[None, :] < targets[:, None])
    placed = lax.optimization_barrier(jnp.sum(before_mine.astype(jnp.int32), axis=1))
    return (groups * CAP + placed).astype(jnp.int32)

def norm_cells(values, norm_gain, channel_axis):
    widened = values.astype(jnp.float32)
    square = lax.optimization_barrier(jnp.mean(widened * widened, axis=channel_axis, keepdims=True))
    layout = [1] * values.ndim
    layout[channel_axis] = CHANNELS
    scaled = widened * lax.rsqrt(square + EPSILON) * norm_gain.reshape(layout)
    return scaled.astype(jnp.bfloat16)

def apply_taps(padded, west_strip, east_strip, kernel):
    inner_rows = padded.shape[0] - 2
    columns = (jnp.concatenate([west_strip[..., None], padded[..., :-1]], axis=-1), padded, jnp.concatenate([padded[..., 1:], east_strip[..., None]], axis=-1))
    summed = jnp.zeros(padded[1:-1].shape, jnp.float32)
    for row_step in range(3):
        for col_step in range(3):
            window = columns[col_step][row_step:row_step + inner_rows]
            summed = summed + jnp.einsum('oc,rtcj->rtoj', kernel[row_step * 3 + col_step].astype(jnp.float32), window.astype(jnp.float32))
    return summed

def spread_field(grid_field, edge_flip, kernel):
    tile_count = grid_field.shape[0]
    column_rows = tile_count // TILE_COLS
    tile_ids = jnp.arange(tile_count, dtype=jnp.int32)
    upper_rim = jnp.roll(grid_field, 1, axis=0)[:, -1]
    lower_rim = jnp.roll(grid_field, -1, axis=0)[:, 0]
    blank_rim = jnp.zeros_like(upper_rim)
    upper_rim = jnp.where((tile_ids != 0)[:, None, None, None], upper_rim, blank_rim)
    lower_rim = jnp.where((tile_ids != tile_count - 1)[:, None, None, None], lower_rim, blank_rim)
    padded = jnp.concatenate([upper_rim[:, None], grid_field, lower_rim[:, None]], axis=1)
    west_strip = jnp.roll(padded, column_rows, axis=0)[..., -1]
    east_strip = jnp.roll(padded, -column_rows, axis=0)[..., 0]
    west_strip = jnp.where((edge_flip[:, 0] == 1)[:, None, None, None], west_strip[:, ::-1], west_strip)
    east_strip = jnp.where((edge_flip[:, 1] == 1)[:, None, None, None], east_strip[:, ::-1], east_strip)

    def one_tile(tile_parts):
        return apply_taps(tile_parts[0], tile_parts[1], tile_parts[2], kernel)
    return lax.map(one_tile, (padded, west_strip, east_strip))

def reference(source, weights, block_source, block_target, edge_flip, norm_gain, first_kernel, second_kernel):
    tile_count = N_TILE
    bands = source.reshape(tile_count, ROWS, TIMES, CHANNELS, BLOCK)
    band_weights = weights.reshape(tile_count, ENTRIES, BLOCK, BLOCK)
    band_sources = block_source.reshape(tile_count, ENTRIES)
    band_targets = block_target.reshape(tile_count, ENTRIES)

    def add_band(device, summed):
        chosen = bands[device][band_sources[device]]
        products = jnp.einsum('etck,ekj->etcj', chosen.astype(jnp.float32), band_weights[device].astype(jnp.float32))
        targets = band_targets[device]
        slot_index = slot_plan(targets, device, TILE_ROWS)
        reduced_blocks = jax.ops.segment_sum(products, slot_index, num_segments=SLOTS).astype(jnp.bfloat16)
        destination = jnp.full((SLOTS,), TARGET_ROWS, jnp.int32).at[slot_index].set(targets)
        return summed.at[destination].add(reduced_blocks.astype(jnp.float32), mode='drop')
    summed = lax.fori_loop(0, tile_count, add_band, jnp.zeros((TARGET_ROWS, TIMES, CHANNELS, BLOCK), jnp.float32))
    gridded = summed.astype(jnp.bfloat16)
    grid_field = gridded.reshape(tile_count, ROWS, TIMES, CHANNELS, BLOCK)
    normed = norm_cells(grid_field, norm_gain, 3)
    hidden = jax.nn.gelu(spread_field(normed, edge_flip, first_kernel)).astype(jnp.bfloat16)
    smoothed = (grid_field.astype(jnp.float32) + spread_field(hidden, edge_flip, second_kernel)).astype(jnp.bfloat16)
    return (gridded, smoothed.reshape(TARGET_ROWS, TIMES, CHANNELS, BLOCK))
```

```python
import functools

import jax
import jax.numpy as jnp
from jax import lax
from jax.experimental import pallas as pl
from jax.experimental.pallas import tpu as pltpu
from jax.sharding import PartitionSpec as P

BLOCK = 128
CHANNELS = 69
PADDED = 72
ROWS = 32
TILE_COLS = 8
CAP = 8
GROUPS = 2 * TILE_COLS
SLOTS = GROUPS * CAP
CHUNK = 16
EPSILON = 1e-05
VMEM_LIMIT = 40 * 1024 * 1024


def vmem():
    return pl.BlockSpec(memory_space=pltpu.VMEM)


def smem():
    return pl.BlockSpec(memory_space=pltpu.SMEM)


def lanes(shape):
    return lax.broadcasted_iota(jnp.int32, shape, len(shape) - 1)


def regrid_kernel(key_ref, source_index_ref, source_ref, weight_ref, *rest):
    outs = rest[:GROUPS]
    field, sums, slot_of, used = rest[GROUPS:]
    step = pl.program_id(0)

    @pl.when(step == 0)
    def _():
        field[pl.ds(0, CHANNELS * ROWS), :] = source_ref[...].astype(jnp.float32)
        field[pl.ds(CHANNELS * ROWS, (PADDED - CHANNELS) * ROWS), :] = jnp.zeros(
            ((PADDED - CHANNELS) * ROWS, BLOCK), jnp.float32
        )
        for key in range(GROUPS * ROWS):
            slot_of[key] = -1
        for group in range(GROUPS):
            used[group] = 0

    for at in range(CHUNK):
        entry = step * CHUNK + at
        key = key_ref[entry]
        group = key // ROWS
        known = slot_of[key]
        count = used[group]
        fresh = known < 0
        slot = jnp.where(fresh, group * CAP + count, known)
        slot_of[key] = slot
        used[group] = jnp.where(fresh, count + 1, count)
        block = field[pl.ds(source_index_ref[entry], PADDED, stride=ROWS), :].astype(jnp.bfloat16)
        product = jnp.dot(block, weight_ref[at], preferred_element_type=jnp.float32)
        before = jnp.where(fresh, 0.0, sums[slot])
        sums[slot] = before + product

    @pl.when(step == pl.num_programs(0) - 1)
    def _():
        for group in range(GROUPS):
            for place in range(CAP):
                outs[group][place] = sums[group * CAP + place].astype(jnp.bfloat16)


def regrid(keys, source_index, field, weights):
    entries = weights.shape[0]
    piece = jax.ShapeDtypeStruct((CAP, PADDED, BLOCK), jnp.bfloat16)
    return pl.pallas_call(
        regrid_kernel,
        grid=(entries // CHUNK,),
        in_specs=[
            smem(),
            smem(),
            pl.BlockSpec((CHANNELS * ROWS, BLOCK), lambda step: (0, 0)),
            pl.BlockSpec((CHUNK, BLOCK, BLOCK), lambda step: (step, 0, 0)),
        ],
        out_specs=[pl.BlockSpec((CAP, PADDED, BLOCK), lambda step: (0, 0, 0))] * GROUPS,
        out_shape=[piece] * GROUPS,
        scratch_shapes=[
            pltpu.VMEM((PADDED * ROWS, BLOCK), jnp.float32),
            pltpu.VMEM((SLOTS, PADDED, BLOCK), jnp.float32),
            pltpu.SMEM((GROUPS * ROWS,), jnp.int32),
            pltpu.SMEM((GROUPS,), jnp.int32),
        ],
        compiler_params=pltpu.CompilerParams(vmem_limit_bytes=VMEM_LIMIT),
        name="regrid",
    )(keys, source_index, field, weights)


def gather_kernel(row_ref, gain_ref, *rest):
    pieces = rest[:GROUPS]
    gridded_out, gridded, normed, west_col, east_col, summed, turned = rest[GROUPS:]
    summed[...] = jnp.zeros_like(summed)
    for group in range(GROUPS):
        for place in range(CAP):
            row = row_ref[group * CAP + place]
            summed[row] = summed[row] + pieces[group][place].astype(jnp.float32)
    gain = gain_ref[...]
    lane = lanes((PADDED, BLOCK))
    west = jnp.zeros((PADDED, BLOCK), jnp.float32)
    east = jnp.zeros((PADDED, BLOCK), jnp.float32)
    for row in range(ROWS):
        rounded = summed[row].astype(jnp.bfloat16)
        gridded[row] = rounded
        value = rounded.astype(jnp.float32)
        turned[pl.ds(row, PADDED, stride=ROWS), :] = value
        square = jnp.sum(value * value, axis=0, keepdims=True) * (1.0 / CHANNELS)
        scaled = (value * lax.rsqrt(square + EPSILON) * gain).astype(jnp.bfloat16)
        normed[row] = scaled
        scaled = scaled.astype(jnp.float32)
        west = jnp.where(lane == row + 1, pltpu.roll(scaled, row + 2, 1), west)
        east = jnp.where(lane == row + 1, pltpu.roll(scaled, row + 1, 1), east)
    west_col[...] = west.astype(jnp.bfloat16)
    east_col[...] = east.astype(jnp.bfloat16)
    gridded_out[...] = turned[pl.ds(0, CHANNELS * ROWS), :].astype(jnp.bfloat16)


def gather_rows(rows, gain, pieces):
    field = jax.ShapeDtypeStruct((ROWS, PADDED, BLOCK), jnp.bfloat16)
    strip = jax.ShapeDtypeStruct((PADDED, BLOCK), jnp.bfloat16)
    return pl.pallas_call(
        gather_kernel,
        in_specs=[smem()] + [vmem()] * (1 + GROUPS),
        out_specs=[vmem()] * 5,
        out_shape=[
            jax.ShapeDtypeStruct((CHANNELS * ROWS, BLOCK), jnp.bfloat16),
            field,
            field,
            strip,
            strip,
        ],
        scratch_shapes=[
            pltpu.VMEM((ROWS + 1, PADDED, BLOCK), jnp.float32),
            pltpu.VMEM((PADDED * ROWS, BLOCK), jnp.float32),
        ],
        compiler_params=pltpu.CompilerParams(vmem_limit_bytes=VMEM_LIMIT),
        name="gather_rows",
    )(rows, gain, *pieces)


def tap_sums(flip_ref, field, above, below, west_ref, east_ref, taps_ref, partial):
    lane = lanes((PADDED, BLOCK))
    west = west_ref[...].astype(jnp.float32)
    east = east_ref[...].astype(jnp.float32)
    taps = taps_ref[...]
    last = ROWS + 1
    flip_west = flip_ref[0, 0] == 1
    flip_east = flip_ref[0, 1] == 1

    def columns(p):
        raw = above[...] if p == 0 else below[...] if p == last else field[p - 1]
        value = raw.astype(jnp.float32)
        from_west = jnp.where(flip_west, BLOCK - last + p, (BLOCK - p) % BLOCK)
        from_east = jnp.where(flip_east, BLOCK - 1 - last + p, BLOCK - 1 - p)
        left = jnp.where(lane == 0, pltpu.roll(west, from_west, 1), pltpu.roll(value, 1, 1))
        right = jnp.where(
            lane == BLOCK - 1, pltpu.roll(east, from_east, 1), pltpu.roll(value, BLOCK - 1, 1)
        )
        return jnp.concatenate([left, value, right], axis=0).astype(jnp.bfloat16)

    for p in range(0, ROWS + 2, 2):
        both = jnp.concatenate([columns(p), columns(p + 1)], axis=1)
        result = jnp.dot(taps, both, preferred_element_type=jnp.float32)
        partial[p] = result[:, :BLOCK]
        partial[p + 1] = result[:, BLOCK:]


def conv_row(partial, row):
    return (
        partial[row, :PADDED]
        + partial[row + 1, PADDED : 2 * PADDED]
        + partial[row + 2, 2 * PADDED :]
    )


def first_conv_kernel(
    flip_ref, field, above, below, west_ref, east_ref, taps_ref, hidden, west_col, east_col, partial
):
    tap_sums(flip_ref, field, above, below, west_ref, east_ref, taps_ref, partial)
    lane = lanes((PADDED, BLOCK))
    west = jnp.zeros((PADDED, BLOCK), jnp.float32)
    east = jnp.zeros((PADDED, BLOCK), jnp.float32)
    for row in range(ROWS):
        value = jax.nn.gelu(conv_row(partial, row)).astype(jnp.bfloat16)
        hidden[row] = value
        value = value.astype(jnp.float32)
        west = jnp.where(lane == row + 1, pltpu.roll(value, row + 2, 1), west)
        east = jnp.where(lane == row + 1, pltpu.roll(value, row + 1, 1), east)
    west_col[...] = west.astype(jnp.bfloat16)
    east_col[...] = east.astype(jnp.bfloat16)


def second_conv_kernel(
    flip_ref,
    field,
    above,
    below,
    west_ref,
    east_ref,
    taps_ref,
    gridded,
    smoothed,
    partial,
    turned,
):
    tap_sums(flip_ref, field, above, below, west_ref, east_ref, taps_ref, partial)
    for row in range(ROWS):
        turned[pl.ds(row, PADDED, stride=ROWS), :] = gridded[row].astype(jnp.float32) + conv_row(
            partial, row
        )
    smoothed[...] = turned[pl.ds(0, CHANNELS * ROWS), :].astype(jnp.bfloat16)


PARTIAL = pltpu.VMEM((ROWS + 2, 3 * PADDED, BLOCK), jnp.float32)


def first_conv(edge_flip, field, above, below, west, east, taps):
    strip = jax.ShapeDtypeStruct((PADDED, BLOCK), jnp.bfloat16)
    return pl.pallas_call(
        first_conv_kernel,
        in_specs=[smem()] + [vmem()] * 6,
        out_specs=[vmem()] * 3,
        out_shape=[jax.ShapeDtypeStruct((ROWS, PADDED, BLOCK), jnp.bfloat16), strip, strip],
        scratch_shapes=[PARTIAL],
        compiler_params=pltpu.CompilerParams(vmem_limit_bytes=VMEM_LIMIT),
        name="first_conv",
    )(edge_flip, field, above, below, west, east, taps)


def second_conv(edge_flip, field, above, below, west, east, taps, gridded):
    return pl.pallas_call(
        second_conv_kernel,
        in_specs=[smem()] + [vmem()] * 7,
        out_specs=vmem(),
        out_shape=jax.ShapeDtypeStruct((CHANNELS * ROWS, BLOCK), jnp.bfloat16),
        scratch_shapes=[PARTIAL, pltpu.VMEM((PADDED * ROWS, BLOCK), jnp.float32)],
        compiler_params=pltpu.CompilerParams(vmem_limit_bytes=VMEM_LIMIT),
        name="second_conv",
    )(edge_flip, field, above, below, west, east, taps, gridded)


def tap_matrix(kernel):
    pad = PADDED - CHANNELS
    taps = jnp.pad(kernel, ((0, 0), (0, pad), (0, pad))).reshape(3, 3, PADDED, PADDED)
    return taps.transpose(0, 2, 1, 3).reshape(3 * PADDED, 3 * PADDED)


def halos(field, west_col, east_col, column_rows):
    count = lax.axis_size("tile")
    above = lax.ppermute(field[ROWS - 1], "tile", [(i, i + 1) for i in range(count - 1)])
    below = lax.ppermute(field[0], "tile", [(i + 1, i) for i in range(count - 1)])
    lane = lanes((PADDED, BLOCK))

    def whole(strip, column):
        strip = jnp.where(lane == 0, above[:, column : column + 1], strip)
        return jnp.where(lane == ROWS + 1, below[:, column : column + 1], strip)

    west = lax.ppermute(
        whole(west_col, BLOCK - 1), "tile", [(i, (i + column_rows) % count) for i in range(count)]
    )
    east = lax.ppermute(
        whole(east_col, 0), "tile", [((i + column_rows) % count, i) for i in range(count)]
    )
    return above, below, west, east


def received_rows(targets, tile, column_rows):
    count = lax.axis_size("tile")
    column, position = tile // column_rows, tile % column_rows
    bands, here = [], []
    for group in range(GROUPS):
        across, lower = group // 2, group % 2
        band = (column ^ across) * column_rows + position - lower
        bands.append(jnp.clip(band, 0, count - 1))
        here.append(position >= lower)
    chosen = jnp.take(targets, jnp.stack(bands), axis=0)
    entries = targets.shape[1]
    rows = jnp.arange(ROWS, dtype=jnp.int32)
    hit = (chosen[:, None, :] == tile * ROWS + rows[None, :, None]) & jnp.stack(here)[:, None, None]
    order = jnp.arange(entries, dtype=jnp.int32)
    first = jnp.min(jnp.where(hit, order, entries), axis=2)
    rank = jnp.sum((first[:, None, :] < first[:, :, None]).astype(jnp.int32), axis=2)
    rank = jnp.where(first < entries, rank, -1)
    place = jnp.arange(CAP, dtype=jnp.int32)
    match = rank[:, None, :] == place[None, :, None]
    found = jnp.sum(jnp.where(match, rows - ROWS, 0), axis=2) + ROWS
    return found.reshape(SLOTS)


def per_device(
    source, weights, block_source, block_target, edge_flip, norm_gain, first_kernel, second_kernel
):
    count = lax.axis_size("tile")
    column_rows = count // TILE_COLS
    tile = lax.axis_index("tile")
    targets = lax.all_gather(block_target, "tile")

    owner = block_target // ROWS
    lower = owner % column_rows - tile % column_rows
    across = (owner // column_rows) ^ (tile // column_rows)
    keys = (across * 2 + lower) * ROWS + block_target % ROWS
    field = source.reshape(ROWS, CHANNELS, BLOCK).transpose(1, 0, 2).reshape(-1, BLOCK)
    outgoing = regrid(keys, block_source, field, weights)

    pieces = [None] * GROUPS
    for across in (7, 6, 5, 4, 3, 2, 1, 0):
        for lower in (1, 0):
            group = across * 2 + lower
            if group == 0:
                pieces[group] = outgoing[group]
                continue
            pairs = [
                (c * column_rows + p, (c ^ across) * column_rows + p + lower)
                for c in range(TILE_COLS)
                for p in range(column_rows - lower)
            ]
            pieces[group] = lax.ppermute(outgoing[group], "tile", pairs)

    rows = received_rows(targets, tile, column_rows)
    gain = jnp.broadcast_to(
        jnp.pad(norm_gain, (0, PADDED - CHANNELS))[:, None], (PADDED, BLOCK)
    )
    gridded_out, gridded, normed, west_col, east_col = gather_rows(rows, gain, pieces)
    exchange = functools.partial(halos, column_rows=column_rows)
    hidden, west_col, east_col = first_conv(
        edge_flip, normed, *exchange(normed, west_col, east_col), tap_matrix(first_kernel)
    )
    smoothed = second_conv(
        edge_flip, hidden, *exchange(hidden, west_col, east_col), tap_matrix(second_kernel), gridded
    )

    def placed(value):
        return value.reshape(CHANNELS, ROWS, BLOCK).transpose(1, 0, 2)[:, None]

    return placed(gridded_out), placed(smoothed)


def solution(mesh):
    in_specs = (
        P("tile", "groups", None, None),
        P("tile", None, None),
        P("tile"),
        P("tile"),
        P("tile", None),
        P(),
        P(),
        P(),
    )
    out_specs = (P("tile", "groups", None, None), P("tile", "groups", None, None))
    return jax.shard_map(
        per_device, mesh=mesh, in_specs=in_specs, out_specs=out_specs, check_vma=False
    )
```

```python
import functools

import jax
import jax.numpy as jnp
from jax import lax
from jax.experimental import pallas as pl
from jax.experimental.pallas import tpu as pltpu
from jax.sharding import PartitionSpec as P

BLOCK = 128
CHANNELS = 69
PADDED = 72
ROWS = 32
TILE_COLS = 8
CAP = 8
GROUPS = 2 * TILE_COLS
SLOTS = GROUPS * CAP
CHUNK = 16
MARK = CHANNELS
EPSILON = 1e-05
VMEM_LIMIT = 40 * 1024 * 1024
REGRID_VMEM_LIMIT = 60 * 1024 * 1024


def vmem():
    return pl.BlockSpec(memory_space=pltpu.VMEM)


def smem():
    return pl.BlockSpec(memory_space=pltpu.SMEM)


def lanes(shape):
    return lax.broadcasted_iota(jnp.int32, shape, len(shape) - 1)


def regrid_kernel(column_rows, target_ref, index_ref, source_hbm, weight_hbm, *rest):
    same_out, next_outs = rest[0], rest[1 : 1 + TILE_COLS]
    source, weight, field, sums, slot_of, used, source_sem, weight_sems = rest[1 + TILE_COLS :]
    chunks = weight.shape[0] // CHUNK
    tile = lax.axis_index("tile")
    column, position = lax.div(tile, column_rows), lax.rem(tile, column_rows)

    source_copy = pltpu.make_async_copy(source_hbm, source, source_sem)
    source_copy.start()

    def chunk_copy(chunk):
        part = pl.ds(chunk * CHUNK, CHUNK)
        return pltpu.make_async_copy(weight_hbm.at[part], weight.at[part], weight_sems.at[chunk])

    for chunk in range(chunks):
        chunk_copy(chunk).start()
    for key in range(GROUPS * ROWS):
        slot_of[key] = -1
    for group in range(GROUPS):
        used[group] = 0
    for slot in range(SLOTS):
        sums[slot, MARK : MARK + 1] = jnp.full((1, BLOCK), ROWS, jnp.float32)
    field[pl.ds(CHANNELS * ROWS, (PADDED - CHANNELS) * ROWS), :] = jnp.zeros(
        ((PADDED - CHANNELS) * ROWS, BLOCK), jnp.float32
    )
    source_copy.wait()
    field[pl.ds(0, CHANNELS * ROWS), :] = source[...].astype(jnp.float32)

    def chunk_step(chunk, carry):
        chunk_copy(chunk).wait()
        for at in range(CHUNK):
            entry = chunk * CHUNK + at
            target = target_ref[entry]
            owner, row = lax.div(target, ROWS), lax.rem(target, ROWS)
            owner_column = lax.div(owner, column_rows)
            lower = lax.rem(owner, column_rows) - position
            group = jnp.where(lower == 0, owner_column, TILE_COLS + (owner_column ^ column))
            key = group * ROWS + row
            known = slot_of[key]
            count = used[group]
            fresh = known < 0
            slot = jnp.where(fresh, group * CAP + count, known)
            slot_of[key] = slot
            used[group] = jnp.where(fresh, count + 1, count)
            block = field[pl.ds(index_ref[entry], PADDED, stride=ROWS), :].astype(jnp.bfloat16)
            product = jnp.dot(block, weight[entry], preferred_element_type=jnp.float32)
            before = jnp.where(fresh, 0.0, sums[slot])
            sums[slot] = before + product
            sums[slot, MARK : MARK + 1] = jnp.full((1, BLOCK), row, jnp.int32).astype(jnp.float32)
        return carry

    lax.fori_loop(0, chunks, chunk_step, 0)
    for group in range(TILE_COLS):
        for place in range(CAP):
            same_out[group, place] = sums[group * CAP + place].astype(jnp.bfloat16)
            slot = (TILE_COLS + group) * CAP + place
            next_outs[group][place] = sums[slot].astype(jnp.bfloat16)


def regrid(target, source_index, field, weights, column_rows):
    piece = jax.ShapeDtypeStruct((CAP, PADDED, BLOCK), jnp.bfloat16)
    same = jax.ShapeDtypeStruct((TILE_COLS, CAP, PADDED, BLOCK), jnp.bfloat16)
    hbm = pl.BlockSpec(memory_space=pltpu.HBM)
    return pl.pallas_call(
        functools.partial(regrid_kernel, column_rows),
        in_specs=[smem(), smem(), hbm, hbm],
        out_specs=[vmem()] * (1 + TILE_COLS),
        out_shape=[same] + [piece] * TILE_COLS,
        scratch_shapes=[
            pltpu.VMEM(field.shape, jnp.bfloat16),
            pltpu.VMEM(weights.shape, jnp.bfloat16),
            pltpu.VMEM((PADDED * ROWS, BLOCK), jnp.float32),
            pltpu.VMEM((SLOTS, PADDED, BLOCK), jnp.float32),
            pltpu.SMEM((GROUPS * ROWS,), jnp.int32),
            pltpu.SMEM((GROUPS,), jnp.int32),
            pltpu.SemaphoreType.DMA,
            pltpu.SemaphoreType.DMA((weights.shape[0] // CHUNK,)),
        ],
        compiler_params=pltpu.CompilerParams(vmem_limit_bytes=REGRID_VMEM_LIMIT),
        name="regrid",
    )(target, source_index, field, weights)


def gather_kernel(gain_ref, same, *rest):
    nexts = rest[:TILE_COLS]
    gridded_out, gridded, normed, edges, summed, turned, marks, rows, sem = rest[TILE_COLS:]
    pieces = [same.at[group, place] for group in range(TILE_COLS) for place in range(CAP)]
    pieces += [nexts[group].at[place] for group in range(TILE_COLS) for place in range(CAP)]
    lane = lanes((1, BLOCK))
    mark = jnp.zeros((1, BLOCK), jnp.float32)
    for slot, piece in enumerate(pieces):
        mark = jnp.where(lane == slot, piece[MARK : MARK + 1].astype(jnp.float32), mark)
    marks[...] = mark.astype(jnp.int32)
    copy = pltpu.make_async_copy(marks, rows, sem)
    copy.start()
    summed[...] = jnp.zeros_like(summed)
    copy.wait()
    for slot, piece in enumerate(pieces):
        row = rows[0, slot]
        summed[row] = summed[row] + piece[...].astype(jnp.float32)
    gain = gain_ref[...]
    lane = lanes((PADDED, BLOCK))
    west = jnp.zeros((PADDED, BLOCK), jnp.float32)
    east = jnp.zeros((PADDED, BLOCK), jnp.float32)
    for row in range(ROWS):
        rounded = summed[row].astype(jnp.bfloat16)
        gridded[row] = rounded
        value = rounded.astype(jnp.float32)
        turned[pl.ds(row, PADDED, stride=ROWS), :] = value
        value = jnp.where(lax.broadcasted_iota(jnp.int32, value.shape, 0) < CHANNELS, value, 0.0)
        square = jnp.sum(value * value, axis=0, keepdims=True) * (1.0 / CHANNELS)
        scaled = (value * lax.rsqrt(square + EPSILON) * gain).astype(jnp.bfloat16)
        normed[row] = scaled
        if row == 0:
            edges[0] = scaled
        if row == ROWS - 1:
            edges[1] = scaled
        scaled = scaled.astype(jnp.float32)
        west = jnp.where(lane == row + 1, pltpu.roll(scaled, row + 2, 1), west)
        east = jnp.where(lane == row + 1, pltpu.roll(scaled, row + 1, 1), east)
    edges[2] = west.astype(jnp.bfloat16)
    edges[3] = east.astype(jnp.bfloat16)
    gridded_out[...] = turned[pl.ds(0, CHANNELS * ROWS), :].astype(jnp.bfloat16)


FIELD = jax.ShapeDtypeStruct((ROWS, PADDED, BLOCK), jnp.bfloat16)
EDGES = jax.ShapeDtypeStruct((4, PADDED, BLOCK), jnp.bfloat16)


def gather_rows(gain, same, nexts):
    return pl.pallas_call(
        gather_kernel,
        in_specs=[vmem()] * (2 + TILE_COLS),
        out_specs=[vmem()] * 4,
        out_shape=[
            jax.ShapeDtypeStruct((CHANNELS * ROWS, BLOCK), jnp.bfloat16),
            FIELD,
            FIELD,
            EDGES,
        ],
        scratch_shapes=[
            pltpu.VMEM((ROWS + 1, PADDED, BLOCK), jnp.float32),
            pltpu.VMEM((PADDED * ROWS, BLOCK), jnp.float32),
            pltpu.VMEM((1, SLOTS), jnp.int32),
            pltpu.SMEM((1, SLOTS), jnp.int32),
            pltpu.SemaphoreType.DMA,
        ],
        compiler_params=pltpu.CompilerParams(vmem_limit_bytes=VMEM_LIMIT),
        name="gather_rows",
    )(gain, same, *nexts)


def tap_sums(column_rows, flip_ref, field, edges, taps_ref, partial):
    lane = lanes((PADDED, BLOCK))
    count = edges.shape[0]
    tile = lax.axis_index("tile")
    last = ROWS + 1

    def strip(shift, which):
        at = lax.rem(tile + shift + count, count)
        before = edges[lax.rem(at + count - 1, count), which].astype(jnp.float32)
        after = edges[lax.rem(at + 1, count), which].astype(jnp.float32)
        whole = edges[at, which].astype(jnp.float32)
        whole = jnp.where((lane == 0) & (at > 0), pltpu.roll(before, BLOCK - ROWS, 1), whole)
        return jnp.where((lane == last) & (at < count - 1), pltpu.roll(after, ROWS, 1), whole)

    west = strip(-column_rows, 2)
    east = strip(column_rows, 3)
    taps = taps_ref[...]
    flip_west = flip_ref[0, 0] == 1
    flip_east = flip_ref[0, 1] == 1

    def columns(p):
        if p == 0:
            value = edges[lax.rem(tile + count - 1, count), 1].astype(jnp.float32)
            value = jnp.where(tile > 0, value, 0.0)
        elif p == last:
            value = edges[lax.rem(tile + 1, count), 0].astype(jnp.float32)
            value = jnp.where(tile < count - 1, value, 0.0)
        else:
            value = field[p - 1].astype(jnp.float32)
        from_west = jnp.where(flip_west, BLOCK - last + p, (BLOCK - p) % BLOCK)
        from_east = jnp.where(flip_east, BLOCK - 1 - last + p, BLOCK - 1 - p)
        left = jnp.where(lane == 0, pltpu.roll(west, from_west, 1), pltpu.roll(value, 1, 1))
        right = jnp.where(
            lane == BLOCK - 1, pltpu.roll(east, from_east, 1), pltpu.roll(value, BLOCK - 1, 1)
        )
        return jnp.concatenate([left, value, right], axis=0).astype(jnp.bfloat16)

    for p in range(0, ROWS + 2, 2):
        both = jnp.concatenate([columns(p), columns(p + 1)], axis=1)
        result = jnp.dot(taps, both, preferred_element_type=jnp.float32)
        partial[p] = result[:, :BLOCK]
        partial[p + 1] = result[:, BLOCK:]


def conv_row(partial, row):
    return (
        partial[row, :PADDED]
        + partial[row + 1, PADDED : 2 * PADDED]
        + partial[row + 2, 2 * PADDED :]
    )


def first_conv_kernel(column_rows, flip_ref, field, edges, taps_ref, hidden, edges_out, partial):
    tap_sums(column_rows, flip_ref, field, edges, taps_ref, partial)
    lane = lanes((PADDED, BLOCK))
    west = jnp.zeros((PADDED, BLOCK), jnp.float32)
    east = jnp.zeros((PADDED, BLOCK), jnp.float32)
    for row in range(ROWS):
        value = jax.nn.gelu(conv_row(partial, row)).astype(jnp.bfloat16)
        hidden[row] = value
        if row == 0:
            edges_out[0] = value
        if row == ROWS - 1:
            edges_out[1] = value
        value = value.astype(jnp.float32)
        west = jnp.where(lane == row + 1, pltpu.roll(value, row + 2, 1), west)
        east = jnp.where(lane == row + 1, pltpu.roll(value, row + 1, 1), east)
    edges_out[2] = west.astype(jnp.bfloat16)
    edges_out[3] = east.astype(jnp.bfloat16)


def second_conv_kernel(
    column_rows, flip_ref, field, edges, taps_ref, gridded, smoothed, partial, turned
):
    tap_sums(column_rows, flip_ref, field, edges, taps_ref, partial)
    for row in range(ROWS):
        turned[pl.ds(row, PADDED, stride=ROWS), :] = gridded[row].astype(jnp.float32) + conv_row(
            partial, row
        )
    smoothed[...] = turned[pl.ds(0, CHANNELS * ROWS), :].astype(jnp.bfloat16)


PARTIAL = pltpu.VMEM((ROWS + 2, 3 * PADDED, BLOCK), jnp.float32)


def first_conv(column_rows, edge_flip, field, edges, taps):
    return pl.pallas_call(
        functools.partial(first_conv_kernel, column_rows),
        in_specs=[smem()] + [vmem()] * 3,
        out_specs=[vmem()] * 2,
        out_shape=[FIELD, EDGES],
        scratch_shapes=[PARTIAL],
        compiler_params=pltpu.CompilerParams(vmem_limit_bytes=VMEM_LIMIT),
        name="first_conv",
    )(edge_flip, field, edges, taps)


def second_conv(column_rows, edge_flip, field, edges, taps, gridded):
    return pl.pallas_call(
        functools.partial(second_conv_kernel, column_rows),
        in_specs=[smem()] + [vmem()] * 4,
        out_specs=vmem(),
        out_shape=jax.ShapeDtypeStruct((CHANNELS * ROWS, BLOCK), jnp.bfloat16),
        scratch_shapes=[PARTIAL, pltpu.VMEM((PADDED * ROWS, BLOCK), jnp.float32)],
        compiler_params=pltpu.CompilerParams(vmem_limit_bytes=VMEM_LIMIT),
        name="second_conv",
    )(edge_flip, field, edges, taps, gridded)


def tap_matrix(kernel):
    pad = PADDED - CHANNELS
    taps = jnp.pad(kernel, ((0, 0), (0, pad), (0, pad))).reshape(3, 3, PADDED, PADDED)
    return taps.transpose(0, 2, 1, 3).reshape(3 * PADDED, 3 * PADDED)


def per_device(
    source, weights, block_source, block_target, edge_flip, norm_gain, first_kernel, second_kernel
):
    count = lax.axis_size("tile")
    column_rows = count // TILE_COLS
    field = source.reshape(ROWS, CHANNELS, BLOCK).transpose(1, 0, 2).reshape(-1, BLOCK)
    same, *nexts = regrid(block_target, block_source, field, weights, column_rows)

    for across in reversed(range(TILE_COLS)):
        pairs = [
            (c * column_rows + p, (c ^ across) * column_rows + p + 1)
            for c in range(TILE_COLS)
            for p in range(column_rows - 1)
        ]
        nexts[across] = lax.ppermute(nexts[across], "tile", pairs)
    same = lax.all_to_all(
        same,
        "tile",
        0,
        0,
        axis_index_groups=[
            [c * column_rows + p for c in range(TILE_COLS)] for p in range(column_rows)
        ],
        tiled=True,
    )

    gain = jnp.broadcast_to(
        jnp.pad(norm_gain, (0, PADDED - CHANNELS))[:, None], (PADDED, BLOCK)
    )
    first_taps, second_taps = tap_matrix(first_kernel), tap_matrix(second_kernel)
    same, nexts, gain, first_taps, second_taps = lax.optimization_barrier(
        (same, nexts, gain, first_taps, second_taps)
    )
    gridded_out, gridded, normed, edges = gather_rows(gain, same, nexts)
    edges = lax.all_gather(edges, "tile")
    hidden, edges = first_conv(column_rows, edge_flip, normed, edges, first_taps)
    edges = lax.all_gather(edges, "tile")
    smoothed = second_conv(column_rows, edge_flip, hidden, edges, second_taps, gridded)

    def placed(value):
        return value.reshape(CHANNELS, ROWS, BLOCK).transpose(1, 0, 2)[:, None]

    return placed(gridded_out), placed(smoothed)


def solution(mesh):
    in_specs = (
        P("tile", "groups", None, None),
        P("tile", None, None),
        P("tile"),
        P("tile"),
        P("tile", None),
        P(),
        P(),
        P(),
    )
    out_specs = (P("tile", "groups", None, None), P("tile", "groups", None, None))
    return jax.shard_map(
        per_device, mesh=mesh, in_specs=in_specs, out_specs=out_specs, check_vma=False
    )
```

```python
import functools

import jax
import jax.numpy as jnp
from jax import lax
from jax.experimental import pallas as pl
from jax.experimental.pallas import tpu as pltpu
from jax.sharding import PartitionSpec as P

BLOCK = 128
CHANNELS = 69
PADDED = 72
ROWS = 32
TILE_COLS = 8
CAP = 8
GROUPS = 2 * TILE_COLS
SLOTS = GROUPS * CAP
CHUNK = 16
MARK = CHANNELS
EPSILON = 1e-05
VMEM_LIMIT = 40 * 1024 * 1024
FULL_VMEM = 60 * 1024 * 1024


def vmem():
    return pl.BlockSpec(memory_space=pltpu.VMEM)


def smem():
    return pl.BlockSpec(memory_space=pltpu.SMEM)


def lanes(shape):
    return lax.broadcasted_iota(jnp.int32, shape, len(shape) - 1)


def regrid_kernel(column_rows, target_ref, index_ref, source_hbm, weight_hbm, *rest):
    same_out, next_outs = rest[0], rest[1 : 1 + TILE_COLS]
    (
        source,
        weight,
        wide,
        field,
        sums,
        rounded,
        slot_of,
        used,
        entry_slot,
        entry_fresh,
        source_sem,
        weight_sems,
        out_sems,
    ) = rest[1 + TILE_COLS :]
    entries = weight.shape[0]
    chunks = entries // CHUNK
    tile = lax.axis_index("tile")
    column, position = lax.div(tile, column_rows), lax.rem(tile, column_rows)

    source_copy = pltpu.make_async_copy(source_hbm, source, source_sem)
    source_copy.start()

    def chunk_copy(chunk):
        part = pl.ds(chunk * CHUNK, CHUNK)
        return pltpu.make_async_copy(weight_hbm.at[part], weight.at[part], weight_sems.at[chunk])

    for chunk in range(chunks):
        chunk_copy(chunk).start()

    for key in range(GROUPS * ROWS):
        slot_of[key] = -1
    for group in range(GROUPS):
        used[group] = 0

    def plan(entry, carry):
        target = target_ref[entry]
        owner, row = lax.div(target, ROWS), lax.rem(target, ROWS)
        owner_column = lax.div(owner, column_rows)
        lower = lax.rem(owner, column_rows) - position
        group = jnp.where(lower == 0, owner_column, TILE_COLS + (owner_column ^ column))
        key = group * ROWS + row
        known = slot_of[key]
        count = used[group]
        fresh = known < 0
        slot = jnp.where(fresh, group * CAP + count, known)
        slot_of[key] = slot
        used[group] = jnp.where(fresh, count + 1, count)
        entry_slot[entry] = slot
        entry_fresh[entry] = fresh.astype(jnp.int32)
        return carry

    lax.fori_loop(0, entries, plan, 0, unroll=4)

    tail = PADDED - 8
    for slot in range(SLOTS):
        rounded[slot, tail:] = jnp.full((8, BLOCK), ROWS, jnp.bfloat16)
    wide[pl.ds(CHANNELS * ROWS, (PADDED - CHANNELS) * ROWS), :] = jnp.zeros(
        ((PADDED - CHANNELS) * ROWS, BLOCK), jnp.float32
    )
    source_copy.wait()
    wide[pl.ds(0, CHANNELS * ROWS), :] = source[...].astype(jnp.float32)
    for row in range(ROWS):
        field[row] = wide[pl.ds(row, PADDED, stride=ROWS), :].astype(jnp.bfloat16)
    is_mark = lax.broadcasted_iota(jnp.int32, (8, BLOCK), 0) == MARK - tail

    def chunk_step(chunk, carry):
        chunk_copy(chunk).wait()
        for at in range(CHUNK):
            entry = chunk * CHUNK + at
            slot = entry_slot[entry]
            row = lax.rem(target_ref[entry], ROWS)
            product = jnp.dot(
                field[index_ref[entry]], weight[entry], preferred_element_type=jnp.float32
            )
            total = jnp.where(entry_fresh[entry] == 1, 0.0, sums[slot]) + product
            sums[slot] = total
            marked = jnp.where(is_mark, row.astype(jnp.float32), total[tail:])
            rounded[slot] = jnp.concatenate([total[:tail], marked], axis=0).astype(jnp.bfloat16)
        return carry

    lax.fori_loop(0, chunks, chunk_step, 0)
    copies = [
        pltpu.make_async_copy(
            rounded.at[pl.ds(0, SLOTS // 2)], same_out, out_sems.at[0]
        )
    ]
    for group in range(TILE_COLS):
        part = rounded.at[pl.ds((TILE_COLS + group) * CAP, CAP)]
        copies.append(pltpu.make_async_copy(part, next_outs[group], out_sems.at[1 + group]))
    for copy in copies:
        copy.start()
    for copy in copies:
        copy.wait()


def regrid(target, source_index, field, weights, column_rows):
    piece = jax.ShapeDtypeStruct((CAP, PADDED, BLOCK), jnp.bfloat16)
    same = jax.ShapeDtypeStruct((TILE_COLS * CAP, PADDED, BLOCK), jnp.bfloat16)
    hbm = pl.BlockSpec(memory_space=pl.ANY)
    entries = weights.shape[0]
    return pl.pallas_call(
        functools.partial(regrid_kernel, column_rows),
        in_specs=[smem(), smem(), hbm, hbm],
        out_specs=[hbm] * (1 + TILE_COLS),
        out_shape=[same] + [piece] * TILE_COLS,
        scratch_shapes=[
            pltpu.VMEM(field.shape, jnp.bfloat16),
            pltpu.VMEM(weights.shape, jnp.bfloat16),
            pltpu.VMEM((PADDED * ROWS, BLOCK), jnp.float32),
            pltpu.VMEM((ROWS, PADDED, BLOCK), jnp.bfloat16),
            pltpu.VMEM((SLOTS, PADDED, BLOCK), jnp.float32),
            pltpu.VMEM((SLOTS, PADDED, BLOCK), jnp.bfloat16),
            pltpu.SMEM((GROUPS * ROWS,), jnp.int32),
            pltpu.SMEM((GROUPS,), jnp.int32),
            pltpu.SMEM((entries,), jnp.int32),
            pltpu.SMEM((entries,), jnp.int32),
            pltpu.SemaphoreType.DMA,
            pltpu.SemaphoreType.DMA((entries // CHUNK,)),
            pltpu.SemaphoreType.DMA((1 + TILE_COLS,)),
        ],
        compiler_params=pltpu.CompilerParams(vmem_limit_bytes=FULL_VMEM),
        name="regrid",
    )(target, source_index, field, weights)


def gather_kernel(gain_ref, same_hbm, *rest):
    nexts_hbm = rest[:TILE_COLS]
    (
        gridded_out,
        gridded,
        normed,
        first_row,
        last_row,
        west_col,
        east_col,
        pieces,
        summed,
        turned,
        marks,
        rows,
        mark_sem,
        piece_sems,
    ) = rest[TILE_COLS:]
    half = SLOTS // 2
    copies = [pltpu.make_async_copy(same_hbm, pieces.at[pl.ds(0, half)], piece_sems.at[0])]
    for group, source in enumerate(nexts_hbm):
        part = pieces.at[pl.ds(half + group * CAP, CAP)]
        copies.append(pltpu.make_async_copy(source, part, piece_sems.at[1 + group]))
    for copy in copies:
        copy.start()
    summed[...] = jnp.zeros_like(summed)
    for copy in copies:
        copy.wait()
    lane = lanes((1, BLOCK))
    mark = jnp.zeros((1, BLOCK), jnp.float32)
    for slot in range(SLOTS):
        mark = jnp.where(lane == slot, pieces[slot, MARK : MARK + 1].astype(jnp.float32), mark)
    marks[...] = mark.astype(jnp.int32)
    copy = pltpu.make_async_copy(marks, rows, mark_sem)
    copy.start()
    copy.wait()

    def add(step, carry):
        for at in range(CAP):
            slot = step * CAP + at
            row = rows[0, slot]
            summed[row] = summed[row] + pieces[slot].astype(jnp.float32)
        return carry

    lax.fori_loop(0, SLOTS // CAP, add, 0)
    gain = gain_ref[...]
    lane = lanes((PADDED, BLOCK))
    real = lax.broadcasted_iota(jnp.int32, (PADDED, BLOCK), 0) < CHANNELS
    west = jnp.zeros((PADDED, BLOCK), jnp.float32)
    east = jnp.zeros((PADDED, BLOCK), jnp.float32)
    for row in range(ROWS):
        rounded = summed[row].astype(jnp.bfloat16)
        gridded[row] = rounded
        value = rounded.astype(jnp.float32)
        turned[pl.ds(row, PADDED, stride=ROWS), :] = value
        value = jnp.where(real, value, 0.0)
        square = jnp.sum(value * value, axis=0, keepdims=True) * (1.0 / CHANNELS)
        scaled = (value * lax.rsqrt(square + EPSILON) * gain).astype(jnp.bfloat16)
        normed[row] = scaled
        if row == 0:
            first_row[...] = scaled
        if row == ROWS - 1:
            last_row[...] = scaled
        scaled = scaled.astype(jnp.float32)
        west = jnp.where(lane == row + 1, pltpu.roll(scaled, row + 2, 1), west)
        east = jnp.where(lane == row + 1, pltpu.roll(scaled, row + 1, 1), east)
    west_col[...] = west.astype(jnp.bfloat16)
    east_col[...] = east.astype(jnp.bfloat16)
    gridded_out[...] = turned[pl.ds(0, CHANNELS * ROWS), :].astype(jnp.bfloat16)


FIELD = jax.ShapeDtypeStruct((ROWS, PADDED, BLOCK), jnp.bfloat16)
PLANE = jax.ShapeDtypeStruct((PADDED, BLOCK), jnp.bfloat16)
FIELD_EDGES = [FIELD, PLANE, PLANE, PLANE, PLANE]


def gather_rows(gain, same, nexts):
    return pl.pallas_call(
        gather_kernel,
        in_specs=[vmem()] + [pl.BlockSpec(memory_space=pl.ANY)] * (1 + TILE_COLS),
        out_specs=[vmem()] * (2 + len(FIELD_EDGES)),
        out_shape=[jax.ShapeDtypeStruct((CHANNELS * ROWS, BLOCK), jnp.bfloat16), FIELD]
        + FIELD_EDGES,
        scratch_shapes=[
            pltpu.VMEM((SLOTS, PADDED, BLOCK), jnp.bfloat16),
            pltpu.VMEM((ROWS + 1, PADDED, BLOCK), jnp.float32),
            pltpu.VMEM((PADDED * ROWS, BLOCK), jnp.float32),
            pltpu.VMEM((1, SLOTS), jnp.int32),
            pltpu.SMEM((1, SLOTS), jnp.int32),
            pltpu.SemaphoreType.DMA,
            pltpu.SemaphoreType.DMA((1 + TILE_COLS,)),
        ],
        compiler_params=pltpu.CompilerParams(vmem_limit_bytes=VMEM_LIMIT),
        name="gather_rows",
    )(gain, same, *nexts)


def tap_sums(flip_ref, field, above, below, west_ref, east_ref, taps_ref, partial):
    lane = lanes((PADDED, BLOCK))
    last = ROWS + 1
    west = west_ref[...].astype(jnp.float32)
    east = east_ref[...].astype(jnp.float32)
    taps = taps_ref[...]
    flip_west = flip_ref[0, 0] == 1
    flip_east = flip_ref[0, 1] == 1

    def columns(p):
        raw = above[...] if p == 0 else below[...] if p == last else field[p - 1]
        value = raw.astype(jnp.float32)
        from_west = jnp.where(flip_west, BLOCK - last + p, (BLOCK - p) % BLOCK)
        from_east = jnp.where(flip_east, BLOCK - 1 - last + p, BLOCK - 1 - p)
        left = jnp.where(lane == 0, pltpu.roll(west, from_west, 1), pltpu.roll(value, 1, 1))
        right = jnp.where(
            lane == BLOCK - 1, pltpu.roll(east, from_east, 1), pltpu.roll(value, BLOCK - 1, 1)
        )
        return jnp.concatenate([left, value, right], axis=0).astype(jnp.bfloat16)

    for p in range(0, ROWS + 2, 2):
        both = jnp.concatenate([columns(p), columns(p + 1)], axis=1)
        result = jnp.dot(taps, both, preferred_element_type=jnp.float32)
        partial[p] = result[:, :BLOCK]
        partial[p + 1] = result[:, BLOCK:]


def conv_row(partial, row):
    return (
        partial[row, :PADDED]
        + partial[row + 1, PADDED : 2 * PADDED]
        + partial[row + 2, 2 * PADDED :]
    )


def first_conv_kernel(
    flip_ref,
    field,
    above,
    below,
    west_ref,
    east_ref,
    taps_ref,
    hidden,
    first_row,
    last_row,
    west_col,
    east_col,
    partial,
):
    tap_sums(flip_ref, field, above, below, west_ref, east_ref, taps_ref, partial)
    lane = lanes((PADDED, BLOCK))
    west = jnp.zeros((PADDED, BLOCK), jnp.float32)
    east = jnp.zeros((PADDED, BLOCK), jnp.float32)
    for row in range(ROWS):
        value = jax.nn.gelu(conv_row(partial, row)).astype(jnp.bfloat16)
        hidden[row] = value
        if row == 0:
            first_row[...] = value
        if row == ROWS - 1:
            last_row[...] = value
        value = value.astype(jnp.float32)
        west = jnp.where(lane == row + 1, pltpu.roll(value, row + 2, 1), west)
        east = jnp.where(lane == row + 1, pltpu.roll(value, row + 1, 1), east)
    west_col[...] = west.astype(jnp.bfloat16)
    east_col[...] = east.astype(jnp.bfloat16)


def second_conv_kernel(
    flip_ref,
    field,
    above,
    below,
    west_ref,
    east_ref,
    taps_ref,
    gridded,
    smoothed,
    partial,
    turned,
):
    tap_sums(flip_ref, field, above, below, west_ref, east_ref, taps_ref, partial)
    for row in range(ROWS):
        turned[pl.ds(row, PADDED, stride=ROWS), :] = gridded[row].astype(jnp.float32) + conv_row(
            partial, row
        )
    smoothed[...] = turned[pl.ds(0, CHANNELS * ROWS), :].astype(jnp.bfloat16)


PARTIAL = pltpu.VMEM((ROWS + 2, 3 * PADDED, BLOCK), jnp.float32)


def first_conv(edge_flip, field, above, below, west, east, taps):
    return pl.pallas_call(
        first_conv_kernel,
        in_specs=[smem()] + [vmem()] * 6,
        out_specs=[vmem()] * len(FIELD_EDGES),
        out_shape=FIELD_EDGES,
        scratch_shapes=[PARTIAL],
        compiler_params=pltpu.CompilerParams(vmem_limit_bytes=VMEM_LIMIT),
        name="first_conv",
    )(edge_flip, field, above, below, west, east, taps)


def second_conv(edge_flip, field, above, below, west, east, taps, gridded):
    return pl.pallas_call(
        second_conv_kernel,
        in_specs=[smem()] + [vmem()] * 7,
        out_specs=vmem(),
        out_shape=jax.ShapeDtypeStruct((CHANNELS * ROWS, BLOCK), jnp.bfloat16),
        scratch_shapes=[PARTIAL, pltpu.VMEM((PADDED * ROWS, BLOCK), jnp.float32)],
        compiler_params=pltpu.CompilerParams(vmem_limit_bytes=VMEM_LIMIT),
        name="second_conv",
    )(edge_flip, field, above, below, west, east, taps, gridded)


def tap_matrix(kernel):
    pad = PADDED - CHANNELS
    taps = jnp.pad(kernel, ((0, 0), (0, pad), (0, pad))).reshape(3, 3, PADDED, PADDED)
    return taps.transpose(0, 2, 1, 3).reshape(3 * PADDED, 3 * PADDED)


def halos(first_row, last_row, west_col, east_col, column_rows):
    count = lax.axis_size("tile")
    above = lax.ppermute(last_row, "tile", [(i, i + 1) for i in range(count - 1)])
    below = lax.ppermute(first_row, "tile", [(i + 1, i) for i in range(count - 1)])
    lane = lanes((PADDED, BLOCK))

    def whole(strip, column):
        strip = jnp.where(lane == 0, above[:, column : column + 1], strip)
        return jnp.where(lane == ROWS + 1, below[:, column : column + 1], strip)

    west = lax.ppermute(
        whole(west_col, BLOCK - 1), "tile", [(i, (i + column_rows) % count) for i in range(count)]
    )
    east = lax.ppermute(
        whole(east_col, 0), "tile", [((i + column_rows) % count, i) for i in range(count)]
    )
    return above, below, west, east


def per_device(
    source, weights, block_source, block_target, edge_flip, norm_gain, first_kernel, second_kernel
):
    count = lax.axis_size("tile")
    column_rows = count // TILE_COLS
    field = source.reshape(ROWS, CHANNELS, BLOCK).transpose(1, 0, 2).reshape(-1, BLOCK)
    same, *nexts = regrid(block_target, block_source, field, weights, column_rows)

    for across in reversed(range(TILE_COLS)):
        pairs = [
            (c * column_rows + p, (c ^ across) * column_rows + p + 1)
            for c in range(TILE_COLS)
            for p in range(column_rows - 1)
        ]
        nexts[across] = lax.ppermute(nexts[across], "tile", pairs)
    same = lax.all_to_all(
        same,
        "tile",
        0,
        0,
        axis_index_groups=[
            [c * column_rows + p for c in range(TILE_COLS)] for p in range(column_rows)
        ],
        tiled=True,
    )

    gain = jnp.broadcast_to(
        jnp.pad(norm_gain, (0, PADDED - CHANNELS))[:, None], (PADDED, BLOCK)
    )
    first_taps, second_taps = tap_matrix(first_kernel), tap_matrix(second_kernel)
    same, nexts, gain, first_taps, second_taps = lax.optimization_barrier(
        (same, nexts, gain, first_taps, second_taps)
    )
    gridded_out, gridded, normed, *edges = gather_rows(gain, same, nexts)
    hidden, *edges_hidden = first_conv(
        edge_flip, normed, *halos(*edges, column_rows), first_taps
    )
    smoothed = second_conv(
        edge_flip, hidden, *halos(*edges_hidden, column_rows), second_taps, gridded
    )

    def placed(value):
        return value.reshape(CHANNELS, ROWS, BLOCK).transpose(1, 0, 2)[:, None]

    return placed(gridded_out), placed(smoothed)


def solution(mesh):
    in_specs = (
        P("tile", "groups", None, None),
        P("tile", None, None),
        P("tile"),
        P("tile"),
        P("tile", None),
        P(),
        P(),
        P(),
    )
    out_specs = (P("tile", "groups", None, None), P("tile", "groups", None, None))
    return jax.shard_map(
        per_device, mesh=mesh, in_specs=in_specs, out_specs=out_specs, check_vma=False
    )
```

```python
import functools

import jax
import jax.numpy as jnp
from jax import lax
from jax.experimental import pallas as pl
from jax.experimental.pallas import tpu as pltpu
from jax.sharding import PartitionSpec as P

BLOCK = 128
CHANNELS = 69
PADDED = 72
ROWS = 32
TILE_COLS = 8
CAP = 8
GROUPS = 2 * TILE_COLS
SLOTS = GROUPS * CAP
CHUNK = 16
MARK = CHANNELS
EPSILON = 1e-05
VMEM_LIMIT = 40 * 1024 * 1024
FULL_VMEM = 60 * 1024 * 1024


def vmem():
    return pl.BlockSpec(memory_space=pltpu.VMEM)


def smem():
    return pl.BlockSpec(memory_space=pltpu.SMEM)


def lanes(shape):
    return lax.broadcasted_iota(jnp.int32, shape, len(shape) - 1)


def regrid_kernel(column_rows, target_ref, index_ref, source_hbm, weight_hbm, *rest):
    same_out, next_outs = rest[0], rest[1 : 1 + TILE_COLS]
    (
        source,
        weight,
        wide,
        field,
        sums,
        rounded,
        slot_of,
        used,
        entry_slot,
        entry_fresh,
        source_sem,
        weight_sems,
        out_sems,
    ) = rest[1 + TILE_COLS :]
    entries = weight.shape[0]
    chunks = entries // CHUNK
    tile = lax.axis_index("tile")
    column, position = lax.div(tile, column_rows), lax.rem(tile, column_rows)

    source_copy = pltpu.make_async_copy(source_hbm, source, source_sem)
    source_copy.start()

    def chunk_copy(chunk):
        part = pl.ds(chunk * CHUNK, CHUNK)
        return pltpu.make_async_copy(weight_hbm.at[part], weight.at[part], weight_sems.at[chunk])

    for chunk in range(chunks):
        chunk_copy(chunk).start()

    for key in range(GROUPS * ROWS):
        slot_of[key] = -1
    for group in range(GROUPS):
        used[group] = 0

    def plan(entry, carry):
        target = target_ref[entry]
        owner, row = lax.div(target, ROWS), lax.rem(target, ROWS)
        owner_column = lax.div(owner, column_rows)
        lower = lax.rem(owner, column_rows) - position
        group = jnp.where(lower == 0, owner_column, TILE_COLS + (owner_column ^ column))
        key = group * ROWS + row
        known = slot_of[key]
        count = used[group]
        fresh = known < 0
        slot = jnp.where(fresh, group * CAP + count, known)
        slot_of[key] = slot
        used[group] = jnp.where(fresh, count + 1, count)
        entry_slot[entry] = slot
        entry_fresh[entry] = fresh.astype(jnp.int32)
        return carry

    lax.fori_loop(0, entries, plan, 0, unroll=4)

    tail = PADDED - 8
    for slot in range(SLOTS):
        rounded[slot, tail:] = jnp.full((8, BLOCK), ROWS, jnp.bfloat16)
    wide[pl.ds(CHANNELS * ROWS, (PADDED - CHANNELS) * ROWS), :] = jnp.zeros(
        ((PADDED - CHANNELS) * ROWS, BLOCK), jnp.float32
    )
    source_copy.wait()
    wide[pl.ds(0, CHANNELS * ROWS), :] = source[...].astype(jnp.float32)
    for row in range(ROWS):
        field[row] = wide[pl.ds(row, PADDED, stride=ROWS), :].astype(jnp.bfloat16)
    is_mark = lax.broadcasted_iota(jnp.int32, (8, BLOCK), 0) == MARK - tail

    def chunk_step(chunk, carry):
        chunk_copy(chunk).wait()
        for at in range(CHUNK):
            entry = chunk * CHUNK + at
            slot = entry_slot[entry]
            row = lax.rem(target_ref[entry], ROWS)
            product = jnp.dot(
                field[index_ref[entry]], weight[entry], preferred_element_type=jnp.float32
            )
            total = jnp.where(entry_fresh[entry] == 1, 0.0, sums[slot]) + product
            sums[slot] = total
            marked = jnp.where(is_mark, row.astype(jnp.float32), total[tail:])
            rounded[slot] = jnp.concatenate([total[:tail], marked], axis=0).astype(jnp.bfloat16)
        return carry

    lax.fori_loop(0, chunks, chunk_step, 0)
    copies = [
        pltpu.make_async_copy(
            rounded.at[pl.ds(0, SLOTS // 2)], same_out, out_sems.at[0]
        )
    ]
    for group in range(TILE_COLS):
        part = rounded.at[pl.ds((TILE_COLS + group) * CAP, CAP)]
        copies.append(pltpu.make_async_copy(part, next_outs[group], out_sems.at[1 + group]))
    for copy in copies:
        copy.start()
    for copy in copies:
        copy.wait()


def regrid(target, source_index, field, weights, column_rows):
    piece = jax.ShapeDtypeStruct((CAP, PADDED, BLOCK), jnp.bfloat16)
    same = jax.ShapeDtypeStruct((TILE_COLS * CAP, PADDED, BLOCK), jnp.bfloat16)
    hbm = pl.BlockSpec(memory_space=pl.ANY)
    entries = weights.shape[0]
    return pl.pallas_call(
        functools.partial(regrid_kernel, column_rows),
        in_specs=[smem(), smem(), hbm, hbm],
        out_specs=[hbm] * (1 + TILE_COLS),
        out_shape=[same] + [piece] * TILE_COLS,
        scratch_shapes=[
            pltpu.VMEM(field.shape, jnp.bfloat16),
            pltpu.VMEM(weights.shape, jnp.bfloat16),
            pltpu.VMEM((PADDED * ROWS, BLOCK), jnp.float32),
            pltpu.VMEM((ROWS, PADDED, BLOCK), jnp.bfloat16),
            pltpu.VMEM((SLOTS, PADDED, BLOCK), jnp.float32),
            pltpu.VMEM((SLOTS, PADDED, BLOCK), jnp.bfloat16),
            pltpu.SMEM((GROUPS * ROWS,), jnp.int32),
            pltpu.SMEM((GROUPS,), jnp.int32),
            pltpu.SMEM((entries,), jnp.int32),
            pltpu.SMEM((entries,), jnp.int32),
            pltpu.SemaphoreType.DMA,
            pltpu.SemaphoreType.DMA((entries // CHUNK,)),
            pltpu.SemaphoreType.DMA((1 + TILE_COLS,)),
        ],
        compiler_params=pltpu.CompilerParams(vmem_limit_bytes=FULL_VMEM),
        name="regrid",
    )(target, source_index, field, weights)


def gather_kernel(column_rows, flip_ref, gain_ref, same, *rest):
    nexts = rest[:TILE_COLS]
    (
        gridded_out,
        gridded,
        normed,
        upward,
        downward,
        strip_out,
        summed,
        turned,
        marks,
        rows,
        mark_sem,
    ) = rest[TILE_COLS:]
    position = lax.rem(lax.axis_index("tile"), column_rows)
    half = SLOTS // 2
    lane = lanes((1, BLOCK))
    mark = jnp.zeros((1, BLOCK), jnp.float32)
    for slot in range(SLOTS):
        piece = same.at[slot] if slot < half else nexts[slot // CAP - TILE_COLS].at[slot % CAP]
        mark = jnp.where(lane == slot, piece[MARK : MARK + 1].astype(jnp.float32), mark)
    marks[...] = mark.astype(jnp.int32)
    copy = pltpu.make_async_copy(marks, rows, mark_sem)
    copy.start()
    summed[...] = jnp.zeros_like(summed)
    copy.wait()

    def add(slot, piece):
        row = rows[0, slot]
        summed[row] = summed[row] + piece.astype(jnp.float32)

    def add_same(step, carry):
        for at in range(CAP):
            add(step * CAP + at, same[step * CAP + at])
        return carry

    lax.fori_loop(0, TILE_COLS, add_same, 0)

    @pl.when(position > 0)
    def _():
        for group in range(TILE_COLS):
            for place in range(CAP):
                add(half + group * CAP + place, nexts[group][place])

    gain = gain_ref[...]
    lane = lanes((PADDED, BLOCK))
    channel = lax.broadcasted_iota(jnp.int32, (PADDED, BLOCK), 0)
    strip = jnp.zeros((PADDED, BLOCK), jnp.float32)
    for row in range(ROWS):
        rounded = summed[row].astype(jnp.bfloat16)
        gridded[row] = rounded
        value = rounded.astype(jnp.float32)
        turned[pl.ds(row, PADDED, stride=ROWS), :] = value
        value = jnp.where(channel < CHANNELS, value, 0.0)
        square = jnp.sum(value * value, axis=0, keepdims=True) * (1.0 / CHANNELS)
        scaled = (value * lax.rsqrt(square + EPSILON) * gain).astype(jnp.bfloat16)
        normed[row] = scaled
        if row < 2:
            upward[row] = scaled
        if row >= ROWS - 2:
            downward[row - ROWS + 2] = scaled
        scaled = scaled.astype(jnp.float32)
        for place, column in enumerate(STRIP_COLUMNS):
            at = place * ROWS + row
            strip = jnp.where(lane == at, pltpu.roll(scaled, (at - column) % BLOCK, 1), strip)
    for side in range(2):
        strip = jnp.where(channel == CHANNELS + side, flip_ref[0, side].astype(jnp.float32), strip)
    strip = strip.astype(jnp.bfloat16)
    upward[2] = strip
    downward[2] = strip
    strip_out[...] = strip
    gridded_out[...] = turned[pl.ds(0, CHANNELS * ROWS), :].astype(jnp.bfloat16)


FIELD = jax.ShapeDtypeStruct((ROWS, PADDED, BLOCK), jnp.bfloat16)
RIM = jax.ShapeDtypeStruct((3, PADDED, BLOCK), jnp.bfloat16)
STRIP_COLUMNS = (0, 1, BLOCK - 2, BLOCK - 1)
STRIP = jax.ShapeDtypeStruct((PADDED, BLOCK), jnp.bfloat16)


def gather_rows(column_rows, edge_flip, gain, same, nexts):
    return pl.pallas_call(
        functools.partial(gather_kernel, column_rows),
        in_specs=[smem()] + [vmem()] * (2 + TILE_COLS),
        out_specs=[vmem()] * 6,
        out_shape=[
            jax.ShapeDtypeStruct((CHANNELS * ROWS, BLOCK), jnp.bfloat16),
            FIELD,
            FIELD,
            RIM,
            RIM,
            STRIP,
        ],
        scratch_shapes=[
            pltpu.VMEM((ROWS + 1, PADDED, BLOCK), jnp.float32),
            pltpu.VMEM((PADDED * ROWS, BLOCK), jnp.float32),
            pltpu.VMEM((1, SLOTS), jnp.int32),
            pltpu.SMEM((1, SLOTS), jnp.int32),
            pltpu.SemaphoreType.DMA,
        ],
        compiler_params=pltpu.CompilerParams(vmem_limit_bytes=VMEM_LIMIT),
        name="gather_rows",
    )(edge_flip, gain, same, *nexts)


def strip_shifts(column_rows):
    around = range(-2, 3)
    shifts = {near + far for near in around for far in (-column_rows, 0, column_rows)}
    return sorted(shifts - {-1, 0, 1})


def conv_kernel(
    column_rows, first_taps_ref, second_taps_ref, field, gridded, above, below, own_strip, *rest
):
    shifts = strip_shifts(column_rows)
    far_strips = rest[: len(shifts)]
    smoothed, hidden, partial, turned = rest[len(shifts) :]
    count = lax.axis_size("tile")
    tile = lax.axis_index("tile")
    lane = lanes((PADDED, BLOCK))
    last = ROWS + 1
    R = column_rows

    strips = {-1: above[2], 0: own_strip[...], 1: below[2]}
    strips.update((shift, ref[...]) for shift, ref in zip(shifts, far_strips))
    strips = {shift: value.astype(jnp.float32) for shift, value in strips.items()}

    def place(shift):
        return lax.rem(tile + shift + count, count)

    def ends(shift, before, after, middle):
        before = jnp.where(place(shift) > 0, before, 0.0)
        after = jnp.where(place(shift) < count - 1, after, 0.0)
        return jnp.where(lane == 0, before, jnp.where(lane == last, after, middle))

    memo = {}

    def padded_column(shift, which):
        if (shift, which) not in memo:
            base = which * ROWS
            memo[shift, which] = ends(
                shift,
                pltpu.roll(strips[shift - 1], (1 - base - ROWS) % BLOCK, 1),
                pltpu.roll(strips[shift + 1], (last - base) % BLOCK, 1),
                pltpu.roll(strips[shift], (1 - base) % BLOCK, 1),
            )
        return memo[shift, which]

    row_id = lax.broadcasted_iota(jnp.int32, (BLOCK, BLOCK), 0)
    reversal = (row_id + lanes((BLOCK, BLOCK)) == last).astype(jnp.bfloat16)

    def reversed_lanes(planes):
        stacked = jnp.concatenate(planes, axis=0).astype(jnp.bfloat16)
        turned_round = jnp.dot(stacked, reversal, preferred_element_type=jnp.float32)
        return [turned_round[at * PADDED : (at + 1) * PADDED] for at in range(len(planes))]

    west_of = {shift: (shift - R, 3) for shift in {-1, 0, 1, R - 1, R, R + 1}}
    east_of = {shift: (shift + R, 0) for shift in {-1, 0, 1, -R - 1, -R, -R + 1}}
    keys = sorted(set(west_of.values()) | set(east_of.values()))
    flipped = dict(zip(keys, reversed_lanes([padded_column(*key) for key in keys])))

    def side(shift, which, table):
        key = table[shift]
        flip = strips[shift][CHANNELS + which : CHANNELS + which + 1] > 0.5
        return jnp.where(flip, flipped[key], padded_column(*key))

    west = {shift: side(shift, 0, west_of) for shift in sorted(west_of)}
    east = {shift: side(shift, 1, east_of) for shift in sorted(east_of)}

    def columns(value, west_plane, west_row, east_plane, east_row):
        value = value.astype(jnp.float32)
        west_value = pltpu.roll(west_plane, (BLOCK - west_row) % BLOCK, 1)
        east_value = pltpu.roll(east_plane, BLOCK - 1 - east_row, 1)
        left = jnp.where(lane == 0, west_value, pltpu.roll(value, 1, 1))
        right = jnp.where(lane == BLOCK - 1, east_value, pltpu.roll(value, BLOCK - 1, 1))
        return jnp.concatenate([left, value, right], axis=0).astype(jnp.bfloat16)

    def tap_sums(taps, one, two):
        both = jnp.concatenate([one, two], axis=1)
        result = jnp.dot(taps, both, preferred_element_type=jnp.float32)
        return result[:, :BLOCK], result[:, BLOCK:]

    def all_rows(taps, read, west_plane, east_plane):
        for p in range(0, ROWS + 2, 2):
            partial[p], partial[p + 1] = tap_sums(
                taps,
                columns(read(p), west_plane, p, east_plane, p),
                columns(read(p + 1), west_plane, p + 1, east_plane, p + 1),
            )

    def conv_row(row):
        return (
            partial[row, :PADDED]
            + partial[row + 1, PADDED : 2 * PADDED]
            + partial[row + 2, 2 * PADDED :]
        )

    def activated(value):
        return jax.nn.gelu(value).astype(jnp.bfloat16)

    first_taps = first_taps_ref[...]
    up = [jnp.where(tile > 0, above[at], 0.0) for at in range(2)]
    down = [jnp.where(tile < count - 1, below[at], 0.0) for at in range(2)]

    def read_normed(p):
        return up[1] if p == 0 else down[0] if p == last else field[p - 1]

    all_rows(first_taps, read_normed, west[0], east[0])
    for row in range(ROWS):
        hidden[row + 1] = activated(conv_row(row))

    upper, lower = 0.0, 0.0
    for at, (high, low) in enumerate(
        [(up[0], field[ROWS - 1]), (up[1], down[0]), (field[0], down[1])]
    ):
        from_row = ROWS - 1 + at
        one, two = tap_sums(
            first_taps,
            columns(high, west[-1], from_row, east[-1], from_row),
            columns(low, west[1], at, east[1], at),
        )
        upper += one[at * PADDED : (at + 1) * PADDED]
        lower += two[at * PADDED : (at + 1) * PADDED]
    hidden[0] = jnp.where(tile > 0, activated(upper), 0.0)
    hidden[last] = jnp.where(tile < count - 1, activated(lower), 0.0)

    def along(result):
        raw = (
            result[:PADDED]
            + pltpu.roll(result[PADDED : 2 * PADDED], BLOCK - 1, 1)
            + pltpu.roll(result[2 * PADDED :], BLOCK - 2, 1)
        )
        return activated(raw).astype(jnp.float32)

    west_hidden, east_hidden = {}, {}
    for at in (-1, 0, 1):
        q = at - R
        one = [padded_column(q, 2), padded_column(q, 3), east[q]]
        q = at + R
        two = [west[q], padded_column(q, 0), padded_column(q, 1)]
        one, two = tap_sums(
            first_taps,
            jnp.concatenate(one, axis=0).astype(jnp.bfloat16),
            jnp.concatenate(two, axis=0).astype(jnp.bfloat16),
        )
        west_hidden[at], east_hidden[at] = along(one), along(two)

    def hidden_side(shift, values):
        return ends(
            shift,
            pltpu.roll(values[-1], BLOCK - ROWS + 1, 1),
            pltpu.roll(values[1], last, 1),
            pltpu.roll(values[0], 1, 1),
        )

    sides = [hidden_side(-R, west_hidden), hidden_side(R, east_hidden)]
    for which, turned_side in enumerate(reversed_lanes(sides)):
        flip = strips[0][CHANNELS + which : CHANNELS + which + 1] > 0.5
        sides[which] = jnp.where(flip, turned_side, sides[which])

    all_rows(second_taps_ref[...], lambda p: hidden[p], sides[0], sides[1])
    for row in range(ROWS):
        turned[pl.ds(row, PADDED, stride=ROWS), :] = gridded[row].astype(jnp.float32) + conv_row(row)
    smoothed[...] = turned[pl.ds(0, CHANNELS * ROWS), :].astype(jnp.bfloat16)


def convolutions(column_rows, first_taps, second_taps, field, gridded, rims, own_strip, strips):
    operands = [first_taps, second_taps, field, gridded, *rims, own_strip, *strips]
    return pl.pallas_call(
        functools.partial(conv_kernel, column_rows),
        in_specs=[vmem()] * len(operands),
        out_specs=vmem(),
        out_shape=jax.ShapeDtypeStruct((CHANNELS * ROWS, BLOCK), jnp.bfloat16),
        scratch_shapes=[
            pltpu.VMEM((ROWS + 2, PADDED, BLOCK), jnp.bfloat16),
            pltpu.VMEM((ROWS + 2, 3 * PADDED, BLOCK), jnp.float32),
            pltpu.VMEM((PADDED * ROWS, BLOCK), jnp.float32),
        ],
        compiler_params=pltpu.CompilerParams(vmem_limit_bytes=VMEM_LIMIT),
        name="convolutions",
    )(*operands)


def tap_matrix(kernel):
    pad = PADDED - CHANNELS
    taps = jnp.pad(kernel, ((0, 0), (0, pad), (0, pad))).reshape(3, 3, PADDED, PADDED)
    return taps.transpose(0, 2, 1, 3).reshape(3 * PADDED, 3 * PADDED)


def from_shift(value, shift):
    count = lax.axis_size("tile")
    return lax.ppermute(value, "tile", [(i, (i - shift) % count) for i in range(count)])


def per_device(
    source, weights, block_source, block_target, edge_flip, norm_gain, first_kernel, second_kernel
):
    count = lax.axis_size("tile")
    column_rows = count // TILE_COLS
    field = source.reshape(ROWS, CHANNELS, BLOCK).transpose(1, 0, 2).reshape(-1, BLOCK)
    same, *nexts = regrid(block_target, block_source, field, weights, column_rows)

    for across in reversed(range(TILE_COLS)):
        pairs = [
            (c * column_rows + p, (c ^ across) * column_rows + p + 1)
            for c in range(TILE_COLS)
            for p in range(column_rows - 1)
        ]
        nexts[across] = lax.ppermute(nexts[across], "tile", pairs)
    same = lax.all_to_all(
        same,
        "tile",
        0,
        0,
        axis_index_groups=[
            [c * column_rows + p for c in range(TILE_COLS)] for p in range(column_rows)
        ],
        tiled=True,
    )

    gain = jnp.broadcast_to(
        jnp.pad(norm_gain, (0, PADDED - CHANNELS))[:, None], (PADDED, BLOCK)
    )
    first_taps, second_taps = tap_matrix(first_kernel), tap_matrix(second_kernel)
    same, nexts, gain, first_taps, second_taps = lax.optimization_barrier(
        (same, nexts, gain, first_taps, second_taps)
    )
    gridded_out, gridded, normed, upward, downward, strip = gather_rows(
        column_rows, edge_flip, gain, same, nexts
    )
    rims = [from_shift(downward, -1), from_shift(upward, 1)]
    strips = [from_shift(strip, shift) for shift in strip_shifts(column_rows)]
    smoothed = convolutions(
        column_rows, first_taps, second_taps, normed, gridded, rims, strip, strips
    )

    def placed(value):
        return value.reshape(CHANNELS, ROWS, BLOCK).transpose(1, 0, 2)[:, None]

    return placed(gridded_out), placed(smoothed)


def solution(mesh):
    in_specs = (
        P("tile", "groups", None, None),
        P("tile", None, None),
        P("tile"),
        P("tile"),
        P("tile", None),
        P(),
        P(),
        P(),
    )
    out_specs = (P("tile", "groups", None, None), P("tile", "groups", None, None))
    return jax.shard_map(
        per_device, mesh=mesh, in_specs=in_specs, out_specs=out_specs, check_vma=False
    )
```

```python
import functools

import jax
import jax.numpy as jnp
from jax import lax
from jax.experimental import pallas as pl
from jax.experimental.pallas import tpu as pltpu
from jax.sharding import PartitionSpec as P

BLOCK = 128
CHANNELS = 69
PADDED = 72
ROWS = 32
TILE_COLS = 8
CAP = 8
GROUPS = 2 * TILE_COLS
SLOTS = GROUPS * CAP
CHUNK = 32
MARK = CHANNELS
EPSILON = 1e-05
VMEM_LIMIT = 40 * 1024 * 1024
FULL_VMEM = 60 * 1024 * 1024


def vmem():
    return pl.BlockSpec(memory_space=pltpu.VMEM)


def smem():
    return pl.BlockSpec(memory_space=pltpu.SMEM)


def split(value, size):
    if size & (size - 1) == 0:
        return value >> (size.bit_length() - 1), value & (size - 1)
    return lax.div(value, size), lax.rem(value, size)


def lanes(shape):
    return lax.broadcasted_iota(jnp.int32, shape, len(shape) - 1)


def regrid_kernel(column_rows, target_ref, index_ref, source_hbm, weight_hbm, *rest):
    same_out, next_outs = rest[0], rest[1 : 1 + TILE_COLS]
    (
        source,
        weight,
        wide,
        field,
        sums,
        rounded,
        slot_of,
        used,
        entry_slot,
        entry_fresh,
        source_sem,
        weight_sems,
        out_sems,
    ) = rest[1 + TILE_COLS :]
    entries = weight.shape[0]
    chunks = entries // CHUNK
    tile = lax.axis_index("tile")
    column, position = split(tile, column_rows)

    source_copy = pltpu.make_async_copy(source_hbm, source, source_sem)
    source_copy.start()

    def chunk_copy(chunk):
        part = pl.ds(chunk * CHUNK, CHUNK)
        return pltpu.make_async_copy(weight_hbm.at[part], weight.at[part], weight_sems.at[chunk])

    for chunk in range(chunks):
        chunk_copy(chunk).start()

    for key in range(GROUPS * ROWS):
        slot_of[key] = -1
    for group in range(GROUPS):
        used[group] = 0

    def plan(entry, carry):
        target = target_ref[entry]
        owner, row = split(target, ROWS)
        owner_column, owner_position = split(owner, column_rows)
        same = owner_position == position
        group = jnp.where(same, owner_column, TILE_COLS + (owner_column ^ column))
        key = group * ROWS + row
        known = slot_of[key]
        count = used[group]
        fresh = known < 0
        slot = jnp.where(fresh, group * CAP + count, known)
        slot_of[key] = slot
        used[group] = jnp.where(fresh, count + 1, count)
        entry_slot[entry] = slot
        entry_fresh[entry] = fresh.astype(jnp.int32)
        return carry

    lax.fori_loop(0, entries, plan, 0, unroll=4)

    tail = PADDED - 8
    for slot in range(SLOTS):
        rounded[slot, tail:] = jnp.full((8, BLOCK), ROWS, jnp.bfloat16)
    wide[pl.ds(CHANNELS * ROWS, (PADDED - CHANNELS) * ROWS), :] = jnp.zeros(
        ((PADDED - CHANNELS) * ROWS, BLOCK), jnp.float32
    )
    source_copy.wait()
    wide[pl.ds(0, CHANNELS * ROWS), :] = source[...].astype(jnp.float32)
    for row in range(ROWS):
        field[row] = wide[pl.ds(row, PADDED, stride=ROWS), :].astype(jnp.bfloat16)
    is_mark = lax.broadcasted_iota(jnp.int32, (8, BLOCK), 0) == MARK - tail

    def chunk_step(chunk, carry):
        chunk_copy(chunk).wait()
        for at in range(CHUNK):
            entry = chunk * CHUNK + at
            slot = entry_slot[entry]
            row = split(target_ref[entry], ROWS)[1]
            product = jnp.dot(
                field[index_ref[entry]], weight[entry], preferred_element_type=jnp.float32
            )
            total = jnp.where(entry_fresh[entry] == 1, 0.0, sums[slot]) + product
            sums[slot] = total
            marked = jnp.where(is_mark, row.astype(jnp.float32), total[tail:])
            rounded[slot] = jnp.concatenate([total[:tail], marked], axis=0).astype(jnp.bfloat16)
        return carry

    lax.fori_loop(0, chunks, chunk_step, 0)
    copies = [
        pltpu.make_async_copy(
            rounded.at[pl.ds(0, SLOTS // 2)], same_out, out_sems.at[0]
        )
    ]
    for group in range(TILE_COLS):
        part = rounded.at[pl.ds((TILE_COLS + group) * CAP, CAP)]
        copies.append(pltpu.make_async_copy(part, next_outs[group], out_sems.at[1 + group]))
    for copy in copies:
        copy.start()
    for copy in copies:
        copy.wait()


def regrid(target, source_index, field, weights, column_rows):
    piece = jax.ShapeDtypeStruct((CAP, PADDED, BLOCK), jnp.bfloat16)
    same = jax.ShapeDtypeStruct((TILE_COLS * CAP, PADDED, BLOCK), jnp.bfloat16)
    hbm = pl.BlockSpec(memory_space=pl.ANY)
    entries = weights.shape[0]
    return pl.pallas_call(
        functools.partial(regrid_kernel, column_rows),
        in_specs=[smem(), smem(), hbm, hbm],
        out_specs=[hbm] * (1 + TILE_COLS),
        out_shape=[same] + [piece] * TILE_COLS,
        scratch_shapes=[
            pltpu.VMEM(field.shape, jnp.bfloat16),
            pltpu.VMEM(weights.shape, jnp.bfloat16),
            pltpu.VMEM((PADDED * ROWS, BLOCK), jnp.float32),
            pltpu.VMEM((ROWS, PADDED, BLOCK), jnp.bfloat16),
            pltpu.VMEM((SLOTS, PADDED, BLOCK), jnp.float32),
            pltpu.VMEM((SLOTS, PADDED, BLOCK), jnp.bfloat16),
            pltpu.SMEM((GROUPS * ROWS,), jnp.int32),
            pltpu.SMEM((GROUPS,), jnp.int32),
            pltpu.SMEM((entries,), jnp.int32),
            pltpu.SMEM((entries,), jnp.int32),
            pltpu.SemaphoreType.DMA,
            pltpu.SemaphoreType.DMA((entries // CHUNK,)),
            pltpu.SemaphoreType.DMA((1 + TILE_COLS,)),
        ],
        compiler_params=pltpu.CompilerParams(vmem_limit_bytes=FULL_VMEM),
        name="regrid",
    )(target, source_index, field, weights)


def gather_kernel(column_rows, flip_ref, gain_ref, same, *rest):
    nexts = rest[:TILE_COLS]
    (
        gridded,
        normed,
        upward,
        downward,
        strip_out,
        summed,
        marks,
        rows,
        mark_sem,
    ) = rest[TILE_COLS:]
    position = lax.rem(lax.axis_index("tile"), column_rows)
    half = SLOTS // 2
    lane = lanes((1, BLOCK))
    mark = jnp.zeros((1, BLOCK), jnp.float32)
    for slot in range(SLOTS):
        piece = same.at[slot] if slot < half else nexts[slot // CAP - TILE_COLS].at[slot % CAP]
        mark = jnp.where(lane == slot, piece[MARK : MARK + 1].astype(jnp.float32), mark)
    marks[...] = mark.astype(jnp.int32)
    copy = pltpu.make_async_copy(marks, rows, mark_sem)
    copy.start()
    summed[...] = jnp.zeros_like(summed)
    copy.wait()

    def add(slot, piece):
        row = rows[0, slot]
        summed[row] = summed[row] + piece.astype(jnp.float32)

    def add_same(step, carry):
        for at in range(CAP):
            add(step * CAP + at, same[step * CAP + at])
        return carry

    lax.fori_loop(0, TILE_COLS, add_same, 0)

    @pl.when(position > 0)
    def _():
        for group in range(TILE_COLS):
            for place in range(CAP):
                add(half + group * CAP + place, nexts[group][place])

    gain = gain_ref[...]
    lane = lanes((PADDED, BLOCK))
    channel = lax.broadcasted_iota(jnp.int32, (PADDED, BLOCK), 0)
    strip = jnp.zeros((PADDED, BLOCK), jnp.float32)
    for row in range(ROWS):
        rounded = summed[row].astype(jnp.bfloat16)
        gridded[row] = rounded
        value = rounded.astype(jnp.float32)
        value = jnp.where(channel < CHANNELS, value, 0.0)
        square = jnp.sum(value * value, axis=0, keepdims=True) * (1.0 / CHANNELS)
        scaled = (value * lax.rsqrt(square + EPSILON) * gain).astype(jnp.bfloat16)
        normed[row] = scaled
        if row < 2:
            upward[row] = scaled
        if row >= ROWS - 2:
            downward[row - ROWS + 2] = scaled
        scaled = scaled.astype(jnp.float32)
        for place, column in enumerate(STRIP_COLUMNS):
            at = place * ROWS + row
            strip = jnp.where(lane == at, pltpu.roll(scaled, (at - column) % BLOCK, 1), strip)
    for side in range(2):
        strip = jnp.where(channel == CHANNELS + side, flip_ref[0, side].astype(jnp.float32), strip)
    strip = strip.astype(jnp.bfloat16)
    upward[2] = strip
    downward[2] = strip
    strip_out[...] = strip


FIELD = jax.ShapeDtypeStruct((ROWS, PADDED, BLOCK), jnp.bfloat16)
RIM = jax.ShapeDtypeStruct((3, PADDED, BLOCK), jnp.bfloat16)
STRIP_COLUMNS = (0, 1, BLOCK - 2, BLOCK - 1)
STRIP = jax.ShapeDtypeStruct((PADDED, BLOCK), jnp.bfloat16)


def gather_rows(column_rows, edge_flip, gain, same, nexts):
    return pl.pallas_call(
        functools.partial(gather_kernel, column_rows),
        in_specs=[smem()] + [vmem()] * (2 + TILE_COLS),
        out_specs=[vmem()] * 5,
        out_shape=[FIELD, FIELD, RIM, RIM, STRIP],
        scratch_shapes=[
            pltpu.VMEM((ROWS + 1, PADDED, BLOCK), jnp.float32),
            pltpu.VMEM((1, SLOTS), jnp.int32),
            pltpu.SMEM((1, SLOTS), jnp.int32),
            pltpu.SemaphoreType.DMA,
        ],
        compiler_params=pltpu.CompilerParams(vmem_limit_bytes=VMEM_LIMIT),
        name="gather_rows",
    )(edge_flip, gain, same, *nexts)


def turn_kernel(field, out, turned):
    for row in range(ROWS):
        turned[pl.ds(row, PADDED, stride=ROWS), :] = field[row].astype(jnp.float32)
    out[...] = turned[pl.ds(0, CHANNELS * ROWS), :].astype(jnp.bfloat16)


def channels_first(field):
    return pl.pallas_call(
        turn_kernel,
        in_specs=[vmem()],
        out_specs=vmem(),
        out_shape=jax.ShapeDtypeStruct((CHANNELS * ROWS, BLOCK), jnp.bfloat16),
        scratch_shapes=[pltpu.VMEM((PADDED * ROWS, BLOCK), jnp.float32)],
        compiler_params=pltpu.CompilerParams(vmem_limit_bytes=VMEM_LIMIT),
        name="channels_first",
    )(field)


def strip_plan(column_rows):
    if column_rows == 2:
        return [], 3, 1
    return [-2, 2], column_rows, 2


def conv_kernel(
    column_rows, first_taps_ref, second_taps_ref, field, gridded, above, below, own_strip, *rest
):
    near, far, reach = strip_plan(column_rows)
    near_strips, (west_pack, east_pack) = rest[: len(near)], rest[len(near) : len(near) + 2]
    smoothed, hidden, partial, turned = rest[len(near) + 2 :]
    count = lax.axis_size("tile")
    tile = lax.axis_index("tile")
    lane = lanes((PADDED, BLOCK))
    last = ROWS + 1
    R = column_rows

    strips = {-1: above[2], 0: own_strip[...], 1: below[2]}
    strips.update((shift, ref[...]) for shift, ref in zip(near, near_strips))
    for at in range(-reach, reach + 1):
        strips[at - far], strips[at + far] = west_pack[at + reach], east_pack[at + reach]
    strips = {shift: value.astype(jnp.float32) for shift, value in strips.items()}

    def place(shift):
        return lax.rem(tile + shift + count, count)

    def ends(shift, before, after, middle):
        before = jnp.where(place(shift) > 0, before, 0.0)
        after = jnp.where(place(shift) < count - 1, after, 0.0)
        return jnp.where(lane == 0, before, jnp.where(lane == last, after, middle))

    memo = {}

    def padded_column(shift, which):
        if (shift, which) not in memo:
            base = which * ROWS
            memo[shift, which] = ends(
                shift,
                pltpu.roll(strips[shift - 1], (1 - base - ROWS) % BLOCK, 1),
                pltpu.roll(strips[shift + 1], (last - base) % BLOCK, 1),
                pltpu.roll(strips[shift], (1 - base) % BLOCK, 1),
            )
        return memo[shift, which]

    row_id = lax.broadcasted_iota(jnp.int32, (BLOCK, BLOCK), 0)
    reversal = (row_id + lanes((BLOCK, BLOCK)) == last).astype(jnp.bfloat16)

    def reversed_lanes(planes):
        stacked = jnp.concatenate(planes, axis=0).astype(jnp.bfloat16)
        turned_round = jnp.dot(stacked, reversal, preferred_element_type=jnp.float32)
        return [turned_round[at * PADDED : (at + 1) * PADDED] for at in range(len(planes))]

    west_of = {shift: (shift - R, 3) for shift in {-1, 0, 1, R - 1, R, R + 1}}
    east_of = {shift: (shift + R, 0) for shift in {-1, 0, 1, -R - 1, -R, -R + 1}}
    keys = sorted(set(west_of.values()) | set(east_of.values()))
    flipped = dict(zip(keys, reversed_lanes([padded_column(*key) for key in keys])))

    def side(shift, which, table):
        key = table[shift]
        flip = strips[shift][CHANNELS + which : CHANNELS + which + 1] > 0.5
        return jnp.where(flip, flipped[key], padded_column(*key))

    west = {shift: side(shift, 0, west_of) for shift in sorted(west_of)}
    east = {shift: side(shift, 1, east_of) for shift in sorted(east_of)}

    def columns(value, west_plane, west_row, east_plane, east_row):
        value = value.astype(jnp.float32)
        west_value = pltpu.roll(west_plane, (BLOCK - west_row) % BLOCK, 1)
        east_value = pltpu.roll(east_plane, BLOCK - 1 - east_row, 1)
        left = jnp.where(lane == 0, west_value, pltpu.roll(value, 1, 1))
        right = jnp.where(lane == BLOCK - 1, east_value, pltpu.roll(value, BLOCK - 1, 1))
        return jnp.concatenate([left, value, right], axis=0).astype(jnp.bfloat16)

    def tap_sums(taps, one, two):
        both = jnp.concatenate([one, two], axis=1)
        result = jnp.dot(taps, both, preferred_element_type=jnp.float32)
        return result[:, :BLOCK], result[:, BLOCK:]

    def all_rows(taps, read, west_plane, east_plane):
        for p in range(0, ROWS + 2, 2):
            partial[p], partial[p + 1] = tap_sums(
                taps,
                columns(read(p), west_plane, p, east_plane, p),
                columns(read(p + 1), west_plane, p + 1, east_plane, p + 1),
            )

    def conv_row(row):
        return (
            partial[row, :PADDED]
            + partial[row + 1, PADDED : 2 * PADDED]
            + partial[row + 2, 2 * PADDED :]
        )

    def activated(value):
        return jax.nn.gelu(value).astype(jnp.bfloat16)

    first_taps = first_taps_ref[...]
    up = [jnp.where(tile > 0, above[at], 0.0) for at in range(2)]
    down = [jnp.where(tile < count - 1, below[at], 0.0) for at in range(2)]

    def read_normed(p):
        return up[1] if p == 0 else down[0] if p == last else field[p - 1]

    all_rows(first_taps, read_normed, west[0], east[0])
    for row in range(ROWS):
        hidden[row + 1] = activated(conv_row(row))

    upper, lower = 0.0, 0.0
    for at, (high, low) in enumerate(
        [(up[0], field[ROWS - 1]), (up[1], down[0]), (field[0], down[1])]
    ):
        from_row = ROWS - 1 + at
        one, two = tap_sums(
            first_taps,
            columns(high, west[-1], from_row, east[-1], from_row),
            columns(low, west[1], at, east[1], at),
        )
        upper += one[at * PADDED : (at + 1) * PADDED]
        lower += two[at * PADDED : (at + 1) * PADDED]
    hidden[0] = jnp.where(tile > 0, activated(upper), 0.0)
    hidden[last] = jnp.where(tile < count - 1, activated(lower), 0.0)

    def along(result):
        raw = (
            result[:PADDED]
            + pltpu.roll(result[PADDED : 2 * PADDED], BLOCK - 1, 1)
            + pltpu.roll(result[2 * PADDED :], BLOCK - 2, 1)
        )
        return activated(raw).astype(jnp.float32)

    west_hidden, east_hidden = {}, {}
    for at in (-1, 0, 1):
        q = at - R
        one = [padded_column(q, 2), padded_column(q, 3), east[q]]
        q = at + R
        two = [west[q], padded_column(q, 0), padded_column(q, 1)]
        one, two = tap_sums(
            first_taps,
            jnp.concatenate(one, axis=0).astype(jnp.bfloat16),
            jnp.concatenate(two, axis=0).astype(jnp.bfloat16),
        )
        west_hidden[at], east_hidden[at] = along(one), along(two)

    def hidden_side(shift, values):
        return ends(
            shift,
            pltpu.roll(values[-1], BLOCK - ROWS + 1, 1),
            pltpu.roll(values[1], last, 1),
            pltpu.roll(values[0], 1, 1),
        )

    sides = [hidden_side(-R, west_hidden), hidden_side(R, east_hidden)]
    for which, turned_side in enumerate(reversed_lanes(sides)):
        flip = strips[0][CHANNELS + which : CHANNELS + which + 1] > 0.5
        sides[which] = jnp.where(flip, turned_side, sides[which])

    all_rows(second_taps_ref[...], lambda p: hidden[p], sides[0], sides[1])
    for row in range(ROWS):
        turned[pl.ds(row, PADDED, stride=ROWS), :] = gridded[row].astype(jnp.float32) + conv_row(row)
    smoothed[...] = turned[pl.ds(0, CHANNELS * ROWS), :].astype(jnp.bfloat16)


def convolutions(column_rows, first_taps, second_taps, field, gridded, rims, own_strip, strips):
    operands = [first_taps, second_taps, field, gridded, *rims, own_strip, *strips]
    return pl.pallas_call(
        functools.partial(conv_kernel, column_rows),
        in_specs=[vmem()] * len(operands),
        out_specs=vmem(),
        out_shape=jax.ShapeDtypeStruct((CHANNELS * ROWS, BLOCK), jnp.bfloat16),
        scratch_shapes=[
            pltpu.VMEM((ROWS + 2, PADDED, BLOCK), jnp.bfloat16),
            pltpu.VMEM((ROWS + 2, 3 * PADDED, BLOCK), jnp.float32),
            pltpu.VMEM((PADDED * ROWS, BLOCK), jnp.float32),
        ],
        compiler_params=pltpu.CompilerParams(vmem_limit_bytes=VMEM_LIMIT),
        name="convolutions",
    )(*operands)


def tap_matrix(kernel):
    pad = PADDED - CHANNELS
    taps = jnp.pad(kernel, ((0, 0), (0, pad), (0, pad))).reshape(3, 3, PADDED, PADDED)
    return taps.transpose(0, 2, 1, 3).reshape(3 * PADDED, 3 * PADDED)


def from_shift(value, shift):
    count = lax.axis_size("tile")
    return lax.ppermute(value, "tile", [(i, (i - shift) % count) for i in range(count)])


def per_device(
    source, weights, block_source, block_target, edge_flip, norm_gain, first_kernel, second_kernel
):
    count = lax.axis_size("tile")
    column_rows = count // TILE_COLS
    field = source.reshape(ROWS, CHANNELS, BLOCK).transpose(1, 0, 2).reshape(-1, BLOCK)
    same, *nexts = regrid(block_target, block_source, field, weights, column_rows)

    for across in reversed(range(TILE_COLS)):
        pairs = [
            (c * column_rows + p, (c ^ across) * column_rows + p + 1)
            for c in range(TILE_COLS)
            for p in range(column_rows - 1)
        ]
        nexts[across] = lax.ppermute(nexts[across], "tile", pairs)
    same = lax.all_to_all(
        same,
        "tile",
        0,
        0,
        axis_index_groups=[
            [c * column_rows + p for c in range(TILE_COLS)] for p in range(column_rows)
        ],
        tiled=True,
    )

    gain = jnp.broadcast_to(
        jnp.pad(norm_gain, (0, PADDED - CHANNELS))[:, None], (PADDED, BLOCK)
    )
    first_taps, second_taps = tap_matrix(first_kernel), tap_matrix(second_kernel)
    same, nexts, gain, first_taps, second_taps = lax.optimization_barrier(
        (same, nexts, gain, first_taps, second_taps)
    )
    gridded, normed, upward, downward, strip = gather_rows(
        column_rows, edge_flip, gain, same, nexts
    )
    rims = [from_shift(downward, -1), from_shift(upward, 1)]
    near, far, reach = strip_plan(column_rows)
    strips = [from_shift(strip, shift) for shift in near]
    held = {-1: rims[0][2], 0: strip, 1: rims[1][2], **dict(zip(near, strips))}
    pack = jnp.stack([held[at] for at in range(-reach, reach + 1)])
    strips += [from_shift(pack, -far), from_shift(pack, far)]
    gridded_out = channels_first(gridded)
    smoothed = convolutions(
        column_rows, first_taps, second_taps, normed, gridded, rims, strip, strips
    )

    def placed(value):
        return value.reshape(CHANNELS, ROWS, BLOCK).transpose(1, 0, 2)[:, None]

    return placed(gridded_out), placed(smoothed)


def solution(mesh):
    in_specs = (
        P("tile", "groups", None, None),
        P("tile", None, None),
        P("tile"),
        P("tile"),
        P("tile", None),
        P(),
        P(),
        P(),
    )
    out_specs = (P("tile", "groups", None, None), P("tile", "groups", None, None))
    return jax.shard_map(
        per_device, mesh=mesh, in_specs=in_specs, out_specs=out_specs, check_vma=False
    )
```

```python
import functools

import jax
import jax.numpy as jnp
from jax import lax
from jax.experimental import pallas as pl
from jax.experimental.pallas import tpu as pltpu
from jax.sharding import PartitionSpec as P

BLOCK = 128
CHANNELS = 69
PADDED = 72
ROWS = 32
TILE_COLS = 8
CAP = 8
GROUPS = 2 * TILE_COLS
SLOTS = GROUPS * CAP
CHUNK = 32
MARK = CHANNELS
EPSILON = 1e-05
VMEM_LIMIT = 40 * 1024 * 1024
FULL_VMEM = 60 * 1024 * 1024


def vmem():
    return pl.BlockSpec(memory_space=pltpu.VMEM)


def smem():
    return pl.BlockSpec(memory_space=pltpu.SMEM)


def split(value, size):
    if size & (size - 1) == 0:
        return value >> (size.bit_length() - 1), value & (size - 1)
    return lax.div(value, size), lax.rem(value, size)


def lanes(shape):
    return lax.broadcasted_iota(jnp.int32, shape, len(shape) - 1)


def regrid_kernel(column_rows, target_ref, index_ref, source_hbm, weight_hbm, *rest):
    same_out, next_outs = rest[0], rest[1 : 1 + TILE_COLS]
    (
        source,
        weight,
        wide,
        field,
        sums,
        rounded,
        slot_of,
        used,
        entry_slot,
        entry_fresh,
        source_sem,
        weight_sems,
        out_sems,
    ) = rest[1 + TILE_COLS :]
    entries = weight.shape[0]
    chunks = entries // CHUNK
    tile = lax.axis_index("tile")
    column, position = split(tile, column_rows)

    source_copy = pltpu.make_async_copy(source_hbm, source, source_sem)
    source_copy.start()

    def chunk_copy(chunk):
        part = pl.ds(chunk * CHUNK, CHUNK)
        return pltpu.make_async_copy(weight_hbm.at[part], weight.at[part], weight_sems.at[chunk])

    for chunk in range(chunks):
        chunk_copy(chunk).start()

    for key in range(GROUPS * ROWS):
        slot_of[key] = -1
    for group in range(GROUPS):
        used[group] = 0

    def plan(entry, carry):
        target = target_ref[entry]
        owner, row = split(target, ROWS)
        owner_column, owner_position = split(owner, column_rows)
        same = owner_position == position
        group = jnp.where(same, owner_column, TILE_COLS + (owner_column ^ column))
        key = group * ROWS + row
        known = slot_of[key]
        count = used[group]
        fresh = known < 0
        slot = jnp.where(fresh, group * CAP + count, known)
        slot_of[key] = slot
        used[group] = jnp.where(fresh, count + 1, count)
        entry_slot[entry] = slot
        entry_fresh[entry] = fresh.astype(jnp.int32)
        return carry

    lax.fori_loop(0, entries, plan, 0, unroll=4)

    tail = PADDED - 8
    for slot in range(SLOTS):
        rounded[slot, tail:] = jnp.full((8, BLOCK), ROWS, jnp.bfloat16)
    wide[pl.ds(CHANNELS * ROWS, (PADDED - CHANNELS) * ROWS), :] = jnp.zeros(
        ((PADDED - CHANNELS) * ROWS, BLOCK), jnp.float32
    )
    source_copy.wait()
    wide[pl.ds(0, CHANNELS * ROWS), :] = source[...].astype(jnp.float32)
    for row in range(ROWS):
        field[row] = wide[pl.ds(row, PADDED, stride=ROWS), :].astype(jnp.bfloat16)
    is_mark = lax.broadcasted_iota(jnp.int32, (8, BLOCK), 0) == MARK - tail

    def chunk_step(chunk, carry):
        chunk_copy(chunk).wait()
        for at in range(CHUNK):
            entry = chunk * CHUNK + at
            slot = entry_slot[entry]
            row = split(target_ref[entry], ROWS)[1]
            product = jnp.dot(
                field[index_ref[entry]], weight[entry], preferred_element_type=jnp.float32
            )
            total = jnp.where(entry_fresh[entry] == 1, 0.0, sums[slot]) + product
            sums[slot] = total
            marked = jnp.where(is_mark, row.astype(jnp.float32), total[tail:])
            rounded[slot] = jnp.concatenate([total[:tail], marked], axis=0).astype(jnp.bfloat16)
        return carry

    lax.fori_loop(0, chunks, chunk_step, 0)
    copies = [
        pltpu.make_async_copy(
            rounded.at[pl.ds(0, SLOTS // 2)], same_out, out_sems.at[0]
        )
    ]
    for group in range(TILE_COLS):
        part = rounded.at[pl.ds((TILE_COLS + group) * CAP, CAP)]
        copies.append(pltpu.make_async_copy(part, next_outs[group], out_sems.at[1 + group]))
    for copy in copies:
        copy.start()
    for copy in copies:
        copy.wait()


def regrid(target, source_index, field, weights, column_rows):
    piece = jax.ShapeDtypeStruct((CAP, PADDED, BLOCK), jnp.bfloat16)
    same = jax.ShapeDtypeStruct((TILE_COLS * CAP, PADDED, BLOCK), jnp.bfloat16)
    hbm = pl.BlockSpec(memory_space=pl.ANY)
    entries = weights.shape[0]
    return pl.pallas_call(
        functools.partial(regrid_kernel, column_rows),
        in_specs=[smem(), smem(), hbm, hbm],
        out_specs=[hbm] * (1 + TILE_COLS),
        out_shape=[same] + [piece] * TILE_COLS,
        scratch_shapes=[
            pltpu.VMEM(field.shape, jnp.bfloat16),
            pltpu.VMEM(weights.shape, jnp.bfloat16),
            pltpu.VMEM((PADDED * ROWS, BLOCK), jnp.float32),
            pltpu.VMEM((ROWS, PADDED, BLOCK), jnp.bfloat16),
            pltpu.VMEM((SLOTS, PADDED, BLOCK), jnp.float32),
            pltpu.VMEM((SLOTS, PADDED, BLOCK), jnp.bfloat16),
            pltpu.SMEM((GROUPS * ROWS,), jnp.int32),
            pltpu.SMEM((GROUPS,), jnp.int32),
            pltpu.SMEM((entries,), jnp.int32),
            pltpu.SMEM((entries,), jnp.int32),
            pltpu.SemaphoreType.DMA,
            pltpu.SemaphoreType.DMA((entries // CHUNK,)),
            pltpu.SemaphoreType.DMA((1 + TILE_COLS,)),
        ],
        compiler_params=pltpu.CompilerParams(vmem_limit_bytes=FULL_VMEM),
        name="regrid",
    )(target, source_index, field, weights)


def gather_kernel(column_rows, flip_ref, gain_ref, same, *rest):
    nexts = rest[:TILE_COLS]
    (
        gridded,
        normed,
        upward,
        downward,
        strip_out,
        summed,
        marks,
        rows,
        mark_sem,
    ) = rest[TILE_COLS:]
    position = lax.rem(lax.axis_index("tile"), column_rows)
    half = SLOTS // 2
    lane = lanes((1, BLOCK))
    mark = jnp.zeros((1, BLOCK), jnp.float32)
    for slot in range(SLOTS):
        piece = same.at[slot] if slot < half else nexts[slot // CAP - TILE_COLS].at[slot % CAP]
        mark = jnp.where(lane == slot, piece[MARK : MARK + 1].astype(jnp.float32), mark)
    marks[...] = mark.astype(jnp.int32)
    copy = pltpu.make_async_copy(marks, rows, mark_sem)
    copy.start()
    summed[...] = jnp.zeros_like(summed)
    copy.wait()

    def add(slot, piece):
        row = rows[0, slot]
        summed[row] = summed[row] + piece.astype(jnp.float32)

    def add_same(step, carry):
        for at in range(CAP):
            add(step * CAP + at, same[step * CAP + at])
        return carry

    lax.fori_loop(0, TILE_COLS, add_same, 0)

    @pl.when(position > 0)
    def _():
        for group in range(TILE_COLS):
            for place in range(CAP):
                add(half + group * CAP + place, nexts[group][place])

    gain = gain_ref[...]
    lane = lanes((PADDED, BLOCK))
    channel = lax.broadcasted_iota(jnp.int32, (PADDED, BLOCK), 0)
    strip = jnp.zeros((PADDED, BLOCK), jnp.float32)
    for row in range(ROWS):
        rounded = summed[row].astype(jnp.bfloat16)
        gridded[row] = rounded
        value = rounded.astype(jnp.float32)
        value = jnp.where(channel < CHANNELS, value, 0.0)
        square = jnp.sum(value * value, axis=0, keepdims=True) * (1.0 / CHANNELS)
        scaled = (value * lax.rsqrt(square + EPSILON) * gain).astype(jnp.bfloat16)
        normed[row] = scaled
        if row < 2:
            upward[row] = scaled
        if row >= ROWS - 2:
            downward[row - ROWS + 2] = scaled
        scaled = scaled.astype(jnp.float32)
        for place, column in enumerate(STRIP_COLUMNS):
            at = place * ROWS + row
            strip = jnp.where(lane == at, pltpu.roll(scaled, (at - column) % BLOCK, 1), strip)
    for side in range(2):
        strip = jnp.where(channel == CHANNELS + side, flip_ref[0, side].astype(jnp.float32), strip)
    strip = strip.astype(jnp.bfloat16)
    upward[2] = strip
    downward[2] = strip
    strip_out[...] = strip


FIELD = jax.ShapeDtypeStruct((ROWS, PADDED, BLOCK), jnp.bfloat16)
RIM = jax.ShapeDtypeStruct((3, PADDED, BLOCK), jnp.bfloat16)
STRIP_COLUMNS = (0, 1, BLOCK - 2, BLOCK - 1)
STRIP = jax.ShapeDtypeStruct((PADDED, BLOCK), jnp.bfloat16)


def gather_rows(column_rows, edge_flip, gain, same, nexts):
    return pl.pallas_call(
        functools.partial(gather_kernel, column_rows),
        in_specs=[smem()] + [vmem()] * (2 + TILE_COLS),
        out_specs=[vmem()] * 5,
        out_shape=[FIELD, FIELD, RIM, RIM, STRIP],
        scratch_shapes=[
            pltpu.VMEM((ROWS + 1, PADDED, BLOCK), jnp.float32),
            pltpu.VMEM((1, SLOTS), jnp.int32),
            pltpu.SMEM((1, SLOTS), jnp.int32),
            pltpu.SemaphoreType.DMA,
        ],
        compiler_params=pltpu.CompilerParams(vmem_limit_bytes=VMEM_LIMIT),
        name="gather_rows",
    )(edge_flip, gain, same, *nexts)


def turn_kernel(field, out, turned):
    for row in range(ROWS):
        turned[pl.ds(row, PADDED, stride=ROWS), :] = field[row].astype(jnp.float32)
    out[...] = turned[pl.ds(0, CHANNELS * ROWS), :].astype(jnp.bfloat16)


def channels_first(field):
    return pl.pallas_call(
        turn_kernel,
        in_specs=[vmem()],
        out_specs=vmem(),
        out_shape=jax.ShapeDtypeStruct((CHANNELS * ROWS, BLOCK), jnp.bfloat16),
        scratch_shapes=[pltpu.VMEM((PADDED * ROWS, BLOCK), jnp.float32)],
        compiler_params=pltpu.CompilerParams(vmem_limit_bytes=VMEM_LIMIT),
        name="channels_first",
    )(field)


def strip_plan(column_rows):
    if column_rows == 2:
        return [], 3, 1
    return [-2, 2], column_rows, 2


def conv_kernel(
    column_rows, first_taps_ref, second_taps_ref, field, gridded, above, below, own_strip, *rest
):
    near, far, reach = strip_plan(column_rows)
    near_strips, (west_pack, east_pack) = rest[: len(near)], rest[len(near) : len(near) + 2]
    smoothed, hidden, partial, turned = rest[len(near) + 2 :]
    count = lax.axis_size("tile")
    tile = lax.axis_index("tile")
    lane = lanes((PADDED, BLOCK))
    last = ROWS + 1
    R = column_rows

    strips = {-1: above[2], 0: own_strip[...], 1: below[2]}
    strips.update((shift, ref[...]) for shift, ref in zip(near, near_strips))
    for at in range(-reach, reach + 1):
        strips[at - far], strips[at + far] = west_pack[at + reach], east_pack[at + reach]
    strips = {shift: value.astype(jnp.float32) for shift, value in strips.items()}

    def place(shift):
        return lax.rem(tile + shift + count, count)

    def ends(shift, before, after, middle):
        before = jnp.where(place(shift) > 0, before, 0.0)
        after = jnp.where(place(shift) < count - 1, after, 0.0)
        return jnp.where(lane == 0, before, jnp.where(lane == last, after, middle))

    memo = {}

    def padded_column(shift, which):
        if (shift, which) not in memo:
            base = which * ROWS
            memo[shift, which] = ends(
                shift,
                pltpu.roll(strips[shift - 1], (1 - base - ROWS) % BLOCK, 1),
                pltpu.roll(strips[shift + 1], (last - base) % BLOCK, 1),
                pltpu.roll(strips[shift], (1 - base) % BLOCK, 1),
            )
        return memo[shift, which]

    row_id = lax.broadcasted_iota(jnp.int32, (BLOCK, BLOCK), 0)
    reversal = (row_id + lanes((BLOCK, BLOCK)) == last).astype(jnp.bfloat16)

    def reversed_lanes(planes):
        stacked = jnp.concatenate(planes, axis=0).astype(jnp.bfloat16)
        turned_round = jnp.dot(stacked, reversal, preferred_element_type=jnp.float32)
        return [turned_round[at * PADDED : (at + 1) * PADDED] for at in range(len(planes))]

    west_of = {shift: (shift - R, 3) for shift in {-1, 0, 1, R - 1, R, R + 1}}
    east_of = {shift: (shift + R, 0) for shift in {-1, 0, 1, -R - 1, -R, -R + 1}}
    keys = sorted(set(west_of.values()) | set(east_of.values()))
    flipped = dict(zip(keys, reversed_lanes([padded_column(*key) for key in keys])))

    def side(shift, which, table):
        key = table[shift]
        flip = strips[shift][CHANNELS + which : CHANNELS + which + 1] > 0.5
        return jnp.where(flip, flipped[key], padded_column(*key))

    west = {shift: side(shift, 0, west_of) for shift in sorted(west_of)}
    east = {shift: side(shift, 1, east_of) for shift in sorted(east_of)}

    def columns(value, west_plane, west_row, east_plane, east_row):
        value = value.astype(jnp.float32)
        west_value = pltpu.roll(west_plane, (BLOCK - west_row) % BLOCK, 1)
        east_value = pltpu.roll(east_plane, BLOCK - 1 - east_row, 1)
        left = jnp.where(lane == 0, west_value, pltpu.roll(value, 1, 1))
        right = jnp.where(lane == BLOCK - 1, east_value, pltpu.roll(value, BLOCK - 1, 1))
        return jnp.concatenate([left, value, right], axis=0).astype(jnp.bfloat16)

    def tap_sums(taps, one, two):
        both = jnp.concatenate([one, two], axis=1)
        result = jnp.dot(taps, both, preferred_element_type=jnp.float32)
        return result[:, :BLOCK], result[:, BLOCK:]

    def all_rows(taps, read, west_plane, east_plane):
        for p in range(0, ROWS + 2, 2):
            partial[p], partial[p + 1] = tap_sums(
                taps,
                columns(read(p), west_plane, p, east_plane, p),
                columns(read(p + 1), west_plane, p + 1, east_plane, p + 1),
            )

    def conv_row(row):
        return (
            partial[row, :PADDED]
            + partial[row + 1, PADDED : 2 * PADDED]
            + partial[row + 2, 2 * PADDED :]
        )

    def activated(value):
        return jax.nn.gelu(value).astype(jnp.bfloat16)

    first_taps = first_taps_ref[...]
    up = [jnp.where(tile > 0, above[at], 0.0) for at in range(2)]
    down = [jnp.where(tile < count - 1, below[at], 0.0) for at in range(2)]

    def read_normed(p):
        return up[1] if p == 0 else down[0] if p == last else field[p - 1]

    all_rows(first_taps, read_normed, west[0], east[0])
    for row in range(ROWS):
        hidden[row + 1] = activated(conv_row(row))

    upper, lower = 0.0, 0.0
    for at, (high, low) in enumerate(
        [(up[0], field[ROWS - 1]), (up[1], down[0]), (field[0], down[1])]
    ):
        from_row = ROWS - 1 + at
        one, two = tap_sums(
            first_taps,
            columns(high, west[-1], from_row, east[-1], from_row),
            columns(low, west[1], at, east[1], at),
        )
        upper += one[at * PADDED : (at + 1) * PADDED]
        lower += two[at * PADDED : (at + 1) * PADDED]
    hidden[0] = jnp.where(tile > 0, activated(upper), 0.0)
    hidden[last] = jnp.where(tile < count - 1, activated(lower), 0.0)

    def along(result):
        raw = (
            result[:PADDED]
            + pltpu.roll(result[PADDED : 2 * PADDED], BLOCK - 1, 1)
            + pltpu.roll(result[2 * PADDED :], BLOCK - 2, 1)
        )
        return activated(raw).astype(jnp.float32)

    west_hidden, east_hidden = {}, {}
    for at in (-1, 0, 1):
        q = at - R
        one = [padded_column(q, 2), padded_column(q, 3), east[q]]
        q = at + R
        two = [west[q], padded_column(q, 0), padded_column(q, 1)]
        one, two = tap_sums(
            first_taps,
            jnp.concatenate(one, axis=0).astype(jnp.bfloat16),
            jnp.concatenate(two, axis=0).astype(jnp.bfloat16),
        )
        west_hidden[at], east_hidden[at] = along(one), along(two)

    def hidden_side(shift, values):
        return ends(
            shift,
            pltpu.roll(values[-1], BLOCK - ROWS + 1, 1),
            pltpu.roll(values[1], last, 1),
            pltpu.roll(values[0], 1, 1),
        )

    sides = [hidden_side(-R, west_hidden), hidden_side(R, east_hidden)]
    for which, turned_side in enumerate(reversed_lanes(sides)):
        flip = strips[0][CHANNELS + which : CHANNELS + which + 1] > 0.5
        sides[which] = jnp.where(flip, turned_side, sides[which])

    all_rows(second_taps_ref[...], lambda p: hidden[p], sides[0], sides[1])
    for row in range(ROWS):
        turned[pl.ds(row, PADDED, stride=ROWS), :] = gridded[row].astype(jnp.float32) + conv_row(row)
    smoothed[...] = turned[pl.ds(0, CHANNELS * ROWS), :].astype(jnp.bfloat16)


def convolutions(column_rows, first_taps, second_taps, field, gridded, rims, own_strip, strips):
    operands = [first_taps, second_taps, field, gridded, *rims, own_strip, *strips]
    return pl.pallas_call(
        functools.partial(conv_kernel, column_rows),
        in_specs=[vmem()] * len(operands),
        out_specs=vmem(),
        out_shape=jax.ShapeDtypeStruct((CHANNELS * ROWS, BLOCK), jnp.bfloat16),
        scratch_shapes=[
            pltpu.VMEM((ROWS + 2, PADDED, BLOCK), jnp.bfloat16),
            pltpu.VMEM((ROWS + 2, 3 * PADDED, BLOCK), jnp.float32),
            pltpu.VMEM((PADDED * ROWS, BLOCK), jnp.float32),
        ],
        compiler_params=pltpu.CompilerParams(vmem_limit_bytes=VMEM_LIMIT),
        name="convolutions",
    )(*operands)


def tap_matrix(kernel):
    pad = PADDED - CHANNELS
    taps = jnp.pad(kernel, ((0, 0), (0, pad), (0, pad))).reshape(3, 3, PADDED, PADDED)
    return taps.transpose(0, 2, 1, 3).reshape(3 * PADDED, 3 * PADDED)


def from_shift(value, shift):
    count = lax.axis_size("tile")
    return lax.ppermute(value, "tile", [(i, (i - shift) % count) for i in range(count)])


def per_device(
    source, weights, block_source, block_target, edge_flip, norm_gain, first_kernel, second_kernel
):
    count = lax.axis_size("tile")
    column_rows = count // TILE_COLS
    field = source.reshape(ROWS, CHANNELS, BLOCK).transpose(1, 0, 2).reshape(-1, BLOCK)
    same, *nexts = regrid(block_target, block_source, field, weights, column_rows)

    for across in (0, 7, 3, 6, 2, 5, 1, 4):
        pairs = [
            (c * column_rows + p, (c ^ across) * column_rows + p + 1)
            for c in range(TILE_COLS)
            for p in range(column_rows - 1)
        ]
        nexts[across] = lax.ppermute(nexts[across], "tile", pairs)
    same = lax.all_to_all(
        same,
        "tile",
        0,
        0,
        axis_index_groups=[
            [c * column_rows + p for c in range(TILE_COLS)] for p in range(column_rows)
        ],
        tiled=True,
    )

    gain = jnp.broadcast_to(
        jnp.pad(norm_gain, (0, PADDED - CHANNELS))[:, None], (PADDED, BLOCK)
    )
    first_taps, second_taps = tap_matrix(first_kernel), tap_matrix(second_kernel)
    same, nexts, gain, first_taps, second_taps = lax.optimization_barrier(
        (same, nexts, gain, first_taps, second_taps)
    )
    gridded, normed, upward, downward, strip = gather_rows(
        column_rows, edge_flip, gain, same, nexts
    )
    rims = [from_shift(downward, -1), from_shift(upward, 1)]
    near, far, reach = strip_plan(column_rows)
    strips = [from_shift(strip, shift) for shift in near]
    held = {-1: rims[0][2], 0: strip, 1: rims[1][2], **dict(zip(near, strips))}
    pack = jnp.stack([held[at] for at in range(-reach, reach + 1)])
    strips += [from_shift(pack, -far), from_shift(pack, far)]
    gridded_out = channels_first(gridded)
    smoothed = convolutions(
        column_rows, first_taps, second_taps, normed, gridded, rims, strip, strips
    )

    def placed(value):
        return value.reshape(CHANNELS, ROWS, BLOCK).transpose(1, 0, 2)[:, None]

    return placed(gridded_out), placed(smoothed)


def solution(mesh):
    in_specs = (
        P("tile", "groups", None, None),
        P("tile", None, None),
        P("tile"),
        P("tile"),
        P("tile", None),
        P(),
        P(),
        P(),
    )
    out_specs = (P("tile", "groups", None, None), P("tile", "groups", None, None))
    return jax.shard_map(
        per_device, mesh=mesh, in_specs=in_specs, out_specs=out_specs, check_vma=False
    )
```

```python
import functools

import jax
import jax.numpy as jnp
from jax import lax
from jax.experimental import pallas as pl
from jax.experimental.pallas import tpu as pltpu
from jax.sharding import PartitionSpec as P

BLOCK = 128
CHANNELS = 69
PADDED = 72
ROWS = 32
TILE_COLS = 8
CAP = 8
GROUPS = 2 * TILE_COLS
SLOTS = GROUPS * CAP
CHUNK = 32
MARK = CHANNELS
EPSILON = 1e-05
VMEM_LIMIT = 40 * 1024 * 1024
FULL_VMEM = 60 * 1024 * 1024


def vmem():
    return pl.BlockSpec(memory_space=pltpu.VMEM)


def smem():
    return pl.BlockSpec(memory_space=pltpu.SMEM)


def split(value, size):
    if size & (size - 1) == 0:
        return value >> (size.bit_length() - 1), value & (size - 1)
    return lax.div(value, size), lax.rem(value, size)


def lanes(shape):
    return lax.broadcasted_iota(jnp.int32, shape, len(shape) - 1)


def regrid_kernel(column_rows, target_ref, index_ref, source_hbm, weight_hbm, *rest):
    same_out, next_outs = rest[0], rest[1 : 1 + TILE_COLS]
    (
        source,
        weight,
        wide,
        field,
        sums,
        rounded,
        slot_of,
        used,
        entry_slot,
        entry_fresh,
        source_sem,
        weight_sems,
        out_sems,
    ) = rest[1 + TILE_COLS :]
    entries = weight.shape[0]
    chunks = entries // CHUNK
    tile = lax.axis_index("tile")
    column, position = split(tile, column_rows)

    source_copy = pltpu.make_async_copy(source_hbm, source, source_sem)
    source_copy.start()

    def chunk_copy(chunk):
        part = pl.ds(chunk * CHUNK, CHUNK)
        return pltpu.make_async_copy(weight_hbm.at[part], weight.at[part], weight_sems.at[chunk])

    for chunk in range(chunks):
        chunk_copy(chunk).start()

    for key in range(GROUPS * ROWS):
        slot_of[key] = -1
    for group in range(GROUPS):
        used[group] = 0

    def plan(entry, carry):
        target = target_ref[entry]
        owner, row = split(target, ROWS)
        owner_column, owner_position = split(owner, column_rows)
        same = owner_position == position
        group = jnp.where(same, owner_column, TILE_COLS + (owner_column ^ column))
        key = group * ROWS + row
        known = slot_of[key]
        count = used[group]
        fresh = known < 0
        slot = jnp.where(fresh, group * CAP + count, known)
        slot_of[key] = slot
        used[group] = jnp.where(fresh, count + 1, count)
        entry_slot[entry] = slot
        entry_fresh[entry] = fresh.astype(jnp.int32)
        return carry

    lax.fori_loop(0, entries, plan, 0, unroll=4)

    tail = PADDED - 8
    for slot in range(SLOTS):
        rounded[slot, tail:] = jnp.full((8, BLOCK), ROWS, jnp.bfloat16)
    wide[pl.ds(CHANNELS * ROWS, (PADDED - CHANNELS) * ROWS), :] = jnp.zeros(
        ((PADDED - CHANNELS) * ROWS, BLOCK), jnp.float32
    )
    source_copy.wait()
    wide[pl.ds(0, CHANNELS * ROWS), :] = source[...].astype(jnp.float32)
    for row in range(ROWS):
        field[row] = wide[pl.ds(row, PADDED, stride=ROWS), :].astype(jnp.bfloat16)
    is_mark = lax.broadcasted_iota(jnp.int32, (8, BLOCK), 0) == MARK - tail

    def chunk_step(chunk, carry):
        chunk_copy(chunk).wait()
        for at in range(CHUNK):
            entry = chunk * CHUNK + at
            slot = entry_slot[entry]
            row = split(target_ref[entry], ROWS)[1]
            product = jnp.dot(
                field[index_ref[entry]], weight[entry], preferred_element_type=jnp.float32
            )
            total = jnp.where(entry_fresh[entry] == 1, 0.0, sums[slot]) + product
            sums[slot] = total
            marked = jnp.where(is_mark, row.astype(jnp.float32), total[tail:])
            rounded[slot] = jnp.concatenate([total[:tail], marked], axis=0).astype(jnp.bfloat16)
        return carry

    lax.fori_loop(0, chunks, chunk_step, 0)
    copies = [
        pltpu.make_async_copy(
            rounded.at[pl.ds(0, SLOTS // 2)], same_out, out_sems.at[0]
        )
    ]
    for group in range(TILE_COLS):
        part = rounded.at[pl.ds((TILE_COLS + group) * CAP, CAP)]
        copies.append(pltpu.make_async_copy(part, next_outs[group], out_sems.at[1 + group]))
    for copy in copies:
        copy.start()
    for copy in copies:
        copy.wait()


def regrid(target, source_index, field, weights, column_rows):
    piece = jax.ShapeDtypeStruct((CAP, PADDED, BLOCK), jnp.bfloat16)
    same = jax.ShapeDtypeStruct((TILE_COLS * CAP, PADDED, BLOCK), jnp.bfloat16)
    hbm = pl.BlockSpec(memory_space=pl.ANY)
    entries = weights.shape[0]
    return pl.pallas_call(
        functools.partial(regrid_kernel, column_rows),
        in_specs=[smem(), smem(), hbm, hbm],
        out_specs=[hbm] * (1 + TILE_COLS),
        out_shape=[same] + [piece] * TILE_COLS,
        scratch_shapes=[
            pltpu.VMEM(field.shape, jnp.bfloat16),
            pltpu.VMEM(weights.shape, jnp.bfloat16),
            pltpu.VMEM((PADDED * ROWS, BLOCK), jnp.float32),
            pltpu.VMEM((ROWS, PADDED, BLOCK), jnp.bfloat16),
            pltpu.VMEM((SLOTS, PADDED, BLOCK), jnp.float32),
            pltpu.VMEM((SLOTS, PADDED, BLOCK), jnp.bfloat16),
            pltpu.SMEM((GROUPS * ROWS,), jnp.int32),
            pltpu.SMEM((GROUPS,), jnp.int32),
            pltpu.SMEM((entries,), jnp.int32),
            pltpu.SMEM((entries,), jnp.int32),
            pltpu.SemaphoreType.DMA,
            pltpu.SemaphoreType.DMA((entries // CHUNK,)),
            pltpu.SemaphoreType.DMA((1 + TILE_COLS,)),
        ],
        compiler_params=pltpu.CompilerParams(vmem_limit_bytes=FULL_VMEM),
        name="regrid",
    )(target, source_index, field, weights)


def gather_kernel(column_rows, flip_ref, gain_ref, same, *rest):
    nexts = rest[:TILE_COLS]
    (
        gridded,
        normed,
        upward,
        downward,
        strip_out,
        summed,
        marks,
        rows,
        mark_sem,
    ) = rest[TILE_COLS:]
    position = lax.rem(lax.axis_index("tile"), column_rows)
    half = SLOTS // 2
    lane = lanes((1, BLOCK))
    mark = jnp.zeros((1, BLOCK), jnp.float32)
    for slot in range(SLOTS):
        piece = same.at[slot] if slot < half else nexts[slot // CAP - TILE_COLS].at[slot % CAP]
        mark = jnp.where(lane == slot, piece[MARK : MARK + 1].astype(jnp.float32), mark)
    marks[...] = mark.astype(jnp.int32)
    copy = pltpu.make_async_copy(marks, rows, mark_sem)
    copy.start()
    summed[...] = jnp.zeros_like(summed)
    copy.wait()

    def add(slot, piece):
        row = rows[0, slot]
        summed[row] = summed[row] + piece.astype(jnp.float32)

    def add_same(step, carry):
        for at in range(CAP):
            add(step * CAP + at, same[step * CAP + at])
        return carry

    lax.fori_loop(0, TILE_COLS, add_same, 0)

    @pl.when(position > 0)
    def _():
        for group in range(TILE_COLS):
            for place in range(CAP):
                add(half + group * CAP + place, nexts[group][place])

    gain = gain_ref[...]
    lane = lanes((PADDED, BLOCK))
    channel = lax.broadcasted_iota(jnp.int32, (PADDED, BLOCK), 0)
    strip = jnp.zeros((PADDED, BLOCK), jnp.float32)
    for row in range(ROWS):
        rounded = summed[row].astype(jnp.bfloat16)
        gridded[row] = rounded
        value = rounded.astype(jnp.float32)
        value = jnp.where(channel < CHANNELS, value, 0.0)
        square = jnp.sum(value * value, axis=0, keepdims=True) * (1.0 / CHANNELS)
        scaled = (value * lax.rsqrt(square + EPSILON) * gain).astype(jnp.bfloat16)
        normed[row] = scaled
        if row < 2:
            upward[row] = scaled
        if row >= ROWS - 2:
            downward[row - ROWS + 2] = scaled
        scaled = scaled.astype(jnp.float32)
        for place, column in enumerate(STRIP_COLUMNS):
            at = place * ROWS + row
            strip = jnp.where(lane == at, pltpu.roll(scaled, (at - column) % BLOCK, 1), strip)
    for side in range(2):
        strip = jnp.where(channel == CHANNELS + side, flip_ref[0, side].astype(jnp.float32), strip)
    strip = strip.astype(jnp.bfloat16)
    upward[2] = strip
    downward[2] = strip
    strip_out[...] = strip


FIELD = jax.ShapeDtypeStruct((ROWS, PADDED, BLOCK), jnp.bfloat16)
RIM = jax.ShapeDtypeStruct((3, PADDED, BLOCK), jnp.bfloat16)
STRIP_COLUMNS = (0, 1, BLOCK - 2, BLOCK - 1)
STRIP = jax.ShapeDtypeStruct((PADDED, BLOCK), jnp.bfloat16)


def gather_rows(column_rows, edge_flip, gain, same, nexts):
    return pl.pallas_call(
        functools.partial(gather_kernel, column_rows),
        in_specs=[smem()] + [vmem()] * (2 + TILE_COLS),
        out_specs=[vmem()] * 5,
        out_shape=[FIELD, FIELD, RIM, RIM, STRIP],
        scratch_shapes=[
            pltpu.VMEM((ROWS + 1, PADDED, BLOCK), jnp.float32),
            pltpu.VMEM((1, SLOTS), jnp.int32),
            pltpu.SMEM((1, SLOTS), jnp.int32),
            pltpu.SemaphoreType.DMA,
        ],
        compiler_params=pltpu.CompilerParams(vmem_limit_bytes=VMEM_LIMIT),
        name="gather_rows",
    )(edge_flip, gain, same, *nexts)


def turn_kernel(field, out, turned):
    for row in range(ROWS):
        turned[pl.ds(row, PADDED, stride=ROWS), :] = field[row].astype(jnp.float32)
    out[...] = turned[pl.ds(0, CHANNELS * ROWS), :].astype(jnp.bfloat16)


def channels_first(field):
    return pl.pallas_call(
        turn_kernel,
        in_specs=[vmem()],
        out_specs=vmem(),
        out_shape=jax.ShapeDtypeStruct((CHANNELS * ROWS, BLOCK), jnp.bfloat16),
        scratch_shapes=[pltpu.VMEM((PADDED * ROWS, BLOCK), jnp.float32)],
        compiler_params=pltpu.CompilerParams(vmem_limit_bytes=VMEM_LIMIT),
        name="channels_first",
    )(field)


def strip_plan(column_rows):
    if column_rows == 2:
        return [], 3, 1
    return [-2, 2], column_rows, 2


def conv_kernel(
    column_rows, first_taps_ref, second_taps_ref, field, gridded, above, below, own_strip, *rest
):
    near, far, reach = strip_plan(column_rows)
    near_strips, (west_pack, east_pack) = rest[: len(near)], rest[len(near) : len(near) + 2]
    smoothed, hidden, partial, turned = rest[len(near) + 2 :]
    count = lax.axis_size("tile")
    tile = lax.axis_index("tile")
    lane = lanes((PADDED, BLOCK))
    last = ROWS + 1
    R = column_rows

    strips = {-1: above[2], 0: own_strip[...], 1: below[2]}
    strips.update((shift, ref[...]) for shift, ref in zip(near, near_strips))
    for at in range(-reach, reach + 1):
        strips[at - far], strips[at + far] = west_pack[at + reach], east_pack[at + reach]
    strips = {shift: value.astype(jnp.float32) for shift, value in strips.items()}

    def place(shift):
        return lax.rem(tile + shift + count, count)

    def ends(shift, before, after, middle):
        before = jnp.where(place(shift) > 0, before, 0.0)
        after = jnp.where(place(shift) < count - 1, after, 0.0)
        return jnp.where(lane == 0, before, jnp.where(lane == last, after, middle))

    memo = {}

    def padded_column(shift, which):
        if (shift, which) not in memo:
            base = which * ROWS
            memo[shift, which] = ends(
                shift,
                pltpu.roll(strips[shift - 1], (1 - base - ROWS) % BLOCK, 1),
                pltpu.roll(strips[shift + 1], (last - base) % BLOCK, 1),
                pltpu.roll(strips[shift], (1 - base) % BLOCK, 1),
            )
        return memo[shift, which]

    row_id = lax.broadcasted_iota(jnp.int32, (BLOCK, BLOCK), 0)
    reversal = (row_id + lanes((BLOCK, BLOCK)) == last).astype(jnp.bfloat16)

    def reversed_lanes(planes):
        stacked = jnp.concatenate(planes, axis=0).astype(jnp.bfloat16)
        turned_round = jnp.dot(stacked, reversal, preferred_element_type=jnp.float32)
        return [turned_round[at * PADDED : (at + 1) * PADDED] for at in range(len(planes))]

    west_of = {shift: (shift - R, 3) for shift in {-1, 0, 1, R - 1, R, R + 1}}
    east_of = {shift: (shift + R, 0) for shift in {-1, 0, 1, -R - 1, -R, -R + 1}}
    keys = sorted(set(west_of.values()) | set(east_of.values()))
    flipped = dict(zip(keys, reversed_lanes([padded_column(*key) for key in keys])))

    def side(shift, which, table):
        key = table[shift]
        flip = strips[shift][CHANNELS + which : CHANNELS + which + 1] > 0.5
        return jnp.where(flip, flipped[key], padded_column(*key))

    west = {shift: side(shift, 0, west_of) for shift in sorted(west_of)}
    east = {shift: side(shift, 1, east_of) for shift in sorted(east_of)}

    def columns(value, west_plane, west_row, east_plane, east_row):
        value = value.astype(jnp.float32)
        west_value = pltpu.roll(west_plane, (BLOCK - west_row) % BLOCK, 1)
        east_value = pltpu.roll(east_plane, BLOCK - 1 - east_row, 1)
        left = jnp.where(lane == 0, west_value, pltpu.roll(value, 1, 1))
        right = jnp.where(lane == BLOCK - 1, east_value, pltpu.roll(value, BLOCK - 1, 1))
        return jnp.concatenate([left, value, right], axis=0).astype(jnp.bfloat16)

    def tap_sums(taps, one, two):
        both = jnp.concatenate([one, two], axis=1)
        result = jnp.dot(taps, both, preferred_element_type=jnp.float32)
        return result[:, :BLOCK], result[:, BLOCK:]

    def all_rows(taps, read, west_plane, east_plane):
        for p in range(0, ROWS + 2, 2):
            partial[p], partial[p + 1] = tap_sums(
                taps,
                columns(read(p), west_plane, p, east_plane, p),
                columns(read(p + 1), west_plane, p + 1, east_plane, p + 1),
            )

    def conv_row(row):
        return (
            partial[row, :PADDED]
            + partial[row + 1, PADDED : 2 * PADDED]
            + partial[row + 2, 2 * PADDED :]
        )

    def activated(value):
        return jax.nn.gelu(value).astype(jnp.bfloat16)

    first_taps = first_taps_ref[...]
    up = [jnp.where(tile > 0, above[at], 0.0) for at in range(2)]
    down = [jnp.where(tile < count - 1, below[at], 0.0) for at in range(2)]

    def read_normed(p):
        return up[1] if p == 0 else down[0] if p == last else field[p - 1]

    all_rows(first_taps, read_normed, west[0], east[0])
    for row in range(ROWS):
        hidden[row + 1] = activated(conv_row(row))

    upper, lower = 0.0, 0.0
    for at, (high, low) in enumerate(
        [(up[0], field[ROWS - 1]), (up[1], down[0]), (field[0], down[1])]
    ):
        from_row = ROWS - 1 + at
        one, two = tap_sums(
            first_taps,
            columns(high, west[-1], from_row, east[-1], from_row),
            columns(low, west[1], at, east[1], at),
        )
        upper += one[at * PADDED : (at + 1) * PADDED]
        lower += two[at * PADDED : (at + 1) * PADDED]
    hidden[0] = jnp.where(tile > 0, activated(upper), 0.0)
    hidden[last] = jnp.where(tile < count - 1, activated(lower), 0.0)

    def along(result):
        raw = (
            result[:PADDED]
            + pltpu.roll(result[PADDED : 2 * PADDED], BLOCK - 1, 1)
            + pltpu.roll(result[2 * PADDED :], BLOCK - 2, 1)
        )
        return activated(raw).astype(jnp.float32)

    west_hidden, east_hidden = {}, {}
    for at in (-1, 0, 1):
        q = at - R
        one = [padded_column(q, 2), padded_column(q, 3), east[q]]
        q = at + R
        two = [west[q], padded_column(q, 0), padded_column(q, 1)]
        one, two = tap_sums(
            first_taps,
            jnp.concatenate(one, axis=0).astype(jnp.bfloat16),
            jnp.concatenate(two, axis=0).astype(jnp.bfloat16),
        )
        west_hidden[at], east_hidden[at] = along(one), along(two)

    def hidden_side(shift, values):
        return ends(
            shift,
            pltpu.roll(values[-1], BLOCK - ROWS + 1, 1),
            pltpu.roll(values[1], last, 1),
            pltpu.roll(values[0], 1, 1),
        )

    sides = [hidden_side(-R, west_hidden), hidden_side(R, east_hidden)]
    for which, turned_side in enumerate(reversed_lanes(sides)):
        flip = strips[0][CHANNELS + which : CHANNELS + which + 1] > 0.5
        sides[which] = jnp.where(flip, turned_side, sides[which])

    all_rows(second_taps_ref[...], lambda p: hidden[p], sides[0], sides[1])
    for row in range(ROWS):
        turned[pl.ds(row, PADDED, stride=ROWS), :] = gridded[row].astype(jnp.float32) + conv_row(row)
    smoothed[...] = turned[pl.ds(0, CHANNELS * ROWS), :].astype(jnp.bfloat16)


def convolutions(column_rows, first_taps, second_taps, field, gridded, rims, own_strip, strips):
    operands = [first_taps, second_taps, field, gridded, *rims, own_strip, *strips]
    return pl.pallas_call(
        functools.partial(conv_kernel, column_rows),
        in_specs=[vmem()] * len(operands),
        out_specs=vmem(),
        out_shape=jax.ShapeDtypeStruct((CHANNELS * ROWS, BLOCK), jnp.bfloat16),
        scratch_shapes=[
            pltpu.VMEM((ROWS + 2, PADDED, BLOCK), jnp.bfloat16),
            pltpu.VMEM((ROWS + 2, 3 * PADDED, BLOCK), jnp.float32),
            pltpu.VMEM((PADDED * ROWS, BLOCK), jnp.float32),
        ],
        compiler_params=pltpu.CompilerParams(vmem_limit_bytes=VMEM_LIMIT),
        name="convolutions",
    )(*operands)


def tap_matrix(kernel):
    pad = PADDED - CHANNELS
    taps = jnp.pad(kernel, ((0, 0), (0, pad), (0, pad))).reshape(3, 3, PADDED, PADDED)
    return taps.transpose(0, 2, 1, 3).reshape(3 * PADDED, 3 * PADDED)


def from_shift(value, shift):
    count = lax.axis_size("tile")
    return lax.ppermute(value, "tile", [(i, (i - shift) % count) for i in range(count)])


def per_device(
    source, weights, block_source, block_target, edge_flip, norm_gain, first_kernel, second_kernel
):
    count = lax.axis_size("tile")
    column_rows = count // TILE_COLS
    field = source.reshape(ROWS, CHANNELS, BLOCK).transpose(1, 0, 2).reshape(-1, BLOCK)
    same, *nexts = regrid(block_target, block_source, field, weights, column_rows)

    for across in range(TILE_COLS):
        pairs = [
            (c * column_rows + p, (c ^ across) * column_rows + p + 1)
            for c in range(TILE_COLS)
            for p in range(column_rows - 1)
        ]
        nexts[across] = lax.ppermute(nexts[across], "tile", pairs)
    nexts = nexts[::-1]
    same = lax.all_to_all(
        same,
        "tile",
        0,
        0,
        axis_index_groups=[
            [c * column_rows + p for c in range(TILE_COLS)] for p in range(column_rows)
        ],
        tiled=True,
    )

    gain = jnp.broadcast_to(
        jnp.pad(norm_gain, (0, PADDED - CHANNELS))[:, None], (PADDED, BLOCK)
    )
    first_taps, second_taps = tap_matrix(first_kernel), tap_matrix(second_kernel)
    same, nexts, gain, first_taps, second_taps = lax.optimization_barrier(
        (same, nexts, gain, first_taps, second_taps)
    )
    gridded, normed, upward, downward, strip = gather_rows(
        column_rows, edge_flip, gain, same, nexts
    )
    rims = [from_shift(downward, -1), from_shift(upward, 1)]
    near, far, reach = strip_plan(column_rows)
    strips = [from_shift(strip, shift) for shift in near]
    held = {-1: rims[0][2], 0: strip, 1: rims[1][2], **dict(zip(near, strips))}
    pack = jnp.stack([held[at] for at in range(-reach, reach + 1)])
    strips += [from_shift(pack, -far), from_shift(pack, far)]
    gridded_out = channels_first(gridded)
    smoothed = convolutions(
        column_rows, first_taps, second_taps, normed, gridded, rims, strip, strips
    )

    def placed(value):
        return value.reshape(CHANNELS, ROWS, BLOCK).transpose(1, 0, 2)[:, None]

    return placed(gridded_out), placed(smoothed)


def solution(mesh):
    in_specs = (
        P("tile", "groups", None, None),
        P("tile", None, None),
        P("tile"),
        P("tile"),
        P("tile", None),
        P(),
        P(),
        P(),
    )
    out_specs = (P("tile", "groups", None, None), P("tile", "groups", None, None))
    return jax.shard_map(
        per_device, mesh=mesh, in_specs=in_specs, out_specs=out_specs, check_vma=False
    )
```

```python
import functools

import jax
import jax.numpy as jnp
from jax import lax
from jax.experimental import pallas as pl
from jax.experimental.pallas import tpu as pltpu
from jax.sharding import PartitionSpec as P

BLOCK = 128
CHANNELS = 69
PADDED = 72
ROWS = 32
TILE_COLS = 8
CAP = 8
GROUPS = 2 * TILE_COLS
SLOTS = GROUPS * CAP
CHUNK = 32
MARK = CHANNELS
EPSILON = 1e-05
VMEM_LIMIT = 40 * 1024 * 1024
FULL_VMEM = 60 * 1024 * 1024


def vmem():
    return pl.BlockSpec(memory_space=pltpu.VMEM)


def smem():
    return pl.BlockSpec(memory_space=pltpu.SMEM)


def split(value, size):
    if size & (size - 1) == 0:
        return value >> (size.bit_length() - 1), value & (size - 1)
    return lax.div(value, size), lax.rem(value, size)


def lanes(shape):
    return lax.broadcasted_iota(jnp.int32, shape, len(shape) - 1)


def regrid_kernel(column_rows, target_ref, index_ref, source_hbm, weight_hbm, *rest):
    same_out, next_outs = rest[0], rest[1 : 1 + TILE_COLS]
    (
        source,
        weight,
        wide,
        field,
        sums,
        rounded,
        slot_of,
        used,
        entry_slot,
        entry_fresh,
        source_sem,
        weight_sems,
        out_sems,
    ) = rest[1 + TILE_COLS :]
    entries = weight.shape[0]
    chunks = entries // CHUNK
    tile = lax.axis_index("tile")
    column, position = split(tile, column_rows)

    source_copy = pltpu.make_async_copy(source_hbm, source, source_sem)
    source_copy.start()

    def chunk_copy(chunk):
        part = pl.ds(chunk * CHUNK, CHUNK)
        return pltpu.make_async_copy(weight_hbm.at[part], weight.at[part], weight_sems.at[chunk])

    for chunk in range(chunks):
        chunk_copy(chunk).start()

    for key in range(GROUPS * ROWS):
        slot_of[key] = -1
    for group in range(GROUPS):
        used[group] = 0

    def plan(entry, carry):
        target = target_ref[entry]
        owner, row = split(target, ROWS)
        owner_column, owner_position = split(owner, column_rows)
        same = owner_position == position
        group = jnp.where(same, owner_column, TILE_COLS + (owner_column ^ column))
        key = group * ROWS + row
        known = slot_of[key]
        count = used[group]
        fresh = known < 0
        slot = jnp.where(fresh, group * CAP + count, known)
        slot_of[key] = slot
        used[group] = jnp.where(fresh, count + 1, count)
        entry_slot[entry] = slot
        entry_fresh[entry] = fresh.astype(jnp.int32)
        return carry

    lax.fori_loop(0, entries, plan, 0, unroll=4)

    tail = PADDED - 8
    for slot in range(SLOTS):
        rounded[slot, tail:] = jnp.full((8, BLOCK), ROWS, jnp.bfloat16)
    wide[pl.ds(CHANNELS * ROWS, (PADDED - CHANNELS) * ROWS), :] = jnp.zeros(
        ((PADDED - CHANNELS) * ROWS, BLOCK), jnp.float32
    )
    source_copy.wait()
    wide[pl.ds(0, CHANNELS * ROWS), :] = source[...].astype(jnp.float32)
    for row in range(ROWS):
        field[row] = wide[pl.ds(row, PADDED, stride=ROWS), :].astype(jnp.bfloat16)
    is_mark = lax.broadcasted_iota(jnp.int32, (8, BLOCK), 0) == MARK - tail

    def chunk_step(chunk, carry):
        chunk_copy(chunk).wait()
        for at in range(CHUNK):
            entry = chunk * CHUNK + at
            slot = entry_slot[entry]
            row = split(target_ref[entry], ROWS)[1]
            product = jnp.dot(
                field[index_ref[entry]], weight[entry], preferred_element_type=jnp.float32
            )
            total = jnp.where(entry_fresh[entry] == 1, 0.0, sums[slot]) + product
            sums[slot] = total
            marked = jnp.where(is_mark, row.astype(jnp.float32), total[tail:])
            rounded[slot] = jnp.concatenate([total[:tail], marked], axis=0).astype(jnp.bfloat16)
        return carry

    lax.fori_loop(0, chunks, chunk_step, 0)
    copies = [
        pltpu.make_async_copy(
            rounded.at[pl.ds(0, SLOTS // 2)], same_out, out_sems.at[0]
        )
    ]
    for group in range(TILE_COLS):
        part = rounded.at[pl.ds((TILE_COLS + group) * CAP, CAP)]
        copies.append(pltpu.make_async_copy(part, next_outs[group], out_sems.at[1 + group]))
    for copy in copies:
        copy.start()
    for copy in copies:
        copy.wait()


def regrid(target, source_index, field, weights, column_rows):
    piece = jax.ShapeDtypeStruct((CAP, PADDED, BLOCK), jnp.bfloat16)
    same = jax.ShapeDtypeStruct((TILE_COLS * CAP, PADDED, BLOCK), jnp.bfloat16)
    hbm = pl.BlockSpec(memory_space=pl.ANY)
    entries = weights.shape[0]
    return pl.pallas_call(
        functools.partial(regrid_kernel, column_rows),
        in_specs=[smem(), smem(), hbm, hbm],
        out_specs=[hbm] * (1 + TILE_COLS),
        out_shape=[same] + [piece] * TILE_COLS,
        scratch_shapes=[
            pltpu.VMEM(field.shape, jnp.bfloat16),
            pltpu.VMEM(weights.shape, jnp.bfloat16),
            pltpu.VMEM((PADDED * ROWS, BLOCK), jnp.float32),
            pltpu.VMEM((ROWS, PADDED, BLOCK), jnp.bfloat16),
            pltpu.VMEM((SLOTS, PADDED, BLOCK), jnp.float32),
            pltpu.VMEM((SLOTS, PADDED, BLOCK), jnp.bfloat16),
            pltpu.SMEM((GROUPS * ROWS,), jnp.int32),
            pltpu.SMEM((GROUPS,), jnp.int32),
            pltpu.SMEM((entries,), jnp.int32),
            pltpu.SMEM((entries,), jnp.int32),
            pltpu.SemaphoreType.DMA,
            pltpu.SemaphoreType.DMA((entries // CHUNK,)),
            pltpu.SemaphoreType.DMA((1 + TILE_COLS,)),
        ],
        compiler_params=pltpu.CompilerParams(vmem_limit_bytes=FULL_VMEM),
        name="regrid",
    )(target, source_index, field, weights)


def gather_kernel(column_rows, flip_ref, gain_ref, same, *rest):
    nexts = rest[:TILE_COLS]
    (
        gridded,
        normed,
        upward,
        downward,
        strip_out,
        summed,
        marks,
        rows,
        mark_sem,
    ) = rest[TILE_COLS:]
    position = lax.rem(lax.axis_index("tile"), column_rows)
    half = SLOTS // 2
    lane = lanes((1, BLOCK))
    mark = jnp.zeros((1, BLOCK), jnp.float32)
    for slot in range(SLOTS):
        piece = same.at[slot] if slot < half else nexts[slot // CAP - TILE_COLS].at[slot % CAP]
        mark = jnp.where(lane == slot, piece[MARK : MARK + 1].astype(jnp.float32), mark)
    marks[...] = mark.astype(jnp.int32)
    copy = pltpu.make_async_copy(marks, rows, mark_sem)
    copy.start()
    summed[...] = jnp.zeros_like(summed)
    copy.wait()

    def add(slot, piece):
        row = rows[0, slot]
        summed[row] = summed[row] + piece.astype(jnp.float32)

    def add_same(step, carry):
        for at in range(CAP):
            add(step * CAP + at, same[step * CAP + at])
        return carry

    lax.fori_loop(0, TILE_COLS, add_same, 0)

    @pl.when(position > 0)
    def _():
        for group in range(TILE_COLS):
            for place in range(CAP):
                add(half + group * CAP + place, nexts[group][place])

    gain = gain_ref[...]
    lane = lanes((PADDED, BLOCK))
    channel = lax.broadcasted_iota(jnp.int32, (PADDED, BLOCK), 0)
    strip = jnp.zeros((PADDED, BLOCK), jnp.float32)
    for row in range(ROWS):
        rounded = summed[row].astype(jnp.bfloat16)
        gridded[row] = rounded
        value = rounded.astype(jnp.float32)
        value = jnp.where(channel < CHANNELS, value, 0.0)
        square = jnp.sum(value * value, axis=0, keepdims=True) * (1.0 / CHANNELS)
        scaled = (value * lax.rsqrt(square + EPSILON) * gain).astype(jnp.bfloat16)
        normed[row] = scaled
        if row < 2:
            upward[row] = scaled
        if row >= ROWS - 2:
            downward[row - ROWS + 2] = scaled
        scaled = scaled.astype(jnp.float32)
        for place, column in enumerate(STRIP_COLUMNS):
            at = place * ROWS + row
            strip = jnp.where(lane == at, pltpu.roll(scaled, (at - column) % BLOCK, 1), strip)
    for side in range(2):
        strip = jnp.where(channel == CHANNELS + side, flip_ref[0, side].astype(jnp.float32), strip)
    strip = strip.astype(jnp.bfloat16)
    upward[2] = strip
    downward[2] = strip
    strip_out[...] = strip


FIELD = jax.ShapeDtypeStruct((ROWS, PADDED, BLOCK), jnp.bfloat16)
RIM = jax.ShapeDtypeStruct((3, PADDED, BLOCK), jnp.bfloat16)
STRIP_COLUMNS = (0, 1, BLOCK - 2, BLOCK - 1)
STRIP = jax.ShapeDtypeStruct((PADDED, BLOCK), jnp.bfloat16)


def gather_rows(column_rows, edge_flip, gain, same, nexts):
    return pl.pallas_call(
        functools.partial(gather_kernel, column_rows),
        in_specs=[smem()] + [vmem()] * (2 + TILE_COLS),
        out_specs=[vmem()] * 5,
        out_shape=[FIELD, FIELD, RIM, RIM, STRIP],
        scratch_shapes=[
            pltpu.VMEM((ROWS + 1, PADDED, BLOCK), jnp.float32),
            pltpu.VMEM((1, SLOTS), jnp.int32),
            pltpu.SMEM((1, SLOTS), jnp.int32),
            pltpu.SemaphoreType.DMA,
        ],
        compiler_params=pltpu.CompilerParams(vmem_limit_bytes=VMEM_LIMIT),
        name="gather_rows",
    )(edge_flip, gain, same, *nexts)


def turn_kernel(field, out, turned):
    for row in range(ROWS):
        turned[pl.ds(row, PADDED, stride=ROWS), :] = field[row].astype(jnp.float32)
    out[...] = turned[pl.ds(0, CHANNELS * ROWS), :].astype(jnp.bfloat16)


def channels_first(field):
    return pl.pallas_call(
        turn_kernel,
        in_specs=[vmem()],
        out_specs=vmem(),
        out_shape=jax.ShapeDtypeStruct((CHANNELS * ROWS, BLOCK), jnp.bfloat16),
        scratch_shapes=[pltpu.VMEM((PADDED * ROWS, BLOCK), jnp.float32)],
        compiler_params=pltpu.CompilerParams(vmem_limit_bytes=VMEM_LIMIT),
        name="channels_first",
    )(field)


def strip_plan(column_rows):
    if column_rows == 2:
        return [], 3, 1
    return [-2, 2], column_rows, 2


def conv_kernel(
    column_rows, first_taps_ref, second_taps_ref, field, gridded, above, below, own_strip, *rest
):
    near, far, reach = strip_plan(column_rows)
    near_strips, (west_pack, east_pack) = rest[: len(near)], rest[len(near) : len(near) + 2]
    smoothed, hidden, partial, turned = rest[len(near) + 2 :]
    count = lax.axis_size("tile")
    tile = lax.axis_index("tile")
    lane = lanes((PADDED, BLOCK))
    last = ROWS + 1
    R = column_rows

    strips = {-1: above[2], 0: own_strip[...], 1: below[2]}
    strips.update((shift, ref[...]) for shift, ref in zip(near, near_strips))
    for at in range(-reach, reach + 1):
        strips[at - far], strips[at + far] = west_pack[at + reach], east_pack[at + reach]
    strips = {shift: value.astype(jnp.float32) for shift, value in strips.items()}

    def place(shift):
        return lax.rem(tile + shift + count, count)

    def ends(shift, before, after, middle):
        before = jnp.where(place(shift) > 0, before, 0.0)
        after = jnp.where(place(shift) < count - 1, after, 0.0)
        return jnp.where(lane == 0, before, jnp.where(lane == last, after, middle))

    memo = {}

    def padded_column(shift, which):
        if (shift, which) not in memo:
            base = which * ROWS
            memo[shift, which] = ends(
                shift,
                pltpu.roll(strips[shift - 1], (1 - base - ROWS) % BLOCK, 1),
                pltpu.roll(strips[shift + 1], (last - base) % BLOCK, 1),
                pltpu.roll(strips[shift], (1 - base) % BLOCK, 1),
            )
        return memo[shift, which]

    row_id = lax.broadcasted_iota(jnp.int32, (BLOCK, BLOCK), 0)
    reversal = (row_id + lanes((BLOCK, BLOCK)) == last).astype(jnp.bfloat16)

    def reversed_lanes(planes):
        stacked = jnp.concatenate(planes, axis=0).astype(jnp.bfloat16)
        turned_round = jnp.dot(stacked, reversal, preferred_element_type=jnp.float32)
        return [turned_round[at * PADDED : (at + 1) * PADDED] for at in range(len(planes))]

    west_of = {shift: (shift - R, 3) for shift in {-1, 0, 1, R - 1, R, R + 1}}
    east_of = {shift: (shift + R, 0) for shift in {-1, 0, 1, -R - 1, -R, -R + 1}}
    keys = sorted(set(west_of.values()) | set(east_of.values()))
    flipped = dict(zip(keys, reversed_lanes([padded_column(*key) for key in keys])))

    def side(shift, which, table):
        key = table[shift]
        flip = strips[shift][CHANNELS + which : CHANNELS + which + 1] > 0.5
        return jnp.where(flip, flipped[key], padded_column(*key))

    west = {shift: side(shift, 0, west_of) for shift in sorted(west_of)}
    east = {shift: side(shift, 1, east_of) for shift in sorted(east_of)}

    def columns(value, west_plane, west_row, east_plane, east_row):
        value = value.astype(jnp.float32)
        west_value = pltpu.roll(west_plane, (BLOCK - west_row) % BLOCK, 1)
        east_value = pltpu.roll(east_plane, BLOCK - 1 - east_row, 1)
        left = jnp.where(lane == 0, west_value, pltpu.roll(value, 1, 1))
        right = jnp.where(lane == BLOCK - 1, east_value, pltpu.roll(value, BLOCK - 1, 1))
        return jnp.concatenate([left, value, right], axis=0).astype(jnp.bfloat16)

    def tap_sums(taps, one, two):
        both = jnp.concatenate([one, two], axis=1)
        result = jnp.dot(taps, both, preferred_element_type=jnp.float32)
        return result[:, :BLOCK], result[:, BLOCK:]

    def all_rows(taps, read, west_plane, east_plane):
        for p in range(0, ROWS + 2, 2):
            partial[p], partial[p + 1] = tap_sums(
                taps,
                columns(read(p), west_plane, p, east_plane, p),
                columns(read(p + 1), west_plane, p + 1, east_plane, p + 1),
            )

    def conv_row(row):
        return (
            partial[row, :PADDED]
            + partial[row + 1, PADDED : 2 * PADDED]
            + partial[row + 2, 2 * PADDED :]
        )

    def activated(value):
        return jax.nn.gelu(value).astype(jnp.bfloat16)

    first_taps = first_taps_ref[...]
    up = [jnp.where(tile > 0, above[at], 0.0) for at in range(2)]
    down = [jnp.where(tile < count - 1, below[at], 0.0) for at in range(2)]

    def read_normed(p):
        return up[1] if p == 0 else down[0] if p == last else field[p - 1]

    all_rows(first_taps, read_normed, west[0], east[0])
    for row in range(ROWS):
        hidden[row + 1] = activated(conv_row(row))

    upper, lower = 0.0, 0.0
    for at, (high, low) in enumerate(
        [(up[0], field[ROWS - 1]), (up[1], down[0]), (field[0], down[1])]
    ):
        from_row = ROWS - 1 + at
        one, two = tap_sums(
            first_taps,
            columns(high, west[-1], from_row, east[-1], from_row),
            columns(low, west[1], at, east[1], at),
        )
        upper += one[at * PADDED : (at + 1) * PADDED]
        lower += two[at * PADDED : (at + 1) * PADDED]
    hidden[0] = jnp.where(tile > 0, activated(upper), 0.0)
    hidden[last] = jnp.where(tile < count - 1, activated(lower), 0.0)

    def along(result):
        raw = (
            result[:PADDED]
            + pltpu.roll(result[PADDED : 2 * PADDED], BLOCK - 1, 1)
            + pltpu.roll(result[2 * PADDED :], BLOCK - 2, 1)
        )
        return activated(raw).astype(jnp.float32)

    west_hidden, east_hidden = {}, {}
    for at in (-1, 0, 1):
        q = at - R
        one = [padded_column(q, 2), padded_column(q, 3), east[q]]
        q = at + R
        two = [west[q], padded_column(q, 0), padded_column(q, 1)]
        one, two = tap_sums(
            first_taps,
            jnp.concatenate(one, axis=0).astype(jnp.bfloat16),
            jnp.concatenate(two, axis=0).astype(jnp.bfloat16),
        )
        west_hidden[at], east_hidden[at] = along(one), along(two)

    def hidden_side(shift, values):
        return ends(
            shift,
            pltpu.roll(values[-1], BLOCK - ROWS + 1, 1),
            pltpu.roll(values[1], last, 1),
            pltpu.roll(values[0], 1, 1),
        )

    sides = [hidden_side(-R, west_hidden), hidden_side(R, east_hidden)]
    for which, turned_side in enumerate(reversed_lanes(sides)):
        flip = strips[0][CHANNELS + which : CHANNELS + which + 1] > 0.5
        sides[which] = jnp.where(flip, turned_side, sides[which])

    all_rows(second_taps_ref[...], lambda p: hidden[p], sides[0], sides[1])
    for row in range(ROWS):
        turned[pl.ds(row, PADDED, stride=ROWS), :] = gridded[row].astype(jnp.float32) + conv_row(row)
    smoothed[...] = turned[pl.ds(0, CHANNELS * ROWS), :].astype(jnp.bfloat16)


def convolutions(column_rows, first_taps, second_taps, field, gridded, rims, own_strip, strips):
    operands = [first_taps, second_taps, field, gridded, *rims, own_strip, *strips]
    return pl.pallas_call(
        functools.partial(conv_kernel, column_rows),
        in_specs=[vmem()] * len(operands),
        out_specs=vmem(),
        out_shape=jax.ShapeDtypeStruct((CHANNELS * ROWS, BLOCK), jnp.bfloat16),
        scratch_shapes=[
            pltpu.VMEM((ROWS + 2, PADDED, BLOCK), jnp.bfloat16),
            pltpu.VMEM((ROWS + 2, 3 * PADDED, BLOCK), jnp.float32),
            pltpu.VMEM((PADDED * ROWS, BLOCK), jnp.float32),
        ],
        compiler_params=pltpu.CompilerParams(vmem_limit_bytes=VMEM_LIMIT),
        name="convolutions",
    )(*operands)


def tap_matrix(kernel):
    pad = PADDED - CHANNELS
    taps = jnp.pad(kernel, ((0, 0), (0, pad), (0, pad))).reshape(3, 3, PADDED, PADDED)
    return taps.transpose(0, 2, 1, 3).reshape(3 * PADDED, 3 * PADDED)


def from_shift(value, shift):
    count = lax.axis_size("tile")
    return lax.ppermute(value, "tile", [(i, (i - shift) % count) for i in range(count)])


def per_device(
    source, weights, block_source, block_target, edge_flip, norm_gain, first_kernel, second_kernel
):
    count = lax.axis_size("tile")
    column_rows = count // TILE_COLS
    field = source.reshape(ROWS, CHANNELS, BLOCK).transpose(1, 0, 2).reshape(-1, BLOCK)
    same, *nexts = regrid(block_target, block_source, field, weights, column_rows)

    def to_next(across):
        pairs = [
            (c * column_rows + p, (c ^ across) * column_rows + p + 1)
            for c in range(TILE_COLS)
            for p in range(column_rows - 1)
        ]
        return lax.ppermute(nexts[across], "tile", pairs)

    early = [to_next(across) for across in (7, 0, 1)]
    same, *early = lax.optimization_barrier((same, *early))
    late = [to_next(across) for across in (6, 5, 4, 3, 2)]
    same = lax.all_to_all(
        same,
        "tile",
        0,
        0,
        axis_index_groups=[
            [c * column_rows + p for c in range(TILE_COLS)] for p in range(column_rows)
        ],
        tiled=True,
    )
    nexts = early + late

    gain = jnp.broadcast_to(
        jnp.pad(norm_gain, (0, PADDED - CHANNELS))[:, None], (PADDED, BLOCK)
    )
    first_taps, second_taps = tap_matrix(first_kernel), tap_matrix(second_kernel)
    same, nexts, gain, first_taps, second_taps = lax.optimization_barrier(
        (same, nexts, gain, first_taps, second_taps)
    )
    gridded, normed, upward, downward, strip = gather_rows(
        column_rows, edge_flip, gain, same, nexts
    )
    rims = [from_shift(downward, -1), from_shift(upward, 1)]
    near, far, reach = strip_plan(column_rows)
    strips = [from_shift(strip, shift) for shift in near]
    held = {-1: rims[0][2], 0: strip, 1: rims[1][2], **dict(zip(near, strips))}
    pack = jnp.stack([held[at] for at in range(-reach, reach + 1)])
    strips += [from_shift(pack, -far), from_shift(pack, far)]
    gridded_out = channels_first(gridded)
    smoothed = convolutions(
        column_rows, first_taps, second_taps, normed, gridded, rims, strip, strips
    )

    def placed(value):
        return value.reshape(CHANNELS, ROWS, BLOCK).transpose(1, 0, 2)[:, None]

    return placed(gridded_out), placed(smoothed)


def solution(mesh):
    in_specs = (
        P("tile", "groups", None, None),
        P("tile", None, None),
        P("tile"),
        P("tile"),
        P("tile", None),
        P(),
        P(),
        P(),
    )
    out_specs = (P("tile", "groups", None, None), P("tile", "groups", None, None))
    return jax.shard_map(
        per_device, mesh=mesh, in_specs=in_specs, out_specs=out_specs, check_vma=False
    )
```

```python
import functools

import jax
import jax.numpy as jnp
from jax import lax
from jax.experimental import pallas as pl
from jax.experimental.pallas import tpu as pltpu
from jax.sharding import PartitionSpec as P

BLOCK = 128
CHANNELS = 69
PADDED = 72
ROWS = 32
TILE_COLS = 8
CAP = 8
GROUPS = 2 * TILE_COLS
SLOTS = GROUPS * CAP
CHUNK = 32
MARK = CHANNELS
EPSILON = 1e-05
VMEM_LIMIT = 40 * 1024 * 1024
FULL_VMEM = 60 * 1024 * 1024


def vmem():
    return pl.BlockSpec(memory_space=pltpu.VMEM)


def smem():
    return pl.BlockSpec(memory_space=pltpu.SMEM)


def split(value, size):
    if size & (size - 1) == 0:
        return value >> (size.bit_length() - 1), value & (size - 1)
    return lax.div(value, size), lax.rem(value, size)


def lanes(shape):
    return lax.broadcasted_iota(jnp.int32, shape, len(shape) - 1)


def regrid_kernel(column_rows, target_ref, index_ref, source_hbm, weight_hbm, *rest):
    same_out, next_outs = rest[0], rest[1 : 1 + TILE_COLS]
    (
        source,
        weight,
        wide,
        field,
        sums,
        rounded,
        slot_of,
        used,
        entry_slot,
        entry_fresh,
        source_sem,
        weight_sems,
        out_sems,
    ) = rest[1 + TILE_COLS :]
    entries = weight.shape[0]
    chunks = entries // CHUNK
    tile = lax.axis_index("tile")
    column, position = split(tile, column_rows)

    source_copy = pltpu.make_async_copy(source_hbm, source, source_sem)
    source_copy.start()

    def chunk_copy(chunk):
        part = pl.ds(chunk * CHUNK, CHUNK)
        return pltpu.make_async_copy(weight_hbm.at[part], weight.at[part], weight_sems.at[chunk])

    for chunk in range(chunks):
        chunk_copy(chunk).start()

    for key in range(GROUPS * ROWS):
        slot_of[key] = -1
    for group in range(GROUPS):
        used[group] = 0

    def plan(entry, carry):
        target = target_ref[entry]
        owner, row = split(target, ROWS)
        owner_column, owner_position = split(owner, column_rows)
        same = owner_position == position
        group = jnp.where(same, owner_column, TILE_COLS + (owner_column ^ column))
        key = group * ROWS + row
        known = slot_of[key]
        count = used[group]
        fresh = known < 0
        slot = jnp.where(fresh, group * CAP + count, known)
        slot_of[key] = slot
        used[group] = jnp.where(fresh, count + 1, count)
        entry_slot[entry] = slot
        entry_fresh[entry] = fresh.astype(jnp.int32)
        return carry

    lax.fori_loop(0, entries, plan, 0, unroll=4)

    tail = PADDED - 8
    for slot in range(SLOTS):
        rounded[slot, tail:] = jnp.full((8, BLOCK), ROWS, jnp.bfloat16)
    wide[pl.ds(CHANNELS * ROWS, (PADDED - CHANNELS) * ROWS), :] = jnp.zeros(
        ((PADDED - CHANNELS) * ROWS, BLOCK), jnp.float32
    )
    source_copy.wait()
    wide[pl.ds(0, CHANNELS * ROWS), :] = source[...].astype(jnp.float32)
    for row in range(ROWS):
        field[row] = wide[pl.ds(row, PADDED, stride=ROWS), :].astype(jnp.bfloat16)
    is_mark = lax.broadcasted_iota(jnp.int32, (8, BLOCK), 0) == MARK - tail

    def chunk_step(chunk, carry):
        chunk_copy(chunk).wait()
        for at in range(CHUNK):
            entry = chunk * CHUNK + at
            slot = entry_slot[entry]
            row = split(target_ref[entry], ROWS)[1]
            product = jnp.dot(
                field[index_ref[entry]], weight[entry], preferred_element_type=jnp.float32
            )
            total = jnp.where(entry_fresh[entry] == 1, 0.0, sums[slot]) + product
            sums[slot] = total
            marked = jnp.where(is_mark, row.astype(jnp.float32), total[tail:])
            rounded[slot] = jnp.concatenate([total[:tail], marked], axis=0).astype(jnp.bfloat16)
        return carry

    lax.fori_loop(0, chunks, chunk_step, 0)
    copies = [
        pltpu.make_async_copy(
            rounded.at[pl.ds(0, SLOTS // 2)], same_out, out_sems.at[0]
        )
    ]
    for group in range(TILE_COLS):
        part = rounded.at[pl.ds((TILE_COLS + group) * CAP, CAP)]
        copies.append(pltpu.make_async_copy(part, next_outs[group], out_sems.at[1 + group]))
    for copy in copies:
        copy.start()
    for copy in copies:
        copy.wait()


def regrid(target, source_index, field, weights, column_rows):
    piece = jax.ShapeDtypeStruct((CAP, PADDED, BLOCK), jnp.bfloat16)
    same = jax.ShapeDtypeStruct((TILE_COLS * CAP, PADDED, BLOCK), jnp.bfloat16)
    hbm = pl.BlockSpec(memory_space=pl.ANY)
    entries = weights.shape[0]
    return pl.pallas_call(
        functools.partial(regrid_kernel, column_rows),
        in_specs=[smem(), smem(), hbm, hbm],
        out_specs=[hbm] * (1 + TILE_COLS),
        out_shape=[same] + [piece] * TILE_COLS,
        scratch_shapes=[
            pltpu.VMEM(field.shape, jnp.bfloat16),
            pltpu.VMEM(weights.shape, jnp.bfloat16),
            pltpu.VMEM((PADDED * ROWS, BLOCK), jnp.float32),
            pltpu.VMEM((ROWS, PADDED, BLOCK), jnp.bfloat16),
            pltpu.VMEM((SLOTS, PADDED, BLOCK), jnp.float32),
            pltpu.VMEM((SLOTS, PADDED, BLOCK), jnp.bfloat16),
            pltpu.SMEM((GROUPS * ROWS,), jnp.int32),
            pltpu.SMEM((GROUPS,), jnp.int32),
            pltpu.SMEM((entries,), jnp.int32),
            pltpu.SMEM((entries,), jnp.int32),
            pltpu.SemaphoreType.DMA,
            pltpu.SemaphoreType.DMA((entries // CHUNK,)),
            pltpu.SemaphoreType.DMA((1 + TILE_COLS,)),
        ],
        compiler_params=pltpu.CompilerParams(vmem_limit_bytes=FULL_VMEM),
        name="regrid",
    )(target, source_index, field, weights)


def gather_kernel(column_rows, flip_ref, gain_ref, same, *rest):
    nexts = rest[:TILE_COLS]
    (
        gridded,
        normed,
        upward,
        downward,
        strip_out,
        summed,
        marks,
        rows,
        mark_sem,
    ) = rest[TILE_COLS:]
    position = lax.rem(lax.axis_index("tile"), column_rows)
    half = SLOTS // 2
    lane = lanes((1, BLOCK))
    mark = jnp.zeros((1, BLOCK), jnp.float32)
    for slot in range(SLOTS):
        piece = same.at[slot] if slot < half else nexts[slot // CAP - TILE_COLS].at[slot % CAP]
        mark = jnp.where(lane == slot, piece[MARK : MARK + 1].astype(jnp.float32), mark)
    marks[...] = mark.astype(jnp.int32)
    copy = pltpu.make_async_copy(marks, rows, mark_sem)
    copy.start()
    summed[...] = jnp.zeros_like(summed)
    copy.wait()

    def add(slot, piece):
        row = rows[0, slot]
        summed[row] = summed[row] + piece.astype(jnp.float32)

    def add_same(step, carry):
        for at in range(CAP):
            add(step * CAP + at, same[step * CAP + at])
        return carry

    lax.fori_loop(0, TILE_COLS, add_same, 0)

    @pl.when(position > 0)
    def _():
        for group in range(TILE_COLS):
            for place in range(CAP):
                add(half + group * CAP + place, nexts[group][place])

    gain = gain_ref[...]
    lane = lanes((PADDED, BLOCK))
    channel = lax.broadcasted_iota(jnp.int32, (PADDED, BLOCK), 0)
    strip = jnp.zeros((PADDED, BLOCK), jnp.float32)
    for row in range(ROWS):
        rounded = summed[row].astype(jnp.bfloat16)
        gridded[row] = rounded
        value = rounded.astype(jnp.float32)
        value = jnp.where(channel < CHANNELS, value, 0.0)
        square = jnp.sum(value * value, axis=0, keepdims=True) * (1.0 / CHANNELS)
        scaled = (value * lax.rsqrt(square + EPSILON) * gain).astype(jnp.bfloat16)
        normed[row] = scaled
        if row < 2:
            upward[row] = scaled
        if row >= ROWS - 2:
            downward[row - ROWS + 2] = scaled
        scaled = scaled.astype(jnp.float32)
        for place, column in enumerate(STRIP_COLUMNS):
            at = place * ROWS + row
            strip = jnp.where(lane == at, pltpu.roll(scaled, (at - column) % BLOCK, 1), strip)
    for side in range(2):
        strip = jnp.where(channel == CHANNELS + side, flip_ref[0, side].astype(jnp.float32), strip)
    strip = strip.astype(jnp.bfloat16)
    upward[2] = strip
    downward[2] = strip
    strip_out[...] = strip


FIELD = jax.ShapeDtypeStruct((ROWS, PADDED, BLOCK), jnp.bfloat16)
RIM = jax.ShapeDtypeStruct((3, PADDED, BLOCK), jnp.bfloat16)
STRIP_COLUMNS = (0, 1, BLOCK - 2, BLOCK - 1)
STRIP = jax.ShapeDtypeStruct((PADDED, BLOCK), jnp.bfloat16)


def gather_rows(column_rows, edge_flip, gain, same, nexts):
    return pl.pallas_call(
        functools.partial(gather_kernel, column_rows),
        in_specs=[smem()] + [vmem()] * (2 + TILE_COLS),
        out_specs=[vmem()] * 5,
        out_shape=[FIELD, FIELD, RIM, RIM, STRIP],
        scratch_shapes=[
            pltpu.VMEM((ROWS + 1, PADDED, BLOCK), jnp.float32),
            pltpu.VMEM((1, SLOTS), jnp.int32),
            pltpu.SMEM((1, SLOTS), jnp.int32),
            pltpu.SemaphoreType.DMA,
        ],
        compiler_params=pltpu.CompilerParams(vmem_limit_bytes=VMEM_LIMIT),
        name="gather_rows",
    )(edge_flip, gain, same, *nexts)


def turn_kernel(field, out, turned):
    for row in range(ROWS):
        turned[pl.ds(row, PADDED, stride=ROWS), :] = field[row].astype(jnp.float32)
    out[...] = turned[pl.ds(0, CHANNELS * ROWS), :].astype(jnp.bfloat16)


def channels_first(field):
    return pl.pallas_call(
        turn_kernel,
        in_specs=[vmem()],
        out_specs=vmem(),
        out_shape=jax.ShapeDtypeStruct((CHANNELS * ROWS, BLOCK), jnp.bfloat16),
        scratch_shapes=[pltpu.VMEM((PADDED * ROWS, BLOCK), jnp.float32)],
        compiler_params=pltpu.CompilerParams(vmem_limit_bytes=VMEM_LIMIT),
        name="channels_first",
    )(field)


def strip_plan(column_rows):
    if column_rows == 2:
        return [], 3, 1
    return [-2, 2], column_rows, 2


def conv_kernel(
    column_rows, first_taps_ref, second_taps_ref, field, gridded, above, below, own_strip, *rest
):
    near, far, reach = strip_plan(column_rows)
    near_strips, (west_pack, east_pack) = rest[: len(near)], rest[len(near) : len(near) + 2]
    smoothed, hidden, partial, turned = rest[len(near) + 2 :]
    count = lax.axis_size("tile")
    tile = lax.axis_index("tile")
    lane = lanes((PADDED, BLOCK))
    last = ROWS + 1
    R = column_rows

    strips = {-1: above[2], 0: own_strip[...], 1: below[2]}
    strips.update((shift, ref[...]) for shift, ref in zip(near, near_strips))
    for at in range(-reach, reach + 1):
        strips[at - far], strips[at + far] = west_pack[at + reach], east_pack[at + reach]
    strips = {shift: value.astype(jnp.float32) for shift, value in strips.items()}

    def place(shift):
        return lax.rem(tile + shift + count, count)

    def ends(shift, before, after, middle):
        before = jnp.where(place(shift) > 0, before, 0.0)
        after = jnp.where(place(shift) < count - 1, after, 0.0)
        return jnp.where(lane == 0, before, jnp.where(lane == last, after, middle))

    memo = {}

    def padded_column(shift, which):
        if (shift, which) not in memo:
            base = which * ROWS
            memo[shift, which] = ends(
                shift,
                pltpu.roll(strips[shift - 1], (1 - base - ROWS) % BLOCK, 1),
                pltpu.roll(strips[shift + 1], (last - base) % BLOCK, 1),
                pltpu.roll(strips[shift], (1 - base) % BLOCK, 1),
            )
        return memo[shift, which]

    row_id = lax.broadcasted_iota(jnp.int32, (BLOCK, BLOCK), 0)
    reversal = (row_id + lanes((BLOCK, BLOCK)) == last).astype(jnp.bfloat16)

    def reversed_lanes(planes):
        stacked = jnp.concatenate(planes, axis=0).astype(jnp.bfloat16)
        turned_round = jnp.dot(stacked, reversal, preferred_element_type=jnp.float32)
        return [turned_round[at * PADDED : (at + 1) * PADDED] for at in range(len(planes))]

    west_of = {shift: (shift - R, 3) for shift in {-1, 0, 1, R - 1, R, R + 1}}
    east_of = {shift: (shift + R, 0) for shift in {-1, 0, 1, -R - 1, -R, -R + 1}}
    keys = sorted(set(west_of.values()) | set(east_of.values()))
    flipped = dict(zip(keys, reversed_lanes([padded_column(*key) for key in keys])))

    def side(shift, which, table):
        key = table[shift]
        flip = strips[shift][CHANNELS + which : CHANNELS + which + 1] > 0.5
        return jnp.where(flip, flipped[key], padded_column(*key))

    west = {shift: side(shift, 0, west_of) for shift in sorted(west_of)}
    east = {shift: side(shift, 1, east_of) for shift in sorted(east_of)}

    def columns(value, west_plane, west_row, east_plane, east_row):
        value = value.astype(jnp.float32)
        west_value = pltpu.roll(west_plane, (BLOCK - west_row) % BLOCK, 1)
        east_value = pltpu.roll(east_plane, BLOCK - 1 - east_row, 1)
        left = jnp.where(lane == 0, west_value, pltpu.roll(value, 1, 1))
        right = jnp.where(lane == BLOCK - 1, east_value, pltpu.roll(value, BLOCK - 1, 1))
        return jnp.concatenate([left, value, right], axis=0).astype(jnp.bfloat16)

    def tap_sums(taps, one, two):
        both = jnp.concatenate([one, two], axis=1)
        result = jnp.dot(taps, both, preferred_element_type=jnp.float32)
        return result[:, :BLOCK], result[:, BLOCK:]

    def all_rows(taps, read, west_plane, east_plane):
        for p in range(0, ROWS + 2, 2):
            partial[p], partial[p + 1] = tap_sums(
                taps,
                columns(read(p), west_plane, p, east_plane, p),
                columns(read(p + 1), west_plane, p + 1, east_plane, p + 1),
            )

    def conv_row(row):
        return (
            partial[row, :PADDED]
            + partial[row + 1, PADDED : 2 * PADDED]
            + partial[row + 2, 2 * PADDED :]
        )

    def activated(value):
        return jax.nn.gelu(value).astype(jnp.bfloat16)

    first_taps = first_taps_ref[...]
    up = [jnp.where(tile > 0, above[at], 0.0) for at in range(2)]
    down = [jnp.where(tile < count - 1, below[at], 0.0) for at in range(2)]

    def read_normed(p):
        return up[1] if p == 0 else down[0] if p == last else field[p - 1]

    all_rows(first_taps, read_normed, west[0], east[0])
    for row in range(ROWS):
        hidden[row + 1] = activated(conv_row(row))

    upper, lower = 0.0, 0.0
    for at, (high, low) in enumerate(
        [(up[0], field[ROWS - 1]), (up[1], down[0]), (field[0], down[1])]
    ):
        from_row = ROWS - 1 + at
        one, two = tap_sums(
            first_taps,
            columns(high, west[-1], from_row, east[-1], from_row),
            columns(low, west[1], at, east[1], at),
        )
        upper += one[at * PADDED : (at + 1) * PADDED]
        lower += two[at * PADDED : (at + 1) * PADDED]
    hidden[0] = jnp.where(tile > 0, activated(upper), 0.0)
    hidden[last] = jnp.where(tile < count - 1, activated(lower), 0.0)

    def along(result):
        raw = (
            result[:PADDED]
            + pltpu.roll(result[PADDED : 2 * PADDED], BLOCK - 1, 1)
            + pltpu.roll(result[2 * PADDED :], BLOCK - 2, 1)
        )
        return activated(raw).astype(jnp.float32)

    west_hidden, east_hidden = {}, {}
    for at in (-1, 0, 1):
        q = at - R
        one = [padded_column(q, 2), padded_column(q, 3), east[q]]
        q = at + R
        two = [west[q], padded_column(q, 0), padded_column(q, 1)]
        one, two = tap_sums(
            first_taps,
            jnp.concatenate(one, axis=0).astype(jnp.bfloat16),
            jnp.concatenate(two, axis=0).astype(jnp.bfloat16),
        )
        west_hidden[at], east_hidden[at] = along(one), along(two)

    def hidden_side(shift, values):
        return ends(
            shift,
            pltpu.roll(values[-1], BLOCK - ROWS + 1, 1),
            pltpu.roll(values[1], last, 1),
            pltpu.roll(values[0], 1, 1),
        )

    sides = [hidden_side(-R, west_hidden), hidden_side(R, east_hidden)]
    for which, turned_side in enumerate(reversed_lanes(sides)):
        flip = strips[0][CHANNELS + which : CHANNELS + which + 1] > 0.5
        sides[which] = jnp.where(flip, turned_side, sides[which])

    all_rows(second_taps_ref[...], lambda p: hidden[p], sides[0], sides[1])
    for row in range(ROWS):
        turned[pl.ds(row, PADDED, stride=ROWS), :] = gridded[row].astype(jnp.float32) + conv_row(row)
    smoothed[...] = turned[pl.ds(0, CHANNELS * ROWS), :].astype(jnp.bfloat16)


def convolutions(column_rows, first_taps, second_taps, field, gridded, rims, own_strip, strips):
    operands = [first_taps, second_taps, field, gridded, *rims, own_strip, *strips]
    return pl.pallas_call(
        functools.partial(conv_kernel, column_rows),
        in_specs=[vmem()] * len(operands),
        out_specs=vmem(),
        out_shape=jax.ShapeDtypeStruct((CHANNELS * ROWS, BLOCK), jnp.bfloat16),
        scratch_shapes=[
            pltpu.VMEM((ROWS + 2, PADDED, BLOCK), jnp.bfloat16),
            pltpu.VMEM((ROWS + 2, 3 * PADDED, BLOCK), jnp.float32),
            pltpu.VMEM((PADDED * ROWS, BLOCK), jnp.float32),
        ],
        compiler_params=pltpu.CompilerParams(vmem_limit_bytes=VMEM_LIMIT),
        name="convolutions",
    )(*operands)


def tap_matrix(kernel):
    pad = PADDED - CHANNELS
    taps = jnp.pad(kernel, ((0, 0), (0, pad), (0, pad))).reshape(3, 3, PADDED, PADDED)
    return taps.transpose(0, 2, 1, 3).reshape(3 * PADDED, 3 * PADDED)


def from_shift(value, shift):
    count = lax.axis_size("tile")
    return lax.ppermute(value, "tile", [(i, (i - shift) % count) for i in range(count)])


def per_device(
    source, weights, block_source, block_target, edge_flip, norm_gain, first_kernel, second_kernel
):
    count = lax.axis_size("tile")
    column_rows = count // TILE_COLS
    field = source.reshape(ROWS, CHANNELS, BLOCK).transpose(1, 0, 2).reshape(-1, BLOCK)
    same, *nexts = regrid(block_target, block_source, field, weights, column_rows)

    for across in range(TILE_COLS):
        pairs = [
            (c * column_rows + p, (c ^ across) * column_rows + p + 1)
            for c in range(TILE_COLS)
            for p in range(column_rows - 1)
        ]
        nexts[across] = lax.ppermute(nexts[across], "tile", pairs)
    nexts = [nexts[across] for across in (0, 1, 7, 6, 5, 4, 3, 2)]
    same = lax.all_to_all(
        same,
        "tile",
        0,
        0,
        axis_index_groups=[
            [c * column_rows + p for c in range(TILE_COLS)] for p in range(column_rows)
        ],
        tiled=True,
    )

    gain = jnp.broadcast_to(
        jnp.pad(norm_gain, (0, PADDED - CHANNELS))[:, None], (PADDED, BLOCK)
    )
    first_taps, second_taps = tap_matrix(first_kernel), tap_matrix(second_kernel)
    same, nexts, gain, first_taps, second_taps = lax.optimization_barrier(
        (same, nexts, gain, first_taps, second_taps)
    )
    gridded, normed, upward, downward, strip = gather_rows(
        column_rows, edge_flip, gain, same, nexts
    )
    rims = [from_shift(downward, -1), from_shift(upward, 1)]
    near, far, reach = strip_plan(column_rows)
    strips = [from_shift(strip, shift) for shift in near]
    held = {-1: rims[0][2], 0: strip, 1: rims[1][2], **dict(zip(near, strips))}
    pack = jnp.stack([held[at] for at in range(-reach, reach + 1)])
    strips += [from_shift(pack, -far), from_shift(pack, far)]
    gridded_out = channels_first(gridded)
    smoothed = convolutions(
        column_rows, first_taps, second_taps, normed, gridded, rims, strip, strips
    )

    def placed(value):
        return value.reshape(CHANNELS, ROWS, BLOCK).transpose(1, 0, 2)[:, None]

    return placed(gridded_out), placed(smoothed)


def solution(mesh):
    in_specs = (
        P("tile", "groups", None, None),
        P("tile", None, None),
        P("tile"),
        P("tile"),
        P("tile", None),
        P(),
        P(),
        P(),
    )
    out_specs = (P("tile", "groups", None, None), P("tile", "groups", None, None))
    return jax.shard_map(
        per_device, mesh=mesh, in_specs=in_specs, out_specs=out_specs, check_vma=False
    )
```

```python
import functools

import jax
import jax.numpy as jnp
from jax import lax
from jax.experimental import pallas as pl
from jax.experimental.pallas import tpu as pltpu
from jax.sharding import PartitionSpec as P

BLOCK = 128
CHANNELS = 69
PADDED = 72
WIDE = 80
ROWS = 32
TILE_COLS = 8
CAP = 8
GROUPS = 2 * TILE_COLS
SLOTS = GROUPS * CAP
CHUNK = 32
MARK = CHANNELS
EPSILON = 1e-05
VMEM_LIMIT = 40 * 1024 * 1024
FULL_VMEM = 60 * 1024 * 1024


def vmem():
    return pl.BlockSpec(memory_space=pltpu.VMEM)


def smem():
    return pl.BlockSpec(memory_space=pltpu.SMEM)


def split(value, size):
    if size & (size - 1) == 0:
        return value >> (size.bit_length() - 1), value & (size - 1)
    return lax.div(value, size), lax.rem(value, size)


def lanes(shape):
    return lax.broadcasted_iota(jnp.int32, shape, len(shape) - 1)


def regrid_kernel(column_rows, target_ref, index_ref, source_hbm, weight_hbm, *rest):
    same_out, next_outs = rest[0], rest[1 : 1 + TILE_COLS]
    (
        source,
        weight,
        wide,
        field,
        sums,
        rounded,
        slot_of,
        used,
        entry_slot,
        entry_fresh,
        source_sem,
        weight_sems,
        out_sems,
    ) = rest[1 + TILE_COLS :]
    entries = weight.shape[0]
    chunks = entries // CHUNK
    tile = lax.axis_index("tile")
    column, position = split(tile, column_rows)

    source_copy = pltpu.make_async_copy(source_hbm, source, source_sem)
    source_copy.start()

    def chunk_copy(chunk):
        part = pl.ds(chunk * CHUNK, CHUNK)
        return pltpu.make_async_copy(weight_hbm.at[part], weight.at[part], weight_sems.at[chunk])

    for chunk in range(chunks):
        chunk_copy(chunk).start()

    for key in range(GROUPS * ROWS):
        slot_of[key] = -1
    for group in range(GROUPS):
        used[group] = 0

    def plan(entry, carry):
        target = target_ref[entry]
        owner, row = split(target, ROWS)
        owner_column, owner_position = split(owner, column_rows)
        same = owner_position == position
        group = jnp.where(same, owner_column, TILE_COLS + (owner_column ^ column))
        key = group * ROWS + row
        known = slot_of[key]
        count = used[group]
        fresh = known < 0
        slot = jnp.where(fresh, group * CAP + count, known)
        slot_of[key] = slot
        used[group] = jnp.where(fresh, count + 1, count)
        entry_slot[entry] = slot
        entry_fresh[entry] = fresh.astype(jnp.int32)
        return carry

    lax.fori_loop(0, entries, plan, 0, unroll=4)

    tail = PADDED - 8
    for slot in range(SLOTS):
        rounded[slot, tail:] = jnp.full((8, BLOCK), ROWS, jnp.bfloat16)
    wide[pl.ds(CHANNELS * ROWS, (PADDED - CHANNELS) * ROWS), :] = jnp.zeros(
        ((PADDED - CHANNELS) * ROWS, BLOCK), jnp.float32
    )
    nothing = jnp.zeros((WIDE - PADDED, BLOCK), jnp.float32)
    source_copy.wait()
    wide[pl.ds(0, CHANNELS * ROWS), :] = source[...].astype(jnp.float32)
    for row in range(ROWS):
        block = wide[pl.ds(row, PADDED, stride=ROWS), :]
        field[row] = jnp.concatenate([block, nothing], axis=0).astype(jnp.bfloat16)
    is_mark = lax.broadcasted_iota(jnp.int32, (8, BLOCK), 0) == MARK - tail

    for chunk in range(chunks):
        chunk_copy(chunk).wait()
        for entry in range(chunk * CHUNK, (chunk + 1) * CHUNK):
            slot = entry_slot[entry]
            row = split(target_ref[entry], ROWS)[1]
            product = jnp.dot(
                field[index_ref[entry]], weight[entry], preferred_element_type=jnp.float32
            )
            total = jnp.where(entry_fresh[entry] == 1, 0.0, sums[slot]) + product[:PADDED]
            sums[slot] = total
            marked = jnp.where(is_mark, row.astype(jnp.float32), total[tail:])
            rounded[slot] = jnp.concatenate([total[:tail], marked], axis=0).astype(jnp.bfloat16)
    copies = [
        pltpu.make_async_copy(
            rounded.at[pl.ds(0, SLOTS // 2)], same_out, out_sems.at[0]
        )
    ]
    for group in range(TILE_COLS):
        part = rounded.at[pl.ds((TILE_COLS + group) * CAP, CAP)]
        copies.append(pltpu.make_async_copy(part, next_outs[group], out_sems.at[1 + group]))
    for copy in copies:
        copy.start()
    for copy in copies:
        copy.wait()


def regrid(target, source_index, field, weights, column_rows):
    piece = jax.ShapeDtypeStruct((CAP, PADDED, BLOCK), jnp.bfloat16)
    same = jax.ShapeDtypeStruct((TILE_COLS * CAP, PADDED, BLOCK), jnp.bfloat16)
    hbm = pl.BlockSpec(memory_space=pl.ANY)
    entries = weights.shape[0]
    return pl.pallas_call(
        functools.partial(regrid_kernel, column_rows),
        in_specs=[smem(), smem(), hbm, hbm],
        out_specs=[hbm] * (1 + TILE_COLS),
        out_shape=[same] + [piece] * TILE_COLS,
        scratch_shapes=[
            pltpu.VMEM(field.shape, jnp.bfloat16),
            pltpu.VMEM(weights.shape, jnp.bfloat16),
            pltpu.VMEM((PADDED * ROWS, BLOCK), jnp.float32),
            pltpu.VMEM((ROWS, WIDE, BLOCK), jnp.bfloat16),
            pltpu.VMEM((SLOTS, PADDED, BLOCK), jnp.float32),
            pltpu.VMEM((SLOTS, PADDED, BLOCK), jnp.bfloat16),
            pltpu.SMEM((GROUPS * ROWS,), jnp.int32),
            pltpu.SMEM((GROUPS,), jnp.int32),
            pltpu.SMEM((entries,), jnp.int32),
            pltpu.SMEM((entries,), jnp.int32),
            pltpu.SemaphoreType.DMA,
            pltpu.SemaphoreType.DMA((entries // CHUNK,)),
            pltpu.SemaphoreType.DMA((1 + TILE_COLS,)),
        ],
        compiler_params=pltpu.CompilerParams(vmem_limit_bytes=FULL_VMEM),
        name="regrid",
    )(target, source_index, field, weights)


def gather_kernel(column_rows, flip_ref, gain_ref, same, *rest):
    nexts = rest[:TILE_COLS]
    (
        gridded,
        normed,
        upward,
        downward,
        strip_out,
        summed,
        marks,
        rows,
        mark_sem,
    ) = rest[TILE_COLS:]
    position = lax.rem(lax.axis_index("tile"), column_rows)
    half = SLOTS // 2
    lane = lanes((1, BLOCK))
    mark = jnp.zeros((1, BLOCK), jnp.float32)
    for slot in range(SLOTS):
        piece = same.at[slot] if slot < half else nexts[slot // CAP - TILE_COLS].at[slot % CAP]
        mark = jnp.where(lane == slot, piece[MARK : MARK + 1].astype(jnp.float32), mark)
    marks[...] = mark.astype(jnp.int32)
    copy = pltpu.make_async_copy(marks, rows, mark_sem)
    copy.start()
    summed[...] = jnp.zeros_like(summed)
    copy.wait()

    def add(slot, piece):
        row = rows[0, slot]
        summed[row] = summed[row] + piece.astype(jnp.float32)

    def add_same(step, carry):
        for at in range(CAP):
            add(step * CAP + at, same[step * CAP + at])
        return carry

    lax.fori_loop(0, TILE_COLS, add_same, 0)

    @pl.when(position > 0)
    def _():
        for group in range(TILE_COLS):
            for place in range(CAP):
                add(half + group * CAP + place, nexts[group][place])

    gain = gain_ref[...]
    channel = lax.broadcasted_iota(jnp.int32, (PADDED, BLOCK), 0)
    nothing = jnp.zeros((WIDE - PADDED, BLOCK), jnp.float32)
    lane = lanes((WIDE, BLOCK))
    strip = jnp.zeros((WIDE, BLOCK), jnp.bfloat16)
    for row in range(ROWS):
        rounded = summed[row].astype(jnp.bfloat16)
        gridded[row] = rounded
        value = rounded.astype(jnp.float32)
        value = jnp.where(channel < CHANNELS, value, 0.0)
        square = jnp.sum(value * value, axis=0, keepdims=True) * (1.0 / CHANNELS)
        scaled = value * lax.rsqrt(square + EPSILON) * gain
        scaled = jnp.concatenate([scaled, nothing], axis=0).astype(jnp.bfloat16)
        normed[row] = scaled
        if row < 2:
            upward[row] = scaled
        if row >= ROWS - 2:
            downward[row - ROWS + 2] = scaled
        for place, column in enumerate(STRIP_COLUMNS):
            at = place * ROWS + row
            strip = jnp.where(lane == at, pltpu.roll(scaled, (at - column) % BLOCK, 1), strip)
    strip = strip.astype(jnp.float32)
    channel = lax.broadcasted_iota(jnp.int32, (WIDE, BLOCK), 0)
    for side in range(2):
        strip = jnp.where(channel == CHANNELS + side, flip_ref[0, side].astype(jnp.float32), strip)
    strip = strip.astype(jnp.bfloat16)
    upward[2] = strip
    downward[2] = strip
    strip_out[...] = strip


GRIDDED = jax.ShapeDtypeStruct((ROWS, PADDED, BLOCK), jnp.bfloat16)
FIELD = jax.ShapeDtypeStruct((ROWS, WIDE, BLOCK), jnp.bfloat16)
RIM = jax.ShapeDtypeStruct((3, WIDE, BLOCK), jnp.bfloat16)
STRIP_COLUMNS = (0, 1, BLOCK - 2, BLOCK - 1)
STRIP = jax.ShapeDtypeStruct((WIDE, BLOCK), jnp.bfloat16)


def gather_rows(column_rows, edge_flip, gain, same, nexts):
    return pl.pallas_call(
        functools.partial(gather_kernel, column_rows),
        in_specs=[smem()] + [vmem()] * (2 + TILE_COLS),
        out_specs=[vmem()] * 5,
        out_shape=[GRIDDED, FIELD, RIM, RIM, STRIP],
        scratch_shapes=[
            pltpu.VMEM((ROWS + 1, PADDED, BLOCK), jnp.float32),
            pltpu.VMEM((1, SLOTS), jnp.int32),
            pltpu.SMEM((1, SLOTS), jnp.int32),
            pltpu.SemaphoreType.DMA,
        ],
        compiler_params=pltpu.CompilerParams(vmem_limit_bytes=VMEM_LIMIT),
        name="gather_rows",
    )(edge_flip, gain, same, *nexts)


def turn_kernel(field, out, turned):
    for row in range(ROWS):
        turned[pl.ds(row, PADDED, stride=ROWS), :] = field[row].astype(jnp.float32)
    out[...] = turned[pl.ds(0, CHANNELS * ROWS), :].astype(jnp.bfloat16)


def channels_first(field):
    return pl.pallas_call(
        turn_kernel,
        in_specs=[vmem()],
        out_specs=vmem(),
        out_shape=jax.ShapeDtypeStruct((CHANNELS * ROWS, BLOCK), jnp.bfloat16),
        scratch_shapes=[pltpu.VMEM((PADDED * ROWS, BLOCK), jnp.float32)],
        compiler_params=pltpu.CompilerParams(vmem_limit_bytes=VMEM_LIMIT),
        name="channels_first",
    )(field)


def shifted_columns(value, left_end, right_end):
    lane = lanes((WIDE, BLOCK))
    left = jnp.where(lane == 0, left_end, pltpu.roll(value, 1, 1))
    right = jnp.where(lane == BLOCK - 1, right_end, pltpu.roll(value, BLOCK - 1, 1))
    return jnp.concatenate([left, value, right], axis=0)


def tap_sums(taps, one, two):
    both = jnp.concatenate([one, two], axis=1)
    result = jnp.dot(taps, both, preferred_element_type=jnp.float32)
    return result[:, :BLOCK], result[:, BLOCK:]


def row_tap(sums, at):
    return sums[at * WIDE : (at + 1) * WIDE]


def activated(value):
    return jax.nn.gelu(value).astype(jnp.bfloat16)


def inner_kernel(taps_ref, field, hidden, ends, sides, partial):
    taps = taps_ref[...]
    blank = jnp.zeros((WIDE, BLOCK), jnp.bfloat16)
    for row in range(0, ROWS, 2):
        partial[row], partial[row + 1] = tap_sums(
            taps,
            shifted_columns(field[row], blank, blank),
            shifted_columns(field[row + 1], blank, blank),
        )
    lane = lanes((WIDE, BLOCK))
    west = jnp.zeros((WIDE, BLOCK), jnp.float32)
    east = jnp.zeros((WIDE, BLOCK), jnp.float32)
    for row in range(ROWS):
        value = partial[row, WIDE : 2 * WIDE]
        if row > 0:
            value = value + partial[row - 1, :WIDE]
        if row < ROWS - 1:
            value = value + partial[row + 1, 2 * WIDE :]
        if row == 0:
            ends[0] = value
        elif row == ROWS - 1:
            ends[1] = value
        else:
            hidden[row] = activated(value)
        west = jnp.where(lane == row, pltpu.roll(value, row, 1), west)
        east = jnp.where(lane == row, pltpu.roll(value, row + 1, 1), east)
    hidden[0] = blank
    hidden[ROWS - 1] = blank
    sides[0] = west
    sides[1] = east


def inner_convolution(taps, field):
    pair = jax.ShapeDtypeStruct((2, WIDE, BLOCK), jnp.float32)
    return pl.pallas_call(
        inner_kernel,
        in_specs=[vmem()] * 2,
        out_specs=[vmem()] * 3,
        out_shape=[FIELD, pair, pair],
        scratch_shapes=[pltpu.VMEM((ROWS, 3 * WIDE, BLOCK), jnp.float32)],
        compiler_params=pltpu.CompilerParams(vmem_limit_bytes=VMEM_LIMIT),
        cost_estimate=pl.CostEstimate(
            flops=2 * 9 * WIDE * WIDE * ROWS * BLOCK, bytes_accessed=2 << 20, transcendentals=0
        ),
        name="inner_convolution",
    )(taps, field)


def strip_plan(column_rows):
    if column_rows == 2:
        return [], 3, 1
    return [-2, 2], column_rows, 2


def conv_kernel(
    column_rows,
    first_taps_ref,
    second_taps_ref,
    field,
    gridded,
    inner,
    ends_ref,
    sides_ref,
    above,
    below,
    own_strip,
    *rest,
):
    near, far, reach = strip_plan(column_rows)
    near_strips, (west_pack, east_pack) = rest[: len(near)], rest[len(near) : len(near) + 2]
    smoothed, hidden, partial, turned = rest[len(near) + 2 :]
    count = lax.axis_size("tile")
    tile = lax.axis_index("tile")
    lane = lanes((WIDE, BLOCK))
    last = ROWS + 1
    R = column_rows
    blank = jnp.zeros((WIDE, BLOCK), jnp.bfloat16)

    strips = {-1: above[2], 0: own_strip[...], 1: below[2]}
    strips.update((shift, ref[...]) for shift, ref in zip(near, near_strips))
    for at in range(-reach, reach + 1):
        strips[at - far], strips[at + far] = west_pack[at + reach], east_pack[at + reach]

    def place(shift):
        return lax.rem(tile + shift + count, count)

    def ends(shift, before, after, middle):
        before = jnp.where(place(shift) > 0, before, blank)
        after = jnp.where(place(shift) < count - 1, after, blank)
        return jnp.where(lane == 0, before, jnp.where(lane == last, after, middle))

    memo = {}

    def padded_column(shift, which):
        if (shift, which) not in memo:
            base = which * ROWS
            memo[shift, which] = ends(
                shift,
                pltpu.roll(strips[shift - 1], (1 - base - ROWS) % BLOCK, 1),
                pltpu.roll(strips[shift + 1], (last - base) % BLOCK, 1),
                pltpu.roll(strips[shift], (1 - base) % BLOCK, 1),
            )
        return memo[shift, which]

    row_id = lax.broadcasted_iota(jnp.int32, (BLOCK, BLOCK), 0)
    reversal = (row_id + lanes((BLOCK, BLOCK)) == last).astype(jnp.bfloat16)

    def reversed_lanes(planes):
        stacked = jnp.concatenate(planes, axis=0)
        turned_round = jnp.dot(stacked, reversal, preferred_element_type=jnp.float32)
        return [row_tap(turned_round, at) for at in range(len(planes))]

    def choose(shift, which, turned_round, plain):
        flips = strips[shift].astype(jnp.float32)[CHANNELS + which : CHANNELS + which + 1]
        return jnp.where(flips > 0.5, turned_round, plain.astype(jnp.float32)).astype(jnp.bfloat16)

    west_of = {shift: (shift - R, 3) for shift in {-1, 0, 1, R - 1, R, R + 1}}
    east_of = {shift: (shift + R, 0) for shift in {-1, 0, 1, -R - 1, -R, -R + 1}}
    keys = sorted(set(west_of.values()) | set(east_of.values()))
    flipped = dict(zip(keys, reversed_lanes([padded_column(*key) for key in keys])))
    west = {
        shift: choose(shift, 0, flipped[west_of[shift]], padded_column(*west_of[shift]))
        for shift in sorted(west_of)
    }
    east = {
        shift: choose(shift, 1, flipped[east_of[shift]], padded_column(*east_of[shift]))
        for shift in sorted(east_of)
    }

    def columns(value, west_plane, west_row, east_plane, east_row):
        return shifted_columns(
            value,
            pltpu.roll(west_plane, (BLOCK - west_row) % BLOCK, 1),
            pltpu.roll(east_plane, BLOCK - 1 - east_row, 1),
        )

    def along(result):
        return (
            row_tap(result, 0)
            + pltpu.roll(row_tap(result, 1), BLOCK - 1, 1)
            + pltpu.roll(row_tap(result, 2), BLOCK - 2, 1)
        )

    first_taps = first_taps_ref[...]
    up = [jnp.where(tile > 0, above[at], blank) for at in range(2)]
    down = [jnp.where(tile < count - 1, below[at], blank) for at in range(2)]
    from_up, from_down = tap_sums(
        first_taps, shifted_columns(up[1], blank, blank), shifted_columns(down[0], blank, blank)
    )
    from_up, from_down = row_tap(from_up, 0), row_tap(from_down, 2)
    from_west, from_east = tap_sums(
        first_taps,
        jnp.concatenate([west[0], blank, blank], axis=0),
        jnp.concatenate([blank, blank, east[0]], axis=0),
    )
    from_west, from_east = along(from_west), along(from_east)
    first = ends_ref[0] + from_up
    first = first + jnp.where(lane == 0, from_west, 0.0)
    first = first + jnp.where(lane == BLOCK - 1, pltpu.roll(from_east, BLOCK - 1, 1), 0.0)
    final = ends_ref[1] + from_down
    final = final + jnp.where(lane == 0, pltpu.roll(from_west, BLOCK - ROWS + 1, 1), 0.0)
    final = final + jnp.where(lane == BLOCK - 1, pltpu.roll(from_east, BLOCK - ROWS, 1), 0.0)
    hidden[1] = activated(first)
    hidden[ROWS] = activated(final)
    first_column = activated(sides_ref[0] + from_west)
    last_column = activated(sides_ref[1] + from_east)
    for row in range(1, ROWS - 1):
        value = jnp.where(lane == 0, pltpu.roll(first_column, BLOCK - row, 1), inner[row])
        hidden[row + 1] = jnp.where(
            lane == BLOCK - 1, pltpu.roll(last_column, BLOCK - 1 - row, 1), value
        )

    upper = jnp.zeros((WIDE, BLOCK), jnp.float32)
    lower = jnp.zeros((WIDE, BLOCK), jnp.float32)
    for at, (high, low) in enumerate(
        [(up[0], field[ROWS - 1]), (up[1], down[0]), (field[0], down[1])]
    ):
        from_row = ROWS - 1 + at
        one, two = tap_sums(
            first_taps,
            columns(high, west[-1], from_row, east[-1], from_row),
            columns(low, west[1], at, east[1], at),
        )
        upper += row_tap(one, at)
        lower += row_tap(two, at)
    hidden[0] = jnp.where(tile > 0, activated(upper), blank)
    hidden[last] = jnp.where(tile < count - 1, activated(lower), blank)

    west_hidden, east_hidden = {}, {}
    for at in (-1, 0, 1):
        q = at - R
        one = jnp.concatenate([padded_column(q, 2), padded_column(q, 3), east[q]], axis=0)
        q = at + R
        two = jnp.concatenate([west[q], padded_column(q, 0), padded_column(q, 1)], axis=0)
        one, two = tap_sums(first_taps, one, two)
        west_hidden[at], east_hidden[at] = activated(along(one)), activated(along(two))

    def hidden_side(shift, values):
        return ends(
            shift,
            pltpu.roll(values[-1], BLOCK - ROWS + 1, 1),
            pltpu.roll(values[1], last, 1),
            pltpu.roll(values[0], 1, 1),
        )

    plain = [hidden_side(-R, west_hidden), hidden_side(R, east_hidden)]
    west_side, east_side = [
        choose(0, which, turned_side, plain[which])
        for which, turned_side in enumerate(reversed_lanes(plain))
    ]

    second_taps = second_taps_ref[...]
    for p in range(0, ROWS + 2, 2):
        partial[p], partial[p + 1] = tap_sums(
            second_taps,
            columns(hidden[p], west_side, p, east_side, p),
            columns(hidden[p + 1], west_side, p + 1, east_side, p + 1),
        )
    for row in range(ROWS):
        branch = (
            partial[row, :PADDED]
            + partial[row + 1, WIDE : WIDE + PADDED]
            + partial[row + 2, 2 * WIDE : 2 * WIDE + PADDED]
        )
        turned[pl.ds(row, PADDED, stride=ROWS), :] = gridded[row].astype(jnp.float32) + branch
    smoothed[...] = turned[pl.ds(0, CHANNELS * ROWS), :].astype(jnp.bfloat16)


def convolutions(column_rows, *operands):
    return pl.pallas_call(
        functools.partial(conv_kernel, column_rows),
        in_specs=[vmem()] * len(operands),
        out_specs=vmem(),
        out_shape=jax.ShapeDtypeStruct((CHANNELS * ROWS, BLOCK), jnp.bfloat16),
        scratch_shapes=[
            pltpu.VMEM((ROWS + 2, WIDE, BLOCK), jnp.bfloat16),
            pltpu.VMEM((ROWS + 2, 3 * WIDE, BLOCK), jnp.float32),
            pltpu.VMEM((PADDED * ROWS, BLOCK), jnp.float32),
        ],
        compiler_params=pltpu.CompilerParams(vmem_limit_bytes=VMEM_LIMIT),
        name="convolutions",
    )(*operands)


def tap_matrix(kernel):
    pad = WIDE - CHANNELS
    taps = jnp.pad(kernel, ((0, 0), (0, pad), (0, pad))).reshape(3, 3, WIDE, WIDE)
    return taps.transpose(0, 2, 1, 3).reshape(3 * WIDE, 3 * WIDE)


def from_shift(value, shift):
    count = lax.axis_size("tile")
    return lax.ppermute(value, "tile", [(i, (i - shift) % count) for i in range(count)])


def per_device(
    source, weights, block_source, block_target, edge_flip, norm_gain, first_kernel, second_kernel
):
    count = lax.axis_size("tile")
    column_rows = count // TILE_COLS
    field = source.reshape(ROWS, CHANNELS, BLOCK).transpose(1, 0, 2).reshape(-1, BLOCK)
    same, *nexts = regrid(block_target, block_source, field, weights, column_rows)

    for across in reversed(range(TILE_COLS)):
        pairs = [
            (c * column_rows + p, (c ^ across) * column_rows + p + 1)
            for c in range(TILE_COLS)
            for p in range(column_rows - 1)
        ]
        nexts[across] = lax.ppermute(nexts[across], "tile", pairs)
    same = lax.all_to_all(
        same,
        "tile",
        0,
        0,
        axis_index_groups=[
            [c * column_rows + p for c in range(TILE_COLS)] for p in range(column_rows)
        ],
        tiled=True,
    )

    gain = jnp.broadcast_to(
        jnp.pad(norm_gain, (0, PADDED - CHANNELS))[:, None], (PADDED, BLOCK)
    )
    first_taps, second_taps = tap_matrix(first_kernel), tap_matrix(second_kernel)
    same, nexts, gain, first_taps, second_taps = lax.optimization_barrier(
        (same, nexts, gain, first_taps, second_taps)
    )
    gridded, normed, upward, downward, strip = gather_rows(
        column_rows, edge_flip, gain, same, nexts
    )
    rims = [from_shift(downward, -1), from_shift(upward, 1)]
    near, far, reach = strip_plan(column_rows)
    strips = [from_shift(strip, shift) for shift in near]
    inner = inner_convolution(first_taps, normed)
    held = {-1: rims[0][2], 0: strip, 1: rims[1][2], **dict(zip(near, strips))}
    pack = jnp.stack([held[at] for at in range(-reach, reach + 1)])
    pack, inner = lax.optimization_barrier((pack, inner))
    strips += [from_shift(pack, -far), from_shift(pack, far)]
    gridded_out = channels_first(gridded)
    smoothed = convolutions(
        column_rows, first_taps, second_taps, normed, gridded, *inner, *rims, strip, *strips
    )

    def placed(value):
        return value.reshape(CHANNELS, ROWS, BLOCK).transpose(1, 0, 2)[:, None]

    return placed(gridded_out), placed(smoothed)


def solution(mesh):
    in_specs = (
        P("tile", "groups", None, None),
        P("tile", None, None),
        P("tile"),
        P("tile"),
        P("tile", None),
        P(),
        P(),
        P(),
    )
    out_specs = (P("tile", "groups", None, None), P("tile", "groups", None, None))
    return jax.shard_map(
        per_device, mesh=mesh, in_specs=in_specs, out_specs=out_specs, check_vma=False
    )
```

```python
import functools

import jax
import jax.numpy as jnp
from jax import lax
from jax.experimental import pallas as pl
from jax.experimental.pallas import tpu as pltpu
from jax.sharding import PartitionSpec as P

BLOCK = 128
CHANNELS = 69
PADDED = 72
WIDE = 80
ROWS = 32
ROW_BITS = 5
TILE_COLS = 8
CAP = 8
GROUPS = 2 * TILE_COLS
SLOTS = GROUPS * CAP
CHUNK = 32
MARK = CHANNELS
EARLY = 6
EPSILON = 1e-05
VMEM_LIMIT = 40 * 1024 * 1024
FULL_VMEM = 60 * 1024 * 1024


def vmem():
    return pl.BlockSpec(memory_space=pltpu.VMEM)


def smem():
    return pl.BlockSpec(memory_space=pltpu.SMEM)


def split(value, size):
    if size & (size - 1) == 0:
        return value >> (size.bit_length() - 1), value & (size - 1)
    return lax.div(value, size), lax.rem(value, size)


def lanes(shape):
    return lax.broadcasted_iota(jnp.int32, shape, len(shape) - 1)


def regrid_kernel(
    column_rows, target_ref, index_ref, target_row_ref, source_hbm, weight_hbm, *rest
):
    same_out, next_outs = rest[0], rest[1 : 1 + TILE_COLS]
    (
        source,
        weight,
        wide,
        field,
        sums,
        rounded,
        plan,
        plan_scalars,
        plan_sem,
        source_sem,
        weight_sems,
        out_sems,
    ) = rest[1 + TILE_COLS :]
    entries = weight.shape[0]
    chunks = entries // CHUNK
    tile = lax.axis_index("tile")
    column, position = split(tile, column_rows)

    source_copy = pltpu.make_async_copy(source_hbm, source, source_sem)
    source_copy.start()

    def chunk_copy(chunk):
        part = pl.ds(chunk * CHUNK, CHUNK)
        return pltpu.make_async_copy(weight_hbm.at[part], weight.at[part], weight_sems.at[chunk])

    for chunk in range(chunks):
        chunk_copy(chunk).start()

    target = target_row_ref[...]
    owner, row = split(target, ROWS)
    owner_column, owner_position = split(owner, column_rows)
    group = jnp.where(
        owner_position == position, owner_column, TILE_COLS + (owner_column ^ column)
    )
    key = group * ROWS + row
    square = (entries, entries)
    down = lax.broadcasted_iota(jnp.int32, square, 0)
    along = lanes(square)
    key_along = jnp.broadcast_to(key.astype(jnp.float32), square)
    key_down = jnp.broadcast_to(
        jnp.sum(jnp.where(down == along, key_along, 0.0), axis=1, keepdims=True), square
    )
    equal = key_along == key_down
    doubles = jnp.sum(jnp.where(equal & (along < down), 1.0, 0.0), axis=1, keepdims=True)
    in_group = (key_down.astype(jnp.int32) >> ROW_BITS) == (key_along.astype(jnp.int32) >> ROW_BITS)
    below = in_group & (key_down < key_along) & (jnp.broadcast_to(doubles, square) == 0.0)
    rank = jnp.sum(jnp.where(below, 1.0, 0.0), axis=0, keepdims=True)
    mentions = jnp.sum(jnp.where(equal & (down < along), 1.0, 0.0), axis=0, keepdims=True)
    slots = group * CAP + rank.astype(jnp.int32)
    plan[...] = slots + jnp.where(mentions == 0.0, SLOTS, 0)
    plan_copy = pltpu.make_async_copy(plan, plan_scalars, plan_sem)
    plan_copy.start()

    tail = PADDED - 8
    for slot in range(SLOTS):
        rounded[slot, tail:] = jnp.full((8, BLOCK), ROWS, jnp.bfloat16)
    wide[pl.ds(CHANNELS * ROWS, (PADDED - CHANNELS) * ROWS), :] = jnp.zeros(
        ((PADDED - CHANNELS) * ROWS, BLOCK), jnp.float32
    )
    nothing = jnp.zeros((WIDE - PADDED, BLOCK), jnp.float32)
    source_copy.wait()
    wide[pl.ds(0, CHANNELS * ROWS), :] = source[...].astype(jnp.float32)
    for row in range(ROWS):
        block = wide[pl.ds(row, PADDED, stride=ROWS), :]
        field[row] = jnp.concatenate([block, nothing], axis=0).astype(jnp.bfloat16)
    is_mark = lax.broadcasted_iota(jnp.int32, (8, BLOCK), 0) == MARK - tail
    plan_copy.wait()

    for chunk in range(chunks):
        chunk_copy(chunk).wait()
        for entry in range(chunk * CHUNK, (chunk + 1) * CHUNK):
            code = plan_scalars[0, entry]
            slot = code & (SLOTS - 1)
            row = split(target_ref[entry], ROWS)[1]
            product = jnp.dot(
                field[index_ref[entry]], weight[entry], preferred_element_type=jnp.float32
            )
            total = jnp.where(code >= SLOTS, 0.0, sums[slot]) + product[:PADDED]
            sums[slot] = total
            marked = jnp.where(is_mark, row.astype(jnp.float32), total[tail:])
            rounded[slot] = jnp.concatenate([total[:tail], marked], axis=0).astype(jnp.bfloat16)
    copies = [
        pltpu.make_async_copy(
            rounded.at[pl.ds(0, SLOTS // 2)], same_out, out_sems.at[0]
        )
    ]
    for group in range(TILE_COLS):
        part = rounded.at[pl.ds((TILE_COLS + group) * CAP, CAP)]
        copies.append(pltpu.make_async_copy(part, next_outs[group], out_sems.at[1 + group]))
    for copy in copies:
        copy.start()
    for copy in copies:
        copy.wait()


def regrid(target, source_index, field, weights, column_rows):
    piece = jax.ShapeDtypeStruct((CAP, PADDED, BLOCK), jnp.bfloat16)
    same = jax.ShapeDtypeStruct((TILE_COLS * CAP, PADDED, BLOCK), jnp.bfloat16)
    hbm = pl.BlockSpec(memory_space=pl.ANY)
    entries = weights.shape[0]
    return pl.pallas_call(
        functools.partial(regrid_kernel, column_rows),
        in_specs=[smem(), smem(), vmem(), hbm, hbm],
        out_specs=[hbm] * (1 + TILE_COLS),
        out_shape=[same] + [piece] * TILE_COLS,
        scratch_shapes=[
            pltpu.VMEM(field.shape, jnp.bfloat16),
            pltpu.VMEM(weights.shape, jnp.bfloat16),
            pltpu.VMEM((PADDED * ROWS, BLOCK), jnp.float32),
            pltpu.VMEM((ROWS, WIDE, BLOCK), jnp.bfloat16),
            pltpu.VMEM((SLOTS, PADDED, BLOCK), jnp.float32),
            pltpu.VMEM((SLOTS, PADDED, BLOCK), jnp.bfloat16),
            pltpu.VMEM((1, entries), jnp.int32),
            pltpu.SMEM((1, entries), jnp.int32),
            pltpu.SemaphoreType.DMA,
            pltpu.SemaphoreType.DMA,
            pltpu.SemaphoreType.DMA((entries // CHUNK,)),
            pltpu.SemaphoreType.DMA((1 + TILE_COLS,)),
        ],
        compiler_params=pltpu.CompilerParams(vmem_limit_bytes=FULL_VMEM),
        name="regrid",
    )(target, source_index, target.reshape(1, -1), field, weights)


def scatter_rows(summed, marks, rows, sem, pieces):
    lane = lanes((1, BLOCK))
    mark = jnp.zeros((1, BLOCK), jnp.float32)
    for at, piece in enumerate(pieces):
        mark = jnp.where(lane == at, piece[MARK : MARK + 1].astype(jnp.float32), mark)
    marks[...] = mark.astype(jnp.int32)
    copy = pltpu.make_async_copy(marks, rows, sem)
    copy.start()
    copy.wait()
    for at, piece in enumerate(pieces):
        row = rows[0, at]
        summed[row] = summed[row] + piece[...].astype(jnp.float32)


def scatter_scratch():
    return [
        pltpu.VMEM((1, SLOTS), jnp.int32),
        pltpu.SMEM((1, SLOTS), jnp.int32),
        pltpu.SemaphoreType.DMA,
    ]


SUMMED = (ROWS + 1, PADDED, BLOCK)


def early_kernel(column_rows, same, *rest):
    nexts, (summed, marks, rows, sem) = rest[:EARLY], rest[EARLY:]
    position = lax.rem(lax.axis_index("tile"), column_rows)
    summed[...] = jnp.zeros_like(summed)
    scatter_rows(summed, marks, rows, sem, [same.at[slot] for slot in range(SLOTS // 2)])

    @pl.when(position > 0)
    def _():
        pieces = [piece.at[place] for piece in nexts for place in range(CAP)]
        scatter_rows(summed, marks, rows, sem, pieces)


def early_rows(column_rows, same, nexts):
    return pl.pallas_call(
        functools.partial(early_kernel, column_rows),
        in_specs=[vmem()] * (1 + EARLY),
        out_specs=vmem(),
        out_shape=jax.ShapeDtypeStruct(SUMMED, jnp.float32),
        scratch_shapes=scatter_scratch(),
        compiler_params=pltpu.CompilerParams(vmem_limit_bytes=VMEM_LIMIT),
        cost_estimate=pl.CostEstimate(flops=SLOTS << 14, bytes_accessed=4 << 20, transcendentals=0),
        name="early_rows",
    )(same, *nexts)


def gather_kernel(column_rows, flip_ref, gain_ref, before, *rest):
    nexts = rest[: TILE_COLS - EARLY]
    (
        gridded,
        normed,
        upward,
        downward,
        strip_out,
        late,
        marks,
        rows,
        sem,
    ) = rest[TILE_COLS - EARLY :]
    position = lax.rem(lax.axis_index("tile"), column_rows)
    late[...] = jnp.zeros_like(late)

    @pl.when(position > 0)
    def _():
        pieces = [piece.at[place] for piece in nexts for place in range(CAP)]
        scatter_rows(late, marks, rows, sem, pieces)

    gain = gain_ref[...]
    channel = lax.broadcasted_iota(jnp.int32, (PADDED, BLOCK), 0)
    nothing = jnp.zeros((WIDE - PADDED, BLOCK), jnp.float32)
    lane = lanes((WIDE, BLOCK))
    strip = jnp.zeros((WIDE, BLOCK), jnp.bfloat16)
    for row in range(ROWS):
        rounded = (before[row] + late[row]).astype(jnp.bfloat16)
        gridded[row] = rounded
        value = rounded.astype(jnp.float32)
        value = jnp.where(channel < CHANNELS, value, 0.0)
        square = jnp.sum(value * value, axis=0, keepdims=True) * (1.0 / CHANNELS)
        scaled = value * lax.rsqrt(square + EPSILON) * gain
        scaled = jnp.concatenate([scaled, nothing], axis=0).astype(jnp.bfloat16)
        normed[row] = scaled
        if row < 2:
            upward[row] = scaled
        if row >= ROWS - 2:
            downward[row - ROWS + 2] = scaled
        for place, column in enumerate(STRIP_COLUMNS):
            at = place * ROWS + row
            strip = jnp.where(lane == at, pltpu.roll(scaled, (at - column) % BLOCK, 1), strip)
    strip = strip.astype(jnp.float32)
    channel = lax.broadcasted_iota(jnp.int32, (WIDE, BLOCK), 0)
    for side in range(2):
        strip = jnp.where(channel == CHANNELS + side, flip_ref[0, side].astype(jnp.float32), strip)
    strip = strip.astype(jnp.bfloat16)
    upward[2] = strip
    downward[2] = strip
    strip_out[...] = strip


GRIDDED = jax.ShapeDtypeStruct((ROWS, PADDED, BLOCK), jnp.bfloat16)
FIELD = jax.ShapeDtypeStruct((ROWS, WIDE, BLOCK), jnp.bfloat16)
RIM = jax.ShapeDtypeStruct((3, WIDE, BLOCK), jnp.bfloat16)
STRIP_COLUMNS = (0, 1, BLOCK - 2, BLOCK - 1)
STRIP = jax.ShapeDtypeStruct((WIDE, BLOCK), jnp.bfloat16)


def gather_rows(column_rows, edge_flip, gain, before, nexts):
    return pl.pallas_call(
        functools.partial(gather_kernel, column_rows),
        in_specs=[smem()] + [vmem()] * (2 + len(nexts)),
        out_specs=[vmem()] * 5,
        out_shape=[GRIDDED, FIELD, RIM, RIM, STRIP],
        scratch_shapes=[pltpu.VMEM(SUMMED, jnp.float32), *scatter_scratch()],
        compiler_params=pltpu.CompilerParams(vmem_limit_bytes=VMEM_LIMIT),
        name="gather_rows",
    )(edge_flip, gain, before, *nexts)


def turn_kernel(field, out, turned):
    for row in range(ROWS):
        turned[pl.ds(row, PADDED, stride=ROWS), :] = field[row].astype(jnp.float32)
    out[...] = turned[pl.ds(0, CHANNELS * ROWS), :].astype(jnp.bfloat16)


def channels_first(field):
    return pl.pallas_call(
        turn_kernel,
        in_specs=[vmem()],
        out_specs=vmem(),
        out_shape=jax.ShapeDtypeStruct((CHANNELS * ROWS, BLOCK), jnp.bfloat16),
        scratch_shapes=[pltpu.VMEM((PADDED * ROWS, BLOCK), jnp.float32)],
        compiler_params=pltpu.CompilerParams(vmem_limit_bytes=VMEM_LIMIT),
        name="channels_first",
    )(field)


def shifted_columns(value, left_end, right_end):
    lane = lanes((WIDE, BLOCK))
    left = jnp.where(lane == 0, left_end, pltpu.roll(value, 1, 1))
    right = jnp.where(lane == BLOCK - 1, right_end, pltpu.roll(value, BLOCK - 1, 1))
    return jnp.concatenate([left, value, right], axis=0)


def tap_sums(taps, one, two):
    both = jnp.concatenate([one, two], axis=1)
    result = jnp.dot(taps, both, preferred_element_type=jnp.float32)
    return result[:, :BLOCK], result[:, BLOCK:]


def row_tap(sums, at):
    return sums[at * WIDE : (at + 1) * WIDE]


def activated(value):
    return jax.nn.gelu(value).astype(jnp.bfloat16)


def inner_kernel(taps_ref, field, hidden, ends, sides, partial):
    taps = taps_ref[...]
    blank = jnp.zeros((WIDE, BLOCK), jnp.bfloat16)
    for row in range(0, ROWS, 2):
        partial[row], partial[row + 1] = tap_sums(
            taps,
            shifted_columns(field[row], blank, blank),
            shifted_columns(field[row + 1], blank, blank),
        )
    lane = lanes((WIDE, BLOCK))
    west = jnp.zeros((WIDE, BLOCK), jnp.float32)
    east = jnp.zeros((WIDE, BLOCK), jnp.float32)
    for row in range(ROWS):
        value = partial[row, WIDE : 2 * WIDE]
        if row > 0:
            value = value + partial[row - 1, :WIDE]
        if row < ROWS - 1:
            value = value + partial[row + 1, 2 * WIDE :]
        if row == 0:
            ends[0] = value
        elif row == ROWS - 1:
            ends[1] = value
        else:
            hidden[row] = activated(value)
        west = jnp.where(lane == row, pltpu.roll(value, row, 1), west)
        east = jnp.where(lane == row, pltpu.roll(value, row + 1, 1), east)
    hidden[0] = blank
    hidden[ROWS - 1] = blank
    sides[0] = west
    sides[1] = east


def inner_convolution(taps, field):
    pair = jax.ShapeDtypeStruct((2, WIDE, BLOCK), jnp.float32)
    return pl.pallas_call(
        inner_kernel,
        in_specs=[vmem()] * 2,
        out_specs=[vmem()] * 3,
        out_shape=[FIELD, pair, pair],
        scratch_shapes=[pltpu.VMEM((ROWS, 3 * WIDE, BLOCK), jnp.float32)],
        compiler_params=pltpu.CompilerParams(vmem_limit_bytes=VMEM_LIMIT),
        cost_estimate=pl.CostEstimate(
            flops=2 * 9 * WIDE * WIDE * ROWS * BLOCK, bytes_accessed=2 << 20, transcendentals=0
        ),
        name="inner_convolution",
    )(taps, field)


def strip_plan(column_rows):
    if column_rows == 2:
        return [], 3, 1
    return [-2, 2], column_rows, 2


def conv_kernel(
    column_rows,
    first_taps_ref,
    second_taps_ref,
    field,
    gridded,
    inner,
    ends_ref,
    sides_ref,
    above,
    below,
    own_strip,
    *rest,
):
    near, far, reach = strip_plan(column_rows)
    near_strips, (west_pack, east_pack) = rest[: len(near)], rest[len(near) : len(near) + 2]
    smoothed, hidden, partial, turned = rest[len(near) + 2 :]
    count = lax.axis_size("tile")
    tile = lax.axis_index("tile")
    lane = lanes((WIDE, BLOCK))
    last = ROWS + 1
    R = column_rows
    blank = jnp.zeros((WIDE, BLOCK), jnp.bfloat16)

    strips = {-1: above[2], 0: own_strip[...], 1: below[2]}
    strips.update((shift, ref[...]) for shift, ref in zip(near, near_strips))
    for at in range(-reach, reach + 1):
        strips[at - far], strips[at + far] = west_pack[at + reach], east_pack[at + reach]

    def place(shift):
        return lax.rem(tile + shift + count, count)

    def ends(shift, before, after, middle):
        before = jnp.where(place(shift) > 0, before, blank)
        after = jnp.where(place(shift) < count - 1, after, blank)
        return jnp.where(lane == 0, before, jnp.where(lane == last, after, middle))

    memo = {}

    def padded_column(shift, which):
        if (shift, which) not in memo:
            base = which * ROWS
            memo[shift, which] = ends(
                shift,
                pltpu.roll(strips[shift - 1], (1 - base - ROWS) % BLOCK, 1),
                pltpu.roll(strips[shift + 1], (last - base) % BLOCK, 1),
                pltpu.roll(strips[shift], (1 - base) % BLOCK, 1),
            )
        return memo[shift, which]

    row_id = lax.broadcasted_iota(jnp.int32, (BLOCK, BLOCK), 0)
    reversal = (row_id + lanes((BLOCK, BLOCK)) == last).astype(jnp.bfloat16)

    def reversed_lanes(planes):
        stacked = jnp.concatenate(planes, axis=0)
        turned_round = jnp.dot(stacked, reversal, preferred_element_type=jnp.float32)
        return [row_tap(turned_round, at) for at in range(len(planes))]

    def choose(shift, which, turned_round, plain):
        flips = strips[shift].astype(jnp.float32)[CHANNELS + which : CHANNELS + which + 1]
        return jnp.where(flips > 0.5, turned_round, plain.astype(jnp.float32)).astype(jnp.bfloat16)

    west_of = {shift: (shift - R, 3) for shift in {-1, 0, 1, R - 1, R, R + 1}}
    east_of = {shift: (shift + R, 0) for shift in {-1, 0, 1, -R - 1, -R, -R + 1}}
    keys = sorted(set(west_of.values()) | set(east_of.values()))
    flipped = dict(zip(keys, reversed_lanes([padded_column(*key) for key in keys])))
    west = {
        shift: choose(shift, 0, flipped[west_of[shift]], padded_column(*west_of[shift]))
        for shift in sorted(west_of)
    }
    east = {
        shift: choose(shift, 1, flipped[east_of[shift]], padded_column(*east_of[shift]))
        for shift in sorted(east_of)
    }

    def columns(value, west_plane, west_row, east_plane, east_row):
        return shifted_columns(
            value,
            pltpu.roll(west_plane, (BLOCK - west_row) % BLOCK, 1),
            pltpu.roll(east_plane, BLOCK - 1 - east_row, 1),
        )

    def along(result):
        return (
            row_tap(result, 0)
            + pltpu.roll(row_tap(result, 1), BLOCK - 1, 1)
            + pltpu.roll(row_tap(result, 2), BLOCK - 2, 1)
        )

    first_taps = first_taps_ref[...]
    up = [jnp.where(tile > 0, above[at], blank) for at in range(2)]
    down = [jnp.where(tile < count - 1, below[at], blank) for at in range(2)]
    from_up, from_down = tap_sums(
        first_taps, shifted_columns(up[1], blank, blank), shifted_columns(down[0], blank, blank)
    )
    from_up, from_down = row_tap(from_up, 0), row_tap(from_down, 2)
    from_west, from_east = tap_sums(
        first_taps,
        jnp.concatenate([west[0], blank, blank], axis=0),
        jnp.concatenate([blank, blank, east[0]], axis=0),
    )
    from_west, from_east = along(from_west), along(from_east)
    first = ends_ref[0] + from_up
    first = first + jnp.where(lane == 0, from_west, 0.0)
    first = first + jnp.where(lane == BLOCK - 1, pltpu.roll(from_east, BLOCK - 1, 1), 0.0)
    final = ends_ref[1] + from_down
    final = final + jnp.where(lane == 0, pltpu.roll(from_west, BLOCK - ROWS + 1, 1), 0.0)
    final = final + jnp.where(lane == BLOCK - 1, pltpu.roll(from_east, BLOCK - ROWS, 1), 0.0)
    hidden[1] = activated(first)
    hidden[ROWS] = activated(final)
    first_column = activated(sides_ref[0] + from_west)
    last_column = activated(sides_ref[1] + from_east)
    for row in range(1, ROWS - 1):
        value = jnp.where(lane == 0, pltpu.roll(first_column, BLOCK - row, 1), inner[row])
        hidden[row + 1] = jnp.where(
            lane == BLOCK - 1, pltpu.roll(last_column, BLOCK - 1 - row, 1), value
        )

    upper = jnp.zeros((WIDE, BLOCK), jnp.float32)
    lower = jnp.zeros((WIDE, BLOCK), jnp.float32)
    for at, (high, low) in enumerate(
        [(up[0], field[ROWS - 1]), (up[1], down[0]), (field[0], down[1])]
    ):
        from_row = ROWS - 1 + at
        one, two = tap_sums(
            first_taps,
            columns(high, west[-1], from_row, east[-1], from_row),
            columns(low, west[1], at, east[1], at),
        )
        upper += row_tap(one, at)
        lower += row_tap(two, at)
    hidden[0] = jnp.where(tile > 0, activated(upper), blank)
    hidden[last] = jnp.where(tile < count - 1, activated(lower), blank)

    west_hidden, east_hidden = {}, {}
    for at in (-1, 0, 1):
        q = at - R
        one = jnp.concatenate([padded_column(q, 2), padded_column(q, 3), east[q]], axis=0)
        q = at + R
        two = jnp.concatenate([west[q], padded_column(q, 0), padded_column(q, 1)], axis=0)
        one, two = tap_sums(first_taps, one, two)
        west_hidden[at], east_hidden[at] = activated(along(one)), activated(along(two))

    def hidden_side(shift, values):
        return ends(
            shift,
            pltpu.roll(values[-1], BLOCK - ROWS + 1, 1),
            pltpu.roll(values[1], last, 1),
            pltpu.roll(values[0], 1, 1),
        )

    plain = [hidden_side(-R, west_hidden), hidden_side(R, east_hidden)]
    west_side, east_side = [
        choose(0, which, turned_side, plain[which])
        for which, turned_side in enumerate(reversed_lanes(plain))
    ]

    second_taps = second_taps_ref[...]
    for p in range(0, ROWS + 2, 2):
        partial[p], partial[p + 1] = tap_sums(
            second_taps,
            columns(hidden[p], west_side, p, east_side, p),
            columns(hidden[p + 1], west_side, p + 1, east_side, p + 1),
        )
    for row in range(ROWS):
        branch = (
            partial[row, :PADDED]
            + partial[row + 1, WIDE : WIDE + PADDED]
            + partial[row + 2, 2 * WIDE : 2 * WIDE + PADDED]
        )
        turned[pl.ds(row, PADDED, stride=ROWS), :] = gridded[row].astype(jnp.float32) + branch
    smoothed[...] = turned[pl.ds(0, CHANNELS * ROWS), :].astype(jnp.bfloat16)


def convolutions(column_rows, *operands):
    return pl.pallas_call(
        functools.partial(conv_kernel, column_rows),
        in_specs=[vmem()] * len(operands),
        out_specs=vmem(),
        out_shape=jax.ShapeDtypeStruct((CHANNELS * ROWS, BLOCK), jnp.bfloat16),
        scratch_shapes=[
            pltpu.VMEM((ROWS + 2, WIDE, BLOCK), jnp.bfloat16),
            pltpu.VMEM((ROWS + 2, 3 * WIDE, BLOCK), jnp.float32),
            pltpu.VMEM((PADDED * ROWS, BLOCK), jnp.float32),
        ],
        compiler_params=pltpu.CompilerParams(vmem_limit_bytes=VMEM_LIMIT),
        name="convolutions",
    )(*operands)


def tap_matrix(kernel):
    pad = WIDE - CHANNELS
    taps = jnp.pad(kernel, ((0, 0), (0, pad), (0, pad))).reshape(3, 3, WIDE, WIDE)
    return taps.transpose(0, 2, 1, 3).reshape(3 * WIDE, 3 * WIDE)


def from_shift(value, shift):
    count = lax.axis_size("tile")
    return lax.ppermute(value, "tile", [(i, (i - shift) % count) for i in range(count)])


def per_device(
    source, weights, block_source, block_target, edge_flip, norm_gain, first_kernel, second_kernel
):
    count = lax.axis_size("tile")
    column_rows = count // TILE_COLS
    field = source.reshape(ROWS, CHANNELS, BLOCK).transpose(1, 0, 2).reshape(-1, BLOCK)
    same, *nexts = regrid(block_target, block_source, field, weights, column_rows)

    for across in range(TILE_COLS):
        pairs = [
            (c * column_rows + p, (c ^ across) * column_rows + p + 1)
            for c in range(TILE_COLS)
            for p in range(column_rows - 1)
        ]
        nexts[across] = lax.ppermute(nexts[across], "tile", pairs)
    same = lax.all_to_all(
        same,
        "tile",
        0,
        0,
        axis_index_groups=[
            [c * column_rows + p for c in range(TILE_COLS)] for p in range(column_rows)
        ],
        tiled=True,
    )

    gain = jnp.broadcast_to(
        jnp.pad(norm_gain, (0, PADDED - CHANNELS))[:, None], (PADDED, BLOCK)
    )
    first_taps, second_taps = tap_matrix(first_kernel), tap_matrix(second_kernel)
    before = early_rows(column_rows, same, nexts[:EARLY])
    nexts, gain, first_taps, second_taps = lax.optimization_barrier(
        (nexts[EARLY:], gain, first_taps, second_taps)
    )
    gridded, normed, upward, downward, strip = gather_rows(
        column_rows, edge_flip, gain, before, nexts
    )
    rims = [from_shift(downward, -1), from_shift(upward, 1)]
    near, far, reach = strip_plan(column_rows)
    strips = [from_shift(strip, shift) for shift in near]
    inner = inner_convolution(first_taps, normed)
    held = {-1: rims[0][2], 0: strip, 1: rims[1][2], **dict(zip(near, strips))}
    pack = jnp.stack([held[at] for at in range(-reach, reach + 1)])
    pack, inner = lax.optimization_barrier((pack, inner))
    strips += [from_shift(pack, -far), from_shift(pack, far)]
    gridded_out = channels_first(gridded)
    smoothed = convolutions(
        column_rows, first_taps, second_taps, normed, gridded, *inner, *rims, strip, *strips
    )

    def placed(value):
        return value.reshape(CHANNELS, ROWS, BLOCK).transpose(1, 0, 2)[:, None]

    return placed(gridded_out), placed(smoothed)


def solution(mesh):
    in_specs = (
        P("tile", "groups", None, None),
        P("tile", None, None),
        P("tile"),
        P("tile"),
        P("tile", None),
        P(),
        P(),
        P(),
    )
    out_specs = (P("tile", "groups", None, None), P("tile", "groups", None, None))
    return jax.shard_map(
        per_device, mesh=mesh, in_specs=in_specs, out_specs=out_specs, check_vma=False
    )
```

```python
import functools

import jax
import jax.numpy as jnp
from jax import lax
from jax.experimental import pallas as pl
from jax.experimental.pallas import tpu as pltpu
from jax.sharding import PartitionSpec as P

BLOCK = 128
CHANNELS = 69
PADDED = 72
WIDE = 80
ROWS = 32
ROW_BITS = 5
TILE_COLS = 8
CAP = 8
GROUPS = 2 * TILE_COLS
SLOTS = GROUPS * CAP
CHUNK = 8
MARK = CHANNELS
EPSILON = 1e-05
VMEM_LIMIT = 40 * 1024 * 1024
REGRID_VMEM = 60 * 1024 * 1024


def vmem():
    return pl.BlockSpec(memory_space=pltpu.VMEM)


def smem():
    return pl.BlockSpec(memory_space=pltpu.SMEM)


def split(value, size):
    if size & (size - 1) == 0:
        return value >> (size.bit_length() - 1), value & (size - 1)
    return lax.div(value, size), lax.rem(value, size)


def lanes(shape):
    return lax.broadcasted_iota(jnp.int32, shape, len(shape) - 1)


def regrid_kernel(
    column_rows, target_hbm, target_row_hbm, index_hbm, source_hbm, weight_hbm, *rest
):
    same_out, next_outs = rest[0], rest[1 : 1 + TILE_COLS]
    (
        target_ref,
        target_row_ref,
        index_ref,
        source,
        weight,
        wide,
        field,
        sums,
        rounded,
        plan,
        plan_scalars,
        plan_sem,
        in_sems,
        weight_sems,
        out_sems,
    ) = rest[1 + TILE_COLS :]
    entries = weight.shape[0]
    chunks = entries // CHUNK
    tile = lax.axis_index("tile")
    column, position = split(tile, column_rows)

    small_copies = [
        pltpu.make_async_copy(target_row_hbm, target_row_ref, in_sems.at[0]),
        pltpu.make_async_copy(target_hbm, target_ref, in_sems.at[1]),
        pltpu.make_async_copy(index_hbm, index_ref, in_sems.at[2]),
    ]
    source_copy = pltpu.make_async_copy(source_hbm, source, in_sems.at[3])
    for copy in small_copies:
        copy.start()
    source_copy.start()

    def chunk_copy(chunk):
        part = pl.ds(chunk * CHUNK, CHUNK)
        return pltpu.make_async_copy(weight_hbm.at[part], weight.at[part], weight_sems.at[chunk])

    for chunk in range(chunks):
        chunk_copy(chunk).start()

    small_copies[0].wait()
    target = target_row_ref[...]
    owner, row = split(target, ROWS)
    owner_column, owner_position = split(owner, column_rows)
    group = jnp.where(
        owner_position == position, owner_column, TILE_COLS + (owner_column ^ column)
    )
    key = group * ROWS + row
    square = (entries, entries)
    down = lax.broadcasted_iota(jnp.int32, square, 0)
    along = lanes(square)
    key_along = jnp.broadcast_to(key.astype(jnp.float32), square)
    key_down = jnp.broadcast_to(
        jnp.sum(jnp.where(down == along, key_along, 0.0), axis=1, keepdims=True), square
    )
    equal = key_along == key_down
    doubles = jnp.sum(jnp.where(equal & (along < down), 1.0, 0.0), axis=1, keepdims=True)
    in_group = (key_down.astype(jnp.int32) >> ROW_BITS) == (key_along.astype(jnp.int32) >> ROW_BITS)
    below = in_group & (key_down < key_along) & (jnp.broadcast_to(doubles, square) == 0.0)
    rank = jnp.sum(jnp.where(below, 1.0, 0.0), axis=0, keepdims=True)
    mentions = jnp.sum(jnp.where(equal & (down < along), 1.0, 0.0), axis=0, keepdims=True)
    slots = group * CAP + rank.astype(jnp.int32)
    plan[...] = slots + jnp.where(mentions == 0.0, SLOTS, 0)
    plan_copy = pltpu.make_async_copy(plan, plan_scalars, plan_sem)
    plan_copy.start()

    tail = PADDED - 8
    for slot in range(SLOTS):
        rounded[slot, tail:] = jnp.full((8, BLOCK), ROWS, jnp.bfloat16)
    wide[pl.ds(CHANNELS * ROWS, (PADDED - CHANNELS) * ROWS), :] = jnp.zeros(
        ((PADDED - CHANNELS) * ROWS, BLOCK), jnp.float32
    )
    nothing = jnp.zeros((WIDE - PADDED, BLOCK), jnp.float32)
    source_copy.wait()
    wide[pl.ds(0, CHANNELS * ROWS), :] = source[...].astype(jnp.float32)
    for row in range(ROWS):
        block = wide[pl.ds(row, PADDED, stride=ROWS), :]
        field[row] = jnp.concatenate([block, nothing], axis=0).astype(jnp.bfloat16)
    is_mark = lax.broadcasted_iota(jnp.int32, (8, BLOCK), 0) == MARK - tail
    small_copies[1].wait()
    small_copies[2].wait()
    plan_copy.wait()

    for chunk in range(chunks):
        chunk_copy(chunk).wait()
        for entry in range(chunk * CHUNK, (chunk + 1) * CHUNK):
            code = plan_scalars[0, entry]
            slot = code & (SLOTS - 1)
            row = split(target_ref[entry], ROWS)[1]
            product = jnp.dot(
                field[index_ref[entry]], weight[entry], preferred_element_type=jnp.float32
            )
            total = jnp.where(code >= SLOTS, 0.0, sums[slot]) + product[:PADDED]
            sums[slot] = total
            marked = jnp.where(is_mark, row.astype(jnp.float32), total[tail:])
            rounded[slot] = jnp.concatenate([total[:tail], marked], axis=0).astype(jnp.bfloat16)
    copies = []
    for group in range(GROUPS):
        part = rounded.at[pl.ds(group * CAP, CAP)]
        if group < TILE_COLS:
            out = same_out.at[pl.ds(group * CAP, CAP)]
        else:
            out = next_outs[group - TILE_COLS]
        copies.append(pltpu.make_async_copy(part, out, out_sems.at[group]))
    for copy in copies:
        copy.start()
    for copy in copies:
        copy.wait()


def regrid(target, source_index, field, weights, column_rows):
    piece = jax.ShapeDtypeStruct((CAP, PADDED, BLOCK), jnp.bfloat16)
    same = jax.ShapeDtypeStruct((TILE_COLS * CAP, PADDED, BLOCK), jnp.bfloat16)
    hbm = pl.BlockSpec(memory_space=pl.ANY)
    entries = weights.shape[0]
    return pl.pallas_call(
        functools.partial(regrid_kernel, column_rows),
        in_specs=[hbm] * 5,
        out_specs=[hbm] * (1 + TILE_COLS),
        out_shape=[same] + [piece] * TILE_COLS,
        scratch_shapes=[
            pltpu.SMEM(target.shape, jnp.int32),
            pltpu.VMEM((1, entries), jnp.int32),
            pltpu.SMEM(source_index.shape, jnp.int32),
            pltpu.VMEM(field.shape, jnp.bfloat16),
            pltpu.VMEM(weights.shape, jnp.bfloat16),
            pltpu.VMEM((PADDED * ROWS, BLOCK), jnp.float32),
            pltpu.VMEM((ROWS, WIDE, BLOCK), jnp.bfloat16),
            pltpu.VMEM((SLOTS, PADDED, BLOCK), jnp.float32),
            pltpu.VMEM((SLOTS, PADDED, BLOCK), jnp.bfloat16),
            pltpu.VMEM((1, entries), jnp.int32),
            pltpu.SMEM((1, entries), jnp.int32),
            pltpu.SemaphoreType.DMA,
            pltpu.SemaphoreType.DMA((4,)),
            pltpu.SemaphoreType.DMA((entries // CHUNK,)),
            pltpu.SemaphoreType.DMA((GROUPS,)),
        ],
        compiler_params=pltpu.CompilerParams(vmem_limit_bytes=REGRID_VMEM),
        name="regrid",
    )(target, target.reshape(1, -1), source_index, field, weights)


def gather_kernel(column_rows, flip_ref, gain_ref, same, *rest):
    nexts = rest[:TILE_COLS]
    (
        gridded,
        normed,
        upward,
        downward,
        strip_out,
        summed,
        marks,
        rows,
        mark_sem,
    ) = rest[TILE_COLS:]
    position = lax.rem(lax.axis_index("tile"), column_rows)
    half = SLOTS // 2
    lane = lanes((1, BLOCK))
    mark = jnp.zeros((1, BLOCK), jnp.float32)
    for slot in range(SLOTS):
        piece = same.at[slot] if slot < half else nexts[slot // CAP - TILE_COLS].at[slot % CAP]
        mark = jnp.where(lane == slot, piece[MARK : MARK + 1].astype(jnp.float32), mark)
    marks[...] = mark.astype(jnp.int32)
    copy = pltpu.make_async_copy(marks, rows, mark_sem)
    copy.start()
    summed[...] = jnp.zeros_like(summed)
    copy.wait()

    def add(slot, piece):
        row = rows[0, slot]
        summed[row] = summed[row] + piece.astype(jnp.float32)

    def add_same(step, carry):
        for at in range(CAP):
            add(step * CAP + at, same[step * CAP + at])
        return carry

    lax.fori_loop(0, TILE_COLS, add_same, 0)

    @pl.when(position > 0)
    def _():
        for group in range(TILE_COLS):
            for place in range(CAP):
                add(half + group * CAP + place, nexts[group][place])

    gain = gain_ref[...]
    channel = lax.broadcasted_iota(jnp.int32, (PADDED, BLOCK), 0)
    nothing = jnp.zeros((WIDE - PADDED, BLOCK), jnp.float32)
    lane = lanes((WIDE, BLOCK))
    strip = jnp.zeros((WIDE, BLOCK), jnp.bfloat16)
    for row in range(ROWS):
        rounded = summed[row].astype(jnp.bfloat16)
        gridded[row] = rounded
        value = rounded.astype(jnp.float32)
        value = jnp.where(channel < CHANNELS, value, 0.0)
        square = jnp.sum(value * value, axis=0, keepdims=True) * (1.0 / CHANNELS)
        scaled = value * lax.rsqrt(square + EPSILON) * gain
        scaled = jnp.concatenate([scaled, nothing], axis=0).astype(jnp.bfloat16)
        normed[row] = scaled
        if row < 2:
            upward[row] = scaled
        if row >= ROWS - 2:
            downward[row - ROWS + 2] = scaled
        strip = jnp.where((lane >> 2) == row, pltpu.roll(scaled, 4 * row + 2, 1), strip)
    to_lane = lanes((BLOCK, BLOCK))
    from_lane = 4 * (to_lane & (ROWS - 1)) + (((to_lane >> ROW_BITS) + 2) & 3)
    order = lax.broadcasted_iota(jnp.int32, (BLOCK, BLOCK), 0) == from_lane
    strip = jnp.dot(strip, order.astype(jnp.bfloat16), preferred_element_type=jnp.float32)
    channel = lax.broadcasted_iota(jnp.int32, (WIDE, BLOCK), 0)
    for side in range(2):
        strip = jnp.where(channel == CHANNELS + side, flip_ref[0, side].astype(jnp.float32), strip)
    strip = strip.astype(jnp.bfloat16)
    upward[2] = strip
    downward[2] = strip
    strip_out[...] = strip


GRIDDED = jax.ShapeDtypeStruct((ROWS, PADDED, BLOCK), jnp.bfloat16)
FIELD = jax.ShapeDtypeStruct((ROWS, WIDE, BLOCK), jnp.bfloat16)
RIM = jax.ShapeDtypeStruct((3, WIDE, BLOCK), jnp.bfloat16)
STRIP_COLUMNS = (0, 1, BLOCK - 2, BLOCK - 1)
STRIP = jax.ShapeDtypeStruct((WIDE, BLOCK), jnp.bfloat16)


def gather_rows(column_rows, edge_flip, gain, same, nexts):
    return pl.pallas_call(
        functools.partial(gather_kernel, column_rows),
        in_specs=[smem()] + [vmem()] * (2 + TILE_COLS),
        out_specs=[vmem()] * 5,
        out_shape=[GRIDDED, FIELD, RIM, RIM, STRIP],
        scratch_shapes=[
            pltpu.VMEM((ROWS + 1, PADDED, BLOCK), jnp.float32),
            pltpu.VMEM((1, SLOTS), jnp.int32),
            pltpu.SMEM((1, SLOTS), jnp.int32),
            pltpu.SemaphoreType.DMA,
        ],
        compiler_params=pltpu.CompilerParams(vmem_limit_bytes=VMEM_LIMIT),
        name="gather_rows",
    )(edge_flip, gain, same, *nexts)


def turn_kernel(field, out, turned):
    for row in range(ROWS):
        turned[pl.ds(row, PADDED, stride=ROWS), :] = field[row].astype(jnp.float32)
    out[...] = turned[pl.ds(0, CHANNELS * ROWS), :].astype(jnp.bfloat16)


def channels_first(field):
    return pl.pallas_call(
        turn_kernel,
        in_specs=[vmem()],
        out_specs=vmem(),
        out_shape=jax.ShapeDtypeStruct((CHANNELS * ROWS, BLOCK), jnp.bfloat16),
        scratch_shapes=[pltpu.VMEM((PADDED * ROWS, BLOCK), jnp.float32)],
        compiler_params=pltpu.CompilerParams(vmem_limit_bytes=VMEM_LIMIT),
        name="channels_first",
    )(field)


def shifted_columns(value, left_end, right_end):
    lane = lanes((WIDE, BLOCK))
    left = jnp.where(lane == 0, left_end, pltpu.roll(value, 1, 1))
    right = jnp.where(lane == BLOCK - 1, right_end, pltpu.roll(value, BLOCK - 1, 1))
    return jnp.concatenate([left, value, right], axis=0)


def tap_sums(taps, one, two):
    both = jnp.concatenate([one, two], axis=1)
    result = jnp.dot(taps, both, preferred_element_type=jnp.float32)
    return result[:, :BLOCK], result[:, BLOCK:]


def row_tap(sums, at):
    return sums[at * WIDE : (at + 1) * WIDE]


def activated(value):
    return jax.nn.gelu(value).astype(jnp.bfloat16)


def inner_kernel(taps_ref, field, hidden, ends, sides, partial):
    taps = taps_ref[...]
    blank = jnp.zeros((WIDE, BLOCK), jnp.bfloat16)
    for row in range(0, ROWS, 2):
        partial[row], partial[row + 1] = tap_sums(
            taps,
            shifted_columns(field[row], blank, blank),
            shifted_columns(field[row + 1], blank, blank),
        )
    lane = lanes((WIDE, BLOCK))
    west = jnp.zeros((WIDE, BLOCK), jnp.float32)
    east = jnp.zeros((WIDE, BLOCK), jnp.float32)
    for row in range(ROWS):
        value = partial[row, WIDE : 2 * WIDE]
        if row > 0:
            value = value + partial[row - 1, :WIDE]
        if row < ROWS - 1:
            value = value + partial[row + 1, 2 * WIDE :]
        if row == 0:
            ends[0] = value
        elif row == ROWS - 1:
            ends[1] = value
        else:
            hidden[row] = activated(value)
        west = jnp.where(lane == row, pltpu.roll(value, row, 1), west)
        east = jnp.where(lane == row, pltpu.roll(value, row + 1, 1), east)
    hidden[0] = blank
    hidden[ROWS - 1] = blank
    sides[0] = west
    sides[1] = east


def inner_convolution(taps, field):
    pair = jax.ShapeDtypeStruct((2, WIDE, BLOCK), jnp.float32)
    return pl.pallas_call(
        inner_kernel,
        in_specs=[vmem()] * 2,
        out_specs=[vmem()] * 3,
        out_shape=[FIELD, pair, pair],
        scratch_shapes=[pltpu.VMEM((ROWS, 3 * WIDE, BLOCK), jnp.float32)],
        compiler_params=pltpu.CompilerParams(vmem_limit_bytes=VMEM_LIMIT),
        cost_estimate=pl.CostEstimate(
            flops=2 * 9 * WIDE * WIDE * ROWS * BLOCK, bytes_accessed=2 << 20, transcendentals=0
        ),
        name="inner_convolution",
    )(taps, field)


def strip_plan(column_rows):
    if column_rows == 2:
        return [], 3, 1
    return [-2, 2], column_rows, 2


def conv_kernel(
    column_rows,
    first_taps_ref,
    second_taps_ref,
    field,
    gridded,
    inner,
    ends_ref,
    sides_ref,
    above,
    below,
    own_strip,
    *rest,
):
    near, far, reach = strip_plan(column_rows)
    near_strips, (west_pack, east_pack) = rest[: len(near)], rest[len(near) : len(near) + 2]
    smoothed, hidden, partial, turned = rest[len(near) + 2 :]
    count = lax.axis_size("tile")
    tile = lax.axis_index("tile")
    lane = lanes((WIDE, BLOCK))
    last = ROWS + 1
    R = column_rows
    blank = jnp.zeros((WIDE, BLOCK), jnp.bfloat16)

    strips = {-1: above[2], 0: own_strip[...], 1: below[2]}
    strips.update((shift, ref[...]) for shift, ref in zip(near, near_strips))
    for at in range(-reach, reach + 1):
        strips[at - far], strips[at + far] = west_pack[at + reach], east_pack[at + reach]

    def place(shift):
        return lax.rem(tile + shift + count, count)

    def ends(shift, before, after, middle):
        before = jnp.where(place(shift) > 0, before, blank)
        after = jnp.where(place(shift) < count - 1, after, blank)
        return jnp.where(lane == 0, before, jnp.where(lane == last, after, middle))

    memo = {}

    def padded_column(shift, which):
        if (shift, which) not in memo:
            base = which * ROWS
            memo[shift, which] = ends(
                shift,
                pltpu.roll(strips[shift - 1], (1 - base - ROWS) % BLOCK, 1),
                pltpu.roll(strips[shift + 1], (last - base) % BLOCK, 1),
                pltpu.roll(strips[shift], (1 - base) % BLOCK, 1),
            )
        return memo[shift, which]

    row_id = lax.broadcasted_iota(jnp.int32, (BLOCK, BLOCK), 0)
    reversal = (row_id + lanes((BLOCK, BLOCK)) == last).astype(jnp.bfloat16)

    def reversed_lanes(planes):
        stacked = jnp.concatenate(planes, axis=0)
        turned_round = jnp.dot(stacked, reversal, preferred_element_type=jnp.float32)
        return [row_tap(turned_round, at) for at in range(len(planes))]

    def choose(shift, which, turned_round, plain):
        flips = strips[shift].astype(jnp.float32)[CHANNELS + which : CHANNELS + which + 1]
        return jnp.where(flips > 0.5, turned_round, plain.astype(jnp.float32)).astype(jnp.bfloat16)

    west_of = {shift: (shift - R, 3) for shift in {-1, 0, 1, R - 1, R, R + 1}}
    east_of = {shift: (shift + R, 0) for shift in {-1, 0, 1, -R - 1, -R, -R + 1}}
    keys = sorted(set(west_of.values()) | set(east_of.values()))
    flipped = dict(zip(keys, reversed_lanes([padded_column(*key) for key in keys])))
    west = {
        shift: choose(shift, 0, flipped[west_of[shift]], padded_column(*west_of[shift]))
        for shift in sorted(west_of)
    }
    east = {
        shift: choose(shift, 1, flipped[east_of[shift]], padded_column(*east_of[shift]))
        for shift in sorted(east_of)
    }

    def columns(value, west_plane, west_row, east_plane, east_row):
        return shifted_columns(
            value,
            pltpu.roll(west_plane, (BLOCK - west_row) % BLOCK, 1),
            pltpu.roll(east_plane, BLOCK - 1 - east_row, 1),
        )

    def along(result):
        return (
            row_tap(result, 0)
            + pltpu.roll(row_tap(result, 1), BLOCK - 1, 1)
            + pltpu.roll(row_tap(result, 2), BLOCK - 2, 1)
        )

    first_taps = first_taps_ref[...]
    up = [jnp.where(tile > 0, above[at], blank) for at in range(2)]
    down = [jnp.where(tile < count - 1, below[at], blank) for at in range(2)]
    from_up, from_down = tap_sums(
        first_taps, shifted_columns(up[1], blank, blank), shifted_columns(down[0], blank, blank)
    )
    from_up, from_down = row_tap(from_up, 0), row_tap(from_down, 2)
    from_west, from_east = tap_sums(
        first_taps,
        jnp.concatenate([west[0], blank, blank], axis=0),
        jnp.concatenate([blank, blank, east[0]], axis=0),
    )
    from_west, from_east = along(from_west), along(from_east)
    first = ends_ref[0] + from_up
    first = first + jnp.where(lane == 0, from_west, 0.0)
    first = first + jnp.where(lane == BLOCK - 1, pltpu.roll(from_east, BLOCK - 1, 1), 0.0)
    final = ends_ref[1] + from_down
    final = final + jnp.where(lane == 0, pltpu.roll(from_west, BLOCK - ROWS + 1, 1), 0.0)
    final = final + jnp.where(lane == BLOCK - 1, pltpu.roll(from_east, BLOCK - ROWS, 1), 0.0)
    hidden[1] = activated(first)
    hidden[ROWS] = activated(final)
    first_column = activated(sides_ref[0] + from_west)
    last_column = activated(sides_ref[1] + from_east)
    for row in range(1, ROWS - 1):
        value = jnp.where(lane == 0, pltpu.roll(first_column, BLOCK - row, 1), inner[row])
        hidden[row + 1] = jnp.where(
            lane == BLOCK - 1, pltpu.roll(last_column, BLOCK - 1 - row, 1), value
        )

    upper = jnp.zeros((WIDE, BLOCK), jnp.float32)
    lower = jnp.zeros((WIDE, BLOCK), jnp.float32)
    for at, (high, low) in enumerate(
        [(up[0], field[ROWS - 1]), (up[1], down[0]), (field[0], down[1])]
    ):
        from_row = ROWS - 1 + at
        one, two = tap_sums(
            first_taps,
            columns(high, west[-1], from_row, east[-1], from_row),
            columns(low, west[1], at, east[1], at),
        )
        upper += row_tap(one, at)
        lower += row_tap(two, at)
    hidden[0] = jnp.where(tile > 0, activated(upper), blank)
    hidden[last] = jnp.where(tile < count - 1, activated(lower), blank)

    west_hidden, east_hidden = {}, {}
    for at in (-1, 0, 1):
        q = at - R
        one = jnp.concatenate([padded_column(q, 2), padded_column(q, 3), east[q]], axis=0)
        q = at + R
        two = jnp.concatenate([west[q], padded_column(q, 0), padded_column(q, 1)], axis=0)
        one, two = tap_sums(first_taps, one, two)
        west_hidden[at], east_hidden[at] = activated(along(one)), activated(along(two))

    def hidden_side(shift, values):
        return ends(
            shift,
            pltpu.roll(values[-1], BLOCK - ROWS + 1, 1),
            pltpu.roll(values[1], last, 1),
            pltpu.roll(values[0], 1, 1),
        )

    plain = [hidden_side(-R, west_hidden), hidden_side(R, east_hidden)]
    west_side, east_side = [
        choose(0, which, turned_side, plain[which])
        for which, turned_side in enumerate(reversed_lanes(plain))
    ]

    second_taps = second_taps_ref[...]
    for p in range(0, ROWS + 2, 2):
        partial[p], partial[p + 1] = tap_sums(
            second_taps,
            columns(hidden[p], west_side, p, east_side, p),
            columns(hidden[p + 1], west_side, p + 1, east_side, p + 1),
        )
    for row in range(ROWS):
        branch = (
            partial[row, :PADDED]
            + partial[row + 1, WIDE : WIDE + PADDED]
            + partial[row + 2, 2 * WIDE : 2 * WIDE + PADDED]
        )
        turned[pl.ds(row, PADDED, stride=ROWS), :] = gridded[row].astype(jnp.float32) + branch
    smoothed[...] = turned[pl.ds(0, CHANNELS * ROWS), :].astype(jnp.bfloat16)


def convolutions(column_rows, *operands):
    return pl.pallas_call(
        functools.partial(conv_kernel, column_rows),
        in_specs=[vmem()] * len(operands),
        out_specs=vmem(),
        out_shape=jax.ShapeDtypeStruct((CHANNELS * ROWS, BLOCK), jnp.bfloat16),
        scratch_shapes=[
            pltpu.VMEM((ROWS + 2, WIDE, BLOCK), jnp.bfloat16),
            pltpu.VMEM((ROWS + 2, 3 * WIDE, BLOCK), jnp.float32),
            pltpu.VMEM((PADDED * ROWS, BLOCK), jnp.float32),
        ],
        compiler_params=pltpu.CompilerParams(vmem_limit_bytes=VMEM_LIMIT),
        name="convolutions",
    )(*operands)


def tap_matrix(kernel):
    pad = WIDE - CHANNELS
    taps = jnp.pad(kernel, ((0, 0), (0, pad), (0, pad))).reshape(3, 3, WIDE, WIDE)
    return taps.transpose(0, 2, 1, 3).reshape(3 * WIDE, 3 * WIDE)


def from_shift(value, shift):
    count = lax.axis_size("tile")
    return lax.ppermute(value, "tile", [(i, (i - shift) % count) for i in range(count)])


def per_device(
    source, weights, block_source, block_target, edge_flip, norm_gain, first_kernel, second_kernel
):
    count = lax.axis_size("tile")
    column_rows = count // TILE_COLS
    field = source.reshape(ROWS, CHANNELS, BLOCK).transpose(1, 0, 2).reshape(-1, BLOCK)
    same, *nexts = regrid(block_target, block_source, field, weights, column_rows)

    for across in range(TILE_COLS):
        pairs = [
            (c * column_rows + p, (c ^ across) * column_rows + p + 1)
            for c in range(TILE_COLS)
            for p in range(column_rows - 1)
        ]
        nexts[across] = lax.ppermute(nexts[across], "tile", pairs)
    same = lax.all_to_all(
        same,
        "tile",
        0,
        0,
        axis_index_groups=[
            [c * column_rows + p for c in range(TILE_COLS)] for p in range(column_rows)
        ],
        tiled=True,
    )

    gain = jnp.broadcast_to(
        jnp.pad(norm_gain, (0, PADDED - CHANNELS))[:, None], (PADDED, BLOCK)
    )
    first_taps, second_taps = tap_matrix(first_kernel), tap_matrix(second_kernel)
    same, nexts, gain, first_taps, second_taps = lax.optimization_barrier(
        (same, nexts, gain, first_taps, second_taps)
    )
    gridded, normed, upward, downward, strip = gather_rows(
        column_rows, edge_flip, gain, same, nexts
    )
    rims = [from_shift(downward, -1), from_shift(upward, 1)]
    near, far, reach = strip_plan(column_rows)
    strips = [from_shift(strip, shift) for shift in near]
    inner = inner_convolution(first_taps, normed)
    held = {-1: rims[0][2], 0: strip, 1: rims[1][2], **dict(zip(near, strips))}
    pack = jnp.stack([held[at] for at in range(-reach, reach + 1)])
    pack, inner = lax.optimization_barrier((pack, inner))
    strips += [from_shift(pack, -far), from_shift(pack, far)]
    gridded_out = channels_first(gridded)
    smoothed = convolutions(
        column_rows, first_taps, second_taps, normed, gridded, *inner, *rims, strip, *strips
    )

    def placed(value):
        return value.reshape(CHANNELS, ROWS, BLOCK).transpose(1, 0, 2)[:, None]

    return placed(gridded_out), placed(smoothed)


def solution(mesh):
    in_specs = (
        P("tile", "groups", None, None),
        P("tile", None, None),
        P("tile"),
        P("tile"),
        P("tile", None),
        P(),
        P(),
        P(),
    )
    out_specs = (P("tile", "groups", None, None), P("tile", "groups", None, None))
    return jax.shard_map(
        per_device, mesh=mesh, in_specs=in_specs, out_specs=out_specs, check_vma=False
    )
```

```python
import functools

import jax
import jax.numpy as jnp
from jax import lax
from jax.experimental import pallas as pl
from jax.experimental.pallas import tpu as pltpu
from jax.sharding import PartitionSpec as P

BLOCK = 128
CHANNELS = 69
PADDED = 72
WIDE = 80
ROWS = 32
ROW_BITS = 5
TILE_COLS = 8
CAP = 8
GROUPS = 2 * TILE_COLS
SLOTS = GROUPS * CAP
CHUNK = 48
MARK = CHANNELS
EPSILON = 1e-05
VMEM_LIMIT = 40 * 1024 * 1024
REGRID_VMEM = 60 * 1024 * 1024


def vmem():
    return pl.BlockSpec(memory_space=pltpu.VMEM)


def smem():
    return pl.BlockSpec(memory_space=pltpu.SMEM)


def split(value, size):
    if size & (size - 1) == 0:
        return value >> (size.bit_length() - 1), value & (size - 1)
    return lax.div(value, size), lax.rem(value, size)


def lanes(shape):
    return lax.broadcasted_iota(jnp.int32, shape, len(shape) - 1)


def regrid_kernel(
    column_rows, target_hbm, target_row_hbm, index_hbm, source_hbm, weight_hbm, *rest
):
    same_out, next_outs = rest[0], rest[1 : 1 + TILE_COLS]
    (
        target_ref,
        target_row_ref,
        index_ref,
        source,
        weight,
        wide,
        field,
        sums,
        rounded,
        plan,
        plan_scalars,
        plan_sem,
        in_sems,
        weight_sems,
        out_sems,
    ) = rest[1 + TILE_COLS :]
    entries = weight.shape[0]
    chunks = entries // CHUNK
    tile = lax.axis_index("tile")
    column, position = split(tile, column_rows)

    small_copies = [
        pltpu.make_async_copy(target_row_hbm, target_row_ref, in_sems.at[0]),
        pltpu.make_async_copy(target_hbm, target_ref, in_sems.at[1]),
        pltpu.make_async_copy(index_hbm, index_ref, in_sems.at[2]),
    ]
    source_copy = pltpu.make_async_copy(source_hbm, source, in_sems.at[3])
    for copy in small_copies:
        copy.start()
    source_copy.start()

    def chunk_copy(chunk):
        part = pl.ds(chunk * CHUNK, CHUNK)
        return pltpu.make_async_copy(weight_hbm.at[part], weight.at[part], weight_sems.at[chunk])

    for chunk in range(chunks):
        chunk_copy(chunk).start()

    small_copies[0].wait()
    target = target_row_ref[...]
    owner, row = split(target, ROWS)
    owner_column, owner_position = split(owner, column_rows)
    group = jnp.where(
        owner_position == position, owner_column, TILE_COLS + (owner_column ^ column)
    )
    key = group * ROWS + row
    square = (entries, entries)
    down = lax.broadcasted_iota(jnp.int32, square, 0)
    along = lanes(square)
    key_along = jnp.broadcast_to(key.astype(jnp.float32), square)
    key_down = jnp.broadcast_to(
        jnp.sum(jnp.where(down == along, key_along, 0.0), axis=1, keepdims=True), square
    )
    equal = key_along == key_down
    doubles = jnp.sum(jnp.where(equal & (along < down), 1.0, 0.0), axis=1, keepdims=True)
    in_group = (key_down.astype(jnp.int32) >> ROW_BITS) == (key_along.astype(jnp.int32) >> ROW_BITS)
    below = in_group & (key_down < key_along) & (jnp.broadcast_to(doubles, square) == 0.0)
    rank = jnp.sum(jnp.where(below, 1.0, 0.0), axis=0, keepdims=True)
    mentions = jnp.sum(jnp.where(equal & (down < along), 1.0, 0.0), axis=0, keepdims=True)
    slots = group * CAP + rank.astype(jnp.int32)
    plan[...] = slots + jnp.where(mentions == 0.0, SLOTS, 0)
    plan_copy = pltpu.make_async_copy(plan, plan_scalars, plan_sem)
    plan_copy.start()

    tail = PADDED - 8
    for slot in range(SLOTS):
        rounded[slot, tail:] = jnp.full((8, BLOCK), ROWS, jnp.bfloat16)
    wide[pl.ds(CHANNELS * ROWS, (PADDED - CHANNELS) * ROWS), :] = jnp.zeros(
        ((PADDED - CHANNELS) * ROWS, BLOCK), jnp.float32
    )
    nothing = jnp.zeros((WIDE - PADDED, BLOCK), jnp.float32)
    source_copy.wait()
    wide[pl.ds(0, CHANNELS * ROWS), :] = source[...].astype(jnp.float32)
    for row in range(ROWS):
        block = wide[pl.ds(row, PADDED, stride=ROWS), :]
        field[row] = jnp.concatenate([block, nothing], axis=0).astype(jnp.bfloat16)
    is_mark = lax.broadcasted_iota(jnp.int32, (8, BLOCK), 0) == MARK - tail
    blank = jnp.zeros((WIDE, BLOCK), jnp.bfloat16)
    small_copies[1].wait()
    small_copies[2].wait()
    plan_copy.wait()

    for chunk in range(chunks):
        chunk_copy(chunk).wait()
        for entry in range(chunk * CHUNK, (chunk + 1) * CHUNK, 2):
            one = jnp.concatenate([field[index_ref[entry]], blank], axis=1)
            two = jnp.concatenate([blank, field[index_ref[entry + 1]]], axis=1)
            products = jnp.dot(
                jnp.concatenate([one, two], axis=0),
                weight[entry : entry + 2].reshape(2 * BLOCK, BLOCK),
                preferred_element_type=jnp.float32,
            )
            for at in range(2):
                code = plan_scalars[0, entry + at]
                slot = code & (SLOTS - 1)
                row = split(target_ref[entry + at], ROWS)[1]
                product = products[at * WIDE : at * WIDE + PADDED]
                total = jnp.where(code >= SLOTS, 0.0, sums[slot]) + product
                sums[slot] = total
                marked = jnp.where(is_mark, row.astype(jnp.float32), total[tail:])
                rounded[slot] = jnp.concatenate([total[:tail], marked], axis=0).astype(jnp.bfloat16)
    copies = []
    for group in range(GROUPS):
        part = rounded.at[pl.ds(group * CAP, CAP)]
        if group < TILE_COLS:
            out = same_out.at[pl.ds(group * CAP, CAP)]
        else:
            out = next_outs[group - TILE_COLS]
        copies.append(pltpu.make_async_copy(part, out, out_sems.at[group]))
    for copy in copies:
        copy.start()
    for copy in copies:
        copy.wait()


def regrid(target, source_index, field, weights, column_rows):
    piece = jax.ShapeDtypeStruct((CAP, PADDED, BLOCK), jnp.bfloat16)
    same = jax.ShapeDtypeStruct((TILE_COLS * CAP, PADDED, BLOCK), jnp.bfloat16)
    hbm = pl.BlockSpec(memory_space=pl.ANY)
    entries = weights.shape[0]
    return pl.pallas_call(
        functools.partial(regrid_kernel, column_rows),
        in_specs=[hbm] * 5,
        out_specs=[hbm] * (1 + TILE_COLS),
        out_shape=[same] + [piece] * TILE_COLS,
        scratch_shapes=[
            pltpu.SMEM(target.shape, jnp.int32),
            pltpu.VMEM((1, entries), jnp.int32),
            pltpu.SMEM(source_index.shape, jnp.int32),
            pltpu.VMEM(field.shape, jnp.bfloat16),
            pltpu.VMEM(weights.shape, jnp.bfloat16),
            pltpu.VMEM((PADDED * ROWS, BLOCK), jnp.float32),
            pltpu.VMEM((ROWS, WIDE, BLOCK), jnp.bfloat16),
            pltpu.VMEM((SLOTS, PADDED, BLOCK), jnp.float32),
            pltpu.VMEM((SLOTS, PADDED, BLOCK), jnp.bfloat16),
            pltpu.VMEM((1, entries), jnp.int32),
            pltpu.SMEM((1, entries), jnp.int32),
            pltpu.SemaphoreType.DMA,
            pltpu.SemaphoreType.DMA((4,)),
            pltpu.SemaphoreType.DMA((entries // CHUNK,)),
            pltpu.SemaphoreType.DMA((GROUPS,)),
        ],
        compiler_params=pltpu.CompilerParams(vmem_limit_bytes=REGRID_VMEM),
        name="regrid",
    )(target, target.reshape(1, -1), source_index, field, weights)


def gather_kernel(column_rows, flip_ref, gain_ref, same, *rest):
    nexts = rest[:TILE_COLS]
    (
        gridded,
        normed,
        upward,
        downward,
        strip_out,
        summed,
        marks,
        rows,
        mark_sem,
    ) = rest[TILE_COLS:]
    position = lax.rem(lax.axis_index("tile"), column_rows)
    half = SLOTS // 2
    lane = lanes((1, BLOCK))
    mark = jnp.zeros((1, BLOCK), jnp.float32)
    for slot in range(SLOTS):
        piece = same.at[slot] if slot < half else nexts[slot // CAP - TILE_COLS].at[slot % CAP]
        mark = jnp.where(lane == slot, piece[MARK : MARK + 1].astype(jnp.float32), mark)
    marks[...] = mark.astype(jnp.int32)
    copy = pltpu.make_async_copy(marks, rows, mark_sem)
    copy.start()
    summed[...] = jnp.zeros_like(summed)
    copy.wait()

    def add(slot, piece):
        row = rows[0, slot]
        summed[row] = summed[row] + piece.astype(jnp.float32)

    def add_same(step, carry):
        for at in range(CAP):
            add(step * CAP + at, same[step * CAP + at])
        return carry

    lax.fori_loop(0, TILE_COLS, add_same, 0)

    @pl.when(position > 0)
    def _():
        for group in range(TILE_COLS):
            for place in range(CAP):
                add(half + group * CAP + place, nexts[group][place])

    gain = gain_ref[...]
    channel = lax.broadcasted_iota(jnp.int32, (PADDED, BLOCK), 0)
    nothing = jnp.zeros((WIDE - PADDED, BLOCK), jnp.float32)
    lane = lanes((WIDE, BLOCK))
    strip = jnp.zeros((WIDE, BLOCK), jnp.bfloat16)
    for row in range(ROWS):
        rounded = summed[row].astype(jnp.bfloat16)
        gridded[row] = rounded
        value = rounded.astype(jnp.float32)
        value = jnp.where(channel < CHANNELS, value, 0.0)
        square = jnp.sum(value * value, axis=0, keepdims=True) * (1.0 / CHANNELS)
        scaled = value * lax.rsqrt(square + EPSILON) * gain
        scaled = jnp.concatenate([scaled, nothing], axis=0).astype(jnp.bfloat16)
        normed[row] = scaled
        if row < 2:
            upward[row] = scaled
        if row >= ROWS - 2:
            downward[row - ROWS + 2] = scaled
        strip = jnp.where((lane >> 2) == row, pltpu.roll(scaled, 4 * row + 2, 1), strip)
    to_lane = lanes((BLOCK, BLOCK))
    from_lane = 4 * (to_lane & (ROWS - 1)) + (((to_lane >> ROW_BITS) + 2) & 3)
    order = lax.broadcasted_iota(jnp.int32, (BLOCK, BLOCK), 0) == from_lane
    strip = jnp.dot(strip, order.astype(jnp.bfloat16), preferred_element_type=jnp.float32)
    channel = lax.broadcasted_iota(jnp.int32, (WIDE, BLOCK), 0)
    for side in range(2):
        strip = jnp.where(channel == CHANNELS + side, flip_ref[0, side].astype(jnp.float32), strip)
    strip = strip.astype(jnp.bfloat16)
    upward[2] = strip
    downward[2] = strip
    strip_out[...] = strip


GRIDDED = jax.ShapeDtypeStruct((ROWS, PADDED, BLOCK), jnp.bfloat16)
FIELD = jax.ShapeDtypeStruct((ROWS, WIDE, BLOCK), jnp.bfloat16)
RIM = jax.ShapeDtypeStruct((3, WIDE, BLOCK), jnp.bfloat16)
STRIP_COLUMNS = (0, 1, BLOCK - 2, BLOCK - 1)
STRIP = jax.ShapeDtypeStruct((WIDE, BLOCK), jnp.bfloat16)


def gather_rows(column_rows, edge_flip, gain, same, nexts):
    return pl.pallas_call(
        functools.partial(gather_kernel, column_rows),
        in_specs=[smem()] + [vmem()] * (2 + TILE_COLS),
        out_specs=[vmem()] * 5,
        out_shape=[GRIDDED, FIELD, RIM, RIM, STRIP],
        scratch_shapes=[
            pltpu.VMEM((ROWS + 1, PADDED, BLOCK), jnp.float32),
            pltpu.VMEM((1, SLOTS), jnp.int32),
            pltpu.SMEM((1, SLOTS), jnp.int32),
            pltpu.SemaphoreType.DMA,
        ],
        compiler_params=pltpu.CompilerParams(vmem_limit_bytes=VMEM_LIMIT),
        name="gather_rows",
    )(edge_flip, gain, same, *nexts)


def turn_kernel(field, out, turned):
    for row in range(ROWS):
        turned[pl.ds(row, PADDED, stride=ROWS), :] = field[row].astype(jnp.float32)
    out[...] = turned[pl.ds(0, CHANNELS * ROWS), :].astype(jnp.bfloat16)


def channels_first(field):
    return pl.pallas_call(
        turn_kernel,
        in_specs=[vmem()],
        out_specs=vmem(),
        out_shape=jax.ShapeDtypeStruct((CHANNELS * ROWS, BLOCK), jnp.bfloat16),
        scratch_shapes=[pltpu.VMEM((PADDED * ROWS, BLOCK), jnp.float32)],
        compiler_params=pltpu.CompilerParams(vmem_limit_bytes=VMEM_LIMIT),
        name="channels_first",
    )(field)


def shifted_columns(value, left_end, right_end):
    lane = lanes((WIDE, BLOCK))
    left = jnp.where(lane == 0, left_end, pltpu.roll(value, 1, 1))
    right = jnp.where(lane == BLOCK - 1, right_end, pltpu.roll(value, BLOCK - 1, 1))
    return jnp.concatenate([left, value, right], axis=0)


def tap_sums(taps, one, two):
    both = jnp.concatenate([one, two], axis=1)
    result = jnp.dot(taps, both, preferred_element_type=jnp.float32)
    return result[:, :BLOCK], result[:, BLOCK:]


def row_tap(sums, at):
    return sums[at * WIDE : (at + 1) * WIDE]


def activated(value):
    return jax.nn.gelu(value).astype(jnp.bfloat16)


def inner_kernel(taps_ref, field, hidden, ends, sides, partial):
    taps = taps_ref[...]
    blank = jnp.zeros((WIDE, BLOCK), jnp.bfloat16)
    for row in range(0, ROWS, 2):
        partial[row], partial[row + 1] = tap_sums(
            taps,
            shifted_columns(field[row], blank, blank),
            shifted_columns(field[row + 1], blank, blank),
        )
    lane = lanes((WIDE, BLOCK))
    west = jnp.zeros((WIDE, BLOCK), jnp.float32)
    east = jnp.zeros((WIDE, BLOCK), jnp.float32)
    for row in range(ROWS):
        value = partial[row, WIDE : 2 * WIDE]
        if row > 0:
            value = value + partial[row - 1, :WIDE]
        if row < ROWS - 1:
            value = value + partial[row + 1, 2 * WIDE :]
        if row == 0:
            ends[0] = value
        elif row == ROWS - 1:
            ends[1] = value
        else:
            hidden[row] = activated(value)
        west = jnp.where(lane == row, pltpu.roll(value, row, 1), west)
        east = jnp.where(lane == row, pltpu.roll(value, row + 1, 1), east)
    hidden[0] = blank
    hidden[ROWS - 1] = blank
    sides[0] = west
    sides[1] = east


def inner_convolution(taps, field):
    pair = jax.ShapeDtypeStruct((2, WIDE, BLOCK), jnp.float32)
    return pl.pallas_call(
        inner_kernel,
        in_specs=[vmem()] * 2,
        out_specs=[vmem()] * 3,
        out_shape=[FIELD, pair, pair],
        scratch_shapes=[pltpu.VMEM((ROWS, 3 * WIDE, BLOCK), jnp.float32)],
        compiler_params=pltpu.CompilerParams(vmem_limit_bytes=VMEM_LIMIT),
        cost_estimate=pl.CostEstimate(
            flops=2 * 9 * WIDE * WIDE * ROWS * BLOCK, bytes_accessed=2 << 20, transcendentals=0
        ),
        name="inner_convolution",
    )(taps, field)


def strip_plan(column_rows):
    if column_rows == 2:
        return [], 3, 1
    return [-2, 2], column_rows, 2


def conv_kernel(
    column_rows,
    first_taps_ref,
    second_taps_ref,
    field,
    gridded,
    inner,
    ends_ref,
    sides_ref,
    above,
    below,
    own_strip,
    *rest,
):
    near, far, reach = strip_plan(column_rows)
    near_strips, (west_pack, east_pack) = rest[: len(near)], rest[len(near) : len(near) + 2]
    smoothed, hidden, partial, turned = rest[len(near) + 2 :]
    count = lax.axis_size("tile")
    tile = lax.axis_index("tile")
    lane = lanes((WIDE, BLOCK))
    last = ROWS + 1
    R = column_rows
    blank = jnp.zeros((WIDE, BLOCK), jnp.bfloat16)

    strips = {-1: above[2], 0: own_strip[...], 1: below[2]}
    strips.update((shift, ref[...]) for shift, ref in zip(near, near_strips))
    for at in range(-reach, reach + 1):
        strips[at - far], strips[at + far] = west_pack[at + reach], east_pack[at + reach]

    def place(shift):
        return lax.rem(tile + shift + count, count)

    def ends(shift, before, after, middle):
        before = jnp.where(place(shift) > 0, before, blank)
        after = jnp.where(place(shift) < count - 1, after, blank)
        return jnp.where(lane == 0, before, jnp.where(lane == last, after, middle))

    memo = {}

    def padded_column(shift, which):
        if (shift, which) not in memo:
            base = which * ROWS
            memo[shift, which] = ends(
                shift,
                pltpu.roll(strips[shift - 1], (1 - base - ROWS) % BLOCK, 1),
                pltpu.roll(strips[shift + 1], (last - base) % BLOCK, 1),
                pltpu.roll(strips[shift], (1 - base) % BLOCK, 1),
            )
        return memo[shift, which]

    row_id = lax.broadcasted_iota(jnp.int32, (BLOCK, BLOCK), 0)
    reversal = (row_id + lanes((BLOCK, BLOCK)) == last).astype(jnp.bfloat16)

    def reversed_lanes(planes):
        stacked = jnp.concatenate(planes, axis=0)
        turned_round = jnp.dot(stacked, reversal, preferred_element_type=jnp.float32)
        return [row_tap(turned_round, at) for at in range(len(planes))]

    def choose(shift, which, turned_round, plain):
        flips = strips[shift].astype(jnp.float32)[CHANNELS + which : CHANNELS + which + 1]
        return jnp.where(flips > 0.5, turned_round, plain.astype(jnp.float32)).astype(jnp.bfloat16)

    west_of = {shift: (shift - R, 3) for shift in {-1, 0, 1, R - 1, R, R + 1}}
    east_of = {shift: (shift + R, 0) for shift in {-1, 0, 1, -R - 1, -R, -R + 1}}
    keys = sorted(set(west_of.values()) | set(east_of.values()))
    flipped = dict(zip(keys, reversed_lanes([padded_column(*key) for key in keys])))
    west = {
        shift: choose(shift, 0, flipped[west_of[shift]], padded_column(*west_of[shift]))
        for shift in sorted(west_of)
    }
    east = {
        shift: choose(shift, 1, flipped[east_of[shift]], padded_column(*east_of[shift]))
        for shift in sorted(east_of)
    }

    def columns(value, west_plane, west_row, east_plane, east_row):
        return shifted_columns(
            value,
            pltpu.roll(west_plane, (BLOCK - west_row) % BLOCK, 1),
            pltpu.roll(east_plane, BLOCK - 1 - east_row, 1),
        )

    def along(result):
        return (
            row_tap(result, 0)
            + pltpu.roll(row_tap(result, 1), BLOCK - 1, 1)
            + pltpu.roll(row_tap(result, 2), BLOCK - 2, 1)
        )

    first_taps = first_taps_ref[...]
    up = [jnp.where(tile > 0, above[at], blank) for at in range(2)]
    down = [jnp.where(tile < count - 1, below[at], blank) for at in range(2)]
    from_up, from_down = tap_sums(
        first_taps, shifted_columns(up[1], blank, blank), shifted_columns(down[0], blank, blank)
    )
    from_up, from_down = row_tap(from_up, 0), row_tap(from_down, 2)
    from_west, from_east = tap_sums(
        first_taps,
        jnp.concatenate([west[0], blank, blank], axis=0),
        jnp.concatenate([blank, blank, east[0]], axis=0),
    )
    from_west, from_east = along(from_west), along(from_east)
    first = ends_ref[0] + from_up
    first = first + jnp.where(lane == 0, from_west, 0.0)
    first = first + jnp.where(lane == BLOCK - 1, pltpu.roll(from_east, BLOCK - 1, 1), 0.0)
    final = ends_ref[1] + from_down
    final = final + jnp.where(lane == 0, pltpu.roll(from_west, BLOCK - ROWS + 1, 1), 0.0)
    final = final + jnp.where(lane == BLOCK - 1, pltpu.roll(from_east, BLOCK - ROWS, 1), 0.0)
    hidden[1] = activated(first)
    hidden[ROWS] = activated(final)
    first_column = activated(sides_ref[0] + from_west)
    last_column = activated(sides_ref[1] + from_east)
    for row in range(1, ROWS - 1):
        value = jnp.where(lane == 0, pltpu.roll(first_column, BLOCK - row, 1), inner[row])
        hidden[row + 1] = jnp.where(
            lane == BLOCK - 1, pltpu.roll(last_column, BLOCK - 1 - row, 1), value
        )

    upper = jnp.zeros((WIDE, BLOCK), jnp.float32)
    lower = jnp.zeros((WIDE, BLOCK), jnp.float32)
    for at, (high, low) in enumerate(
        [(up[0], field[ROWS - 1]), (up[1], down[0]), (field[0], down[1])]
    ):
        from_row = ROWS - 1 + at
        one, two = tap_sums(
            first_taps,
            columns(high, west[-1], from_row, east[-1], from_row),
            columns(low, west[1], at, east[1], at),
        )
        upper += row_tap(one, at)
        lower += row_tap(two, at)
    hidden[0] = jnp.where(tile > 0, activated(upper), blank)
    hidden[last] = jnp.where(tile < count - 1, activated(lower), blank)

    west_hidden, east_hidden = {}, {}
    for at in (-1, 0, 1):
        q = at - R
        one = jnp.concatenate([padded_column(q, 2), padded_column(q, 3), east[q]], axis=0)
        q = at + R
        two = jnp.concatenate([west[q], padded_column(q, 0), padded_column(q, 1)], axis=0)
        one, two = tap_sums(first_taps, one, two)
        west_hidden[at], east_hidden[at] = activated(along(one)), activated(along(two))

    def hidden_side(shift, values):
        return ends(
            shift,
            pltpu.roll(values[-1], BLOCK - ROWS + 1, 1),
            pltpu.roll(values[1], last, 1),
            pltpu.roll(values[0], 1, 1),
        )

    plain = [hidden_side(-R, west_hidden), hidden_side(R, east_hidden)]
    west_side, east_side = [
        choose(0, which, turned_side, plain[which])
        for which, turned_side in enumerate(reversed_lanes(plain))
    ]

    second_taps = second_taps_ref[...]
    for p in range(0, ROWS + 2, 2):
        partial[p], partial[p + 1] = tap_sums(
            second_taps,
            columns(hidden[p], west_side, p, east_side, p),
            columns(hidden[p + 1], west_side, p + 1, east_side, p + 1),
        )
    for row in range(ROWS):
        branch = (
            partial[row, :PADDED]
            + partial[row + 1, WIDE : WIDE + PADDED]
            + partial[row + 2, 2 * WIDE : 2 * WIDE + PADDED]
        )
        turned[pl.ds(row, PADDED, stride=ROWS), :] = gridded[row].astype(jnp.float32) + branch
    smoothed[...] = turned[pl.ds(0, CHANNELS * ROWS), :].astype(jnp.bfloat16)


def convolutions(column_rows, *operands):
    return pl.pallas_call(
        functools.partial(conv_kernel, column_rows),
        in_specs=[vmem()] * len(operands),
        out_specs=vmem(),
        out_shape=jax.ShapeDtypeStruct((CHANNELS * ROWS, BLOCK), jnp.bfloat16),
        scratch_shapes=[
            pltpu.VMEM((ROWS + 2, WIDE, BLOCK), jnp.bfloat16),
            pltpu.VMEM((ROWS + 2, 3 * WIDE, BLOCK), jnp.float32),
            pltpu.VMEM((PADDED * ROWS, BLOCK), jnp.float32),
        ],
        compiler_params=pltpu.CompilerParams(vmem_limit_bytes=VMEM_LIMIT),
        name="convolutions",
    )(*operands)


def tap_matrix(kernel):
    pad = WIDE - CHANNELS
    taps = jnp.pad(kernel, ((0, 0), (0, pad), (0, pad))).reshape(3, 3, WIDE, WIDE)
    return taps.transpose(0, 2, 1, 3).reshape(3 * WIDE, 3 * WIDE)


def from_shift(value, shift):
    count = lax.axis_size("tile")
    return lax.ppermute(value, "tile", [(i, (i - shift) % count) for i in range(count)])


def per_device(
    source, weights, block_source, block_target, edge_flip, norm_gain, first_kernel, second_kernel
):
    count = lax.axis_size("tile")
    column_rows = count // TILE_COLS
    field = source.reshape(ROWS, CHANNELS, BLOCK).transpose(1, 0, 2).reshape(-1, BLOCK)
    same, *nexts = regrid(block_target, block_source, field, weights, column_rows)

    for across in range(TILE_COLS):
        pairs = [
            (c * column_rows + p, (c ^ across) * column_rows + p + 1)
            for c in range(TILE_COLS)
            for p in range(column_rows - 1)
        ]
        nexts[across] = lax.ppermute(nexts[across], "tile", pairs)
    same = lax.all_to_all(
        same,
        "tile",
        0,
        0,
        axis_index_groups=[
            [c * column_rows + p for c in range(TILE_COLS)] for p in range(column_rows)
        ],
        tiled=True,
    )

    gain = jnp.broadcast_to(
        jnp.pad(norm_gain, (0, PADDED - CHANNELS))[:, None], (PADDED, BLOCK)
    )
    first_taps, second_taps = tap_matrix(first_kernel), tap_matrix(second_kernel)
    same, nexts, gain, first_taps, second_taps = lax.optimization_barrier(
        (same, nexts, gain, first_taps, second_taps)
    )
    gridded, normed, upward, downward, strip = gather_rows(
        column_rows, edge_flip, gain, same, nexts
    )
    rims = [from_shift(downward, -1), from_shift(upward, 1)]
    near, far, reach = strip_plan(column_rows)
    strips = [from_shift(strip, shift) for shift in near]
    inner = inner_convolution(first_taps, normed)
    held = {-1: rims[0][2], 0: strip, 1: rims[1][2], **dict(zip(near, strips))}
    pack = jnp.stack([held[at] for at in range(-reach, reach + 1)])
    pack, inner = lax.optimization_barrier((pack, inner))
    strips += [from_shift(pack, -far), from_shift(pack, far)]
    gridded_out = channels_first(gridded)
    smoothed = convolutions(
        column_rows, first_taps, second_taps, normed, gridded, *inner, *rims, strip, *strips
    )

    def placed(value):
        return value.reshape(CHANNELS, ROWS, BLOCK).transpose(1, 0, 2)[:, None]

    return placed(gridded_out), placed(smoothed)


def solution(mesh):
    in_specs = (
        P("tile", "groups", None, None),
        P("tile", None, None),
        P("tile"),
        P("tile"),
        P("tile", None),
        P(),
        P(),
        P(),
    )
    out_specs = (P("tile", "groups", None, None), P("tile", "groups", None, None))
    return jax.shard_map(
        per_device, mesh=mesh, in_specs=in_specs, out_specs=out_specs, check_vma=False
    )
```

```python
import functools

import jax
import jax.numpy as jnp
from jax import lax
from jax.experimental import pallas as pl
from jax.experimental.pallas import tpu as pltpu
from jax.sharding import PartitionSpec as P

BLOCK = 128
CHANNELS = 69
PADDED = 72
WIDE = 80
ROWS = 32
ROW_BITS = 5
TILE_COLS = 8
CAP = 8
GROUPS = 2 * TILE_COLS
SLOTS = GROUPS * CAP
CHUNK = 96
MARK = CHANNELS
EPSILON = 1e-05
VMEM_LIMIT = 40 * 1024 * 1024
REGRID_VMEM = 60 * 1024 * 1024


def vmem():
    return pl.BlockSpec(memory_space=pltpu.VMEM)


def smem():
    return pl.BlockSpec(memory_space=pltpu.SMEM)


def split(value, size):
    if size & (size - 1) == 0:
        return value >> (size.bit_length() - 1), value & (size - 1)
    return lax.div(value, size), lax.rem(value, size)


def lanes(shape):
    return lax.broadcasted_iota(jnp.int32, shape, len(shape) - 1)


def regrid_kernel(
    column_rows, target_hbm, target_row_hbm, index_hbm, source_hbm, weight_hbm, *rest
):
    same_out, next_outs = rest[0], rest[1 : 1 + TILE_COLS]
    (
        target_ref,
        target_row_ref,
        index_ref,
        source,
        weight,
        wide,
        field,
        sums,
        rounded,
        plan,
        plan_scalars,
        plan_sem,
        in_sems,
        weight_sems,
        out_sems,
    ) = rest[1 + TILE_COLS :]
    entries = weight.shape[0]
    chunks = entries // CHUNK
    tile = lax.axis_index("tile")
    column, position = split(tile, column_rows)

    small_copies = [
        pltpu.make_async_copy(target_row_hbm, target_row_ref, in_sems.at[0]),
        pltpu.make_async_copy(target_hbm, target_ref, in_sems.at[1]),
        pltpu.make_async_copy(index_hbm, index_ref, in_sems.at[2]),
    ]
    source_copy = pltpu.make_async_copy(source_hbm, source, in_sems.at[3])
    for copy in small_copies:
        copy.start()
    source_copy.start()

    def chunk_copy(chunk):
        part = pl.ds(chunk * CHUNK, CHUNK)
        return pltpu.make_async_copy(weight_hbm.at[part], weight.at[part], weight_sems.at[chunk])

    for chunk in range(chunks):
        chunk_copy(chunk).start()

    small_copies[0].wait()
    target = target_row_ref[...]
    owner, row = split(target, ROWS)
    owner_column, owner_position = split(owner, column_rows)
    group = jnp.where(
        owner_position == position, owner_column, TILE_COLS + (owner_column ^ column)
    )
    key = group * ROWS + row
    square = (entries, entries)
    down = lax.broadcasted_iota(jnp.int32, square, 0)
    along = lanes(square)
    key_along = jnp.broadcast_to(key.astype(jnp.float32), square)
    key_down = jnp.broadcast_to(
        jnp.sum(jnp.where(down == along, key_along, 0.0), axis=1, keepdims=True), square
    )
    equal = key_along == key_down
    doubles = jnp.sum(jnp.where(equal & (along < down), 1.0, 0.0), axis=1, keepdims=True)
    in_group = (key_down.astype(jnp.int32) >> ROW_BITS) == (key_along.astype(jnp.int32) >> ROW_BITS)
    below = in_group & (key_down < key_along) & (jnp.broadcast_to(doubles, square) == 0.0)
    rank = jnp.sum(jnp.where(below, 1.0, 0.0), axis=0, keepdims=True)
    mentions = jnp.sum(jnp.where(equal & (down < along), 1.0, 0.0), axis=0, keepdims=True)
    slots = group * CAP + rank.astype(jnp.int32)
    plan[...] = slots + jnp.where(mentions == 0.0, SLOTS, 0)
    plan_copy = pltpu.make_async_copy(plan, plan_scalars, plan_sem)
    plan_copy.start()

    tail = PADDED - 8
    for slot in range(SLOTS):
        rounded[slot, tail:] = jnp.full((8, BLOCK), ROWS, jnp.bfloat16)
    wide[pl.ds(CHANNELS * ROWS, (PADDED - CHANNELS) * ROWS), :] = jnp.zeros(
        ((PADDED - CHANNELS) * ROWS, BLOCK), jnp.float32
    )
    nothing = jnp.zeros((WIDE - PADDED, BLOCK), jnp.float32)
    source_copy.wait()
    wide[pl.ds(0, CHANNELS * ROWS), :] = source[...].astype(jnp.float32)
    for row in range(ROWS):
        block = wide[pl.ds(row, PADDED, stride=ROWS), :]
        field[row] = jnp.concatenate([block, nothing], axis=0).astype(jnp.bfloat16)
    is_mark = lax.broadcasted_iota(jnp.int32, (8, BLOCK), 0) == MARK - tail
    blank = jnp.zeros((WIDE, BLOCK), jnp.bfloat16)
    small_copies[1].wait()
    small_copies[2].wait()
    plan_copy.wait()

    for chunk in range(chunks):
        chunk_copy(chunk).wait()
        for entry in range(chunk * CHUNK, (chunk + 1) * CHUNK, 2):
            one = jnp.concatenate([field[index_ref[entry]], blank], axis=1)
            two = jnp.concatenate([blank, field[index_ref[entry + 1]]], axis=1)
            products = jnp.dot(
                jnp.concatenate([one, two], axis=0),
                weight[entry : entry + 2].reshape(2 * BLOCK, BLOCK),
                preferred_element_type=jnp.float32,
            )
            for at in range(2):
                code = plan_scalars[0, entry + at]
                slot = code & (SLOTS - 1)
                row = split(target_ref[entry + at], ROWS)[1]
                product = products[at * WIDE : at * WIDE + PADDED]
                total = jnp.where(code >= SLOTS, 0.0, sums[slot]) + product
                sums[slot] = total
                marked = jnp.where(is_mark, row.astype(jnp.float32), total[tail:])
                rounded[slot] = jnp.concatenate([total[:tail], marked], axis=0).astype(jnp.bfloat16)
    copies = []
    for group in range(GROUPS):
        part = rounded.at[pl.ds(group * CAP, CAP)]
        if group < TILE_COLS:
            out = same_out.at[pl.ds(group * CAP, CAP)]
        else:
            out = next_outs[group - TILE_COLS]
        copies.append(pltpu.make_async_copy(part, out, out_sems.at[group]))
    for copy in copies:
        copy.start()
    for copy in copies:
        copy.wait()


def regrid(target, source_index, field, weights, column_rows):
    piece = jax.ShapeDtypeStruct((CAP, PADDED, BLOCK), jnp.bfloat16)
    same = jax.ShapeDtypeStruct((TILE_COLS * CAP, PADDED, BLOCK), jnp.bfloat16)
    hbm = pl.BlockSpec(memory_space=pl.ANY)
    entries = weights.shape[0]
    return pl.pallas_call(
        functools.partial(regrid_kernel, column_rows),
        in_specs=[hbm] * 5,
        out_specs=[hbm] * (1 + TILE_COLS),
        out_shape=[same] + [piece] * TILE_COLS,
        scratch_shapes=[
            pltpu.SMEM(target.shape, jnp.int32),
            pltpu.VMEM((1, entries), jnp.int32),
            pltpu.SMEM(source_index.shape, jnp.int32),
            pltpu.VMEM(field.shape, jnp.bfloat16),
            pltpu.VMEM(weights.shape, jnp.bfloat16),
            pltpu.VMEM((PADDED * ROWS, BLOCK), jnp.float32),
            pltpu.VMEM((ROWS, WIDE, BLOCK), jnp.bfloat16),
            pltpu.VMEM((SLOTS, PADDED, BLOCK), jnp.float32),
            pltpu.VMEM((SLOTS, PADDED, BLOCK), jnp.bfloat16),
            pltpu.VMEM((1, entries), jnp.int32),
            pltpu.SMEM((1, entries), jnp.int32),
            pltpu.SemaphoreType.DMA,
            pltpu.SemaphoreType.DMA((4,)),
            pltpu.SemaphoreType.DMA((entries // CHUNK,)),
            pltpu.SemaphoreType.DMA((GROUPS,)),
        ],
        compiler_params=pltpu.CompilerParams(vmem_limit_bytes=REGRID_VMEM),
        name="regrid",
    )(target, target.reshape(1, -1), source_index, field, weights)


def gather_kernel(column_rows, flip_ref, gain_ref, same, *rest):
    nexts = rest[:TILE_COLS]
    (
        gridded,
        normed,
        upward,
        downward,
        strip_out,
        summed,
    ) = rest[TILE_COLS:]
    position = lax.rem(lax.axis_index("tile"), column_rows)
    summed[...] = jnp.zeros_like(summed)

    def add(piece):
        row = piece[MARK : MARK + 1].astype(jnp.float32).astype(jnp.int32)[0, 0]
        summed[row] = summed[row] + piece[...].astype(jnp.float32)

    for slot in range(SLOTS // 2):
        add(same.at[slot])

    @pl.when(position > 0)
    def _():
        for group in range(TILE_COLS):
            for place in range(CAP):
                add(nexts[group].at[place])

    gain = gain_ref[...]
    channel = lax.broadcasted_iota(jnp.int32, (PADDED, BLOCK), 0)
    nothing = jnp.zeros((WIDE - PADDED, BLOCK), jnp.float32)
    lane = lanes((WIDE, BLOCK))
    strip = jnp.zeros((WIDE, BLOCK), jnp.bfloat16)
    for row in range(ROWS):
        rounded = summed[row].astype(jnp.bfloat16)
        gridded[row] = rounded
        value = rounded.astype(jnp.float32)
        value = jnp.where(channel < CHANNELS, value, 0.0)
        square = jnp.sum(value * value, axis=0, keepdims=True) * (1.0 / CHANNELS)
        scaled = value * lax.rsqrt(square + EPSILON) * gain
        scaled = jnp.concatenate([scaled, nothing], axis=0).astype(jnp.bfloat16)
        normed[row] = scaled
        if row < 2:
            upward[row] = scaled
        if row >= ROWS - 2:
            downward[row - ROWS + 2] = scaled
        strip = jnp.where((lane >> 2) == row, pltpu.roll(scaled, 4 * row + 2, 1), strip)
    to_lane = lanes((BLOCK, BLOCK))
    from_lane = 4 * (to_lane & (ROWS - 1)) + (((to_lane >> ROW_BITS) + 2) & 3)
    order = lax.broadcasted_iota(jnp.int32, (BLOCK, BLOCK), 0) == from_lane
    strip = jnp.dot(strip, order.astype(jnp.bfloat16), preferred_element_type=jnp.float32)
    channel = lax.broadcasted_iota(jnp.int32, (WIDE, BLOCK), 0)
    for side in range(2):
        strip = jnp.where(channel == CHANNELS + side, flip_ref[0, side].astype(jnp.float32), strip)
    strip = strip.astype(jnp.bfloat16)
    upward[2] = strip
    downward[2] = strip
    strip_out[...] = strip


GRIDDED = jax.ShapeDtypeStruct((ROWS, PADDED, BLOCK), jnp.bfloat16)
FIELD = jax.ShapeDtypeStruct((ROWS, WIDE, BLOCK), jnp.bfloat16)
RIM = jax.ShapeDtypeStruct((3, WIDE, BLOCK), jnp.bfloat16)
STRIP_COLUMNS = (0, 1, BLOCK - 2, BLOCK - 1)
STRIP = jax.ShapeDtypeStruct((WIDE, BLOCK), jnp.bfloat16)


def gather_rows(column_rows, edge_flip, gain, same, nexts):
    return pl.pallas_call(
        functools.partial(gather_kernel, column_rows),
        in_specs=[smem()] + [vmem()] * (2 + TILE_COLS),
        out_specs=[vmem()] * 5,
        out_shape=[GRIDDED, FIELD, RIM, RIM, STRIP],
        scratch_shapes=[
            pltpu.VMEM((ROWS + 1, PADDED, BLOCK), jnp.float32),
        ],
        compiler_params=pltpu.CompilerParams(vmem_limit_bytes=VMEM_LIMIT),
        name="gather_rows",
    )(edge_flip, gain, same, *nexts)


def turn_kernel(field, out, turned):
    for row in range(ROWS):
        turned[pl.ds(row, PADDED, stride=ROWS), :] = field[row].astype(jnp.float32)
    out[...] = turned[pl.ds(0, CHANNELS * ROWS), :].astype(jnp.bfloat16)


def channels_first(field):
    return pl.pallas_call(
        turn_kernel,
        in_specs=[vmem()],
        out_specs=vmem(),
        out_shape=jax.ShapeDtypeStruct((CHANNELS * ROWS, BLOCK), jnp.bfloat16),
        scratch_shapes=[pltpu.VMEM((PADDED * ROWS, BLOCK), jnp.float32)],
        compiler_params=pltpu.CompilerParams(vmem_limit_bytes=VMEM_LIMIT),
        name="channels_first",
    )(field)


def shifted_columns(value, left_end, right_end):
    lane = lanes((WIDE, BLOCK))
    left = jnp.where(lane == 0, left_end, pltpu.roll(value, 1, 1))
    right = jnp.where(lane == BLOCK - 1, right_end, pltpu.roll(value, BLOCK - 1, 1))
    return jnp.concatenate([left, value, right], axis=0)


def tap_sums(taps, one, two):
    both = jnp.concatenate([one, two], axis=1)
    result = jnp.dot(taps, both, preferred_element_type=jnp.float32)
    return result[:, :BLOCK], result[:, BLOCK:]


def row_tap(sums, at):
    return sums[at * WIDE : (at + 1) * WIDE]


def activated(value):
    return jax.nn.gelu(value).astype(jnp.bfloat16)


def inner_kernel(taps_ref, field, hidden, ends, sides, partial):
    taps = taps_ref[...]
    blank = jnp.zeros((WIDE, BLOCK), jnp.bfloat16)
    for row in range(0, ROWS, 2):
        partial[row], partial[row + 1] = tap_sums(
            taps,
            shifted_columns(field[row], blank, blank),
            shifted_columns(field[row + 1], blank, blank),
        )
    lane = lanes((WIDE, BLOCK))
    west = jnp.zeros((WIDE, BLOCK), jnp.float32)
    east = jnp.zeros((WIDE, BLOCK), jnp.float32)
    for row in range(ROWS):
        value = partial[row, WIDE : 2 * WIDE]
        if row > 0:
            value = value + partial[row - 1, :WIDE]
        if row < ROWS - 1:
            value = value + partial[row + 1, 2 * WIDE :]
        if row == 0:
            ends[0] = value
        elif row == ROWS - 1:
            ends[1] = value
        else:
            hidden[row] = activated(value)
        west = jnp.where(lane == row, pltpu.roll(value, row, 1), west)
        east = jnp.where(lane == row, pltpu.roll(value, row + 1, 1), east)
    hidden[0] = blank
    hidden[ROWS - 1] = blank
    sides[0] = west
    sides[1] = east


def inner_convolution(taps, field):
    pair = jax.ShapeDtypeStruct((2, WIDE, BLOCK), jnp.float32)
    return pl.pallas_call(
        inner_kernel,
        in_specs=[vmem()] * 2,
        out_specs=[vmem()] * 3,
        out_shape=[FIELD, pair, pair],
        scratch_shapes=[pltpu.VMEM((ROWS, 3 * WIDE, BLOCK), jnp.float32)],
        compiler_params=pltpu.CompilerParams(vmem_limit_bytes=VMEM_LIMIT),
        cost_estimate=pl.CostEstimate(
            flops=2 * 9 * WIDE * WIDE * ROWS * BLOCK, bytes_accessed=2 << 20, transcendentals=0
        ),
        name="inner_convolution",
    )(taps, field)


def strip_plan(column_rows):
    if column_rows == 2:
        return [], 3, 1
    return [-2, 2], column_rows, 2


def conv_kernel(
    column_rows,
    first_taps_ref,
    second_taps_ref,
    field,
    gridded,
    inner,
    ends_ref,
    sides_ref,
    above,
    below,
    own_strip,
    *rest,
):
    near, far, reach = strip_plan(column_rows)
    near_strips, (west_pack, east_pack) = rest[: len(near)], rest[len(near) : len(near) + 2]
    smoothed, hidden, partial, turned = rest[len(near) + 2 :]
    count = lax.axis_size("tile")
    tile = lax.axis_index("tile")
    lane = lanes((WIDE, BLOCK))
    last = ROWS + 1
    R = column_rows
    blank = jnp.zeros((WIDE, BLOCK), jnp.bfloat16)

    strips = {-1: above[2], 0: own_strip[...], 1: below[2]}
    strips.update((shift, ref[...]) for shift, ref in zip(near, near_strips))
    for at in range(-reach, reach + 1):
        strips[at - far], strips[at + far] = west_pack[at + reach], east_pack[at + reach]

    def place(shift):
        return lax.rem(tile + shift + count, count)

    def ends(shift, before, after, middle):
        before = jnp.where(place(shift) > 0, before, blank)
        after = jnp.where(place(shift) < count - 1, after, blank)
        return jnp.where(lane == 0, before, jnp.where(lane == last, after, middle))

    memo = {}

    def padded_column(shift, which):
        if (shift, which) not in memo:
            base = which * ROWS
            memo[shift, which] = ends(
                shift,
                pltpu.roll(strips[shift - 1], (1 - base - ROWS) % BLOCK, 1),
                pltpu.roll(strips[shift + 1], (last - base) % BLOCK, 1),
                pltpu.roll(strips[shift], (1 - base) % BLOCK, 1),
            )
        return memo[shift, which]

    row_id = lax.broadcasted_iota(jnp.int32, (BLOCK, BLOCK), 0)
    reversal = (row_id + lanes((BLOCK, BLOCK)) == last).astype(jnp.bfloat16)

    def reversed_lanes(planes):
        stacked = jnp.concatenate(planes, axis=0)
        turned_round = jnp.dot(stacked, reversal, preferred_element_type=jnp.float32)
        return [row_tap(turned_round, at) for at in range(len(planes))]

    def choose(shift, which, turned_round, plain):
        flips = strips[shift].astype(jnp.float32)[CHANNELS + which : CHANNELS + which + 1]
        return jnp.where(flips > 0.5, turned_round, plain.astype(jnp.float32)).astype(jnp.bfloat16)

    west_of = {shift: (shift - R, 3) for shift in {-1, 0, 1, R - 1, R, R + 1}}
    east_of = {shift: (shift + R, 0) for shift in {-1, 0, 1, -R - 1, -R, -R + 1}}
    keys = sorted(set(west_of.values()) | set(east_of.values()))
    flipped = dict(zip(keys, reversed_lanes([padded_column(*key) for key in keys])))
    west = {
        shift: choose(shift, 0, flipped[west_of[shift]], padded_column(*west_of[shift]))
        for shift in sorted(west_of)
    }
    east = {
        shift: choose(shift, 1, flipped[east_of[shift]], padded_column(*east_of[shift]))
        for shift in sorted(east_of)
    }

    def columns(value, west_plane, west_row, east_plane, east_row):
        return shifted_columns(
            value,
            pltpu.roll(west_plane, (BLOCK - west_row) % BLOCK, 1),
            pltpu.roll(east_plane, BLOCK - 1 - east_row, 1),
        )

    def along(result):
        return (
            row_tap(result, 0)
            + pltpu.roll(row_tap(result, 1), BLOCK - 1, 1)
            + pltpu.roll(row_tap(result, 2), BLOCK - 2, 1)
        )

    first_taps = first_taps_ref[...]
    up = [jnp.where(tile > 0, above[at], blank) for at in range(2)]
    down = [jnp.where(tile < count - 1, below[at], blank) for at in range(2)]
    from_up, from_down = tap_sums(
        first_taps, shifted_columns(up[1], blank, blank), shifted_columns(down[0], blank, blank)
    )
    from_up, from_down = row_tap(from_up, 0), row_tap(from_down, 2)
    from_west, from_east = tap_sums(
        first_taps,
        jnp.concatenate([west[0], blank, blank], axis=0),
        jnp.concatenate([blank, blank, east[0]], axis=0),
    )
    from_west, from_east = along(from_west), along(from_east)
    first = ends_ref[0] + from_up
    first = first + jnp.where(lane == 0, from_west, 0.0)
    first = first + jnp.where(lane == BLOCK - 1, pltpu.roll(from_east, BLOCK - 1, 1), 0.0)
    final = ends_ref[1] + from_down
    final = final + jnp.where(lane == 0, pltpu.roll(from_west, BLOCK - ROWS + 1, 1), 0.0)
    final = final + jnp.where(lane == BLOCK - 1, pltpu.roll(from_east, BLOCK - ROWS, 1), 0.0)
    hidden[1] = activated(first)
    hidden[ROWS] = activated(final)
    first_column = activated(sides_ref[0] + from_west)
    last_column = activated(sides_ref[1] + from_east)
    for row in range(1, ROWS - 1):
        value = jnp.where(lane == 0, pltpu.roll(first_column, BLOCK - row, 1), inner[row])
        hidden[row + 1] = jnp.where(
            lane == BLOCK - 1, pltpu.roll(last_column, BLOCK - 1 - row, 1), value
        )

    upper = jnp.zeros((WIDE, BLOCK), jnp.float32)
    lower = jnp.zeros((WIDE, BLOCK), jnp.float32)
    for at, (high, low) in enumerate(
        [(up[0], field[ROWS - 1]), (up[1], down[0]), (field[0], down[1])]
    ):
        from_row = ROWS - 1 + at
        one, two = tap_sums(
            first_taps,
            columns(high, west[-1], from_row, east[-1], from_row),
            columns(low, west[1], at, east[1], at),
        )
        upper += row_tap(one, at)
        lower += row_tap(two, at)
    hidden[0] = jnp.where(tile > 0, activated(upper), blank)
    hidden[last] = jnp.where(tile < count - 1, activated(lower), blank)

    west_hidden, east_hidden = {}, {}
    for at in (-1, 0, 1):
        q = at - R
        one = jnp.concatenate([padded_column(q, 2), padded_column(q, 3), east[q]], axis=0)
        q = at + R
        two = jnp.concatenate([west[q], padded_column(q, 0), padded_column(q, 1)], axis=0)
        one, two = tap_sums(first_taps, one, two)
        west_hidden[at], east_hidden[at] = activated(along(one)), activated(along(two))

    def hidden_side(shift, values):
        return ends(
            shift,
            pltpu.roll(values[-1], BLOCK - ROWS + 1, 1),
            pltpu.roll(values[1], last, 1),
            pltpu.roll(values[0], 1, 1),
        )

    plain = [hidden_side(-R, west_hidden), hidden_side(R, east_hidden)]
    west_side, east_side = [
        choose(0, which, turned_side, plain[which])
        for which, turned_side in enumerate(reversed_lanes(plain))
    ]

    second_taps = second_taps_ref[...]
    for p in range(0, ROWS + 2, 2):
        partial[p], partial[p + 1] = tap_sums(
            second_taps,
            columns(hidden[p], west_side, p, east_side, p),
            columns(hidden[p + 1], west_side, p + 1, east_side, p + 1),
        )
    for row in range(ROWS):
        branch = (
            partial[row, :PADDED]
            + partial[row + 1, WIDE : WIDE + PADDED]
            + partial[row + 2, 2 * WIDE : 2 * WIDE + PADDED]
        )
        turned[pl.ds(row, PADDED, stride=ROWS), :] = gridded[row].astype(jnp.float32) + branch
    smoothed[...] = turned[pl.ds(0, CHANNELS * ROWS), :].astype(jnp.bfloat16)


def convolutions(column_rows, *operands):
    return pl.pallas_call(
        functools.partial(conv_kernel, column_rows),
        in_specs=[vmem()] * len(operands),
        out_specs=vmem(),
        out_shape=jax.ShapeDtypeStruct((CHANNELS * ROWS, BLOCK), jnp.bfloat16),
        scratch_shapes=[
            pltpu.VMEM((ROWS + 2, WIDE, BLOCK), jnp.bfloat16),
            pltpu.VMEM((ROWS + 2, 3 * WIDE, BLOCK), jnp.float32),
            pltpu.VMEM((PADDED * ROWS, BLOCK), jnp.float32),
        ],
        compiler_params=pltpu.CompilerParams(vmem_limit_bytes=VMEM_LIMIT),
        name="convolutions",
    )(*operands)


def tap_matrix(kernel):
    pad = WIDE - CHANNELS
    taps = jnp.pad(kernel, ((0, 0), (0, pad), (0, pad))).reshape(3, 3, WIDE, WIDE)
    return taps.transpose(0, 2, 1, 3).reshape(3 * WIDE, 3 * WIDE)


def from_shift(value, shift):
    count = lax.axis_size("tile")
    return lax.ppermute(value, "tile", [(i, (i - shift) % count) for i in range(count)])


def per_device(
    source, weights, block_source, block_target, edge_flip, norm_gain, first_kernel, second_kernel
):
    count = lax.axis_size("tile")
    column_rows = count // TILE_COLS
    field = source.reshape(ROWS, CHANNELS, BLOCK).transpose(1, 0, 2).reshape(-1, BLOCK)
    same, *nexts = regrid(block_target, block_source, field, weights, column_rows)

    for across in range(TILE_COLS):
        pairs = [
            (c * column_rows + p, (c ^ across) * column_rows + p + 1)
            for c in range(TILE_COLS)
            for p in range(column_rows - 1)
        ]
        nexts[across] = lax.ppermute(nexts[across], "tile", pairs)
    same = lax.all_to_all(
        same,
        "tile",
        0,
        0,
        axis_index_groups=[
            [c * column_rows + p for c in range(TILE_COLS)] for p in range(column_rows)
        ],
        tiled=True,
    )

    gain = jnp.broadcast_to(
        jnp.pad(norm_gain, (0, PADDED - CHANNELS))[:, None], (PADDED, BLOCK)
    )
    first_taps, second_taps = tap_matrix(first_kernel), tap_matrix(second_kernel)
    same, nexts, gain, first_taps, second_taps = lax.optimization_barrier(
        (same, nexts, gain, first_taps, second_taps)
    )
    gridded, normed, upward, downward, strip = gather_rows(
        column_rows, edge_flip, gain, same, nexts
    )
    rims = [from_shift(downward, -1), from_shift(upward, 1)]
    near, far, reach = strip_plan(column_rows)
    strips = [from_shift(strip, shift) for shift in near]
    inner = inner_convolution(first_taps, normed)
    held = {-1: rims[0][2], 0: strip, 1: rims[1][2], **dict(zip(near, strips))}
    pack = jnp.stack([held[at] for at in range(-reach, reach + 1)])
    pack, inner = lax.optimization_barrier((pack, inner))
    strips += [from_shift(pack, -far), from_shift(pack, far)]
    gridded_out = channels_first(gridded)
    smoothed = convolutions(
        column_rows, first_taps, second_taps, normed, gridded, *inner, *rims, strip, *strips
    )

    def placed(value):
        return value.reshape(CHANNELS, ROWS, BLOCK).transpose(1, 0, 2)[:, None]

    return placed(gridded_out), placed(smoothed)


def solution(mesh):
    in_specs = (
        P("tile", "groups", None, None),
        P("tile", None, None),
        P("tile"),
        P("tile"),
        P("tile", None),
        P(),
        P(),
        P(),
    )
    out_specs = (P("tile", "groups", None, None), P("tile", "groups", None, None))
    return jax.shard_map(
        per_device, mesh=mesh, in_specs=in_specs, out_specs=out_specs, check_vma=False
    )
```

```python
import functools

import jax
import jax.numpy as jnp
from jax import lax
from jax.experimental import pallas as pl
from jax.experimental.pallas import tpu as pltpu
from jax.sharding import PartitionSpec as P

BLOCK = 128
CHANNELS = 69
PADDED = 72
WIDE = 80
ROWS = 32
ROW_BITS = 5
TILE_COLS = 8
CAP = 8
GROUPS = 2 * TILE_COLS
SLOTS = GROUPS * CAP
CHUNK = 96
MARK = CHANNELS
EPSILON = 1e-05
VMEM_LIMIT = 40 * 1024 * 1024
REGRID_VMEM = 60 * 1024 * 1024


def vmem():
    return pl.BlockSpec(memory_space=pltpu.VMEM)


def smem():
    return pl.BlockSpec(memory_space=pltpu.SMEM)


def split(value, size):
    if size & (size - 1) == 0:
        return value >> (size.bit_length() - 1), value & (size - 1)
    return lax.div(value, size), lax.rem(value, size)


def lanes(shape):
    return lax.broadcasted_iota(jnp.int32, shape, len(shape) - 1)


def regrid_kernel(
    column_rows, target_hbm, target_row_hbm, index_hbm, source_hbm, weight_hbm, *rest
):
    same_out, next_outs = rest[0], rest[1 : 1 + TILE_COLS]
    (
        target_ref,
        target_row_ref,
        index_ref,
        source,
        weight,
        wide,
        field,
        sums,
        rounded,
        in_sems,
        weight_sems,
        out_sems,
    ) = rest[1 + TILE_COLS :]
    entries = weight.shape[0]
    chunks = entries // CHUNK
    tile = lax.axis_index("tile")
    column, position = split(tile, column_rows)

    small_copies = [
        pltpu.make_async_copy(target_row_hbm, target_row_ref, in_sems.at[0]),
        pltpu.make_async_copy(target_hbm, target_ref, in_sems.at[1]),
        pltpu.make_async_copy(index_hbm, index_ref, in_sems.at[2]),
    ]
    source_copy = pltpu.make_async_copy(source_hbm, source, in_sems.at[3])
    for copy in small_copies:
        copy.start()
    source_copy.start()

    def chunk_copy(chunk):
        part = pl.ds(chunk * CHUNK, CHUNK)
        return pltpu.make_async_copy(weight_hbm.at[part], weight.at[part], weight_sems.at[chunk])

    for chunk in range(chunks):
        chunk_copy(chunk).start()

    small_copies[0].wait()
    target = target_row_ref[...]
    owner, row = split(target, ROWS)
    owner_column, owner_position = split(owner, column_rows)
    group = jnp.where(
        owner_position == position, owner_column, TILE_COLS + (owner_column ^ column)
    )
    key = group * ROWS + row
    square = (entries, entries)
    down = lax.broadcasted_iota(jnp.int32, square, 0)
    along = lanes(square)
    key_along = jnp.broadcast_to(key.astype(jnp.float32), square)
    key_down = jnp.broadcast_to(
        jnp.sum(jnp.where(down == along, key_along, 0.0), axis=1, keepdims=True), square
    )
    equal = key_along == key_down
    doubles = jnp.sum(jnp.where(equal & (along < down), 1.0, 0.0), axis=1, keepdims=True)
    in_group = (key_down.astype(jnp.int32) >> ROW_BITS) == (key_along.astype(jnp.int32) >> ROW_BITS)
    below = in_group & (key_down < key_along) & (jnp.broadcast_to(doubles, square) == 0.0)
    rank = jnp.sum(jnp.where(below, 1.0, 0.0), axis=0, keepdims=True)
    mentions = jnp.sum(jnp.where(equal & (down < along), 1.0, 0.0), axis=0, keepdims=True)
    slots = group * CAP + rank.astype(jnp.int32)
    plan = slots + jnp.where(mentions == 0.0, SLOTS, 0)

    tail = PADDED - 8
    for slot in range(SLOTS):
        rounded[slot, tail:] = jnp.full((8, BLOCK), ROWS, jnp.bfloat16)
    wide[pl.ds(CHANNELS * ROWS, (PADDED - CHANNELS) * ROWS), :] = jnp.zeros(
        ((PADDED - CHANNELS) * ROWS, BLOCK), jnp.float32
    )
    nothing = jnp.zeros((WIDE - PADDED, BLOCK), jnp.float32)
    source_copy.wait()
    wide[pl.ds(0, CHANNELS * ROWS), :] = source[...].astype(jnp.float32)
    for row in range(ROWS):
        block = wide[pl.ds(row, PADDED, stride=ROWS), :]
        field[row] = jnp.concatenate([block, nothing], axis=0).astype(jnp.bfloat16)
    is_mark = lax.broadcasted_iota(jnp.int32, (8, BLOCK), 0) == MARK - tail
    blank = jnp.zeros((WIDE, BLOCK), jnp.bfloat16)
    small_copies[1].wait()
    small_copies[2].wait()

    for chunk in range(chunks):
        chunk_copy(chunk).wait()
        for entry in range(chunk * CHUNK, (chunk + 1) * CHUNK, 2):
            one = jnp.concatenate([field[index_ref[entry]], blank], axis=1)
            two = jnp.concatenate([blank, field[index_ref[entry + 1]]], axis=1)
            products = jnp.dot(
                jnp.concatenate([one, two], axis=0),
                weight[entry : entry + 2].reshape(2 * BLOCK, BLOCK),
                preferred_element_type=jnp.float32,
            )
            for at in range(2):
                code = plan[0, entry + at]
                slot = code & (SLOTS - 1)
                row = split(target_ref[entry + at], ROWS)[1]
                product = products[at * WIDE : at * WIDE + PADDED]
                total = jnp.where(code >= SLOTS, 0.0, sums[slot]) + product
                sums[slot] = total
                marked = jnp.where(is_mark, row.astype(jnp.float32), total[tail:])
                rounded[slot] = jnp.concatenate([total[:tail], marked], axis=0).astype(jnp.bfloat16)
    copies = []
    for group in range(GROUPS):
        part = rounded.at[pl.ds(group * CAP, CAP)]
        if group < TILE_COLS:
            out = same_out.at[pl.ds(group * CAP, CAP)]
        else:
            out = next_outs[group - TILE_COLS]
        copies.append(pltpu.make_async_copy(part, out, out_sems.at[group]))
    for copy in copies:
        copy.start()
    for copy in copies:
        copy.wait()


def regrid(target, source_index, field, weights, column_rows):
    piece = jax.ShapeDtypeStruct((CAP, PADDED, BLOCK), jnp.bfloat16)
    same = jax.ShapeDtypeStruct((TILE_COLS * CAP, PADDED, BLOCK), jnp.bfloat16)
    hbm = pl.BlockSpec(memory_space=pl.ANY)
    entries = weights.shape[0]
    return pl.pallas_call(
        functools.partial(regrid_kernel, column_rows),
        in_specs=[hbm] * 5,
        out_specs=[hbm] * (1 + TILE_COLS),
        out_shape=[same] + [piece] * TILE_COLS,
        scratch_shapes=[
            pltpu.SMEM(target.shape, jnp.int32),
            pltpu.VMEM((1, entries), jnp.int32),
            pltpu.SMEM(source_index.shape, jnp.int32),
            pltpu.VMEM(field.shape, jnp.bfloat16),
            pltpu.VMEM(weights.shape, jnp.bfloat16),
            pltpu.VMEM((PADDED * ROWS, BLOCK), jnp.float32),
            pltpu.VMEM((ROWS, WIDE, BLOCK), jnp.bfloat16),
            pltpu.VMEM((SLOTS, PADDED, BLOCK), jnp.float32),
            pltpu.VMEM((SLOTS, PADDED, BLOCK), jnp.bfloat16),
            pltpu.SemaphoreType.DMA((4,)),
            pltpu.SemaphoreType.DMA((entries // CHUNK,)),
            pltpu.SemaphoreType.DMA((GROUPS,)),
        ],
        compiler_params=pltpu.CompilerParams(vmem_limit_bytes=REGRID_VMEM),
        name="regrid",
    )(target, target.reshape(1, -1), source_index, field, weights)


def gather_kernel(column_rows, flip_ref, gain_ref, same, *rest):
    nexts = rest[:TILE_COLS]
    (
        gridded,
        normed,
        upward,
        downward,
        strip_out,
        summed,
    ) = rest[TILE_COLS:]
    position = lax.rem(lax.axis_index("tile"), column_rows)
    summed[...] = jnp.zeros_like(summed)

    def add(piece):
        row = piece[MARK : MARK + 1].astype(jnp.float32).astype(jnp.int32)[0, 0]
        summed[row] = summed[row] + piece[...].astype(jnp.float32)

    for slot in range(SLOTS // 2):
        add(same.at[slot])

    @pl.when(position > 0)
    def _():
        for group in range(TILE_COLS):
            for place in range(CAP):
                add(nexts[group].at[place])

    gain = gain_ref[...]
    channel = lax.broadcasted_iota(jnp.int32, (PADDED, BLOCK), 0)
    nothing = jnp.zeros((WIDE - PADDED, BLOCK), jnp.float32)
    lane = lanes((WIDE, BLOCK))
    strip = jnp.zeros((WIDE, BLOCK), jnp.bfloat16)
    for row in range(ROWS):
        rounded = summed[row].astype(jnp.bfloat16)
        gridded[row] = rounded
        value = rounded.astype(jnp.float32)
        value = jnp.where(channel < CHANNELS, value, 0.0)
        square = jnp.sum(value * value, axis=0, keepdims=True) * (1.0 / CHANNELS)
        scaled = value * lax.rsqrt(square + EPSILON) * gain
        scaled = jnp.concatenate([scaled, nothing], axis=0).astype(jnp.bfloat16)
        normed[row] = scaled
        if row < 2:
            upward[row] = scaled
        if row >= ROWS - 2:
            downward[row - ROWS + 2] = scaled
        strip = jnp.where((lane >> 2) == row, pltpu.roll(scaled, 4 * row + 2, 1), strip)
    to_lane = lanes((BLOCK, BLOCK))
    from_lane = 4 * (to_lane & (ROWS - 1)) + (((to_lane >> ROW_BITS) + 2) & 3)
    order = lax.broadcasted_iota(jnp.int32, (BLOCK, BLOCK), 0) == from_lane
    strip = jnp.dot(strip, order.astype(jnp.bfloat16), preferred_element_type=jnp.float32)
    channel = lax.broadcasted_iota(jnp.int32, (WIDE, BLOCK), 0)
    for side in range(2):
        strip = jnp.where(channel == CHANNELS + side, flip_ref[0, side].astype(jnp.float32), strip)
    strip = strip.astype(jnp.bfloat16)
    upward[2] = strip
    downward[2] = strip
    strip_out[...] = strip


GRIDDED = jax.ShapeDtypeStruct((ROWS, PADDED, BLOCK), jnp.bfloat16)
FIELD = jax.ShapeDtypeStruct((ROWS, WIDE, BLOCK), jnp.bfloat16)
RIM = jax.ShapeDtypeStruct((3, WIDE, BLOCK), jnp.bfloat16)
STRIP_COLUMNS = (0, 1, BLOCK - 2, BLOCK - 1)
STRIP = jax.ShapeDtypeStruct((WIDE, BLOCK), jnp.bfloat16)


def gather_rows(column_rows, edge_flip, gain, same, nexts):
    return pl.pallas_call(
        functools.partial(gather_kernel, column_rows),
        in_specs=[smem()] + [vmem()] * (2 + TILE_COLS),
        out_specs=[vmem()] * 5,
        out_shape=[GRIDDED, FIELD, RIM, RIM, STRIP],
        scratch_shapes=[
            pltpu.VMEM((ROWS + 1, PADDED, BLOCK), jnp.float32),
        ],
        compiler_params=pltpu.CompilerParams(vmem_limit_bytes=VMEM_LIMIT),
        name="gather_rows",
    )(edge_flip, gain, same, *nexts)


def turn_kernel(field, out, turned):
    for row in range(ROWS):
        turned[pl.ds(row, PADDED, stride=ROWS), :] = field[row].astype(jnp.float32)
    out[...] = turned[pl.ds(0, CHANNELS * ROWS), :].astype(jnp.bfloat16)


def channels_first(field):
    return pl.pallas_call(
        turn_kernel,
        in_specs=[vmem()],
        out_specs=vmem(),
        out_shape=jax.ShapeDtypeStruct((CHANNELS * ROWS, BLOCK), jnp.bfloat16),
        scratch_shapes=[pltpu.VMEM((PADDED * ROWS, BLOCK), jnp.float32)],
        compiler_params=pltpu.CompilerParams(vmem_limit_bytes=VMEM_LIMIT),
        name="channels_first",
    )(field)


def shifted_columns(value, left_end, right_end):
    lane = lanes((WIDE, BLOCK))
    left = jnp.where(lane == 0, left_end, pltpu.roll(value, 1, 1))
    right = jnp.where(lane == BLOCK - 1, right_end, pltpu.roll(value, BLOCK - 1, 1))
    return jnp.concatenate([left, value, right], axis=0)


def tap_sums(taps, one, two):
    both = jnp.concatenate([one, two], axis=1)
    result = jnp.dot(taps, both, preferred_element_type=jnp.float32)
    return result[:, :BLOCK], result[:, BLOCK:]


def row_tap(sums, at):
    return sums[at * WIDE : (at + 1) * WIDE]


def activated(value):
    return jax.nn.gelu(value).astype(jnp.bfloat16)


def inner_kernel(taps_ref, field, hidden, ends, sides, partial):
    taps = taps_ref[...]
    blank = jnp.zeros((WIDE, BLOCK), jnp.bfloat16)
    for row in range(0, ROWS, 2):
        partial[row], partial[row + 1] = tap_sums(
            taps,
            shifted_columns(field[row], blank, blank),
            shifted_columns(field[row + 1], blank, blank),
        )
    lane = lanes((WIDE, BLOCK))
    west = jnp.zeros((WIDE, BLOCK), jnp.float32)
    east = jnp.zeros((WIDE, BLOCK), jnp.float32)
    for row in range(ROWS):
        value = partial[row, WIDE : 2 * WIDE]
        if row > 0:
            value = value + partial[row - 1, :WIDE]
        if row < ROWS - 1:
            value = value + partial[row + 1, 2 * WIDE :]
        if row == 0:
            ends[0] = value
        elif row == ROWS - 1:
            ends[1] = value
        else:
            hidden[row] = activated(value)
        west = jnp.where(lane == row, pltpu.roll(value, row, 1), west)
        east = jnp.where(lane == row, pltpu.roll(value, row + 1, 1), east)
    hidden[0] = blank
    hidden[ROWS - 1] = blank
    sides[0] = west
    sides[1] = east


def inner_convolution(taps, field):
    pair = jax.ShapeDtypeStruct((2, WIDE, BLOCK), jnp.float32)
    return pl.pallas_call(
        inner_kernel,
        in_specs=[vmem()] * 2,
        out_specs=[vmem()] * 3,
        out_shape=[FIELD, pair, pair],
        scratch_shapes=[pltpu.VMEM((ROWS, 3 * WIDE, BLOCK), jnp.float32)],
        compiler_params=pltpu.CompilerParams(vmem_limit_bytes=VMEM_LIMIT),
        cost_estimate=pl.CostEstimate(
            flops=2 * 9 * WIDE * WIDE * ROWS * BLOCK, bytes_accessed=2 << 20, transcendentals=0
        ),
        name="inner_convolution",
    )(taps, field)


def strip_plan(column_rows):
    if column_rows == 2:
        return [], 3, 1
    return [-2, 2], column_rows, 2


def conv_kernel(
    column_rows,
    first_taps_ref,
    second_taps_ref,
    field,
    gridded,
    inner,
    ends_ref,
    sides_ref,
    above,
    below,
    own_strip,
    *rest,
):
    near, far, reach = strip_plan(column_rows)
    near_strips, (west_pack, east_pack) = rest[: len(near)], rest[len(near) : len(near) + 2]
    smoothed, hidden, partial, turned = rest[len(near) + 2 :]
    count = lax.axis_size("tile")
    tile = lax.axis_index("tile")
    lane = lanes((WIDE, BLOCK))
    last = ROWS + 1
    R = column_rows
    blank = jnp.zeros((WIDE, BLOCK), jnp.bfloat16)

    strips = {-1: above[2], 0: own_strip[...], 1: below[2]}
    strips.update((shift, ref[...]) for shift, ref in zip(near, near_strips))
    for at in range(-reach, reach + 1):
        strips[at - far], strips[at + far] = west_pack[at + reach], east_pack[at + reach]

    def place(shift):
        return lax.rem(tile + shift + count, count)

    def ends(shift, before, after, middle):
        before = jnp.where(place(shift) > 0, before, blank)
        after = jnp.where(place(shift) < count - 1, after, blank)
        return jnp.where(lane == 0, before, jnp.where(lane == last, after, middle))

    memo = {}

    def padded_column(shift, which):
        if (shift, which) not in memo:
            base = which * ROWS
            memo[shift, which] = ends(
                shift,
                pltpu.roll(strips[shift - 1], (1 - base - ROWS) % BLOCK, 1),
                pltpu.roll(strips[shift + 1], (last - base) % BLOCK, 1),
                pltpu.roll(strips[shift], (1 - base) % BLOCK, 1),
            )
        return memo[shift, which]

    row_id = lax.broadcasted_iota(jnp.int32, (BLOCK, BLOCK), 0)
    reversal = (row_id + lanes((BLOCK, BLOCK)) == last).astype(jnp.bfloat16)

    def reversed_lanes(planes):
        stacked = jnp.concatenate(planes, axis=0)
        turned_round = jnp.dot(stacked, reversal, preferred_element_type=jnp.float32)
        return [row_tap(turned_round, at) for at in range(len(planes))]

    def choose(shift, which, turned_round, plain):
        flips = strips[shift].astype(jnp.float32)[CHANNELS + which : CHANNELS + which + 1]
        return jnp.where(flips > 0.5, turned_round, plain.astype(jnp.float32)).astype(jnp.bfloat16)

    west_of = {shift: (shift - R, 3) for shift in {-1, 0, 1, R - 1, R, R + 1}}
    east_of = {shift: (shift + R, 0) for shift in {-1, 0, 1, -R - 1, -R, -R + 1}}
    keys = sorted(set(west_of.values()) | set(east_of.values()))
    flipped = dict(zip(keys, reversed_lanes([padded_column(*key) for key in keys])))
    west = {
        shift: choose(shift, 0, flipped[west_of[shift]], padded_column(*west_of[shift]))
        for shift in sorted(west_of)
    }
    east = {
        shift: choose(shift, 1, flipped[east_of[shift]], padded_column(*east_of[shift]))
        for shift in sorted(east_of)
    }

    def columns(value, west_plane, west_row, east_plane, east_row):
        return shifted_columns(
            value,
            pltpu.roll(west_plane, (BLOCK - west_row) % BLOCK, 1),
            pltpu.roll(east_plane, BLOCK - 1 - east_row, 1),
        )

    def along(result):
        return (
            row_tap(result, 0)
            + pltpu.roll(row_tap(result, 1), BLOCK - 1, 1)
            + pltpu.roll(row_tap(result, 2), BLOCK - 2, 1)
        )

    first_taps = first_taps_ref[...]
    up = [jnp.where(tile > 0, above[at], blank) for at in range(2)]
    down = [jnp.where(tile < count - 1, below[at], blank) for at in range(2)]
    from_up, from_down = tap_sums(
        first_taps, shifted_columns(up[1], blank, blank), shifted_columns(down[0], blank, blank)
    )
    from_up, from_down = row_tap(from_up, 0), row_tap(from_down, 2)
    from_west, from_east = tap_sums(
        first_taps,
        jnp.concatenate([west[0], blank, blank], axis=0),
        jnp.concatenate([blank, blank, east[0]], axis=0),
    )
    from_west, from_east = along(from_west), along(from_east)
    first = ends_ref[0] + from_up
    first = first + jnp.where(lane == 0, from_west, 0.0)
    first = first + jnp.where(lane == BLOCK - 1, pltpu.roll(from_east, BLOCK - 1, 1), 0.0)
    final = ends_ref[1] + from_down
    final = final + jnp.where(lane == 0, pltpu.roll(from_west, BLOCK - ROWS + 1, 1), 0.0)
    final = final + jnp.where(lane == BLOCK - 1, pltpu.roll(from_east, BLOCK - ROWS, 1), 0.0)
    hidden[1] = activated(first)
    hidden[ROWS] = activated(final)
    first_column = activated(sides_ref[0] + from_west)
    last_column = activated(sides_ref[1] + from_east)
    for row in range(1, ROWS - 1):
        value = jnp.where(lane == 0, pltpu.roll(first_column, BLOCK - row, 1), inner[row])
        hidden[row + 1] = jnp.where(
            lane == BLOCK - 1, pltpu.roll(last_column, BLOCK - 1 - row, 1), value
        )

    upper = jnp.zeros((WIDE, BLOCK), jnp.float32)
    lower = jnp.zeros((WIDE, BLOCK), jnp.float32)
    for at, (high, low) in enumerate(
        [(up[0], field[ROWS - 1]), (up[1], down[0]), (field[0], down[1])]
    ):
        from_row = ROWS - 1 + at
        one, two = tap_sums(
            first_taps,
            columns(high, west[-1], from_row, east[-1], from_row),
            columns(low, west[1], at, east[1], at),
        )
        upper += row_tap(one, at)
        lower += row_tap(two, at)
    hidden[0] = jnp.where(tile > 0, activated(upper), blank)
    hidden[last] = jnp.where(tile < count - 1, activated(lower), blank)

    west_hidden, east_hidden = {}, {}
    for at in (-1, 0, 1):
        q = at - R
        one = jnp.concatenate([padded_column(q, 2), padded_column(q, 3), east[q]], axis=0)
        q = at + R
        two = jnp.concatenate([west[q], padded_column(q, 0), padded_column(q, 1)], axis=0)
        one, two = tap_sums(first_taps, one, two)
        west_hidden[at], east_hidden[at] = activated(along(one)), activated(along(two))

    def hidden_side(shift, values):
        return ends(
            shift,
            pltpu.roll(values[-1], BLOCK - ROWS + 1, 1),
            pltpu.roll(values[1], last, 1),
            pltpu.roll(values[0], 1, 1),
        )

    plain = [hidden_side(-R, west_hidden), hidden_side(R, east_hidden)]
    west_side, east_side = [
        choose(0, which, turned_side, plain[which])
        for which, turned_side in enumerate(reversed_lanes(plain))
    ]

    second_taps = second_taps_ref[...]
    for p in range(0, ROWS + 2, 2):
        partial[p], partial[p + 1] = tap_sums(
            second_taps,
            columns(hidden[p], west_side, p, east_side, p),
            columns(hidden[p + 1], west_side, p + 1, east_side, p + 1),
        )
    for row in range(ROWS):
        branch = (
            partial[row, :PADDED]
            + partial[row + 1, WIDE : WIDE + PADDED]
            + partial[row + 2, 2 * WIDE : 2 * WIDE + PADDED]
        )
        turned[pl.ds(row, PADDED, stride=ROWS), :] = gridded[row].astype(jnp.float32) + branch
    smoothed[...] = turned[pl.ds(0, CHANNELS * ROWS), :].astype(jnp.bfloat16)


def convolutions(column_rows, *operands):
    return pl.pallas_call(
        functools.partial(conv_kernel, column_rows),
        in_specs=[vmem()] * len(operands),
        out_specs=vmem(),
        out_shape=jax.ShapeDtypeStruct((CHANNELS * ROWS, BLOCK), jnp.bfloat16),
        scratch_shapes=[
            pltpu.VMEM((ROWS + 2, WIDE, BLOCK), jnp.bfloat16),
            pltpu.VMEM((ROWS + 2, 3 * WIDE, BLOCK), jnp.float32),
            pltpu.VMEM((PADDED * ROWS, BLOCK), jnp.float32),
        ],
        compiler_params=pltpu.CompilerParams(vmem_limit_bytes=VMEM_LIMIT),
        name="convolutions",
    )(*operands)


def tap_matrix(kernel):
    pad = WIDE - CHANNELS
    taps = jnp.pad(kernel, ((0, 0), (0, pad), (0, pad))).reshape(3, 3, WIDE, WIDE)
    return taps.transpose(0, 2, 1, 3).reshape(3 * WIDE, 3 * WIDE)


def from_shift(value, shift):
    count = lax.axis_size("tile")
    return lax.ppermute(value, "tile", [(i, (i - shift) % count) for i in range(count)])


def per_device(
    source, weights, block_source, block_target, edge_flip, norm_gain, first_kernel, second_kernel
):
    count = lax.axis_size("tile")
    column_rows = count // TILE_COLS
    field = source.reshape(ROWS, CHANNELS, BLOCK).transpose(1, 0, 2).reshape(-1, BLOCK)
    same, *nexts = regrid(block_target, block_source, field, weights, column_rows)

    for across in range(TILE_COLS):
        pairs = [
            (c * column_rows + p, (c ^ across) * column_rows + p + 1)
            for c in range(TILE_COLS)
            for p in range(column_rows - 1)
        ]
        nexts[across] = lax.ppermute(nexts[across], "tile", pairs)
    nexts = [nexts[across] for across in (0, 1, 2, 4, 5, 6, 7, 3)]
    same = lax.all_to_all(
        same,
        "tile",
        0,
        0,
        axis_index_groups=[
            [c * column_rows + p for c in range(TILE_COLS)] for p in range(column_rows)
        ],
        tiled=True,
    )

    gain = jnp.broadcast_to(
        jnp.pad(norm_gain, (0, PADDED - CHANNELS))[:, None], (PADDED, BLOCK)
    )
    first_taps, second_taps = tap_matrix(first_kernel), tap_matrix(second_kernel)
    same, nexts, gain, first_taps, second_taps = lax.optimization_barrier(
        (same, nexts, gain, first_taps, second_taps)
    )
    gridded, normed, upward, downward, strip = gather_rows(
        column_rows, edge_flip, gain, same, nexts
    )
    rims = [from_shift(downward, -1), from_shift(upward, 1)]
    near, far, reach = strip_plan(column_rows)
    strips = [from_shift(strip, shift) for shift in near]
    inner = inner_convolution(first_taps, normed)
    held = {-1: rims[0][2], 0: strip, 1: rims[1][2], **dict(zip(near, strips))}
    pack = jnp.stack([held[at] for at in range(-reach, reach + 1)])
    pack, inner = lax.optimization_barrier((pack, inner))
    strips += [from_shift(pack, -far), from_shift(pack, far)]
    gridded_out = channels_first(gridded)
    smoothed = convolutions(
        column_rows, first_taps, second_taps, normed, gridded, *inner, *rims, strip, *strips
    )

    def placed(value):
        return value.reshape(CHANNELS, ROWS, BLOCK).transpose(1, 0, 2)[:, None]

    return placed(gridded_out), placed(smoothed)


def solution(mesh):
    in_specs = (
        P("tile", "groups", None, None),
        P("tile", None, None),
        P("tile"),
        P("tile"),
        P("tile", None),
        P(),
        P(),
        P(),
    )
    out_specs = (P("tile", "groups", None, None), P("tile", "groups", None, None))
    return jax.shard_map(
        per_device, mesh=mesh, in_specs=in_specs, out_specs=out_specs, check_vma=False
    )
```

```python
import functools

import jax
import jax.numpy as jnp
from jax import lax
from jax.experimental import pallas as pl
from jax.experimental.pallas import tpu as pltpu
from jax.sharding import PartitionSpec as P

BLOCK = 128
CHANNELS = 69
PADDED = 72
WIDE = 80
ROWS = 32
ROW_BITS = 5
TILE_COLS = 8
CAP = 8
GROUPS = 2 * TILE_COLS
SLOTS = GROUPS * CAP
CHUNK = 96
MARK = CHANNELS
EPSILON = 1e-05
VMEM_LIMIT = 40 * 1024 * 1024
REGRID_VMEM = 60 * 1024 * 1024


def vmem():
    return pl.BlockSpec(memory_space=pltpu.VMEM)


def smem():
    return pl.BlockSpec(memory_space=pltpu.SMEM)


def split(value, size):
    if size & (size - 1) == 0:
        return value >> (size.bit_length() - 1), value & (size - 1)
    return lax.div(value, size), lax.rem(value, size)


def lanes(shape):
    return lax.broadcasted_iota(jnp.int32, shape, len(shape) - 1)


def regrid_kernel(
    column_rows, target_hbm, target_row_hbm, index_hbm, source_hbm, weight_hbm, *rest
):
    same_out, next_outs = rest[0], rest[1 : 1 + TILE_COLS]
    (
        target_ref,
        target_row_ref,
        index_ref,
        source,
        weight,
        wide,
        field,
        sums,
        rounded,
        plan,
        plan_scalars,
        plan_sem,
        in_sems,
        weight_sems,
        out_sems,
    ) = rest[1 + TILE_COLS :]
    entries = weight.shape[0]
    chunks = entries // CHUNK
    tile = lax.axis_index("tile")
    column, position = split(tile, column_rows)

    small_copies = [
        pltpu.make_async_copy(target_row_hbm, target_row_ref, in_sems.at[0]),
        pltpu.make_async_copy(target_hbm, target_ref, in_sems.at[1]),
        pltpu.make_async_copy(index_hbm, index_ref, in_sems.at[2]),
    ]
    source_copy = pltpu.make_async_copy(source_hbm, source, in_sems.at[3])
    for copy in small_copies:
        copy.start()
    source_copy.start()

    def chunk_copy(chunk):
        part = pl.ds(chunk * CHUNK, CHUNK)
        return pltpu.make_async_copy(weight_hbm.at[part], weight.at[part], weight_sems.at[chunk])

    for chunk in range(chunks):
        chunk_copy(chunk).start()

    small_copies[0].wait()
    target = target_row_ref[...]
    owner, row = split(target, ROWS)
    owner_column, owner_position = split(owner, column_rows)
    group = jnp.where(
        owner_position == position, owner_column, TILE_COLS + (owner_column ^ column)
    )
    key = group * ROWS + row
    square = (entries, entries)
    down = lax.broadcasted_iota(jnp.int32, square, 0)
    along = lanes(square)
    key_along = jnp.broadcast_to(key.astype(jnp.float32), square)
    key_down = jnp.broadcast_to(
        jnp.sum(jnp.where(down == along, key_along, 0.0), axis=1, keepdims=True), square
    )
    equal = key_along == key_down
    doubles = jnp.sum(jnp.where(equal & (along < down), 1.0, 0.0), axis=1, keepdims=True)
    in_group = (key_down.astype(jnp.int32) >> ROW_BITS) == (key_along.astype(jnp.int32) >> ROW_BITS)
    below = in_group & (key_down < key_along) & (jnp.broadcast_to(doubles, square) == 0.0)
    rank = jnp.sum(jnp.where(below, 1.0, 0.0), axis=0, keepdims=True)
    mentions = jnp.sum(jnp.where(equal & (down < along), 1.0, 0.0), axis=0, keepdims=True)
    slots = group * CAP + rank.astype(jnp.int32)
    plan[...] = slots + jnp.where(mentions == 0.0, SLOTS, 0)
    plan_copy = pltpu.make_async_copy(plan, plan_scalars, plan_sem)
    plan_copy.start()

    tail = PADDED - 8
    for slot in range(SLOTS):
        rounded[slot, tail:] = jnp.full((8, BLOCK), ROWS, jnp.bfloat16)
    wide[pl.ds(CHANNELS * ROWS, (PADDED - CHANNELS) * ROWS), :] = jnp.zeros(
        ((PADDED - CHANNELS) * ROWS, BLOCK), jnp.float32
    )
    nothing = jnp.zeros((WIDE - PADDED, BLOCK), jnp.float32)
    source_copy.wait()
    wide[pl.ds(0, CHANNELS * ROWS), :] = source[...].astype(jnp.float32)
    for row in range(ROWS):
        block = wide[pl.ds(row, PADDED, stride=ROWS), :]
        field[row] = jnp.concatenate([block, nothing], axis=0).astype(jnp.bfloat16)
    is_mark = lax.broadcasted_iota(jnp.int32, (8, BLOCK), 0) == MARK - tail
    blank = jnp.zeros((WIDE, BLOCK), jnp.bfloat16)
    small_copies[1].wait()
    small_copies[2].wait()
    plan_copy.wait()

    for chunk in range(chunks):
        chunk_copy(chunk).wait()
        for entry in range(chunk * CHUNK, (chunk + 1) * CHUNK, 2):
            one = jnp.concatenate([field[index_ref[entry]], blank], axis=1)
            two = jnp.concatenate([blank, field[index_ref[entry + 1]]], axis=1)
            products = jnp.dot(
                jnp.concatenate([one, two], axis=0),
                weight[entry : entry + 2].reshape(2 * BLOCK, BLOCK),
                preferred_element_type=jnp.float32,
            )
            for at in range(2):
                code = plan_scalars[0, entry + at]
                slot = code & (SLOTS - 1)
                row = split(target_ref[entry + at], ROWS)[1]
                product = products[at * WIDE : at * WIDE + PADDED]
                total = jnp.where(code >= SLOTS, 0.0, sums[slot]) + product
                sums[slot] = total
                marked = jnp.where(is_mark, row.astype(jnp.float32), total[tail:])
                rounded[slot] = jnp.concatenate([total[:tail], marked], axis=0).astype(jnp.bfloat16)
    copies = []
    for group in range(GROUPS):
        part = rounded.at[pl.ds(group * CAP, CAP)]
        if group < TILE_COLS:
            out = same_out.at[pl.ds(group * CAP, CAP)]
        else:
            out = next_outs[group - TILE_COLS]
        copies.append(pltpu.make_async_copy(part, out, out_sems.at[group]))
    for copy in copies:
        copy.start()
    for copy in copies:
        copy.wait()


def regrid(target, source_index, field, weights, column_rows):
    piece = jax.ShapeDtypeStruct((CAP, PADDED, BLOCK), jnp.bfloat16)
    same = jax.ShapeDtypeStruct((TILE_COLS * CAP, PADDED, BLOCK), jnp.bfloat16)
    hbm = pl.BlockSpec(memory_space=pl.ANY)
    entries = weights.shape[0]
    return pl.pallas_call(
        functools.partial(regrid_kernel, column_rows),
        in_specs=[hbm] * 5,
        out_specs=[hbm] * (1 + TILE_COLS),
        out_shape=[same] + [piece] * TILE_COLS,
        scratch_shapes=[
            pltpu.SMEM(target.shape, jnp.int32),
            pltpu.VMEM((1, entries), jnp.int32),
            pltpu.SMEM(source_index.shape, jnp.int32),
            pltpu.VMEM(field.shape, jnp.bfloat16),
            pltpu.VMEM(weights.shape, jnp.bfloat16),
            pltpu.VMEM((PADDED * ROWS, BLOCK), jnp.float32),
            pltpu.VMEM((ROWS, WIDE, BLOCK), jnp.bfloat16),
            pltpu.VMEM((SLOTS, PADDED, BLOCK), jnp.float32),
            pltpu.VMEM((SLOTS, PADDED, BLOCK), jnp.bfloat16),
            pltpu.VMEM((1, entries), jnp.int32),
            pltpu.SMEM((1, entries), jnp.int32),
            pltpu.SemaphoreType.DMA,
            pltpu.SemaphoreType.DMA((4,)),
            pltpu.SemaphoreType.DMA((entries // CHUNK,)),
            pltpu.SemaphoreType.DMA((GROUPS,)),
        ],
        compiler_params=pltpu.CompilerParams(vmem_limit_bytes=REGRID_VMEM),
        name="regrid",
    )(target, target.reshape(1, -1), source_index, field, weights)


def gather_kernel(column_rows, flip_ref, gain_ref, same, *rest):
    nexts = rest[:TILE_COLS]
    (
        gridded,
        normed,
        upward,
        downward,
        strip_out,
        summed,
    ) = rest[TILE_COLS:]
    position = lax.rem(lax.axis_index("tile"), column_rows)
    summed[...] = jnp.zeros_like(summed)

    def add(piece):
        row = piece[MARK : MARK + 1].astype(jnp.float32).astype(jnp.int32)[0, 0]
        summed[row] = summed[row] + piece[...].astype(jnp.float32)

    for slot in range(SLOTS // 2):
        add(same.at[slot])

    @pl.when(position > 0)
    def _():
        for group in range(TILE_COLS):
            for place in range(CAP):
                add(nexts[group].at[place])

    gain = gain_ref[...]
    channel = lax.broadcasted_iota(jnp.int32, (PADDED, BLOCK), 0)
    nothing = jnp.zeros((WIDE - PADDED, BLOCK), jnp.float32)
    lane = lanes((WIDE, BLOCK))
    strip = jnp.zeros((WIDE, BLOCK), jnp.bfloat16)
    for row in range(ROWS):
        rounded = summed[row].astype(jnp.bfloat16)
        gridded[row] = rounded
        value = rounded.astype(jnp.float32)
        value = jnp.where(channel < CHANNELS, value, 0.0)
        square = jnp.sum(value * value, axis=0, keepdims=True) * (1.0 / CHANNELS)
        scaled = value * lax.rsqrt(square + EPSILON) * gain
        scaled = jnp.concatenate([scaled, nothing], axis=0).astype(jnp.bfloat16)
        normed[row] = scaled
        if row < 2:
            upward[row] = scaled
        if row >= ROWS - 2:
            downward[row - ROWS + 2] = scaled
        strip = jnp.where((lane >> 2) == row, pltpu.roll(scaled, 4 * row + 2, 1), strip)
    to_lane = lanes((BLOCK, BLOCK))
    from_lane = 4 * (to_lane & (ROWS - 1)) + (((to_lane >> ROW_BITS) + 2) & 3)
    order = lax.broadcasted_iota(jnp.int32, (BLOCK, BLOCK), 0) == from_lane
    strip = jnp.dot(strip, order.astype(jnp.bfloat16), preferred_element_type=jnp.float32)
    channel = lax.broadcasted_iota(jnp.int32, (WIDE, BLOCK), 0)
    for side in range(2):
        strip = jnp.where(channel == CHANNELS + side, flip_ref[0, side].astype(jnp.float32), strip)
    strip = strip.astype(jnp.bfloat16)
    upward[2] = strip
    downward[2] = strip
    strip_out[...] = strip


GRIDDED = jax.ShapeDtypeStruct((ROWS, PADDED, BLOCK), jnp.bfloat16)
FIELD = jax.ShapeDtypeStruct((ROWS, WIDE, BLOCK), jnp.bfloat16)
RIM = jax.ShapeDtypeStruct((3, WIDE, BLOCK), jnp.bfloat16)
STRIP_COLUMNS = (0, 1, BLOCK - 2, BLOCK - 1)
STRIP = jax.ShapeDtypeStruct((WIDE, BLOCK), jnp.bfloat16)


def gather_rows(column_rows, edge_flip, gain, same, nexts):
    return pl.pallas_call(
        functools.partial(gather_kernel, column_rows),
        in_specs=[smem()] + [vmem()] * (2 + TILE_COLS),
        out_specs=[vmem()] * 5,
        out_shape=[GRIDDED, FIELD, RIM, RIM, STRIP],
        scratch_shapes=[
            pltpu.VMEM((ROWS + 1, PADDED, BLOCK), jnp.float32),
        ],
        compiler_params=pltpu.CompilerParams(vmem_limit_bytes=VMEM_LIMIT),
        name="gather_rows",
    )(edge_flip, gain, same, *nexts)


def turn_kernel(field, out, turned):
    for row in range(ROWS):
        turned[pl.ds(row, PADDED, stride=ROWS), :] = field[row].astype(jnp.float32)
    out[...] = turned[pl.ds(0, CHANNELS * ROWS), :].astype(jnp.bfloat16)


def channels_first(field):
    return pl.pallas_call(
        turn_kernel,
        in_specs=[vmem()],
        out_specs=vmem(),
        out_shape=jax.ShapeDtypeStruct((CHANNELS * ROWS, BLOCK), jnp.bfloat16),
        scratch_shapes=[pltpu.VMEM((PADDED * ROWS, BLOCK), jnp.float32)],
        compiler_params=pltpu.CompilerParams(vmem_limit_bytes=VMEM_LIMIT),
        name="channels_first",
    )(field)


def shifted_columns(value, left_end, right_end):
    lane = lanes((WIDE, BLOCK))
    left = jnp.where(lane == 0, left_end, pltpu.roll(value, 1, 1))
    right = jnp.where(lane == BLOCK - 1, right_end, pltpu.roll(value, BLOCK - 1, 1))
    return jnp.concatenate([left, value, right], axis=0)


def tap_sums(taps, one, two):
    both = jnp.concatenate([one, two], axis=1)
    result = jnp.dot(taps, both, preferred_element_type=jnp.float32)
    return result[:, :BLOCK], result[:, BLOCK:]


def row_tap(sums, at):
    return sums[at * WIDE : (at + 1) * WIDE]


def activated(value):
    return jax.nn.gelu(value).astype(jnp.bfloat16)


def inner_kernel(taps_ref, field, hidden, ends, sides, partial):
    taps = taps_ref[...]
    blank = jnp.zeros((WIDE, BLOCK), jnp.bfloat16)
    for row in range(0, ROWS, 2):
        partial[row], partial[row + 1] = tap_sums(
            taps,
            shifted_columns(field[row], blank, blank),
            shifted_columns(field[row + 1], blank, blank),
        )
    lane = lanes((WIDE, BLOCK))
    west = jnp.zeros((WIDE, BLOCK), jnp.float32)
    east = jnp.zeros((WIDE, BLOCK), jnp.float32)
    for row in range(ROWS):
        value = partial[row, WIDE : 2 * WIDE]
        if row > 0:
            value = value + partial[row - 1, :WIDE]
        if row < ROWS - 1:
            value = value + partial[row + 1, 2 * WIDE :]
        if row == 0:
            ends[0] = value
        elif row == ROWS - 1:
            ends[1] = value
        else:
            hidden[row] = jnp.where((lane == 0) | (lane == BLOCK - 1), blank, activated(value))
        west = jnp.where(lane == row, pltpu.roll(value, row, 1), west)
        east = jnp.where(lane == row, pltpu.roll(value, row + 1, 1), east)
    hidden[0] = blank
    hidden[ROWS - 1] = blank
    sides[0] = west
    sides[1] = east


def inner_convolution(taps, field):
    pair = jax.ShapeDtypeStruct((2, WIDE, BLOCK), jnp.float32)
    return pl.pallas_call(
        inner_kernel,
        in_specs=[vmem()] * 2,
        out_specs=[vmem()] * 3,
        out_shape=[FIELD, pair, pair],
        scratch_shapes=[pltpu.VMEM((ROWS, 3 * WIDE, BLOCK), jnp.float32)],
        compiler_params=pltpu.CompilerParams(vmem_limit_bytes=VMEM_LIMIT),
        cost_estimate=pl.CostEstimate(
            flops=2 * 9 * WIDE * WIDE * ROWS * BLOCK, bytes_accessed=2 << 20, transcendentals=0
        ),
        name="inner_convolution",
    )(taps, field)


def second_kernel_inner(taps_ref, hidden, gridded, base, partial):
    taps = taps_ref[...]
    blank = jnp.zeros((WIDE, BLOCK), jnp.bfloat16)
    for row in range(0, ROWS, 2):
        partial[row], partial[row + 1] = tap_sums(
            taps,
            shifted_columns(hidden[row], blank, blank),
            shifted_columns(hidden[row + 1], blank, blank),
        )
    for row in range(ROWS):
        value = gridded[row].astype(jnp.float32) + partial[row, WIDE : WIDE + PADDED]
        if row > 0:
            value = value + partial[row - 1, :PADDED]
        if row < ROWS - 1:
            value = value + partial[row + 1, 2 * WIDE : 2 * WIDE + PADDED]
        base[row] = value


def inner_second_convolution(taps, hidden, gridded):
    return pl.pallas_call(
        second_kernel_inner,
        in_specs=[vmem()] * 3,
        out_specs=vmem(),
        out_shape=jax.ShapeDtypeStruct((ROWS, PADDED, BLOCK), jnp.float32),
        scratch_shapes=[pltpu.VMEM((ROWS, 3 * WIDE, BLOCK), jnp.float32)],
        compiler_params=pltpu.CompilerParams(vmem_limit_bytes=VMEM_LIMIT),
        cost_estimate=pl.CostEstimate(
            flops=2 * 9 * WIDE * WIDE * ROWS * BLOCK, bytes_accessed=2 << 20, transcendentals=0
        ),
        name="inner_second_convolution",
    )(taps, hidden, gridded)


def strip_plan(column_rows):
    if column_rows == 2:
        return [], 3, 1
    return [-2, 2], column_rows, 2


def conv_kernel(
    column_rows,
    first_taps_ref,
    second_taps_ref,
    field,
    base,
    ends_ref,
    sides_ref,
    above,
    below,
    own_strip,
    *rest,
):
    near, far, reach = strip_plan(column_rows)
    near_strips, (west_pack, east_pack) = rest[: len(near)], rest[len(near) : len(near) + 2]
    smoothed, turned = rest[len(near) + 2 :]
    count = lax.axis_size("tile")
    tile = lax.axis_index("tile")
    lane = lanes((WIDE, BLOCK))
    last = ROWS + 1
    R = column_rows
    blank = jnp.zeros((WIDE, BLOCK), jnp.bfloat16)

    strips = {-1: above[2], 0: own_strip[...], 1: below[2]}
    strips.update((shift, ref[...]) for shift, ref in zip(near, near_strips))
    for at in range(-reach, reach + 1):
        strips[at - far], strips[at + far] = west_pack[at + reach], east_pack[at + reach]

    def place(shift):
        return lax.rem(tile + shift + count, count)

    def ends(shift, before, after, middle):
        before = jnp.where(place(shift) > 0, before, blank)
        after = jnp.where(place(shift) < count - 1, after, blank)
        return jnp.where(lane == 0, before, jnp.where(lane == last, after, middle))

    memo = {}

    def padded_column(shift, which):
        if (shift, which) not in memo:
            base = which * ROWS
            memo[shift, which] = ends(
                shift,
                pltpu.roll(strips[shift - 1], (1 - base - ROWS) % BLOCK, 1),
                pltpu.roll(strips[shift + 1], (last - base) % BLOCK, 1),
                pltpu.roll(strips[shift], (1 - base) % BLOCK, 1),
            )
        return memo[shift, which]

    row_id = lax.broadcasted_iota(jnp.int32, (BLOCK, BLOCK), 0)
    reversal = (row_id + lanes((BLOCK, BLOCK)) == last).astype(jnp.bfloat16)

    def reversed_lanes(planes):
        stacked = jnp.concatenate(planes, axis=0)
        turned_round = jnp.dot(stacked, reversal, preferred_element_type=jnp.float32)
        return [row_tap(turned_round, at) for at in range(len(planes))]

    def choose(shift, which, turned_round, plain):
        flips = strips[shift].astype(jnp.float32)[CHANNELS + which : CHANNELS + which + 1]
        return jnp.where(flips > 0.5, turned_round, plain.astype(jnp.float32)).astype(jnp.bfloat16)

    west_of = {shift: (shift - R, 3) for shift in {-1, 0, 1, R - 1, R, R + 1}}
    east_of = {shift: (shift + R, 0) for shift in {-1, 0, 1, -R - 1, -R, -R + 1}}
    keys = sorted(set(west_of.values()) | set(east_of.values()))
    flipped = dict(zip(keys, reversed_lanes([padded_column(*key) for key in keys])))
    west = {
        shift: choose(shift, 0, flipped[west_of[shift]], padded_column(*west_of[shift]))
        for shift in sorted(west_of)
    }
    east = {
        shift: choose(shift, 1, flipped[east_of[shift]], padded_column(*east_of[shift]))
        for shift in sorted(east_of)
    }

    def columns(value, west_plane, west_row, east_plane, east_row):
        return shifted_columns(
            value,
            pltpu.roll(west_plane, (BLOCK - west_row) % BLOCK, 1),
            pltpu.roll(east_plane, BLOCK - 1 - east_row, 1),
        )

    def along(result):
        return (
            row_tap(result, 0)
            + pltpu.roll(row_tap(result, 1), BLOCK - 1, 1)
            + pltpu.roll(row_tap(result, 2), BLOCK - 2, 1)
        )

    first_taps = first_taps_ref[...]
    up = [jnp.where(tile > 0, above[at], blank) for at in range(2)]
    down = [jnp.where(tile < count - 1, below[at], blank) for at in range(2)]
    from_up, from_down = tap_sums(
        first_taps, shifted_columns(up[1], blank, blank), shifted_columns(down[0], blank, blank)
    )
    from_up, from_down = row_tap(from_up, 0), row_tap(from_down, 2)
    from_west, from_east = tap_sums(
        first_taps,
        jnp.concatenate([west[0], blank, blank], axis=0),
        jnp.concatenate([blank, blank, east[0]], axis=0),
    )
    from_west, from_east = along(from_west), along(from_east)
    first = ends_ref[0] + from_up
    first = first + jnp.where(lane == 0, from_west, 0.0)
    first = first + jnp.where(lane == BLOCK - 1, pltpu.roll(from_east, BLOCK - 1, 1), 0.0)
    final = ends_ref[1] + from_down
    final = final + jnp.where(lane == 0, pltpu.roll(from_west, BLOCK - ROWS + 1, 1), 0.0)
    final = final + jnp.where(lane == BLOCK - 1, pltpu.roll(from_east, BLOCK - ROWS, 1), 0.0)
    first, final = activated(first), activated(final)
    first_column = activated(sides_ref[0] + from_west)
    last_column = activated(sides_ref[1] + from_east)

    upper = jnp.zeros((WIDE, BLOCK), jnp.float32)
    lower = jnp.zeros((WIDE, BLOCK), jnp.float32)
    for at, (high, low) in enumerate(
        [(up[0], field[ROWS - 1]), (up[1], down[0]), (field[0], down[1])]
    ):
        from_row = ROWS - 1 + at
        one, two = tap_sums(
            first_taps,
            columns(high, west[-1], from_row, east[-1], from_row),
            columns(low, west[1], at, east[1], at),
        )
        upper += row_tap(one, at)
        lower += row_tap(two, at)
    top = jnp.where(tile > 0, activated(upper), blank)
    bottom = jnp.where(tile < count - 1, activated(lower), blank)

    west_hidden, east_hidden = {}, {}
    for at in (-1, 0, 1):
        q = at - R
        one = jnp.concatenate([padded_column(q, 2), padded_column(q, 3), east[q]], axis=0)
        q = at + R
        two = jnp.concatenate([west[q], padded_column(q, 0), padded_column(q, 1)], axis=0)
        one, two = tap_sums(first_taps, one, two)
        west_hidden[at], east_hidden[at] = activated(along(one)), activated(along(two))

    def hidden_side(shift, values):
        return ends(
            shift,
            pltpu.roll(values[-1], BLOCK - ROWS + 1, 1),
            pltpu.roll(values[1], last, 1),
            pltpu.roll(values[0], 1, 1),
        )

    plain = [hidden_side(-R, west_hidden), hidden_side(R, east_hidden)]
    west_side, east_side = [
        choose(0, which, turned_side, plain[which])
        for which, turned_side in enumerate(reversed_lanes(plain))
    ]

    second_taps = second_taps_ref[...]
    from_top, from_first = tap_sums(
        second_taps,
        columns(top, west_side, 0, east_side, 0),
        columns(first, west_side, 1, east_side, 1),
    )
    from_final, from_bottom = tap_sums(
        second_taps,
        columns(final, west_side, ROWS, east_side, ROWS),
        columns(bottom, west_side, last, east_side, last),
    )
    rim_rows = {
        0: row_tap(from_top, 0) + row_tap(from_first, 1),
        1: row_tap(from_first, 0),
        ROWS - 2: row_tap(from_final, 2),
        ROWS - 1: row_tap(from_final, 1) + row_tap(from_bottom, 2),
    }

    other = (lane >= 2) & (lane < ROWS)

    def other_rows(plane):
        return jnp.where(other, plane, blank)

    near_west, near_east = other_rows(west_side), other_rows(east_side)
    first_column = other_rows(pltpu.roll(first_column, 1, 1))
    last_column = other_rows(pltpu.roll(last_column, 1, 1))
    to_0, to_1 = tap_sums(
        second_taps,
        jnp.concatenate([near_west, first_column, blank], axis=0),
        jnp.concatenate([first_column, blank, blank], axis=0),
    )
    to_127, to_126 = tap_sums(
        second_taps,
        jnp.concatenate([blank, last_column, near_east], axis=0),
        jnp.concatenate([blank, blank, last_column], axis=0),
    )
    spread = jnp.zeros((WIDE, BLOCK), jnp.float32)
    for at, sums in enumerate((to_126, to_127, to_0, to_1)):
        sums = along(sums)
        high = sums.astype(jnp.bfloat16)
        sums = sums - high.astype(jnp.float32)
        middle = sums.astype(jnp.bfloat16)
        low = (sums - middle.astype(jnp.float32)).astype(jnp.bfloat16)
        to_lane = (lanes((BLOCK, BLOCK)) == 4 * row_id + at).astype(jnp.bfloat16)
        parts = jnp.dot(
            jnp.concatenate([high, middle, low], axis=0),
            to_lane,
            preferred_element_type=jnp.float32,
        )
        spread = spread + (row_tap(parts, 0) + (row_tap(parts, 1) + row_tap(parts, 2)))

    rim_lanes = lanes((PADDED, BLOCK))
    rim_lanes = (rim_lanes < 2) | (rim_lanes >= BLOCK - 2)
    spread = spread[:PADDED]
    for row in range(ROWS):
        value = base[row] + jnp.where(
            rim_lanes, pltpu.roll(spread, (BLOCK - 4 * row - 2) % BLOCK, 1), 0.0
        )
        if row in rim_rows:
            value = value + rim_rows[row][:PADDED]
        turned[pl.ds(row, PADDED, stride=ROWS), :] = value
    smoothed[...] = turned[pl.ds(0, CHANNELS * ROWS), :].astype(jnp.bfloat16)


def convolutions(column_rows, *operands):
    return pl.pallas_call(
        functools.partial(conv_kernel, column_rows),
        in_specs=[vmem()] * len(operands),
        out_specs=vmem(),
        out_shape=jax.ShapeDtypeStruct((CHANNELS * ROWS, BLOCK), jnp.bfloat16),
        scratch_shapes=[
            pltpu.VMEM((PADDED * ROWS, BLOCK), jnp.float32),
        ],
        compiler_params=pltpu.CompilerParams(vmem_limit_bytes=VMEM_LIMIT),
        name="convolutions",
    )(*operands)


def tap_matrix(kernel):
    pad = WIDE - CHANNELS
    taps = jnp.pad(kernel, ((0, 0), (0, pad), (0, pad))).reshape(3, 3, WIDE, WIDE)
    return taps.transpose(0, 2, 1, 3).reshape(3 * WIDE, 3 * WIDE)


def from_shift(value, shift):
    count = lax.axis_size("tile")
    return lax.ppermute(value, "tile", [(i, (i - shift) % count) for i in range(count)])


def per_device(
    source, weights, block_source, block_target, edge_flip, norm_gain, first_kernel, second_kernel
):
    count = lax.axis_size("tile")
    column_rows = count // TILE_COLS
    field = source.reshape(ROWS, CHANNELS, BLOCK).transpose(1, 0, 2).reshape(-1, BLOCK)
    same, *nexts = regrid(block_target, block_source, field, weights, column_rows)

    for across in range(TILE_COLS):
        pairs = [
            (c * column_rows + p, (c ^ across) * column_rows + p + 1)
            for c in range(TILE_COLS)
            for p in range(column_rows - 1)
        ]
        nexts[across] = lax.ppermute(nexts[across], "tile", pairs)
    nexts = [nexts[across] for across in (0, 1, 2, 4, 5, 6, 7, 3)]
    same = lax.all_to_all(
        same,
        "tile",
        0,
        0,
        axis_index_groups=[
            [c * column_rows + p for c in range(TILE_COLS)] for p in range(column_rows)
        ],
        tiled=True,
    )

    gain = jnp.broadcast_to(
        jnp.pad(norm_gain, (0, PADDED - CHANNELS))[:, None], (PADDED, BLOCK)
    )
    first_taps, second_taps = tap_matrix(first_kernel), tap_matrix(second_kernel)
    same, nexts, gain, first_taps, second_taps = lax.optimization_barrier(
        (same, nexts, gain, first_taps, second_taps)
    )
    gridded, normed, upward, downward, strip = gather_rows(
        column_rows, edge_flip, gain, same, nexts
    )
    rims = [from_shift(downward, -1), from_shift(upward, 1)]
    near, far, reach = strip_plan(column_rows)
    strips = [from_shift(strip, shift) for shift in near]
    inner = inner_convolution(first_taps, normed)
    held = {-1: rims[0][2], 0: strip, 1: rims[1][2], **dict(zip(near, strips))}
    pack = jnp.stack([held[at] for at in range(-reach, reach + 1)])
    pack, inner = lax.optimization_barrier((pack, inner))
    strips += [from_shift(pack, -far), from_shift(pack, far)]
    gridded_out = channels_first(gridded)
    hidden, *unfinished = inner
    base = inner_second_convolution(second_taps, hidden, gridded)
    smoothed = convolutions(
        column_rows, first_taps, second_taps, normed, base, *unfinished, *rims, strip, *strips
    )

    def placed(value):
        return value.reshape(CHANNELS, ROWS, BLOCK).transpose(1, 0, 2)[:, None]

    return placed(gridded_out), placed(smoothed)


def solution(mesh):
    in_specs = (
        P("tile", "groups", None, None),
        P("tile", None, None),
        P("tile"),
        P("tile"),
        P("tile", None),
        P(),
        P(),
        P(),
    )
    out_specs = (P("tile", "groups", None, None), P("tile", "groups", None, None))
    return jax.shard_map(
        per_device, mesh=mesh, in_specs=in_specs, out_specs=out_specs, check_vma=False
    )
```

```python
import functools

import jax
import jax.numpy as jnp
from jax import lax
from jax.experimental import pallas as pl
from jax.experimental.pallas import tpu as pltpu
from jax.sharding import PartitionSpec as P

BLOCK = 128
CHANNELS = 69
PADDED = 72
WIDE = 80
ROWS = 32
ROW_BITS = 5
TILE_COLS = 8
CAP = 8
HALF = TILE_COLS // 2
GROUPS = 2 * TILE_COLS
COLUMN_ORDER = [half * HALF + at for at in range(HALF) for half in range(2)]
SLOTS = GROUPS * CAP
CHUNK = 96
MARK = CHANNELS
EPSILON = 1e-05
VMEM_LIMIT = 40 * 1024 * 1024
REGRID_VMEM = 60 * 1024 * 1024


def vmem():
    return pl.BlockSpec(memory_space=pltpu.VMEM)


def smem():
    return pl.BlockSpec(memory_space=pltpu.SMEM)


def split(value, size):
    if size & (size - 1) == 0:
        return value >> (size.bit_length() - 1), value & (size - 1)
    return lax.div(value, size), lax.rem(value, size)


def lanes(shape):
    return lax.broadcasted_iota(jnp.int32, shape, len(shape) - 1)


def regrid_kernel(
    column_rows, target_hbm, target_row_hbm, index_hbm, source_hbm, weight_hbm, *rest
):
    same_out, next_outs = rest[0], rest[1 : 1 + TILE_COLS]
    (
        target_ref,
        target_row_ref,
        index_ref,
        source,
        weight,
        wide,
        field,
        sums,
        rounded,
        plan,
        plan_scalars,
        plan_sem,
        in_sems,
        weight_sems,
        out_sems,
    ) = rest[1 + TILE_COLS :]
    entries = weight.shape[0]
    chunks = entries // CHUNK
    tile = lax.axis_index("tile")
    column, position = split(tile, column_rows)

    small_copies = [
        pltpu.make_async_copy(target_row_hbm, target_row_ref, in_sems.at[0]),
        pltpu.make_async_copy(target_hbm, target_ref, in_sems.at[1]),
        pltpu.make_async_copy(index_hbm, index_ref, in_sems.at[2]),
    ]
    source_copy = pltpu.make_async_copy(source_hbm, source, in_sems.at[3])
    for copy in small_copies:
        copy.start()
    source_copy.start()

    def chunk_copy(chunk):
        part = pl.ds(chunk * CHUNK, CHUNK)
        return pltpu.make_async_copy(weight_hbm.at[part], weight.at[part], weight_sems.at[chunk])

    for chunk in range(chunks):
        chunk_copy(chunk).start()

    small_copies[0].wait()
    target = target_row_ref[...]
    owner, row = split(target, ROWS)
    owner_column, owner_position = split(owner, column_rows)
    place = ((owner_column & (HALF - 1)) << 1) + (owner_column >= HALF).astype(jnp.int32)
    group = jnp.where(owner_position == position, place, TILE_COLS + (owner_column ^ column))
    key = group * ROWS + row
    square = (entries, entries)
    down = lax.broadcasted_iota(jnp.int32, square, 0)
    along = lanes(square)
    key_along = jnp.broadcast_to(key.astype(jnp.float32), square)
    key_down = jnp.broadcast_to(
        jnp.sum(jnp.where(down == along, key_along, 0.0), axis=1, keepdims=True), square
    )
    equal = key_along == key_down
    doubles = jnp.sum(jnp.where(equal & (along < down), 1.0, 0.0), axis=1, keepdims=True)
    in_group = (key_down.astype(jnp.int32) >> ROW_BITS) == (key_along.astype(jnp.int32) >> ROW_BITS)
    below = in_group & (key_down < key_along) & (jnp.broadcast_to(doubles, square) == 0.0)
    rank = jnp.sum(jnp.where(below, 1.0, 0.0), axis=0, keepdims=True)
    mentions = jnp.sum(jnp.where(equal & (down < along), 1.0, 0.0), axis=0, keepdims=True)
    slots = group * CAP + rank.astype(jnp.int32)
    plan[...] = slots + jnp.where(mentions == 0.0, SLOTS, 0)
    plan_copy = pltpu.make_async_copy(plan, plan_scalars, plan_sem)
    plan_copy.start()

    tail = PADDED - 8
    for slot in range(SLOTS):
        rounded[slot, tail:] = jnp.full((8, BLOCK), ROWS, jnp.bfloat16)
    wide[pl.ds(CHANNELS * ROWS, (PADDED - CHANNELS) * ROWS), :] = jnp.zeros(
        ((PADDED - CHANNELS) * ROWS, BLOCK), jnp.float32
    )
    nothing = jnp.zeros((WIDE - PADDED, BLOCK), jnp.float32)
    source_copy.wait()
    wide[pl.ds(0, CHANNELS * ROWS), :] = source[...].astype(jnp.float32)
    for row in range(ROWS):
        block = wide[pl.ds(row, PADDED, stride=ROWS), :]
        field[row] = jnp.concatenate([block, nothing], axis=0).astype(jnp.bfloat16)
    is_mark = lax.broadcasted_iota(jnp.int32, (8, BLOCK), 0) == MARK - tail
    blank = jnp.zeros((WIDE, BLOCK), jnp.bfloat16)
    small_copies[1].wait()
    small_copies[2].wait()
    plan_copy.wait()

    for chunk in range(chunks):
        chunk_copy(chunk).wait()
        for entry in range(chunk * CHUNK, (chunk + 1) * CHUNK, 2):
            one = jnp.concatenate([field[index_ref[entry]], blank], axis=1)
            two = jnp.concatenate([blank, field[index_ref[entry + 1]]], axis=1)
            products = jnp.dot(
                jnp.concatenate([one, two], axis=0),
                weight[entry : entry + 2].reshape(2 * BLOCK, BLOCK),
                preferred_element_type=jnp.float32,
            )
            for at in range(2):
                code = plan_scalars[0, entry + at]
                slot = code & (SLOTS - 1)
                row = split(target_ref[entry + at], ROWS)[1]
                product = products[at * WIDE : at * WIDE + PADDED]
                total = jnp.where(code >= SLOTS, 0.0, sums[slot]) + product
                sums[slot] = total
                marked = jnp.where(is_mark, row.astype(jnp.float32), total[tail:])
                rounded[slot] = jnp.concatenate([total[:tail], marked], axis=0).astype(jnp.bfloat16)
    copies = []
    for group in range(GROUPS):
        part = rounded.at[pl.ds(group * CAP, CAP)]
        if group < TILE_COLS:
            out = same_out.at[pl.ds(group * CAP, CAP)]
        else:
            out = next_outs[group - TILE_COLS]
        copies.append(pltpu.make_async_copy(part, out, out_sems.at[group]))
    for copy in copies:
        copy.start()
    for copy in copies:
        copy.wait()


def regrid(target, source_index, field, weights, column_rows):
    piece = jax.ShapeDtypeStruct((CAP, PADDED, BLOCK), jnp.bfloat16)
    same = jax.ShapeDtypeStruct((TILE_COLS * CAP, PADDED, BLOCK), jnp.bfloat16)
    hbm = pl.BlockSpec(memory_space=pl.ANY)
    entries = weights.shape[0]
    return pl.pallas_call(
        functools.partial(regrid_kernel, column_rows),
        in_specs=[hbm] * 5,
        out_specs=[hbm] * (1 + TILE_COLS),
        out_shape=[same] + [piece] * TILE_COLS,
        scratch_shapes=[
            pltpu.SMEM(target.shape, jnp.int32),
            pltpu.VMEM((1, entries), jnp.int32),
            pltpu.SMEM(source_index.shape, jnp.int32),
            pltpu.VMEM(field.shape, jnp.bfloat16),
            pltpu.VMEM(weights.shape, jnp.bfloat16),
            pltpu.VMEM((PADDED * ROWS, BLOCK), jnp.float32),
            pltpu.VMEM((ROWS, WIDE, BLOCK), jnp.bfloat16),
            pltpu.VMEM((SLOTS, PADDED, BLOCK), jnp.float32),
            pltpu.VMEM((SLOTS, PADDED, BLOCK), jnp.bfloat16),
            pltpu.VMEM((1, entries), jnp.int32),
            pltpu.SMEM((1, entries), jnp.int32),
            pltpu.SemaphoreType.DMA,
            pltpu.SemaphoreType.DMA((4,)),
            pltpu.SemaphoreType.DMA((entries // CHUNK,)),
            pltpu.SemaphoreType.DMA((GROUPS,)),
        ],
        compiler_params=pltpu.CompilerParams(vmem_limit_bytes=REGRID_VMEM),
        name="regrid",
    )(target, target.reshape(1, -1), source_index, field, weights)


def gather_kernel(column_rows, flip_ref, gain_ref, same, *rest):
    nexts = rest[:TILE_COLS]
    (
        gridded,
        normed,
        upward,
        downward,
        strip_out,
        summed,
    ) = rest[TILE_COLS:]
    position = lax.rem(lax.axis_index("tile"), column_rows)
    summed[...] = jnp.zeros_like(summed)

    def add(piece):
        row = piece[MARK : MARK + 1].astype(jnp.float32).astype(jnp.int32)[0, 0]
        summed[row] = summed[row] + piece[...].astype(jnp.float32)

    for slot in range(SLOTS // 2):
        add(same.at[slot])

    @pl.when(position > 0)
    def _():
        for group in range(TILE_COLS):
            for place in range(CAP):
                add(nexts[group].at[place])

    gain = gain_ref[...]
    channel = lax.broadcasted_iota(jnp.int32, (PADDED, BLOCK), 0)
    nothing = jnp.zeros((WIDE - PADDED, BLOCK), jnp.float32)
    lane = lanes((WIDE, BLOCK))
    strip = jnp.zeros((WIDE, BLOCK), jnp.bfloat16)
    for row in range(ROWS):
        rounded = summed[row].astype(jnp.bfloat16)
        gridded[row] = rounded
        value = rounded.astype(jnp.float32)
        value = jnp.where(channel < CHANNELS, value, 0.0)
        square = jnp.sum(value * value, axis=0, keepdims=True) * (1.0 / CHANNELS)
        scaled = value * lax.rsqrt(square + EPSILON) * gain
        scaled = jnp.concatenate([scaled, nothing], axis=0).astype(jnp.bfloat16)
        normed[row] = scaled
        if row < 2:
            upward[row] = scaled
        if row >= ROWS - 2:
            downward[row - ROWS + 2] = scaled
        strip = jnp.where((lane >> 2) == row, pltpu.roll(scaled, 4 * row + 2, 1), strip)
    to_lane = lanes((BLOCK, BLOCK))
    from_lane = 4 * (to_lane & (ROWS - 1)) + (((to_lane >> ROW_BITS) + 2) & 3)
    order = lax.broadcasted_iota(jnp.int32, (BLOCK, BLOCK), 0) == from_lane
    strip = jnp.dot(strip, order.astype(jnp.bfloat16), preferred_element_type=jnp.float32)
    channel = lax.broadcasted_iota(jnp.int32, (WIDE, BLOCK), 0)
    for side in range(2):
        strip = jnp.where(channel == CHANNELS + side, flip_ref[0, side].astype(jnp.float32), strip)
    strip = strip.astype(jnp.bfloat16)
    upward[2] = strip
    downward[2] = strip
    strip_out[...] = strip


GRIDDED = jax.ShapeDtypeStruct((ROWS, PADDED, BLOCK), jnp.bfloat16)
FIELD = jax.ShapeDtypeStruct((ROWS, WIDE, BLOCK), jnp.bfloat16)
RIM = jax.ShapeDtypeStruct((3, WIDE, BLOCK), jnp.bfloat16)
STRIP_COLUMNS = (0, 1, BLOCK - 2, BLOCK - 1)
STRIP = jax.ShapeDtypeStruct((WIDE, BLOCK), jnp.bfloat16)


def gather_rows(column_rows, edge_flip, gain, same, nexts):
    return pl.pallas_call(
        functools.partial(gather_kernel, column_rows),
        in_specs=[smem()] + [vmem()] * (2 + TILE_COLS),
        out_specs=[vmem()] * 5,
        out_shape=[GRIDDED, FIELD, RIM, RIM, STRIP],
        scratch_shapes=[
            pltpu.VMEM((ROWS + 1, PADDED, BLOCK), jnp.float32),
        ],
        compiler_params=pltpu.CompilerParams(vmem_limit_bytes=VMEM_LIMIT),
        name="gather_rows",
    )(edge_flip, gain, same, *nexts)


def turn_kernel(field, out, turned):
    for row in range(ROWS):
        turned[pl.ds(row, PADDED, stride=ROWS), :] = field[row].astype(jnp.float32)
    out[...] = turned[pl.ds(0, CHANNELS * ROWS), :].astype(jnp.bfloat16)


def channels_first(field):
    return pl.pallas_call(
        turn_kernel,
        in_specs=[vmem()],
        out_specs=vmem(),
        out_shape=jax.ShapeDtypeStruct((CHANNELS * ROWS, BLOCK), jnp.bfloat16),
        scratch_shapes=[pltpu.VMEM((PADDED * ROWS, BLOCK), jnp.float32)],
        compiler_params=pltpu.CompilerParams(vmem_limit_bytes=VMEM_LIMIT),
        name="channels_first",
    )(field)


def shifted_columns(value, left_end, right_end):
    lane = lanes((WIDE, BLOCK))
    left = jnp.where(lane == 0, left_end, pltpu.roll(value, 1, 1))
    right = jnp.where(lane == BLOCK - 1, right_end, pltpu.roll(value, BLOCK - 1, 1))
    return jnp.concatenate([left, value, right], axis=0)


def tap_sums(taps, one, two):
    both = jnp.concatenate([one, two], axis=1)
    result = jnp.dot(taps, both, preferred_element_type=jnp.float32)
    return result[:, :BLOCK], result[:, BLOCK:]


def row_tap(sums, at):
    return sums[at * WIDE : (at + 1) * WIDE]


def activated(value):
    return jax.nn.gelu(value).astype(jnp.bfloat16)


def inner_kernel(taps_ref, field, hidden, ends, sides, partial):
    taps = taps_ref[...]
    blank = jnp.zeros((WIDE, BLOCK), jnp.bfloat16)
    for row in range(0, ROWS, 2):
        partial[row], partial[row + 1] = tap_sums(
            taps,
            shifted_columns(field[row], blank, blank),
            shifted_columns(field[row + 1], blank, blank),
        )
    lane = lanes((WIDE, BLOCK))
    west = jnp.zeros((WIDE, BLOCK), jnp.float32)
    east = jnp.zeros((WIDE, BLOCK), jnp.float32)
    for row in range(ROWS):
        value = partial[row, WIDE : 2 * WIDE]
        if row > 0:
            value = value + partial[row - 1, :WIDE]
        if row < ROWS - 1:
            value = value + partial[row + 1, 2 * WIDE :]
        if row == 0:
            ends[0] = value
        elif row == ROWS - 1:
            ends[1] = value
        else:
            hidden[row] = jnp.where((lane == 0) | (lane == BLOCK - 1), blank, activated(value))
        west = jnp.where(lane == row, pltpu.roll(value, row, 1), west)
        east = jnp.where(lane == row, pltpu.roll(value, row + 1, 1), east)
    hidden[0] = blank
    hidden[ROWS - 1] = blank
    sides[0] = west
    sides[1] = east


def inner_convolution(taps, field):
    pair = jax.ShapeDtypeStruct((2, WIDE, BLOCK), jnp.float32)
    return pl.pallas_call(
        inner_kernel,
        in_specs=[vmem()] * 2,
        out_specs=[vmem()] * 3,
        out_shape=[FIELD, pair, pair],
        scratch_shapes=[pltpu.VMEM((ROWS, 3 * WIDE, BLOCK), jnp.float32)],
        compiler_params=pltpu.CompilerParams(vmem_limit_bytes=VMEM_LIMIT),
        cost_estimate=pl.CostEstimate(
            flops=2 * 9 * WIDE * WIDE * ROWS * BLOCK, bytes_accessed=2 << 20, transcendentals=0
        ),
        name="inner_convolution",
    )(taps, field)


def second_kernel_inner(taps_ref, hidden, gridded, base, partial):
    taps = taps_ref[...]
    blank = jnp.zeros((WIDE, BLOCK), jnp.bfloat16)
    for row in range(0, ROWS, 2):
        partial[row], partial[row + 1] = tap_sums(
            taps,
            shifted_columns(hidden[row], blank, blank),
            shifted_columns(hidden[row + 1], blank, blank),
        )
    for row in range(ROWS):
        value = gridded[row].astype(jnp.float32) + partial[row, WIDE : WIDE + PADDED]
        if row > 0:
            value = value + partial[row - 1, :PADDED]
        if row < ROWS - 1:
            value = value + partial[row + 1, 2 * WIDE : 2 * WIDE + PADDED]
        base[row] = value


def inner_second_convolution(taps, hidden, gridded):
    return pl.pallas_call(
        second_kernel_inner,
        in_specs=[vmem()] * 3,
        out_specs=vmem(),
        out_shape=jax.ShapeDtypeStruct((ROWS, PADDED, BLOCK), jnp.float32),
        scratch_shapes=[pltpu.VMEM((ROWS, 3 * WIDE, BLOCK), jnp.float32)],
        compiler_params=pltpu.CompilerParams(vmem_limit_bytes=VMEM_LIMIT),
        cost_estimate=pl.CostEstimate(
            flops=2 * 9 * WIDE * WIDE * ROWS * BLOCK, bytes_accessed=2 << 20, transcendentals=0
        ),
        name="inner_second_convolution",
    )(taps, hidden, gridded)


def strip_plan(column_rows):
    if column_rows == 2:
        return [], 3, 1
    return [-2, 2], column_rows, 2


def conv_kernel(
    column_rows,
    first_taps_ref,
    second_taps_ref,
    field,
    base,
    ends_ref,
    sides_ref,
    above,
    below,
    own_strip,
    *rest,
):
    near, far, reach = strip_plan(column_rows)
    near_strips, (west_pack, east_pack) = rest[: len(near)], rest[len(near) : len(near) + 2]
    smoothed, turned = rest[len(near) + 2 :]
    count = lax.axis_size("tile")
    tile = lax.axis_index("tile")
    lane = lanes((WIDE, BLOCK))
    last = ROWS + 1
    R = column_rows
    blank = jnp.zeros((WIDE, BLOCK), jnp.bfloat16)

    strips = {-1: above[2], 0: own_strip[...], 1: below[2]}
    strips.update((shift, ref[...]) for shift, ref in zip(near, near_strips))
    for at in range(-reach, reach + 1):
        strips[at - far], strips[at + far] = west_pack[at + reach], east_pack[at + reach]

    def place(shift):
        return lax.rem(tile + shift + count, count)

    def ends(shift, before, after, middle):
        before = jnp.where(place(shift) > 0, before, blank)
        after = jnp.where(place(shift) < count - 1, after, blank)
        return jnp.where(lane == 0, before, jnp.where(lane == last, after, middle))

    memo = {}

    def padded_column(shift, which):
        if (shift, which) not in memo:
            base = which * ROWS
            memo[shift, which] = ends(
                shift,
                pltpu.roll(strips[shift - 1], (1 - base - ROWS) % BLOCK, 1),
                pltpu.roll(strips[shift + 1], (last - base) % BLOCK, 1),
                pltpu.roll(strips[shift], (1 - base) % BLOCK, 1),
            )
        return memo[shift, which]

    row_id = lax.broadcasted_iota(jnp.int32, (BLOCK, BLOCK), 0)
    reversal = (row_id + lanes((BLOCK, BLOCK)) == last).astype(jnp.bfloat16)

    def reversed_lanes(planes):
        stacked = jnp.concatenate(planes, axis=0)
        turned_round = jnp.dot(stacked, reversal, preferred_element_type=jnp.float32)
        return [row_tap(turned_round, at) for at in range(len(planes))]

    def choose(shift, which, turned_round, plain):
        flips = strips[shift].astype(jnp.float32)[CHANNELS + which : CHANNELS + which + 1]
        return jnp.where(flips > 0.5, turned_round, plain.astype(jnp.float32)).astype(jnp.bfloat16)

    west_of = {shift: (shift - R, 3) for shift in {-1, 0, 1, R - 1, R, R + 1}}
    east_of = {shift: (shift + R, 0) for shift in {-1, 0, 1, -R - 1, -R, -R + 1}}
    keys = sorted(set(west_of.values()) | set(east_of.values()))
    flipped = dict(zip(keys, reversed_lanes([padded_column(*key) for key in keys])))
    west = {
        shift: choose(shift, 0, flipped[west_of[shift]], padded_column(*west_of[shift]))
        for shift in sorted(west_of)
    }
    east = {
        shift: choose(shift, 1, flipped[east_of[shift]], padded_column(*east_of[shift]))
        for shift in sorted(east_of)
    }

    def columns(value, west_plane, west_row, east_plane, east_row):
        return shifted_columns(
            value,
            pltpu.roll(west_plane, (BLOCK - west_row) % BLOCK, 1),
            pltpu.roll(east_plane, BLOCK - 1 - east_row, 1),
        )

    def along(result):
        return (
            row_tap(result, 0)
            + pltpu.roll(row_tap(result, 1), BLOCK - 1, 1)
            + pltpu.roll(row_tap(result, 2), BLOCK - 2, 1)
        )

    first_taps = first_taps_ref[...]
    up = [jnp.where(tile > 0, above[at], blank) for at in range(2)]
    down = [jnp.where(tile < count - 1, below[at], blank) for at in range(2)]
    from_up, from_down = tap_sums(
        first_taps, shifted_columns(up[1], blank, blank), shifted_columns(down[0], blank, blank)
    )
    from_up, from_down = row_tap(from_up, 0), row_tap(from_down, 2)
    from_west, from_east = tap_sums(
        first_taps,
        jnp.concatenate([west[0], blank, blank], axis=0),
        jnp.concatenate([blank, blank, east[0]], axis=0),
    )
    from_west, from_east = along(from_west), along(from_east)
    first = ends_ref[0] + from_up
    first = first + jnp.where(lane == 0, from_west, 0.0)
    first = first + jnp.where(lane == BLOCK - 1, pltpu.roll(from_east, BLOCK - 1, 1), 0.0)
    final = ends_ref[1] + from_down
    final = final + jnp.where(lane == 0, pltpu.roll(from_west, BLOCK - ROWS + 1, 1), 0.0)
    final = final + jnp.where(lane == BLOCK - 1, pltpu.roll(from_east, BLOCK - ROWS, 1), 0.0)
    first, final = activated(first), activated(final)
    first_column = activated(sides_ref[0] + from_west)
    last_column = activated(sides_ref[1] + from_east)

    upper = jnp.zeros((WIDE, BLOCK), jnp.float32)
    lower = jnp.zeros((WIDE, BLOCK), jnp.float32)
    for at, (high, low) in enumerate(
        [(up[0], field[ROWS - 1]), (up[1], down[0]), (field[0], down[1])]
    ):
        from_row = ROWS - 1 + at
        one, two = tap_sums(
            row_tap(first_taps, at),
            columns(high, west[-1], from_row, east[-1], from_row),
            columns(low, west[1], at, east[1], at),
        )
        upper += one
        lower += two
    top = jnp.where(tile > 0, activated(upper), blank)
    bottom = jnp.where(tile < count - 1, activated(lower), blank)

    west_hidden, east_hidden = {}, {}
    for at in (-1, 0, 1):
        q = at - R
        one = jnp.concatenate([padded_column(q, 2), padded_column(q, 3), east[q]], axis=0)
        q = at + R
        two = jnp.concatenate([west[q], padded_column(q, 0), padded_column(q, 1)], axis=0)
        one, two = tap_sums(first_taps, one, two)
        west_hidden[at], east_hidden[at] = activated(along(one)), activated(along(two))

    def hidden_side(shift, values):
        return ends(
            shift,
            pltpu.roll(values[-1], BLOCK - ROWS + 1, 1),
            pltpu.roll(values[1], last, 1),
            pltpu.roll(values[0], 1, 1),
        )

    plain = [hidden_side(-R, west_hidden), hidden_side(R, east_hidden)]
    west_side, east_side = [
        choose(0, which, turned_side, plain[which])
        for which, turned_side in enumerate(reversed_lanes(plain))
    ]

    second_taps = second_taps_ref[...]
    from_top, from_first = tap_sums(
        second_taps,
        columns(top, west_side, 0, east_side, 0),
        columns(first, west_side, 1, east_side, 1),
    )
    from_final, from_bottom = tap_sums(
        second_taps,
        columns(final, west_side, ROWS, east_side, ROWS),
        columns(bottom, west_side, last, east_side, last),
    )
    rim_rows = {
        0: row_tap(from_top, 0) + row_tap(from_first, 1),
        1: row_tap(from_first, 0),
        ROWS - 2: row_tap(from_final, 2),
        ROWS - 1: row_tap(from_final, 1) + row_tap(from_bottom, 2),
    }

    other = (lane >= 2) & (lane < ROWS)

    def other_rows(plane):
        return jnp.where(other, plane, blank)

    near_west, near_east = other_rows(west_side), other_rows(east_side)
    first_column = other_rows(pltpu.roll(first_column, 1, 1))
    last_column = other_rows(pltpu.roll(last_column, 1, 1))
    to_0, to_1 = tap_sums(
        second_taps,
        jnp.concatenate([near_west, first_column, blank], axis=0),
        jnp.concatenate([first_column, blank, blank], axis=0),
    )
    to_127, to_126 = tap_sums(
        second_taps,
        jnp.concatenate([blank, last_column, near_east], axis=0),
        jnp.concatenate([blank, blank, last_column], axis=0),
    )
    spread = jnp.zeros((WIDE, BLOCK), jnp.float32)
    for at, sums in enumerate((to_126, to_127, to_0, to_1)):
        sums = along(sums)
        high = sums.astype(jnp.bfloat16)
        sums = sums - high.astype(jnp.float32)
        middle = sums.astype(jnp.bfloat16)
        low = (sums - middle.astype(jnp.float32)).astype(jnp.bfloat16)
        to_lane = (lanes((BLOCK, BLOCK)) == 4 * row_id + at).astype(jnp.bfloat16)
        parts = jnp.dot(
            jnp.concatenate([high, middle, low], axis=0),
            to_lane,
            preferred_element_type=jnp.float32,
        )
        spread = spread + (row_tap(parts, 0) + (row_tap(parts, 1) + row_tap(parts, 2)))

    rim_lanes = lanes((PADDED, BLOCK))
    rim_lanes = (rim_lanes < 2) | (rim_lanes >= BLOCK - 2)
    spread = spread[:PADDED]
    for row in range(ROWS):
        value = base[row] + jnp.where(
            rim_lanes, pltpu.roll(spread, (BLOCK - 4 * row - 2) % BLOCK, 1), 0.0
        )
        if row in rim_rows:
            value = value + rim_rows[row][:PADDED]
        turned[pl.ds(row, PADDED, stride=ROWS), :] = value
    smoothed[...] = turned[pl.ds(0, CHANNELS * ROWS), :].astype(jnp.bfloat16)


def convolutions(column_rows, *operands):
    return pl.pallas_call(
        functools.partial(conv_kernel, column_rows),
        in_specs=[vmem()] * len(operands),
        out_specs=vmem(),
        out_shape=jax.ShapeDtypeStruct((CHANNELS * ROWS, BLOCK), jnp.bfloat16),
        scratch_shapes=[
            pltpu.VMEM((PADDED * ROWS, BLOCK), jnp.float32),
        ],
        compiler_params=pltpu.CompilerParams(vmem_limit_bytes=VMEM_LIMIT),
        name="convolutions",
    )(*operands)


def tap_matrix(kernel):
    pad = WIDE - CHANNELS
    taps = jnp.pad(kernel, ((0, 0), (0, pad), (0, pad))).reshape(3, 3, WIDE, WIDE)
    return taps.transpose(0, 2, 1, 3).reshape(3 * WIDE, 3 * WIDE)


def from_shift(value, shift):
    count = lax.axis_size("tile")
    return lax.ppermute(value, "tile", [(i, (i - shift) % count) for i in range(count)])


def per_device(
    source, weights, block_source, block_target, edge_flip, norm_gain, first_kernel, second_kernel
):
    count = lax.axis_size("tile")
    column_rows = count // TILE_COLS
    field = source.reshape(ROWS, CHANNELS, BLOCK).transpose(1, 0, 2).reshape(-1, BLOCK)
    same, *nexts = regrid(block_target, block_source, field, weights, column_rows)

    for across in range(TILE_COLS):
        pairs = [
            (c * column_rows + p, (c ^ across) * column_rows + p + 1)
            for c in range(TILE_COLS)
            for p in range(column_rows - 1)
        ]
        nexts[across] = lax.ppermute(nexts[across], "tile", pairs)
    nexts = [nexts[across] for across in (0, 1, 2, 4, 5, 6, 7, 3)]
    same = lax.all_to_all(
        same,
        "tile",
        0,
        0,
        axis_index_groups=[
            [c * column_rows + p for c in COLUMN_ORDER] for p in range(column_rows)
        ],
        tiled=True,
    )

    gain = jnp.broadcast_to(
        jnp.pad(norm_gain, (0, PADDED - CHANNELS))[:, None], (PADDED, BLOCK)
    )
    first_taps, second_taps = tap_matrix(first_kernel), tap_matrix(second_kernel)
    same, nexts, gain, first_taps, second_taps = lax.optimization_barrier(
        (same, nexts, gain, first_taps, second_taps)
    )
    gridded, normed, upward, downward, strip = gather_rows(
        column_rows, edge_flip, gain, same, nexts
    )
    rims = [from_shift(downward, -1), from_shift(upward, 1)]
    near, far, reach = strip_plan(column_rows)
    strips = [from_shift(strip, shift) for shift in near]
    inner = inner_convolution(first_taps, normed)
    held = {-1: rims[0][2], 0: strip, 1: rims[1][2], **dict(zip(near, strips))}
    pack = jnp.stack([held[at] for at in range(-reach, reach + 1)])
    gridded_out = channels_first(gridded)
    pack, inner, gridded_out = lax.optimization_barrier((pack, inner, gridded_out))
    strips += [from_shift(pack, -far), from_shift(pack, far)]
    hidden, *unfinished = inner
    base = inner_second_convolution(second_taps, hidden, gridded)
    smoothed = convolutions(
        column_rows, first_taps, second_taps, normed, base, *unfinished, *rims, strip, *strips
    )

    def placed(value):
        return value.reshape(CHANNELS, ROWS, BLOCK).transpose(1, 0, 2)[:, None]

    return placed(gridded_out), placed(smoothed)


def solution(mesh):
    in_specs = (
        P("tile", "groups", None, None),
        P("tile", None, None),
        P("tile"),
        P("tile"),
        P("tile", None),
        P(),
        P(),
        P(),
    )
    out_specs = (P("tile", "groups", None, None), P("tile", "groups", None, None))
    return jax.shard_map(
        per_device, mesh=mesh, in_specs=in_specs, out_specs=out_specs, check_vma=False
    )
```

```python
import functools

import jax
import jax.numpy as jnp
from jax import lax
from jax.experimental import pallas as pl
from jax.experimental.pallas import tpu as pltpu
from jax.sharding import PartitionSpec as P

BLOCK = 128
CHANNELS = 69
PADDED = 72
WIDE = 80
ROWS = 32
ROW_BITS = 5
TILE_COLS = 8
CAP = 8
HALF = TILE_COLS // 2
GROUPS = 2 * TILE_COLS
COLUMN_ORDER = [half * HALF + at for at in range(HALF) for half in range(2)]
SLOTS = GROUPS * CAP
CHUNK = 96
MARK = CHANNELS
BODY = 64
TAILS = (MARK + 1 - BODY) * CAP
MESSAGE = CAP * BODY + TAILS
EPSILON = 1e-05
VMEM_LIMIT = 40 * 1024 * 1024
REGRID_VMEM = 60 * 1024 * 1024


def vmem():
    return pl.BlockSpec(memory_space=pltpu.VMEM)


def smem():
    return pl.BlockSpec(memory_space=pltpu.SMEM)


def split(value, size):
    if size & (size - 1) == 0:
        return value >> (size.bit_length() - 1), value & (size - 1)
    return lax.div(value, size), lax.rem(value, size)


def lanes(shape):
    return lax.broadcasted_iota(jnp.int32, shape, len(shape) - 1)


def regrid_kernel(
    column_rows, target_hbm, target_row_hbm, index_hbm, source_hbm, weight_hbm, *rest
):
    same_out, next_outs = rest[0], rest[1 : 1 + TILE_COLS]
    (
        target_ref,
        target_row_ref,
        index_ref,
        source,
        weight,
        wide,
        field,
        sums,
        message,
        tails,
        plan,
        plan_scalars,
        plan_sem,
        in_sems,
        weight_sems,
        out_sems,
    ) = rest[1 + TILE_COLS :]
    entries = weight.shape[0]
    chunks = entries // CHUNK
    tile = lax.axis_index("tile")
    column, position = split(tile, column_rows)

    small_copies = [
        pltpu.make_async_copy(target_row_hbm, target_row_ref, in_sems.at[0]),
        pltpu.make_async_copy(target_hbm, target_ref, in_sems.at[1]),
        pltpu.make_async_copy(index_hbm, index_ref, in_sems.at[2]),
    ]
    source_copy = pltpu.make_async_copy(source_hbm, source, in_sems.at[3])
    for copy in small_copies:
        copy.start()
    source_copy.start()

    def chunk_copy(chunk):
        part = pl.ds(chunk * CHUNK, CHUNK)
        return pltpu.make_async_copy(weight_hbm.at[part], weight.at[part], weight_sems.at[chunk])

    for chunk in range(chunks):
        chunk_copy(chunk).start()

    small_copies[0].wait()
    target = target_row_ref[...]
    owner, row = split(target, ROWS)
    owner_column, owner_position = split(owner, column_rows)
    place = ((owner_column & (HALF - 1)) << 1) + (owner_column >= HALF).astype(jnp.int32)
    group = jnp.where(owner_position == position, place, TILE_COLS + (owner_column ^ column))
    key = group * ROWS + row
    square = (entries, entries)
    down = lax.broadcasted_iota(jnp.int32, square, 0)
    along = lanes(square)
    key_along = jnp.broadcast_to(key.astype(jnp.float32), square)
    key_down = jnp.broadcast_to(
        jnp.sum(jnp.where(down == along, key_along, 0.0), axis=1, keepdims=True), square
    )
    equal = key_along == key_down
    doubles = jnp.sum(jnp.where(equal & (along < down), 1.0, 0.0), axis=1, keepdims=True)
    in_group = (key_down.astype(jnp.int32) >> ROW_BITS) == (key_along.astype(jnp.int32) >> ROW_BITS)
    below = in_group & (key_down < key_along) & (jnp.broadcast_to(doubles, square) == 0.0)
    rank = jnp.sum(jnp.where(below, 1.0, 0.0), axis=0, keepdims=True)
    mentions = jnp.sum(jnp.where(equal & (down < along), 1.0, 0.0), axis=0, keepdims=True)
    slots = group * CAP + rank.astype(jnp.int32)
    plan[...] = slots + jnp.where(mentions == 0.0, SLOTS, 0)
    plan_copy = pltpu.make_async_copy(plan, plan_scalars, plan_sem)
    plan_copy.start()

    for slot in range(SLOTS):
        tails[pl.ds(slot * 8, 8), :] = jnp.full((8, BLOCK), ROWS, jnp.float32)
    wide[pl.ds(CHANNELS * ROWS, (PADDED - CHANNELS) * ROWS), :] = jnp.zeros(
        ((PADDED - CHANNELS) * ROWS, BLOCK), jnp.float32
    )
    nothing = jnp.zeros((WIDE - PADDED, BLOCK), jnp.float32)
    source_copy.wait()
    wide[pl.ds(0, CHANNELS * ROWS), :] = source[...].astype(jnp.float32)
    for row in range(ROWS):
        block = wide[pl.ds(row, PADDED, stride=ROWS), :]
        field[row] = jnp.concatenate([block, nothing], axis=0).astype(jnp.bfloat16)
    is_mark = lax.broadcasted_iota(jnp.int32, (8, BLOCK), 0) == MARK - BODY
    blank = jnp.zeros((WIDE, BLOCK), jnp.bfloat16)
    small_copies[1].wait()
    small_copies[2].wait()
    plan_copy.wait()

    for chunk in range(chunks):
        chunk_copy(chunk).wait()
        for entry in range(chunk * CHUNK, (chunk + 1) * CHUNK, 2):
            one = jnp.concatenate([field[index_ref[entry]], blank], axis=1)
            two = jnp.concatenate([blank, field[index_ref[entry + 1]]], axis=1)
            products = jnp.dot(
                jnp.concatenate([one, two], axis=0),
                weight[entry : entry + 2].reshape(2 * BLOCK, BLOCK),
                preferred_element_type=jnp.float32,
            )
            for at in range(2):
                code = plan_scalars[0, entry + at]
                slot = code & (SLOTS - 1)
                row = split(target_ref[entry + at], ROWS)[1]
                product = products[at * WIDE : at * WIDE + PADDED]
                total = jnp.where(code >= SLOTS, 0.0, sums[slot]) + product
                sums[slot] = total
                group, place = split(slot, CAP)
                message[group, pl.ds(pl.multiple_of(place * BODY, BODY), BODY), :] = total[
                    :BODY
                ].astype(jnp.bfloat16)
                tails[pl.ds(pl.multiple_of(slot * 8, 8), 8), :] = jnp.where(
                    is_mark, row.astype(jnp.float32), total[BODY:]
                )
    copies = []
    for group in range(GROUPS):
        start = group * CAP * 8
        ends = [tails[pl.ds(start + at, CAP, stride=8), :] for at in range(MARK + 1 - BODY)]
        message[group, CAP * BODY :] = jnp.concatenate(ends, axis=0).astype(jnp.bfloat16)
        if group < TILE_COLS:
            out = same_out.at[pl.ds(group * MESSAGE, MESSAGE)]
        else:
            out = next_outs[group - TILE_COLS]
        copies.append(pltpu.make_async_copy(message.at[group], out, out_sems.at[group]))
        copies[-1].start()
    for copy in copies:
        copy.wait()


def regrid(target, source_index, field, weights, column_rows):
    piece = jax.ShapeDtypeStruct((MESSAGE, BLOCK), jnp.bfloat16)
    same = jax.ShapeDtypeStruct((TILE_COLS * MESSAGE, BLOCK), jnp.bfloat16)
    hbm = pl.BlockSpec(memory_space=pl.ANY)
    entries = weights.shape[0]
    return pl.pallas_call(
        functools.partial(regrid_kernel, column_rows),
        in_specs=[hbm] * 5,
        out_specs=[hbm] * (1 + TILE_COLS),
        out_shape=[same] + [piece] * TILE_COLS,
        scratch_shapes=[
            pltpu.SMEM(target.shape, jnp.int32),
            pltpu.VMEM((1, entries), jnp.int32),
            pltpu.SMEM(source_index.shape, jnp.int32),
            pltpu.VMEM(field.shape, jnp.bfloat16),
            pltpu.VMEM(weights.shape, jnp.bfloat16),
            pltpu.VMEM((PADDED * ROWS, BLOCK), jnp.float32),
            pltpu.VMEM((ROWS, WIDE, BLOCK), jnp.bfloat16),
            pltpu.VMEM((SLOTS, PADDED, BLOCK), jnp.float32),
            pltpu.VMEM((GROUPS, MESSAGE, BLOCK), jnp.bfloat16),
            pltpu.VMEM((SLOTS * 8, BLOCK), jnp.float32),
            pltpu.VMEM((1, entries), jnp.int32),
            pltpu.SMEM((1, entries), jnp.int32),
            pltpu.SemaphoreType.DMA,
            pltpu.SemaphoreType.DMA((4,)),
            pltpu.SemaphoreType.DMA((entries // CHUNK,)),
            pltpu.SemaphoreType.DMA((GROUPS,)),
        ],
        compiler_params=pltpu.CompilerParams(vmem_limit_bytes=REGRID_VMEM),
        name="regrid",
    )(target, target.reshape(1, -1), source_index, field, weights)


def gather_kernel(column_rows, flip_ref, gain_ref, same, *rest):
    nexts = rest[:TILE_COLS]
    (
        gridded,
        normed,
        upward,
        downward,
        strip_out,
        summed,
        tails,
    ) = rest[TILE_COLS:]
    position = lax.rem(lax.axis_index("tile"), column_rows)
    summed[...] = jnp.zeros_like(summed)

    def add(group, piece):
        ends = piece[CAP * BODY :].astype(jnp.float32)
        tails[group, :TAILS] = ends
        rows = ends[TAILS - CAP :].astype(jnp.int32)
        for place in range(CAP):
            row = rows[place, 0]
            body = piece[place * BODY : (place + 1) * BODY].astype(jnp.float32)
            summed[row, :BODY] = summed[row, :BODY] + body
            tail = tails[group, pl.ds(place, 8, stride=CAP), :]
            summed[row, BODY:] = summed[row, BODY:] + tail

    tails[:, TAILS:] = jnp.zeros((GROUPS, 8 * CAP - TAILS, BLOCK), jnp.float32)
    for group in range(TILE_COLS):
        add(group, same.at[pl.ds(group * MESSAGE, MESSAGE)])

    @pl.when(position > 0)
    def _():
        for group in range(TILE_COLS):
            add(TILE_COLS + group, nexts[group])

    gain = gain_ref[...]
    channel = lax.broadcasted_iota(jnp.int32, (PADDED, BLOCK), 0)
    nothing = jnp.zeros((WIDE - PADDED, BLOCK), jnp.float32)
    lane = lanes((WIDE, BLOCK))
    strip = jnp.zeros((WIDE, BLOCK), jnp.bfloat16)
    for row in range(ROWS):
        rounded = summed[row].astype(jnp.bfloat16)
        gridded[row] = rounded
        value = rounded.astype(jnp.float32)
        value = jnp.where(channel < CHANNELS, value, 0.0)
        square = jnp.sum(value * value, axis=0, keepdims=True) * (1.0 / CHANNELS)
        scaled = value * lax.rsqrt(square + EPSILON) * gain
        scaled = jnp.concatenate([scaled, nothing], axis=0).astype(jnp.bfloat16)
        normed[row] = scaled
        if row < 2:
            upward[row] = scaled
        if row >= ROWS - 2:
            downward[row - ROWS + 2] = scaled
        strip = jnp.where((lane >> 2) == row, pltpu.roll(scaled, 4 * row + 2, 1), strip)
    to_lane = lanes((BLOCK, BLOCK))
    from_lane = 4 * (to_lane & (ROWS - 1)) + (((to_lane >> ROW_BITS) + 2) & 3)
    order = lax.broadcasted_iota(jnp.int32, (BLOCK, BLOCK), 0) == from_lane
    strip = jnp.dot(strip, order.astype(jnp.bfloat16), preferred_element_type=jnp.float32)
    channel = lax.broadcasted_iota(jnp.int32, (WIDE, BLOCK), 0)
    for side in range(2):
        strip = jnp.where(channel == CHANNELS + side, flip_ref[0, side].astype(jnp.float32), strip)
    strip = strip.astype(jnp.bfloat16)
    upward[2] = strip
    downward[2] = strip
    strip_out[...] = strip


GRIDDED = jax.ShapeDtypeStruct((ROWS, PADDED, BLOCK), jnp.bfloat16)
FIELD = jax.ShapeDtypeStruct((ROWS, WIDE, BLOCK), jnp.bfloat16)
RIM = jax.ShapeDtypeStruct((3, WIDE, BLOCK), jnp.bfloat16)
STRIP_COLUMNS = (0, 1, BLOCK - 2, BLOCK - 1)
STRIP = jax.ShapeDtypeStruct((WIDE, BLOCK), jnp.bfloat16)


def gather_rows(column_rows, edge_flip, gain, same, nexts):
    return pl.pallas_call(
        functools.partial(gather_kernel, column_rows),
        in_specs=[smem()] + [vmem()] * (2 + TILE_COLS),
        out_specs=[vmem()] * 5,
        out_shape=[GRIDDED, FIELD, RIM, RIM, STRIP],
        scratch_shapes=[
            pltpu.VMEM((ROWS + 1, PADDED, BLOCK), jnp.float32),
            pltpu.VMEM((GROUPS, 8 * CAP, BLOCK), jnp.float32),
        ],
        compiler_params=pltpu.CompilerParams(vmem_limit_bytes=VMEM_LIMIT),
        name="gather_rows",
    )(edge_flip, gain, same, *nexts)


def turn_kernel(field, out, turned):
    for row in range(ROWS):
        turned[pl.ds(row, PADDED, stride=ROWS), :] = field[row].astype(jnp.float32)
    out[...] = turned[pl.ds(0, CHANNELS * ROWS), :].astype(jnp.bfloat16)


def channels_first(field):
    return pl.pallas_call(
        turn_kernel,
        in_specs=[vmem()],
        out_specs=vmem(),
        out_shape=jax.ShapeDtypeStruct((CHANNELS * ROWS, BLOCK), jnp.bfloat16),
        scratch_shapes=[pltpu.VMEM((PADDED * ROWS, BLOCK), jnp.float32)],
        compiler_params=pltpu.CompilerParams(vmem_limit_bytes=VMEM_LIMIT),
        name="channels_first",
    )(field)


def shifted_columns(value, left_end, right_end):
    lane = lanes((WIDE, BLOCK))
    left = jnp.where(lane == 0, left_end, pltpu.roll(value, 1, 1))
    right = jnp.where(lane == BLOCK - 1, right_end, pltpu.roll(value, BLOCK - 1, 1))
    return jnp.concatenate([left, value, right], axis=0)


def tap_sums(taps, one, two):
    both = jnp.concatenate([one, two], axis=1)
    result = jnp.dot(taps, both, preferred_element_type=jnp.float32)
    return result[:, :BLOCK], result[:, BLOCK:]


def row_tap(sums, at):
    return sums[at * WIDE : (at + 1) * WIDE]


def activated(value):
    return jax.nn.gelu(value).astype(jnp.bfloat16)


def inner_kernel(taps_ref, field, hidden, ends, sides, partial):
    taps = taps_ref[...]
    blank = jnp.zeros((WIDE, BLOCK), jnp.bfloat16)
    for row in range(0, ROWS, 2):
        partial[row], partial[row + 1] = tap_sums(
            taps,
            shifted_columns(field[row], blank, blank),
            shifted_columns(field[row + 1], blank, blank),
        )
    lane = lanes((WIDE, BLOCK))
    west = jnp.zeros((WIDE, BLOCK), jnp.float32)
    east = jnp.zeros((WIDE, BLOCK), jnp.float32)
    for row in range(ROWS):
        value = partial[row, WIDE : 2 * WIDE]
        if row > 0:
            value = value + partial[row - 1, :WIDE]
        if row < ROWS - 1:
            value = value + partial[row + 1, 2 * WIDE :]
        if row == 0:
            ends[0] = value
        elif row == ROWS - 1:
            ends[1] = value
        else:
            hidden[row] = jnp.where((lane == 0) | (lane == BLOCK - 1), blank, activated(value))
        west = jnp.where(lane == row, pltpu.roll(value, row, 1), west)
        east = jnp.where(lane == row, pltpu.roll(value, row + 1, 1), east)
    hidden[0] = blank
    hidden[ROWS - 1] = blank
    sides[0] = west
    sides[1] = east


def inner_convolution(taps, field):
    pair = jax.ShapeDtypeStruct((2, WIDE, BLOCK), jnp.float32)
    return pl.pallas_call(
        inner_kernel,
        in_specs=[vmem()] * 2,
        out_specs=[vmem()] * 3,
        out_shape=[FIELD, pair, pair],
        scratch_shapes=[pltpu.VMEM((ROWS, 3 * WIDE, BLOCK), jnp.float32)],
        compiler_params=pltpu.CompilerParams(vmem_limit_bytes=VMEM_LIMIT),
        cost_estimate=pl.CostEstimate(
            flops=2 * 9 * WIDE * WIDE * ROWS * BLOCK, bytes_accessed=2 << 20, transcendentals=0
        ),
        name="inner_convolution",
    )(taps, field)


def second_kernel_inner(taps_ref, hidden, gridded, base, partial):
    taps = taps_ref[...]
    blank = jnp.zeros((WIDE, BLOCK), jnp.bfloat16)
    for row in range(0, ROWS, 2):
        partial[row], partial[row + 1] = tap_sums(
            taps,
            shifted_columns(hidden[row], blank, blank),
            shifted_columns(hidden[row + 1], blank, blank),
        )
    for row in range(ROWS):
        value = gridded[row].astype(jnp.float32) + partial[row, WIDE : WIDE + PADDED]
        if row > 0:
            value = value + partial[row - 1, :PADDED]
        if row < ROWS - 1:
            value = value + partial[row + 1, 2 * WIDE : 2 * WIDE + PADDED]
        base[row] = value


def inner_second_convolution(taps, hidden, gridded):
    return pl.pallas_call(
        second_kernel_inner,
        in_specs=[vmem()] * 3,
        out_specs=vmem(),
        out_shape=jax.ShapeDtypeStruct((ROWS, PADDED, BLOCK), jnp.float32),
        scratch_shapes=[pltpu.VMEM((ROWS, 3 * WIDE, BLOCK), jnp.float32)],
        compiler_params=pltpu.CompilerParams(vmem_limit_bytes=VMEM_LIMIT),
        cost_estimate=pl.CostEstimate(
            flops=2 * 9 * WIDE * WIDE * ROWS * BLOCK, bytes_accessed=2 << 20, transcendentals=0
        ),
        name="inner_second_convolution",
    )(taps, hidden, gridded)


def strip_plan(column_rows):
    if column_rows == 2:
        return [], 3, 1
    return [-2, 2], column_rows, 2


def conv_kernel(
    column_rows,
    first_taps_ref,
    second_taps_ref,
    field,
    base,
    ends_ref,
    sides_ref,
    above,
    below,
    own_strip,
    *rest,
):
    near, far, reach = strip_plan(column_rows)
    near_strips, (west_pack, east_pack) = rest[: len(near)], rest[len(near) : len(near) + 2]
    smoothed, turned = rest[len(near) + 2 :]
    count = lax.axis_size("tile")
    tile = lax.axis_index("tile")
    lane = lanes((WIDE, BLOCK))
    last = ROWS + 1
    R = column_rows
    blank = jnp.zeros((WIDE, BLOCK), jnp.bfloat16)

    strips = {-1: above[2], 0: own_strip[...], 1: below[2]}
    strips.update((shift, ref[...]) for shift, ref in zip(near, near_strips))
    for at in range(-reach, reach + 1):
        strips[at - far], strips[at + far] = west_pack[at + reach], east_pack[at + reach]

    def place(shift):
        return lax.rem(tile + shift + count, count)

    def ends(shift, before, after, middle):
        before = jnp.where(place(shift) > 0, before, blank)
        after = jnp.where(place(shift) < count - 1, after, blank)
        return jnp.where(lane == 0, before, jnp.where(lane == last, after, middle))

    memo = {}

    def padded_column(shift, which):
        if (shift, which) not in memo:
            base = which * ROWS
            memo[shift, which] = ends(
                shift,
                pltpu.roll(strips[shift - 1], (1 - base - ROWS) % BLOCK, 1),
                pltpu.roll(strips[shift + 1], (last - base) % BLOCK, 1),
                pltpu.roll(strips[shift], (1 - base) % BLOCK, 1),
            )
        return memo[shift, which]

    row_id = lax.broadcasted_iota(jnp.int32, (BLOCK, BLOCK), 0)
    reversal = (row_id + lanes((BLOCK, BLOCK)) == last).astype(jnp.bfloat16)

    def reversed_lanes(planes):
        stacked = jnp.concatenate(planes, axis=0)
        turned_round = jnp.dot(stacked, reversal, preferred_element_type=jnp.float32)
        return [row_tap(turned_round, at) for at in range(len(planes))]

    def choose(shift, which, turned_round, plain):
        flips = strips[shift].astype(jnp.float32)[CHANNELS + which : CHANNELS + which + 1]
        return jnp.where(flips > 0.5, turned_round, plain.astype(jnp.float32)).astype(jnp.bfloat16)

    west_of = {shift: (shift - R, 3) for shift in {-1, 0, 1, R - 1, R, R + 1}}
    east_of = {shift: (shift + R, 0) for shift in {-1, 0, 1, -R - 1, -R, -R + 1}}
    keys = sorted(set(west_of.values()) | set(east_of.values()))
    flipped = dict(zip(keys, reversed_lanes([padded_column(*key) for key in keys])))
    west = {
        shift: choose(shift, 0, flipped[west_of[shift]], padded_column(*west_of[shift]))
        for shift in sorted(west_of)
    }
    east = {
        shift: choose(shift, 1, flipped[east_of[shift]], padded_column(*east_of[shift]))
        for shift in sorted(east_of)
    }

    def columns(value, west_plane, west_row, east_plane, east_row):
        return shifted_columns(
            value,
            pltpu.roll(west_plane, (BLOCK - west_row) % BLOCK, 1),
            pltpu.roll(east_plane, BLOCK - 1 - east_row, 1),
        )

    def along(result):
        return (
            row_tap(result, 0)
            + pltpu.roll(row_tap(result, 1), BLOCK - 1, 1)
            + pltpu.roll(row_tap(result, 2), BLOCK - 2, 1)
        )

    first_taps = first_taps_ref[...]
    up = [jnp.where(tile > 0, above[at], blank) for at in range(2)]
    down = [jnp.where(tile < count - 1, below[at], blank) for at in range(2)]
    from_up, from_down = tap_sums(
        first_taps, shifted_columns(up[1], blank, blank), shifted_columns(down[0], blank, blank)
    )
    from_up, from_down = row_tap(from_up, 0), row_tap(from_down, 2)
    from_west, from_east = tap_sums(
        first_taps,
        jnp.concatenate([west[0], blank, blank], axis=0),
        jnp.concatenate([blank, blank, east[0]], axis=0),
    )
    from_west, from_east = along(from_west), along(from_east)
    first = ends_ref[0] + from_up
    first = first + jnp.where(lane == 0, from_west, 0.0)
    first = first + jnp.where(lane == BLOCK - 1, pltpu.roll(from_east, BLOCK - 1, 1), 0.0)
    final = ends_ref[1] + from_down
    final = final + jnp.where(lane == 0, pltpu.roll(from_west, BLOCK - ROWS + 1, 1), 0.0)
    final = final + jnp.where(lane == BLOCK - 1, pltpu.roll(from_east, BLOCK - ROWS, 1), 0.0)
    first, final = activated(first), activated(final)
    first_column = activated(sides_ref[0] + from_west)
    last_column = activated(sides_ref[1] + from_east)

    upper = jnp.zeros((WIDE, BLOCK), jnp.float32)
    lower = jnp.zeros((WIDE, BLOCK), jnp.float32)
    for at, (high, low) in enumerate(
        [(up[0], field[ROWS - 1]), (up[1], down[0]), (field[0], down[1])]
    ):
        from_row = ROWS - 1 + at
        one, two = tap_sums(
            row_tap(first_taps, at),
            columns(high, west[-1], from_row, east[-1], from_row),
            columns(low, west[1], at, east[1], at),
        )
        upper += one
        lower += two
    top = jnp.where(tile > 0, activated(upper), blank)
    bottom = jnp.where(tile < count - 1, activated(lower), blank)

    west_hidden, east_hidden = {}, {}
    for at in (-1, 0, 1):
        q = at - R
        one = jnp.concatenate([padded_column(q, 2), padded_column(q, 3), east[q]], axis=0)
        q = at + R
        two = jnp.concatenate([west[q], padded_column(q, 0), padded_column(q, 1)], axis=0)
        one, two = tap_sums(first_taps, one, two)
        west_hidden[at], east_hidden[at] = activated(along(one)), activated(along(two))

    def hidden_side(shift, values):
        return ends(
            shift,
            pltpu.roll(values[-1], BLOCK - ROWS + 1, 1),
            pltpu.roll(values[1], last, 1),
            pltpu.roll(values[0], 1, 1),
        )

    plain = [hidden_side(-R, west_hidden), hidden_side(R, east_hidden)]
    west_side, east_side = [
        choose(0, which, turned_side, plain[which])
        for which, turned_side in enumerate(reversed_lanes(plain))
    ]

    second_taps = second_taps_ref[...]
    from_top, from_first = tap_sums(
        second_taps,
        columns(top, west_side, 0, east_side, 0),
        columns(first, west_side, 1, east_side, 1),
    )
    from_final, from_bottom = tap_sums(
        second_taps,
        columns(final, west_side, ROWS, east_side, ROWS),
        columns(bottom, west_side, last, east_side, last),
    )
    rim_rows = {
        0: row_tap(from_top, 0) + row_tap(from_first, 1),
        1: row_tap(from_first, 0),
        ROWS - 2: row_tap(from_final, 2),
        ROWS - 1: row_tap(from_final, 1) + row_tap(from_bottom, 2),
    }

    other = (lane >= 2) & (lane < ROWS)

    def other_rows(plane):
        return jnp.where(other, plane, blank)

    near_west, near_east = other_rows(west_side), other_rows(east_side)
    first_column = other_rows(pltpu.roll(first_column, 1, 1))
    last_column = other_rows(pltpu.roll(last_column, 1, 1))
    to_0, to_1 = tap_sums(
        second_taps,
        jnp.concatenate([near_west, first_column, blank], axis=0),
        jnp.concatenate([first_column, blank, blank], axis=0),
    )
    to_127, to_126 = tap_sums(
        second_taps,
        jnp.concatenate([blank, last_column, near_east], axis=0),
        jnp.concatenate([blank, blank, last_column], axis=0),
    )
    spread = jnp.zeros((WIDE, BLOCK), jnp.float32)
    for at, sums in enumerate((to_126, to_127, to_0, to_1)):
        sums = along(sums)
        high = sums.astype(jnp.bfloat16)
        sums = sums - high.astype(jnp.float32)
        middle = sums.astype(jnp.bfloat16)
        low = (sums - middle.astype(jnp.float32)).astype(jnp.bfloat16)
        to_lane = (lanes((BLOCK, BLOCK)) == 4 * row_id + at).astype(jnp.bfloat16)
        parts = jnp.dot(
            jnp.concatenate([high, middle, low], axis=0),
            to_lane,
            preferred_element_type=jnp.float32,
        )
        spread = spread + (row_tap(parts, 0) + (row_tap(parts, 1) + row_tap(parts, 2)))

    rim_lanes = lanes((PADDED, BLOCK))
    rim_lanes = (rim_lanes < 2) | (rim_lanes >= BLOCK - 2)
    spread = spread[:PADDED]
    for row in range(ROWS):
        value = base[row] + jnp.where(
            rim_lanes, pltpu.roll(spread, (BLOCK - 4 * row - 2) % BLOCK, 1), 0.0
        )
        if row in rim_rows:
            value = value + rim_rows[row][:PADDED]
        turned[pl.ds(row, PADDED, stride=ROWS), :] = value
    smoothed[...] = turned[pl.ds(0, CHANNELS * ROWS), :].astype(jnp.bfloat16)


def convolutions(column_rows, *operands):
    return pl.pallas_call(
        functools.partial(conv_kernel, column_rows),
        in_specs=[vmem()] * len(operands),
        out_specs=vmem(),
        out_shape=jax.ShapeDtypeStruct((CHANNELS * ROWS, BLOCK), jnp.bfloat16),
        scratch_shapes=[
            pltpu.VMEM((PADDED * ROWS, BLOCK), jnp.float32),
        ],
        compiler_params=pltpu.CompilerParams(vmem_limit_bytes=VMEM_LIMIT),
        name="convolutions",
    )(*operands)


def tap_matrix(kernel):
    pad = WIDE - CHANNELS
    taps = jnp.pad(kernel, ((0, 0), (0, pad), (0, pad))).reshape(3, 3, WIDE, WIDE)
    return taps.transpose(0, 2, 1, 3).reshape(3 * WIDE, 3 * WIDE)


def from_shift(value, shift):
    count = lax.axis_size("tile")
    return lax.ppermute(value, "tile", [(i, (i - shift) % count) for i in range(count)])


def per_device(
    source, weights, block_source, block_target, edge_flip, norm_gain, first_kernel, second_kernel
):
    count = lax.axis_size("tile")
    column_rows = count // TILE_COLS
    field = source.reshape(ROWS, CHANNELS, BLOCK).transpose(1, 0, 2).reshape(-1, BLOCK)
    same, *nexts = regrid(block_target, block_source, field, weights, column_rows)

    for across in range(TILE_COLS):
        pairs = [
            (c * column_rows + p, (c ^ across) * column_rows + p + 1)
            for c in range(TILE_COLS)
            for p in range(column_rows - 1)
        ]
        nexts[across] = lax.ppermute(nexts[across], "tile", pairs)
    nexts = [nexts[across] for across in (0, 1, 2, 4, 5, 6, 7, 3)]
    same = lax.all_to_all(
        same,
        "tile",
        0,
        0,
        axis_index_groups=[
            [c * column_rows + p for c in COLUMN_ORDER] for p in range(column_rows)
        ],
        tiled=True,
    )

    gain = jnp.broadcast_to(
        jnp.pad(norm_gain, (0, PADDED - CHANNELS))[:, None], (PADDED, BLOCK)
    )
    first_taps, second_taps = tap_matrix(first_kernel), tap_matrix(second_kernel)
    same, nexts, gain, first_taps, second_taps = lax.optimization_barrier(
        (same, nexts, gain, first_taps, second_taps)
    )
    gridded, normed, upward, downward, strip = gather_rows(
        column_rows, edge_flip, gain, same, nexts
    )
    rims = [from_shift(downward, -1), from_shift(upward, 1)]
    near, far, reach = strip_plan(column_rows)
    strips = [from_shift(strip, shift) for shift in near]
    inner = inner_convolution(first_taps, normed)
    held = {-1: rims[0][2], 0: strip, 1: rims[1][2], **dict(zip(near, strips))}
    pack = jnp.stack([held[at] for at in range(-reach, reach + 1)])
    gridded_out = channels_first(gridded)
    pack, inner, gridded_out = lax.optimization_barrier((pack, inner, gridded_out))
    strips += [from_shift(pack, -far), from_shift(pack, far)]
    hidden, *unfinished = inner
    base = inner_second_convolution(second_taps, hidden, gridded)
    smoothed = convolutions(
        column_rows, first_taps, second_taps, normed, base, *unfinished, *rims, strip, *strips
    )

    def placed(value):
        return value.reshape(CHANNELS, ROWS, BLOCK).transpose(1, 0, 2)[:, None]

    return placed(gridded_out), placed(smoothed)


def solution(mesh):
    in_specs = (
        P("tile", "groups", None, None),
        P("tile", None, None),
        P("tile"),
        P("tile"),
        P("tile", None),
        P(),
        P(),
        P(),
    )
    out_specs = (P("tile", "groups", None, None), P("tile", "groups", None, None))
    return jax.shard_map(
        per_device, mesh=mesh, in_specs=in_specs, out_specs=out_specs, check_vma=False
    )
```

```python
import functools

import jax
import jax.numpy as jnp
from jax import lax
from jax.experimental import pallas as pl
from jax.experimental.pallas import tpu as pltpu
from jax.sharding import PartitionSpec as P

BLOCK = 128
CHANNELS = 69
PADDED = 72
WIDE = 80
ROWS = 32
ROW_BITS = 5
HALF_ROWS = ROWS // 2
TILE_COLS = 8
CAP = 8
HALF = TILE_COLS // 2
GROUPS = 2 * TILE_COLS
COLUMN_ORDER = [half * HALF + at for at in range(HALF) for half in range(2)]
SLOTS = GROUPS * CAP
CHUNK = 16
MARK = CHANNELS
BODY = 64
TAILS = (MARK + 1 - BODY) * CAP
MESSAGE = CAP * BODY + TAILS
EPSILON = 1e-05
VMEM_LIMIT = 40 * 1024 * 1024
REGRID_VMEM = 60 * 1024 * 1024


def vmem():
    return pl.BlockSpec(memory_space=pltpu.VMEM)


def smem():
    return pl.BlockSpec(memory_space=pltpu.SMEM)


def split(value, size):
    if size & (size - 1) == 0:
        return value >> (size.bit_length() - 1), value & (size - 1)
    return lax.div(value, size), lax.rem(value, size)


def lanes(shape):
    return lax.broadcasted_iota(jnp.int32, shape, len(shape) - 1)


def regrid_kernel(
    column_rows, target_hbm, target_row_hbm, index_hbm, source_hbm, weight_hbm, *rest
):
    same_out, next_outs = rest[0], rest[1 : 1 + TILE_COLS]
    (
        target_ref,
        target_row_ref,
        index_ref,
        source,
        weight,
        wide,
        field,
        sums,
        message,
        tails,
        plan,
        plan_scalars,
        plan_sem,
        in_sems,
        weight_sems,
        out_sems,
    ) = rest[1 + TILE_COLS :]
    entries = weight.shape[0]
    chunks = entries // CHUNK
    tile = lax.axis_index("tile")
    column, position = split(tile, column_rows)

    small_copies = [
        pltpu.make_async_copy(target_row_hbm, target_row_ref, in_sems.at[0]),
        pltpu.make_async_copy(target_hbm, target_ref, in_sems.at[1]),
        pltpu.make_async_copy(index_hbm, index_ref, in_sems.at[2]),
    ]
    source_copy = pltpu.make_async_copy(source_hbm, source, in_sems.at[3])
    for copy in small_copies:
        copy.start()
    source_copy.start()

    def chunk_copy(chunk):
        part = pl.ds(chunk * CHUNK, CHUNK)
        return pltpu.make_async_copy(weight_hbm.at[part], weight.at[part], weight_sems.at[chunk])

    for chunk in range(chunks):
        chunk_copy(chunk).start()

    small_copies[0].wait()
    target = target_row_ref[...]
    owner, row = split(target, ROWS)
    owner_column, owner_position = split(owner, column_rows)
    place = ((owner_column & (HALF - 1)) << 1) + (owner_column >= HALF).astype(jnp.int32)
    group = jnp.where(owner_position == position, place, TILE_COLS + (owner_column ^ column))
    key = group * ROWS + row
    square = (entries, entries)
    down = lax.broadcasted_iota(jnp.int32, square, 0)
    along = lanes(square)
    key_along = jnp.broadcast_to(key.astype(jnp.float32), square)
    key_down = jnp.broadcast_to(
        jnp.sum(jnp.where(down == along, key_along, 0.0), axis=1, keepdims=True), square
    )
    equal = key_along == key_down
    doubles = jnp.sum(jnp.where(equal & (along < down), 1.0, 0.0), axis=1, keepdims=True)
    in_group = (key_down.astype(jnp.int32) >> ROW_BITS) == (key_along.astype(jnp.int32) >> ROW_BITS)
    below = in_group & (key_down < key_along) & (jnp.broadcast_to(doubles, square) == 0.0)
    rank = jnp.sum(jnp.where(below, 1.0, 0.0), axis=0, keepdims=True)
    mentions = jnp.sum(jnp.where(equal & (down < along), 1.0, 0.0), axis=0, keepdims=True)
    slots = group * CAP + rank.astype(jnp.int32)
    plan[...] = slots + jnp.where(mentions == 0.0, SLOTS, 0)
    plan_copy = pltpu.make_async_copy(plan, plan_scalars, plan_sem)
    plan_copy.start()

    for slot in range(SLOTS):
        tails[pl.ds(slot * 8, 8), :] = jnp.full((8, BLOCK), ROWS, jnp.float32)
    wide[pl.ds(CHANNELS * ROWS, (PADDED - CHANNELS) * ROWS), :] = jnp.zeros(
        ((PADDED - CHANNELS) * ROWS, BLOCK), jnp.float32
    )
    nothing = jnp.zeros((WIDE - PADDED, BLOCK), jnp.float32)
    source_copy.wait()
    wide[pl.ds(0, CHANNELS * ROWS), :] = source[...].astype(jnp.float32)
    for row in range(ROWS):
        block = wide[pl.ds(row, PADDED, stride=ROWS), :]
        field[row] = jnp.concatenate([block, nothing], axis=0).astype(jnp.bfloat16)
    is_mark = lax.broadcasted_iota(jnp.int32, (8, BLOCK), 0) == MARK - BODY
    blank = jnp.zeros((WIDE, BLOCK), jnp.bfloat16)
    small_copies[1].wait()
    small_copies[2].wait()
    plan_copy.wait()

    for chunk in range(chunks):
        chunk_copy(chunk).wait()
    for entry in range(0, entries, 2):
        one = jnp.concatenate([field[index_ref[entry]], blank], axis=1)
        two = jnp.concatenate([blank, field[index_ref[entry + 1]]], axis=1)
        products = jnp.dot(
            jnp.concatenate([one, two], axis=0),
            weight[entry : entry + 2].reshape(2 * BLOCK, BLOCK),
            preferred_element_type=jnp.float32,
        )
        for at in range(2):
            code = plan_scalars[0, entry + at]
            slot = code & (SLOTS - 1)
            row = split(target_ref[entry + at], ROWS)[1]
            product = products[at * WIDE : at * WIDE + PADDED]
            total = jnp.where(code >= SLOTS, 0.0, sums[slot]) + product
            sums[slot] = total
            group, place = split(slot, CAP)
            message[group, pl.ds(pl.multiple_of(place * BODY, BODY), BODY), :] = total[
                :BODY
            ].astype(jnp.bfloat16)
            tails[pl.ds(pl.multiple_of(slot * 8, 8), 8), :] = jnp.where(
                is_mark, row.astype(jnp.float32), total[BODY:]
            )
    copies = []
    for group in range(GROUPS):
        start = group * CAP * 8
        ends = [tails[pl.ds(start + at, CAP, stride=8), :] for at in range(MARK + 1 - BODY)]
        message[group, CAP * BODY :] = jnp.concatenate(ends, axis=0).astype(jnp.bfloat16)
        if group < TILE_COLS:
            out = same_out.at[pl.ds(group * MESSAGE, MESSAGE)]
        else:
            out = next_outs[group - TILE_COLS]
        copies.append(pltpu.make_async_copy(message.at[group], out, out_sems.at[group]))
        copies[-1].start()
    for copy in copies:
        copy.wait()


def regrid(target, source_index, field, weights, column_rows):
    piece = jax.ShapeDtypeStruct((MESSAGE, BLOCK), jnp.bfloat16)
    same = jax.ShapeDtypeStruct((TILE_COLS * MESSAGE, BLOCK), jnp.bfloat16)
    hbm = pl.BlockSpec(memory_space=pl.ANY)
    entries = weights.shape[0]
    return pl.pallas_call(
        functools.partial(regrid_kernel, column_rows),
        in_specs=[hbm] * 5,
        out_specs=[hbm] * (1 + TILE_COLS),
        out_shape=[same] + [piece] * TILE_COLS,
        scratch_shapes=[
            pltpu.SMEM(target.shape, jnp.int32),
            pltpu.VMEM((1, entries), jnp.int32),
            pltpu.SMEM(source_index.shape, jnp.int32),
            pltpu.VMEM(field.shape, jnp.bfloat16),
            pltpu.VMEM(weights.shape, jnp.bfloat16),
            pltpu.VMEM((PADDED * ROWS, BLOCK), jnp.float32),
            pltpu.VMEM((ROWS, WIDE, BLOCK), jnp.bfloat16),
            pltpu.VMEM((SLOTS, PADDED, BLOCK), jnp.float32),
            pltpu.VMEM((GROUPS, MESSAGE, BLOCK), jnp.bfloat16),
            pltpu.VMEM((SLOTS * 8, BLOCK), jnp.float32),
            pltpu.VMEM((1, entries), jnp.int32),
            pltpu.SMEM((1, entries), jnp.int32),
            pltpu.SemaphoreType.DMA,
            pltpu.SemaphoreType.DMA((4,)),
            pltpu.SemaphoreType.DMA((entries // CHUNK,)),
            pltpu.SemaphoreType.DMA((GROUPS,)),
        ],
        compiler_params=pltpu.CompilerParams(vmem_limit_bytes=REGRID_VMEM),
        name="regrid",
    )(target, target.reshape(1, -1), source_index, field, weights)


def gather_kernel(column_rows, flip_ref, gain_ref, same, *rest):
    nexts = rest[:TILE_COLS]
    (
        gridded,
        normed,
        upward,
        downward,
        strip_out,
        summed,
        tails,
    ) = rest[TILE_COLS:]
    position = lax.rem(lax.axis_index("tile"), column_rows)
    summed[...] = jnp.zeros_like(summed)

    def add(group, piece):
        ends = piece[CAP * BODY :].astype(jnp.float32)
        tails[group, :TAILS] = ends
        rows = ends[TAILS - CAP :].astype(jnp.int32)
        for place in range(CAP):
            row = rows[place, 0]
            body = piece[place * BODY : (place + 1) * BODY].astype(jnp.float32)
            summed[row, :BODY] = summed[row, :BODY] + body
            tail = tails[group, pl.ds(place, 8, stride=CAP), :]
            summed[row, BODY:] = summed[row, BODY:] + tail

    tails[:, TAILS:] = jnp.zeros((GROUPS, 8 * CAP - TAILS, BLOCK), jnp.float32)
    for group in range(TILE_COLS):
        add(group, same.at[pl.ds(group * MESSAGE, MESSAGE)])

    @pl.when(position > 0)
    def _():
        for group in range(TILE_COLS):
            add(TILE_COLS + group, nexts[group])

    gain = gain_ref[...]
    real = lax.broadcasted_iota(jnp.int32, (PADDED - BODY, BLOCK), 0) < CHANNELS - BODY
    nothing = jnp.zeros((WIDE - PADDED, BLOCK), jnp.float32)
    lane = lanes((WIDE, BLOCK))
    strip = jnp.zeros((WIDE, BLOCK), jnp.bfloat16)
    for row in range(ROWS):
        rounded = summed[row].astype(jnp.bfloat16)
        gridded[row] = rounded
        value = rounded.astype(jnp.float32)
        value = jnp.concatenate([value[:BODY], jnp.where(real, value[BODY:], 0.0)], axis=0)
        square = jnp.sum(value * value, axis=0, keepdims=True) * (1.0 / CHANNELS)
        scaled = value * lax.rsqrt(square + EPSILON) * gain
        scaled = jnp.concatenate([scaled, nothing], axis=0).astype(jnp.bfloat16)
        normed[row] = scaled
        if row < 2:
            upward[row] = scaled
        if row >= ROWS - 2:
            downward[row - ROWS + 2] = scaled
        strip = jnp.where((lane >> 2) == row, pltpu.roll(scaled, 4 * row + 2, 1), strip)
    to_lane = lanes((BLOCK, BLOCK))
    from_lane = 4 * (to_lane & (ROWS - 1)) + (((to_lane >> ROW_BITS) + 2) & 3)
    order = lax.broadcasted_iota(jnp.int32, (BLOCK, BLOCK), 0) == from_lane
    strip = jnp.dot(strip, order.astype(jnp.bfloat16), preferred_element_type=jnp.float32)
    channel = lax.broadcasted_iota(jnp.int32, (WIDE, BLOCK), 0)
    for side in range(2):
        strip = jnp.where(channel == CHANNELS + side, flip_ref[0, side].astype(jnp.float32), strip)
    strip = strip.astype(jnp.bfloat16)
    upward[2] = strip
    downward[2] = strip
    strip_out[...] = strip


GRIDDED = jax.ShapeDtypeStruct((ROWS, PADDED, BLOCK), jnp.bfloat16)
FIELD = jax.ShapeDtypeStruct((ROWS, WIDE, BLOCK), jnp.bfloat16)
RIM = jax.ShapeDtypeStruct((3, WIDE, BLOCK), jnp.bfloat16)
STRIP_COLUMNS = (0, 1, BLOCK - 2, BLOCK - 1)
STRIP = jax.ShapeDtypeStruct((WIDE, BLOCK), jnp.bfloat16)


def gather_rows(column_rows, edge_flip, gain, same, nexts):
    return pl.pallas_call(
        functools.partial(gather_kernel, column_rows),
        in_specs=[smem()] + [vmem()] * (2 + TILE_COLS),
        out_specs=[vmem()] * 5,
        out_shape=[GRIDDED, FIELD, RIM, RIM, STRIP],
        scratch_shapes=[
            pltpu.VMEM((ROWS + 1, PADDED, BLOCK), jnp.float32),
            pltpu.VMEM((GROUPS, 8 * CAP, BLOCK), jnp.float32),
        ],
        compiler_params=pltpu.CompilerParams(vmem_limit_bytes=VMEM_LIMIT),
        name="gather_rows",
    )(edge_flip, gain, same, *nexts)


def turn_kernel(field, out, turned):
    for row in range(ROWS):
        turned[pl.ds(row, PADDED, stride=ROWS), :] = field[row].astype(jnp.float32)
    out[...] = turned[pl.ds(0, CHANNELS * ROWS), :].astype(jnp.bfloat16)


def channels_first(field):
    return pl.pallas_call(
        turn_kernel,
        in_specs=[vmem()],
        out_specs=vmem(),
        out_shape=jax.ShapeDtypeStruct((CHANNELS * ROWS, BLOCK), jnp.bfloat16),
        scratch_shapes=[pltpu.VMEM((PADDED * ROWS, BLOCK), jnp.float32)],
        compiler_params=pltpu.CompilerParams(vmem_limit_bytes=VMEM_LIMIT),
        name="channels_first",
    )(field)


def shifted_columns(value, left_end, right_end):
    lane = lanes((WIDE, BLOCK))
    left = jnp.where(lane == 0, left_end, pltpu.roll(value, 1, 1))
    right = jnp.where(lane == BLOCK - 1, right_end, pltpu.roll(value, BLOCK - 1, 1))
    return jnp.concatenate([left, value, right], axis=0)


def tap_sums(taps, one, two):
    both = jnp.concatenate([one, two], axis=1)
    result = jnp.dot(taps, both, preferred_element_type=jnp.float32)
    return result[:, :BLOCK], result[:, BLOCK:]


def row_tap(sums, at):
    return sums[at * WIDE : (at + 1) * WIDE]


def activated(value):
    return jax.nn.gelu(value).astype(jnp.bfloat16)


def inner_kernel(taps_ref, field, hidden, ends, sides, partial):
    taps = taps_ref[...]
    blank = jnp.zeros((WIDE, BLOCK), jnp.bfloat16)
    for row in range(0, ROWS, 2):
        partial[row], partial[row + 1] = tap_sums(
            taps,
            shifted_columns(field[row], blank, blank),
            shifted_columns(field[row + 1], blank, blank),
        )
    lane = lanes((WIDE, BLOCK))
    west = jnp.zeros((WIDE, BLOCK), jnp.float32)
    east = jnp.zeros((WIDE, BLOCK), jnp.float32)
    for row in range(ROWS):
        value = partial[row, WIDE : 2 * WIDE]
        if row > 0:
            value = value + partial[row - 1, :WIDE]
        if row < ROWS - 1:
            value = value + partial[row + 1, 2 * WIDE :]
        if row == 0:
            ends[0] = value
        elif row == ROWS - 1:
            ends[1] = value
        else:
            hidden[row] = jnp.where((lane == 0) | (lane == BLOCK - 1), blank, activated(value))
        west = jnp.where(lane == row, pltpu.roll(value, row, 1), west)
        east = jnp.where(lane == row, pltpu.roll(value, row + 1, 1), east)
    hidden[0] = blank
    hidden[ROWS - 1] = blank
    sides[0] = west
    sides[1] = east


def inner_convolution(taps, field):
    pair = jax.ShapeDtypeStruct((2, WIDE, BLOCK), jnp.float32)
    return pl.pallas_call(
        inner_kernel,
        in_specs=[vmem()] * 2,
        out_specs=[vmem()] * 3,
        out_shape=[FIELD, pair, pair],
        scratch_shapes=[pltpu.VMEM((ROWS, 3 * WIDE, BLOCK), jnp.float32)],
        compiler_params=pltpu.CompilerParams(vmem_limit_bytes=VMEM_LIMIT),
        cost_estimate=pl.CostEstimate(
            flops=2 * 9 * WIDE * WIDE * ROWS * BLOCK, bytes_accessed=2 << 20, transcendentals=0
        ),
        name="inner_convolution",
    )(taps, field)


def second_kernel_inner(taps_ref, hidden, gridded, base, partial):
    taps = taps_ref[...]
    blank = jnp.zeros((WIDE, BLOCK), jnp.bfloat16)
    for row in range(0, ROWS, 2):
        partial[row], partial[row + 1] = tap_sums(
            taps,
            shifted_columns(hidden[row], blank, blank),
            shifted_columns(hidden[row + 1], blank, blank),
        )
    for row in range(ROWS):
        value = gridded[row].astype(jnp.float32) + partial[row, WIDE : WIDE + PADDED]
        if row > 0:
            value = value + partial[row - 1, :PADDED]
        if row < ROWS - 1:
            value = value + partial[row + 1, 2 * WIDE : 2 * WIDE + PADDED]
        base[row] = value


def inner_second_convolution(taps, hidden, gridded):
    return pl.pallas_call(
        second_kernel_inner,
        in_specs=[vmem()] * 3,
        out_specs=vmem(),
        out_shape=jax.ShapeDtypeStruct((ROWS, PADDED, BLOCK), jnp.float32),
        scratch_shapes=[pltpu.VMEM((ROWS, 3 * WIDE, BLOCK), jnp.float32)],
        compiler_params=pltpu.CompilerParams(vmem_limit_bytes=VMEM_LIMIT),
        cost_estimate=pl.CostEstimate(
            flops=2 * 9 * WIDE * WIDE * ROWS * BLOCK, bytes_accessed=2 << 20, transcendentals=0
        ),
        name="inner_second_convolution",
    )(taps, hidden, gridded)


def strip_plan(column_rows):
    if column_rows == 2:
        return [], 3, 1
    return [-2, 2], column_rows, 2


def conv_kernel(
    column_rows,
    first_taps_ref,
    second_taps_ref,
    field,
    base,
    ends_ref,
    sides_ref,
    above,
    below,
    own_strip,
    *rest,
):
    near, far, reach = strip_plan(column_rows)
    near_strips, (west_pack, east_pack) = rest[: len(near)], rest[len(near) : len(near) + 2]
    smoothed, turned, halves, sems = rest[len(near) + 2 :]
    count = lax.axis_size("tile")
    tile = lax.axis_index("tile")
    lane = lanes((WIDE, BLOCK))
    last = ROWS + 1
    R = column_rows
    blank = jnp.zeros((WIDE, BLOCK), jnp.bfloat16)

    strips = {-1: above[2], 0: own_strip[...], 1: below[2]}
    strips.update((shift, ref[...]) for shift, ref in zip(near, near_strips))
    for at in range(-reach, reach + 1):
        strips[at - far], strips[at + far] = west_pack[at + reach], east_pack[at + reach]

    def place(shift):
        return lax.rem(tile + shift + count, count)

    def ends(shift, before, after, middle):
        before = jnp.where(place(shift) > 0, before, blank)
        after = jnp.where(place(shift) < count - 1, after, blank)
        return jnp.where(lane == 0, before, jnp.where(lane == last, after, middle))

    memo = {}

    def padded_column(shift, which):
        if (shift, which) not in memo:
            base = which * ROWS
            memo[shift, which] = ends(
                shift,
                pltpu.roll(strips[shift - 1], (1 - base - ROWS) % BLOCK, 1),
                pltpu.roll(strips[shift + 1], (last - base) % BLOCK, 1),
                pltpu.roll(strips[shift], (1 - base) % BLOCK, 1),
            )
        return memo[shift, which]

    row_id = lax.broadcasted_iota(jnp.int32, (BLOCK, BLOCK), 0)
    reversal = (row_id + lanes((BLOCK, BLOCK)) == last).astype(jnp.bfloat16)

    def reversed_lanes(planes):
        stacked = jnp.concatenate(planes, axis=0)
        turned_round = jnp.dot(stacked, reversal, preferred_element_type=jnp.float32)
        return [row_tap(turned_round, at) for at in range(len(planes))]

    def choose(shift, which, turned_round, plain):
        flips = strips[shift].astype(jnp.float32)[CHANNELS + which : CHANNELS + which + 1]
        return jnp.where(flips > 0.5, turned_round, plain.astype(jnp.float32)).astype(jnp.bfloat16)

    west_of = {shift: (shift - R, 3) for shift in {-1, 0, 1, R - 1, R, R + 1}}
    east_of = {shift: (shift + R, 0) for shift in {-1, 0, 1, -R - 1, -R, -R + 1}}
    keys = sorted(set(west_of.values()) | set(east_of.values()))
    flipped = dict(zip(keys, reversed_lanes([padded_column(*key) for key in keys])))
    west = {
        shift: choose(shift, 0, flipped[west_of[shift]], padded_column(*west_of[shift]))
        for shift in sorted(west_of)
    }
    east = {
        shift: choose(shift, 1, flipped[east_of[shift]], padded_column(*east_of[shift]))
        for shift in sorted(east_of)
    }

    def columns(value, west_plane, west_row, east_plane, east_row):
        return shifted_columns(
            value,
            pltpu.roll(west_plane, (BLOCK - west_row) % BLOCK, 1),
            pltpu.roll(east_plane, BLOCK - 1 - east_row, 1),
        )

    def along(result):
        return (
            row_tap(result, 0)
            + pltpu.roll(row_tap(result, 1), BLOCK - 1, 1)
            + pltpu.roll(row_tap(result, 2), BLOCK - 2, 1)
        )

    first_taps = first_taps_ref[...]
    up = [jnp.where(tile > 0, above[at], blank) for at in range(2)]
    down = [jnp.where(tile < count - 1, below[at], blank) for at in range(2)]
    from_up, from_down = tap_sums(
        first_taps, shifted_columns(up[1], blank, blank), shifted_columns(down[0], blank, blank)
    )
    from_up, from_down = row_tap(from_up, 0), row_tap(from_down, 2)
    from_west, from_east = tap_sums(
        first_taps,
        jnp.concatenate([west[0], blank, blank], axis=0),
        jnp.concatenate([blank, blank, east[0]], axis=0),
    )
    from_west, from_east = along(from_west), along(from_east)
    first = ends_ref[0] + from_up
    first = first + jnp.where(lane == 0, from_west, 0.0)
    first = first + jnp.where(lane == BLOCK - 1, pltpu.roll(from_east, BLOCK - 1, 1), 0.0)
    final = ends_ref[1] + from_down
    final = final + jnp.where(lane == 0, pltpu.roll(from_west, BLOCK - ROWS + 1, 1), 0.0)
    final = final + jnp.where(lane == BLOCK - 1, pltpu.roll(from_east, BLOCK - ROWS, 1), 0.0)
    first, final = activated(first), activated(final)
    first_column = activated(sides_ref[0] + from_west)
    last_column = activated(sides_ref[1] + from_east)

    upper = jnp.zeros((WIDE, BLOCK), jnp.float32)
    lower = jnp.zeros((WIDE, BLOCK), jnp.float32)
    for at, (high, low) in enumerate(
        [(up[0], field[ROWS - 1]), (up[1], down[0]), (field[0], down[1])]
    ):
        from_row = ROWS - 1 + at
        one, two = tap_sums(
            row_tap(first_taps, at),
            columns(high, west[-1], from_row, east[-1], from_row),
            columns(low, west[1], at, east[1], at),
        )
        upper += one
        lower += two
    top = jnp.where(tile > 0, activated(upper), blank)
    bottom = jnp.where(tile < count - 1, activated(lower), blank)

    west_hidden, east_hidden = {}, {}
    for at in (-1, 0, 1):
        q = at - R
        one = jnp.concatenate([padded_column(q, 2), padded_column(q, 3), east[q]], axis=0)
        q = at + R
        two = jnp.concatenate([west[q], padded_column(q, 0), padded_column(q, 1)], axis=0)
        one, two = tap_sums(first_taps, one, two)
        west_hidden[at], east_hidden[at] = activated(along(one)), activated(along(two))

    def hidden_side(shift, values):
        return ends(
            shift,
            pltpu.roll(values[-1], BLOCK - ROWS + 1, 1),
            pltpu.roll(values[1], last, 1),
            pltpu.roll(values[0], 1, 1),
        )

    plain = [hidden_side(-R, west_hidden), hidden_side(R, east_hidden)]
    west_side, east_side = [
        choose(0, which, turned_side, plain[which])
        for which, turned_side in enumerate(reversed_lanes(plain))
    ]

    second_taps = second_taps_ref[...]
    from_top, from_first = tap_sums(
        second_taps,
        columns(top, west_side, 0, east_side, 0),
        columns(first, west_side, 1, east_side, 1),
    )
    from_final, from_bottom = tap_sums(
        second_taps,
        columns(final, west_side, ROWS, east_side, ROWS),
        columns(bottom, west_side, last, east_side, last),
    )
    rim_rows = {
        0: row_tap(from_top, 0) + row_tap(from_first, 1),
        1: row_tap(from_first, 0),
        ROWS - 2: row_tap(from_final, 2),
        ROWS - 1: row_tap(from_final, 1) + row_tap(from_bottom, 2),
    }

    other = (lane >= 2) & (lane < ROWS)

    def other_rows(plane):
        return jnp.where(other, plane, blank)

    near_west, near_east = other_rows(west_side), other_rows(east_side)
    first_column = other_rows(pltpu.roll(first_column, 1, 1))
    last_column = other_rows(pltpu.roll(last_column, 1, 1))
    to_0, to_1 = tap_sums(
        second_taps,
        jnp.concatenate([near_west, first_column, blank], axis=0),
        jnp.concatenate([first_column, blank, blank], axis=0),
    )
    to_127, to_126 = tap_sums(
        second_taps,
        jnp.concatenate([blank, last_column, near_east], axis=0),
        jnp.concatenate([blank, blank, last_column], axis=0),
    )
    spread = jnp.zeros((WIDE, BLOCK), jnp.float32)
    for at, sums in enumerate((to_126, to_127, to_0, to_1)):
        sums = along(sums)
        high = sums.astype(jnp.bfloat16)
        sums = sums - high.astype(jnp.float32)
        middle = sums.astype(jnp.bfloat16)
        low = (sums - middle.astype(jnp.float32)).astype(jnp.bfloat16)
        to_lane = (lanes((BLOCK, BLOCK)) == 4 * row_id + at).astype(jnp.bfloat16)
        parts = jnp.dot(
            jnp.concatenate([high, middle, low], axis=0),
            to_lane,
            preferred_element_type=jnp.float32,
        )
        spread = spread + (row_tap(parts, 0) + (row_tap(parts, 1) + row_tap(parts, 2)))

    rim_lanes = lanes((PADDED, BLOCK))
    rim_lanes = (rim_lanes < 2) | (rim_lanes >= BLOCK - 2)
    spread = spread[:PADDED]
    copies = []
    for half in range(2):
        for row in range(half * HALF_ROWS, (half + 1) * HALF_ROWS):
            value = base[row] + jnp.where(
                rim_lanes, pltpu.roll(spread, (BLOCK - 4 * row - 2) % BLOCK, 1), 0.0
            )
            if row in rim_rows:
                value = value + rim_rows[row][:PADDED]
            turned[half, pl.ds(row - half * HALF_ROWS, PADDED, stride=HALF_ROWS), :] = value
        rounded = turned[half, pl.ds(0, CHANNELS * HALF_ROWS), :].astype(jnp.bfloat16)
        halves[half] = rounded.reshape(CHANNELS, HALF_ROWS, BLOCK)
        rows = pl.ds(half * HALF_ROWS, HALF_ROWS)
        copies.append(pltpu.make_async_copy(halves.at[half], smoothed.at[:, rows], sems.at[half]))
        copies[-1].start()
    for copy in copies:
        copy.wait()


def convolutions(column_rows, *operands):
    return pl.pallas_call(
        functools.partial(conv_kernel, column_rows),
        in_specs=[vmem()] * len(operands),
        out_specs=pl.BlockSpec(memory_space=pl.ANY),
        out_shape=jax.ShapeDtypeStruct((CHANNELS, ROWS, BLOCK), jnp.bfloat16),
        scratch_shapes=[
            pltpu.VMEM((2, PADDED * HALF_ROWS, BLOCK), jnp.float32),
            pltpu.VMEM((2, CHANNELS, HALF_ROWS, BLOCK), jnp.bfloat16),
            pltpu.SemaphoreType.DMA((2,)),
        ],
        compiler_params=pltpu.CompilerParams(vmem_limit_bytes=VMEM_LIMIT),
        name="convolutions",
    )(*operands)


def tap_matrix(kernel):
    pad = WIDE - CHANNELS
    taps = jnp.pad(kernel, ((0, 0), (0, pad), (0, pad))).reshape(3, 3, WIDE, WIDE)
    return taps.transpose(0, 2, 1, 3).reshape(3 * WIDE, 3 * WIDE)


def from_shift(value, shift):
    count = lax.axis_size("tile")
    return lax.ppermute(value, "tile", [(i, (i - shift) % count) for i in range(count)])


def per_device(
    source, weights, block_source, block_target, edge_flip, norm_gain, first_kernel, second_kernel
):
    count = lax.axis_size("tile")
    column_rows = count // TILE_COLS
    field = source.reshape(ROWS, CHANNELS, BLOCK).transpose(1, 0, 2).reshape(-1, BLOCK)
    same, *nexts = regrid(block_target, block_source, field, weights, column_rows)

    for across in range(TILE_COLS):
        pairs = [
            (c * column_rows + p, (c ^ across) * column_rows + p + 1)
            for c in range(TILE_COLS)
            for p in range(column_rows - 1)
        ]
        nexts[across] = lax.ppermute(nexts[across], "tile", pairs)
    nexts = [nexts[across] for across in (0, 1, 2, 4, 5, 6, 7, 3)]
    same = lax.all_to_all(
        same,
        "tile",
        0,
        0,
        axis_index_groups=[
            [c * column_rows + p for c in COLUMN_ORDER] for p in range(column_rows)
        ],
        tiled=True,
    )

    gain = jnp.broadcast_to(
        jnp.pad(norm_gain, (0, PADDED - CHANNELS))[:, None], (PADDED, BLOCK)
    )
    first_taps, second_taps = tap_matrix(first_kernel), tap_matrix(second_kernel)
    same, nexts, gain, first_taps, second_taps = lax.optimization_barrier(
        (same, nexts, gain, first_taps, second_taps)
    )
    gridded, normed, upward, downward, strip = gather_rows(
        column_rows, edge_flip, gain, same, nexts
    )
    rims = [from_shift(downward, -1), from_shift(upward, 1)]
    near, far, reach = strip_plan(column_rows)
    strips = [from_shift(strip, shift) for shift in near]
    inner = inner_convolution(first_taps, normed)
    held = {-1: rims[0][2], 0: strip, 1: rims[1][2], **dict(zip(near, strips))}
    pack = jnp.stack([held[at] for at in range(-reach, reach + 1)])
    gridded_out = channels_first(gridded)
    pack, inner, gridded_out = lax.optimization_barrier((pack, inner, gridded_out))
    strips += [from_shift(pack, -far), from_shift(pack, far)]
    hidden, *unfinished = inner
    base = inner_second_convolution(second_taps, hidden, gridded)
    smoothed = convolutions(
        column_rows, first_taps, second_taps, normed, base, *unfinished, *rims, strip, *strips
    )

    def placed(value):
        return value.reshape(CHANNELS, ROWS, BLOCK).transpose(1, 0, 2)[:, None]

    return placed(gridded_out), placed(smoothed)


def solution(mesh):
    in_specs = (
        P("tile", "groups", None, None),
        P("tile", None, None),
        P("tile"),
        P("tile"),
        P("tile", None),
        P(),
        P(),
        P(),
    )
    out_specs = (P("tile", "groups", None, None), P("tile", "groups", None, None))
    return jax.shard_map(
        per_device, mesh=mesh, in_specs=in_specs, out_specs=out_specs, check_vma=False
    )
```

```python
import functools

import jax
import jax.numpy as jnp
from jax import lax
from jax.experimental import pallas as pl
from jax.experimental.pallas import tpu as pltpu
from jax.sharding import PartitionSpec as P

BLOCK = 128
CHANNELS = 69
PADDED = 72
WIDE = 80
ROWS = 32
ROW_BITS = 5
HALF_ROWS = ROWS // 2
TILE_COLS = 8
CAP = 8
HALF = TILE_COLS // 2
GROUPS = 2 * TILE_COLS
COLUMN_ORDER = [half * HALF + at for at in range(HALF) for half in range(2)]
SLOTS = GROUPS * CAP
MARK = CHANNELS
BODY = 64
TAILS = (MARK + 1 - BODY) * CAP
MESSAGE = CAP * BODY + TAILS
EPSILON = 1e-05
VMEM_LIMIT = 40 * 1024 * 1024
REGRID_VMEM = 60 * 1024 * 1024


def vmem():
    return pl.BlockSpec(memory_space=pltpu.VMEM)


def smem():
    return pl.BlockSpec(memory_space=pltpu.SMEM)


def split(value, size):
    if size & (size - 1) == 0:
        return value >> (size.bit_length() - 1), value & (size - 1)
    return lax.div(value, size), lax.rem(value, size)


def lanes(shape):
    return lax.broadcasted_iota(jnp.int32, shape, len(shape) - 1)


def regrid_kernel(
    column_rows, target_hbm, index_hbm, source_hbm, weight_hbm, *rest
):
    same_out, next_outs = rest[0], rest[1 : 1 + TILE_COLS]
    (
        target_ref,
        index_ref,
        source,
        weight,
        wide,
        field,
        sums,
        message,
        tails,
        plan,
        plan_scalars,
        plan_sem,
        in_sems,
        out_sems,
    ) = rest[1 + TILE_COLS :]
    entries = weight.shape[0]
    tile = lax.axis_index("tile")
    column, position = split(tile, column_rows)

    target_copy = pltpu.make_async_copy(target_hbm, target_ref, in_sems.at[0])
    source_copy = pltpu.make_async_copy(source_hbm, source, in_sems.at[1])
    index_copy = pltpu.make_async_copy(index_hbm, index_ref, in_sems.at[2])
    target_copy.start()
    source_copy.start()
    index_copy.start()
    weight_copy = pltpu.make_async_copy(weight_hbm, weight, in_sems.at[3])
    weight_copy.start()

    target_copy.wait()
    target = target_ref[...]
    owner, row = split(target, ROWS)
    owner_column, owner_position = split(owner, column_rows)
    place = ((owner_column & (HALF - 1)) << 1) + (owner_column >= HALF).astype(jnp.int32)
    group = jnp.where(owner_position == position, place, TILE_COLS + (owner_column ^ column))
    key = group * ROWS + row
    square = (entries, entries)
    down = lax.broadcasted_iota(jnp.int32, square, 0)
    along = lanes(square)
    key_along = jnp.broadcast_to(key.astype(jnp.float32), square)
    key_down = jnp.broadcast_to(
        jnp.sum(jnp.where(down == along, key_along, 0.0), axis=1, keepdims=True), square
    )
    equal = key_along == key_down
    doubles = jnp.sum(jnp.where(equal & (along < down), 1.0, 0.0), axis=1, keepdims=True)
    in_group = (key_down.astype(jnp.int32) >> ROW_BITS) == (key_along.astype(jnp.int32) >> ROW_BITS)
    below = in_group & (key_down < key_along) & (jnp.broadcast_to(doubles, square) == 0.0)
    rank = jnp.sum(jnp.where(below, 1.0, 0.0), axis=0, keepdims=True)
    mentions = jnp.sum(jnp.where(equal & (down < along), 1.0, 0.0), axis=0, keepdims=True)
    slots = group * CAP + rank.astype(jnp.int32)
    plan[...] = slots + jnp.where(mentions == 0.0, SLOTS, 0) + row * (2 * SLOTS)
    plan_copy = pltpu.make_async_copy(plan, plan_scalars, plan_sem)
    plan_copy.start()

    for slot in range(SLOTS):
        tails[pl.ds(slot * 8, 8), :] = jnp.full((8, BLOCK), ROWS, jnp.float32)
    wide[pl.ds(CHANNELS * ROWS, (PADDED - CHANNELS) * ROWS), :] = jnp.zeros(
        ((PADDED - CHANNELS) * ROWS, BLOCK), jnp.float32
    )
    nothing = jnp.zeros((WIDE - PADDED, BLOCK), jnp.float32)
    source_copy.wait()
    wide[pl.ds(0, CHANNELS * ROWS), :] = source[...].astype(jnp.float32)
    for row in range(ROWS):
        block = wide[pl.ds(row, PADDED, stride=ROWS), :]
        field[row] = jnp.concatenate([block, nothing], axis=0).astype(jnp.bfloat16)
    is_mark = lax.broadcasted_iota(jnp.int32, (8, BLOCK), 0) == MARK - BODY
    blank = jnp.zeros((WIDE, BLOCK), jnp.bfloat16)
    index_copy.wait()
    plan_copy.wait()

    weight_copy.wait()
    for entry in range(0, entries, 2):
        one = jnp.concatenate([field[index_ref[entry]], blank], axis=1)
        two = jnp.concatenate([blank, field[index_ref[entry + 1]]], axis=1)
        products = jnp.dot(
            jnp.concatenate([one, two], axis=0),
            weight[entry : entry + 2].reshape(2 * BLOCK, BLOCK),
            preferred_element_type=jnp.float32,
        )
        for at in range(2):
            code = plan_scalars[0, entry + at]
            slot = code & (SLOTS - 1)
            fresh = (code & SLOTS) != 0
            product = products[at * WIDE : at * WIDE + PADDED]
            total = jnp.where(fresh, 0.0, sums[slot]) + product
            sums[slot] = total
            group, place = split(slot, CAP)
            message[group, pl.ds(pl.multiple_of(place * BODY, BODY), BODY), :] = total[
                :BODY
            ].astype(jnp.bfloat16)
            tails[pl.ds(pl.multiple_of(slot * 8, 8), 8), :] = jnp.where(
                is_mark, split(code, 2 * SLOTS)[0].astype(jnp.float32), total[BODY:]
            )
    copies = []
    for group in range(GROUPS):
        start = group * CAP * 8
        ends = [tails[pl.ds(start + at, CAP, stride=8), :] for at in range(MARK + 1 - BODY)]
        message[group, CAP * BODY :] = jnp.concatenate(ends, axis=0).astype(jnp.bfloat16)
        if group == TILE_COLS - 1:
            source_part, out = message.at[pl.ds(0, TILE_COLS)], same_out
        elif group >= TILE_COLS:
            source_part, out = message.at[group], next_outs[group - TILE_COLS]
        else:
            continue
        copies.append(pltpu.make_async_copy(source_part, out, out_sems.at[len(copies)]))
        copies[-1].start()
    for copy in copies:
        copy.wait()


def regrid(target, source_index, field, weights, column_rows):
    piece = jax.ShapeDtypeStruct((MESSAGE, BLOCK), jnp.bfloat16)
    same = jax.ShapeDtypeStruct((TILE_COLS, MESSAGE, BLOCK), jnp.bfloat16)
    hbm = pl.BlockSpec(memory_space=pl.ANY)
    entries = weights.shape[0]
    return pl.pallas_call(
        functools.partial(regrid_kernel, column_rows),
        in_specs=[hbm] * 4,
        out_specs=[hbm] * (1 + TILE_COLS),
        out_shape=[same] + [piece] * TILE_COLS,
        scratch_shapes=[
            pltpu.VMEM((1, entries), jnp.int32),
            pltpu.SMEM(source_index.shape, jnp.int32),
            pltpu.VMEM(field.shape, jnp.bfloat16),
            pltpu.VMEM(weights.shape, jnp.bfloat16),
            pltpu.VMEM((PADDED * ROWS, BLOCK), jnp.float32),
            pltpu.VMEM((ROWS, WIDE, BLOCK), jnp.bfloat16),
            pltpu.VMEM((SLOTS, PADDED, BLOCK), jnp.float32),
            pltpu.VMEM((GROUPS, MESSAGE, BLOCK), jnp.bfloat16),
            pltpu.VMEM((SLOTS * 8, BLOCK), jnp.float32),
            pltpu.VMEM((1, entries), jnp.int32),
            pltpu.SMEM((1, entries), jnp.int32),
            pltpu.SemaphoreType.DMA,
            pltpu.SemaphoreType.DMA((4,)),
            pltpu.SemaphoreType.DMA((1 + TILE_COLS,)),
        ],
        compiler_params=pltpu.CompilerParams(vmem_limit_bytes=REGRID_VMEM),
        name="regrid",
    )(target.reshape(1, -1), source_index, field, weights)


def gather_kernel(column_rows, flip_ref, gain_ref, same, *rest):
    nexts = rest[:TILE_COLS]
    (
        gridded,
        normed,
        upward,
        downward,
        strip_out,
        summed,
        tails,
    ) = rest[TILE_COLS:]
    position = lax.rem(lax.axis_index("tile"), column_rows)
    summed[...] = jnp.zeros_like(summed)

    def add(group, piece):
        ends = piece[CAP * BODY :].astype(jnp.float32)
        tails[group, :TAILS] = ends
        rows = ends[TAILS - CAP :].astype(jnp.int32)
        for place in range(CAP):
            row = rows[place, 0]
            body = piece[place * BODY : (place + 1) * BODY].astype(jnp.float32)
            summed[row, :BODY] = summed[row, :BODY] + body
            tail = tails[group, pl.ds(place, 8, stride=CAP), :]
            summed[row, BODY:] = summed[row, BODY:] + tail

    tails[:, TAILS:] = jnp.zeros((GROUPS, 8 * CAP - TAILS, BLOCK), jnp.float32)
    for group in range(TILE_COLS):
        add(group, same.at[group])

    @pl.when(position > 0)
    def _():
        for group in range(TILE_COLS):
            add(TILE_COLS + group, nexts[group])

    gain = gain_ref[...]
    real = lax.broadcasted_iota(jnp.int32, (PADDED - BODY, BLOCK), 0) < CHANNELS - BODY
    nothing = jnp.zeros((WIDE - PADDED, BLOCK), jnp.float32)
    lane = lanes((WIDE, BLOCK))
    strip = jnp.zeros((WIDE, BLOCK), jnp.bfloat16)
    for row in range(ROWS):
        rounded = summed[row].astype(jnp.bfloat16)
        gridded[row] = rounded
        value = rounded.astype(jnp.float32)
        value = jnp.concatenate([value[:BODY], jnp.where(real, value[BODY:], 0.0)], axis=0)
        square = jnp.sum(value * value, axis=0, keepdims=True) * (1.0 / CHANNELS)
        scaled = value * lax.rsqrt(square + EPSILON) * gain
        scaled = jnp.concatenate([scaled, nothing], axis=0).astype(jnp.bfloat16)
        normed[row] = scaled
        if row < 2:
            upward[row] = scaled
        if row >= ROWS - 2:
            downward[row - ROWS + 2] = scaled
        strip = jnp.where((lane >> 2) == row, pltpu.roll(scaled, 4 * row + 2, 1), strip)
    to_lane = lanes((BLOCK, BLOCK))
    from_lane = 4 * (to_lane & (ROWS - 1)) + (((to_lane >> ROW_BITS) + 2) & 3)
    order = lax.broadcasted_iota(jnp.int32, (BLOCK, BLOCK), 0) == from_lane
    strip = jnp.dot(strip, order.astype(jnp.bfloat16), preferred_element_type=jnp.float32)
    channel = lax.broadcasted_iota(jnp.int32, (WIDE, BLOCK), 0)
    for side in range(2):
        strip = jnp.where(channel == CHANNELS + side, flip_ref[0, side].astype(jnp.float32), strip)
    strip = strip.astype(jnp.bfloat16)
    upward[2] = strip
    downward[2] = strip
    strip_out[...] = strip


GRIDDED = jax.ShapeDtypeStruct((ROWS, PADDED, BLOCK), jnp.bfloat16)
FIELD = jax.ShapeDtypeStruct((ROWS, WIDE, BLOCK), jnp.bfloat16)
RIM = jax.ShapeDtypeStruct((3, WIDE, BLOCK), jnp.bfloat16)
STRIP_COLUMNS = (0, 1, BLOCK - 2, BLOCK - 1)
STRIP = jax.ShapeDtypeStruct((WIDE, BLOCK), jnp.bfloat16)


def gather_rows(column_rows, edge_flip, gain, same, nexts):
    return pl.pallas_call(
        functools.partial(gather_kernel, column_rows),
        in_specs=[smem()] + [vmem()] * (2 + TILE_COLS),
        out_specs=[vmem()] * 5,
        out_shape=[GRIDDED, FIELD, RIM, RIM, STRIP],
        scratch_shapes=[
            pltpu.VMEM((ROWS + 1, PADDED, BLOCK), jnp.float32),
            pltpu.VMEM((GROUPS, 8 * CAP, BLOCK), jnp.float32),
        ],
        compiler_params=pltpu.CompilerParams(vmem_limit_bytes=VMEM_LIMIT),
        name="gather_rows",
    )(edge_flip, gain, same, *nexts)


def turn_kernel(field, out, turned):
    for row in range(ROWS):
        turned[pl.ds(row, PADDED, stride=ROWS), :] = field[row].astype(jnp.float32)
    out[...] = turned[pl.ds(0, CHANNELS * ROWS), :].astype(jnp.bfloat16)


def channels_first(field):
    return pl.pallas_call(
        turn_kernel,
        in_specs=[vmem()],
        out_specs=vmem(),
        out_shape=jax.ShapeDtypeStruct((CHANNELS * ROWS, BLOCK), jnp.bfloat16),
        scratch_shapes=[pltpu.VMEM((PADDED * ROWS, BLOCK), jnp.float32)],
        compiler_params=pltpu.CompilerParams(vmem_limit_bytes=VMEM_LIMIT),
        name="channels_first",
    )(field)


def shifted_columns(value, left_end, right_end):
    lane = lanes((WIDE, BLOCK))
    left = jnp.where(lane == 0, left_end, pltpu.roll(value, 1, 1))
    right = jnp.where(lane == BLOCK - 1, right_end, pltpu.roll(value, BLOCK - 1, 1))
    return jnp.concatenate([left, value, right], axis=0)


def tap_sums(taps, one, two):
    both = jnp.concatenate([one, two], axis=1)
    result = jnp.dot(taps, both, preferred_element_type=jnp.float32)
    return result[:, :BLOCK], result[:, BLOCK:]


def row_tap(sums, at):
    return sums[at * WIDE : (at + 1) * WIDE]


def activated(value):
    return jax.nn.gelu(value).astype(jnp.bfloat16)


def inner_kernel(taps_ref, field, hidden, ends, sides, partial):
    taps = taps_ref[...]
    blank = jnp.zeros((WIDE, BLOCK), jnp.bfloat16)
    for row in range(0, ROWS, 2):
        partial[row], partial[row + 1] = tap_sums(
            taps,
            shifted_columns(field[row], blank, blank),
            shifted_columns(field[row + 1], blank, blank),
        )
    lane = lanes((WIDE, BLOCK))
    west = jnp.zeros((WIDE, BLOCK), jnp.float32)
    east = jnp.zeros((WIDE, BLOCK), jnp.float32)
    for row in range(ROWS):
        value = partial[row, WIDE : 2 * WIDE]
        if row > 0:
            value = value + partial[row - 1, :WIDE]
        if row < ROWS - 1:
            value = value + partial[row + 1, 2 * WIDE :]
        if row == 0:
            ends[0] = value
        elif row == ROWS - 1:
            ends[1] = value
        else:
            hidden[row] = jnp.where((lane == 0) | (lane == BLOCK - 1), blank, activated(value))
        west = jnp.where(lane == row, pltpu.roll(value, row, 1), west)
        east = jnp.where(lane == row, pltpu.roll(value, row + 1, 1), east)
    hidden[0] = blank
    hidden[ROWS - 1] = blank
    sides[0] = west
    sides[1] = east


def inner_convolution(taps, field):
    pair = jax.ShapeDtypeStruct((2, WIDE, BLOCK), jnp.float32)
    return pl.pallas_call(
        inner_kernel,
        in_specs=[vmem()] * 2,
        out_specs=[vmem()] * 3,
        out_shape=[FIELD, pair, pair],
        scratch_shapes=[pltpu.VMEM((ROWS, 3 * WIDE, BLOCK), jnp.float32)],
        compiler_params=pltpu.CompilerParams(vmem_limit_bytes=VMEM_LIMIT),
        cost_estimate=pl.CostEstimate(
            flops=2 * 9 * WIDE * WIDE * ROWS * BLOCK, bytes_accessed=2 << 20, transcendentals=0
        ),
        name="inner_convolution",
    )(taps, field)


def second_kernel_inner(taps_ref, hidden, gridded, base, partial):
    taps = taps_ref[...]
    blank = jnp.zeros((WIDE, BLOCK), jnp.bfloat16)
    for row in range(0, ROWS, 2):
        partial[row], partial[row + 1] = tap_sums(
            taps,
            shifted_columns(hidden[row], blank, blank),
            shifted_columns(hidden[row + 1], blank, blank),
        )
    for row in range(ROWS):
        value = gridded[row].astype(jnp.float32) + partial[row, WIDE : WIDE + PADDED]
        if row > 0:
            value = value + partial[row - 1, :PADDED]
        if row < ROWS - 1:
            value = value + partial[row + 1, 2 * WIDE : 2 * WIDE + PADDED]
        base[row] = value


def inner_second_convolution(taps, hidden, gridded):
    return pl.pallas_call(
        second_kernel_inner,
        in_specs=[vmem()] * 3,
        out_specs=vmem(),
        out_shape=jax.ShapeDtypeStruct((ROWS, PADDED, BLOCK), jnp.float32),
        scratch_shapes=[pltpu.VMEM((ROWS, 3 * WIDE, BLOCK), jnp.float32)],
        compiler_params=pltpu.CompilerParams(vmem_limit_bytes=VMEM_LIMIT),
        cost_estimate=pl.CostEstimate(
            flops=2 * 9 * WIDE * WIDE * ROWS * BLOCK, bytes_accessed=2 << 20, transcendentals=0
        ),
        name="inner_second_convolution",
    )(taps, hidden, gridded)


def strip_plan(column_rows):
    if column_rows == 2:
        return [], 3, 1
    return [-2, 2], column_rows, 2


def conv_kernel(
    column_rows,
    first_taps_ref,
    second_taps_ref,
    field,
    base,
    ends_ref,
    sides_ref,
    above,
    below,
    own_strip,
    *rest,
):
    near, far, reach = strip_plan(column_rows)
    near_strips, (west_pack, east_pack) = rest[: len(near)], rest[len(near) : len(near) + 2]
    smoothed, turned, halves, sems = rest[len(near) + 2 :]
    count = lax.axis_size("tile")
    tile = lax.axis_index("tile")
    lane = lanes((WIDE, BLOCK))
    last = ROWS + 1
    R = column_rows
    blank = jnp.zeros((WIDE, BLOCK), jnp.bfloat16)

    strips = {-1: above[2], 0: own_strip[...], 1: below[2]}
    strips.update((shift, ref[...]) for shift, ref in zip(near, near_strips))
    for at in range(-reach, reach + 1):
        strips[at - far], strips[at + far] = west_pack[at + reach], east_pack[at + reach]

    def place(shift):
        return lax.rem(tile + shift + count, count)

    def ends(shift, before, after, middle):
        before = jnp.where(place(shift) > 0, before, blank)
        after = jnp.where(place(shift) < count - 1, after, blank)
        return jnp.where(lane == 0, before, jnp.where(lane == last, after, middle))

    memo = {}

    def padded_column(shift, which):
        if (shift, which) not in memo:
            base = which * ROWS
            memo[shift, which] = ends(
                shift,
                pltpu.roll(strips[shift - 1], (1 - base - ROWS) % BLOCK, 1),
                pltpu.roll(strips[shift + 1], (last - base) % BLOCK, 1),
                pltpu.roll(strips[shift], (1 - base) % BLOCK, 1),
            )
        return memo[shift, which]

    row_id = lax.broadcasted_iota(jnp.int32, (BLOCK, BLOCK), 0)
    reversal = (row_id + lanes((BLOCK, BLOCK)) == last).astype(jnp.bfloat16)

    def reversed_lanes(planes):
        stacked = jnp.concatenate(planes, axis=0)
        turned_round = jnp.dot(stacked, reversal, preferred_element_type=jnp.float32)
        return [row_tap(turned_round, at) for at in range(len(planes))]

    def choose(shift, which, turned_round, plain):
        flips = strips[shift].astype(jnp.float32)[CHANNELS + which : CHANNELS + which + 1]
        return jnp.where(flips > 0.5, turned_round, plain.astype(jnp.float32)).astype(jnp.bfloat16)

    west_of = {shift: (shift - R, 3) for shift in {-1, 0, 1, R - 1, R, R + 1}}
    east_of = {shift: (shift + R, 0) for shift in {-1, 0, 1, -R - 1, -R, -R + 1}}
    keys = sorted(set(west_of.values()) | set(east_of.values()))
    flipped = dict(zip(keys, reversed_lanes([padded_column(*key) for key in keys])))
    west = {
        shift: choose(shift, 0, flipped[west_of[shift]], padded_column(*west_of[shift]))
        for shift in sorted(west_of)
    }
    east = {
        shift: choose(shift, 1, flipped[east_of[shift]], padded_column(*east_of[shift]))
        for shift in sorted(east_of)
    }

    def columns(value, west_plane, west_row, east_plane, east_row):
        return shifted_columns(
            value,
            pltpu.roll(west_plane, (BLOCK - west_row) % BLOCK, 1),
            pltpu.roll(east_plane, BLOCK - 1 - east_row, 1),
        )

    def along(result):
        return (
            row_tap(result, 0)
            + pltpu.roll(row_tap(result, 1), BLOCK - 1, 1)
            + pltpu.roll(row_tap(result, 2), BLOCK - 2, 1)
        )

    first_taps = first_taps_ref[...]
    up = [jnp.where(tile > 0, above[at], blank) for at in range(2)]
    down = [jnp.where(tile < count - 1, below[at], blank) for at in range(2)]
    from_up, from_down = tap_sums(
        first_taps, shifted_columns(up[1], blank, blank), shifted_columns(down[0], blank, blank)
    )
    from_up, from_down = row_tap(from_up, 0), row_tap(from_down, 2)
    from_west, from_east = tap_sums(
        first_taps,
        jnp.concatenate([west[0], blank, blank], axis=0),
        jnp.concatenate([blank, blank, east[0]], axis=0),
    )
    from_west, from_east = along(from_west), along(from_east)
    first = ends_ref[0] + from_up
    first = first + jnp.where(lane == 0, from_west, 0.0)
    first = first + jnp.where(lane == BLOCK - 1, pltpu.roll(from_east, BLOCK - 1, 1), 0.0)
    final = ends_ref[1] + from_down
    final = final + jnp.where(lane == 0, pltpu.roll(from_west, BLOCK - ROWS + 1, 1), 0.0)
    final = final + jnp.where(lane == BLOCK - 1, pltpu.roll(from_east, BLOCK - ROWS, 1), 0.0)
    first, final = activated(first), activated(final)
    first_column = activated(sides_ref[0] + from_west)
    last_column = activated(sides_ref[1] + from_east)

    upper = jnp.zeros((WIDE, BLOCK), jnp.float32)
    lower = jnp.zeros((WIDE, BLOCK), jnp.float32)
    for at, (high, low) in enumerate(
        [(up[0], field[ROWS - 1]), (up[1], down[0]), (field[0], down[1])]
    ):
        from_row = ROWS - 1 + at
        one, two = tap_sums(
            row_tap(first_taps, at),
            columns(high, west[-1], from_row, east[-1], from_row),
            columns(low, west[1], at, east[1], at),
        )
        upper += one
        lower += two
    top = jnp.where(tile > 0, activated(upper), blank)
    bottom = jnp.where(tile < count - 1, activated(lower), blank)

    west_hidden, east_hidden = {}, {}
    for at in (-1, 0, 1):
        q = at - R
        one = jnp.concatenate([padded_column(q, 2), padded_column(q, 3), east[q]], axis=0)
        q = at + R
        two = jnp.concatenate([west[q], padded_column(q, 0), padded_column(q, 1)], axis=0)
        one, two = tap_sums(first_taps, one, two)
        west_hidden[at], east_hidden[at] = activated(along(one)), activated(along(two))

    def hidden_side(shift, values):
        return ends(
            shift,
            pltpu.roll(values[-1], BLOCK - ROWS + 1, 1),
            pltpu.roll(values[1], last, 1),
            pltpu.roll(values[0], 1, 1),
        )

    plain = [hidden_side(-R, west_hidden), hidden_side(R, east_hidden)]
    west_side, east_side = [
        choose(0, which, turned_side, plain[which])
        for which, turned_side in enumerate(reversed_lanes(plain))
    ]

    second_taps = second_taps_ref[...]
    from_top, from_first = tap_sums(
        second_taps,
        columns(top, west_side, 0, east_side, 0),
        columns(first, west_side, 1, east_side, 1),
    )
    from_final, from_bottom = tap_sums(
        second_taps,
        columns(final, west_side, ROWS, east_side, ROWS),
        columns(bottom, west_side, last, east_side, last),
    )
    rim_rows = {
        0: row_tap(from_top, 0) + row_tap(from_first, 1),
        1: row_tap(from_first, 0),
        ROWS - 2: row_tap(from_final, 2),
        ROWS - 1: row_tap(from_final, 1) + row_tap(from_bottom, 2),
    }

    other = (lane >= 2) & (lane < ROWS)

    def other_rows(plane):
        return jnp.where(other, plane, blank)

    near_west, near_east = other_rows(west_side), other_rows(east_side)
    first_column = other_rows(pltpu.roll(first_column, 1, 1))
    last_column = other_rows(pltpu.roll(last_column, 1, 1))
    to_0, to_1 = tap_sums(
        second_taps,
        jnp.concatenate([near_west, first_column, blank], axis=0),
        jnp.concatenate([first_column, blank, blank], axis=0),
    )
    to_127, to_126 = tap_sums(
        second_taps,
        jnp.concatenate([blank, last_column, near_east], axis=0),
        jnp.concatenate([blank, blank, last_column], axis=0),
    )
    spread = jnp.zeros((WIDE, BLOCK), jnp.float32)
    for at, sums in enumerate((to_126, to_127, to_0, to_1)):
        sums = along(sums)
        high = sums.astype(jnp.bfloat16)
        sums = sums - high.astype(jnp.float32)
        middle = sums.astype(jnp.bfloat16)
        low = (sums - middle.astype(jnp.float32)).astype(jnp.bfloat16)
        to_lane = (lanes((BLOCK, BLOCK)) == 4 * row_id + at).astype(jnp.bfloat16)
        parts = jnp.dot(
            jnp.concatenate([high, middle, low], axis=0),
            to_lane,
            preferred_element_type=jnp.float32,
        )
        spread = spread + (row_tap(parts, 0) + (row_tap(parts, 1) + row_tap(parts, 2)))

    rim_lanes = lanes((PADDED, BLOCK))
    rim_lanes = (rim_lanes < 2) | (rim_lanes >= BLOCK - 2)
    spread = spread[:PADDED]
    copies = []
    for half in range(2):
        for row in range(half * HALF_ROWS, (half + 1) * HALF_ROWS):
            value = base[row] + jnp.where(
                rim_lanes, pltpu.roll(spread, (BLOCK - 4 * row - 2) % BLOCK, 1), 0.0
            )
            if row in rim_rows:
                value = value + rim_rows[row][:PADDED]
            turned[half, pl.ds(row - half * HALF_ROWS, PADDED, stride=HALF_ROWS), :] = value
        rounded = turned[half, pl.ds(0, CHANNELS * HALF_ROWS), :].astype(jnp.bfloat16)
        halves[half] = rounded.reshape(CHANNELS, HALF_ROWS, BLOCK)
        rows = pl.ds(half * HALF_ROWS, HALF_ROWS)
        copies.append(pltpu.make_async_copy(halves.at[half], smoothed.at[:, rows], sems.at[half]))
        copies[-1].start()
    for copy in copies:
        copy.wait()


def convolutions(column_rows, *operands):
    return pl.pallas_call(
        functools.partial(conv_kernel, column_rows),
        in_specs=[vmem()] * len(operands),
        out_specs=pl.BlockSpec(memory_space=pl.ANY),
        out_shape=jax.ShapeDtypeStruct((CHANNELS, ROWS, BLOCK), jnp.bfloat16),
        scratch_shapes=[
            pltpu.VMEM((2, PADDED * HALF_ROWS, BLOCK), jnp.float32),
            pltpu.VMEM((2, CHANNELS, HALF_ROWS, BLOCK), jnp.bfloat16),
            pltpu.SemaphoreType.DMA((2,)),
        ],
        compiler_params=pltpu.CompilerParams(vmem_limit_bytes=VMEM_LIMIT),
        name="convolutions",
    )(*operands)


def tap_matrix(kernel):
    pad = WIDE - CHANNELS
    taps = jnp.pad(kernel, ((0, 0), (0, pad), (0, pad))).reshape(3, 3, WIDE, WIDE)
    return taps.transpose(0, 2, 1, 3).reshape(3 * WIDE, 3 * WIDE)


def from_shift(value, shift):
    count = lax.axis_size("tile")
    return lax.ppermute(value, "tile", [(i, (i - shift) % count) for i in range(count)])


def per_device(
    source, weights, block_source, block_target, edge_flip, norm_gain, first_kernel, second_kernel
):
    count = lax.axis_size("tile")
    column_rows = count // TILE_COLS
    field = source.reshape(ROWS, CHANNELS, BLOCK).transpose(1, 0, 2).reshape(-1, BLOCK)
    same, *nexts = regrid(block_target, block_source, field, weights, column_rows)

    for across in range(TILE_COLS):
        pairs = [
            (c * column_rows + p, (c ^ across) * column_rows + p + 1)
            for c in range(TILE_COLS)
            for p in range(column_rows - 1)
        ]
        nexts[across] = lax.ppermute(nexts[across], "tile", pairs)
    nexts = [nexts[across] for across in (0, 1, 2, 4, 5, 6, 7, 3)]
    same = lax.all_to_all(
        same,
        "tile",
        0,
        0,
        axis_index_groups=[
            [c * column_rows + p for c in COLUMN_ORDER] for p in range(column_rows)
        ],
        tiled=True,
    )

    gain = jnp.broadcast_to(
        jnp.pad(norm_gain, (0, PADDED - CHANNELS))[:, None], (PADDED, BLOCK)
    )
    first_taps, second_taps = tap_matrix(first_kernel), tap_matrix(second_kernel)
    same, nexts, gain, first_taps, second_taps = lax.optimization_barrier(
        (same, nexts, gain, first_taps, second_taps)
    )
    gridded, normed, upward, downward, strip = gather_rows(
        column_rows, edge_flip, gain, same, nexts
    )
    rims = [from_shift(downward, -1), from_shift(upward, 1)]
    near, far, reach = strip_plan(column_rows)
    strips = [from_shift(strip, shift) for shift in near]
    inner = inner_convolution(first_taps, normed)
    held = {-1: rims[0][2], 0: strip, 1: rims[1][2], **dict(zip(near, strips))}
    pack = jnp.stack([held[at] for at in range(-reach, reach + 1)])
    gridded_out = channels_first(gridded)
    pack, inner, gridded_out = lax.optimization_barrier((pack, inner, gridded_out))
    strips += [from_shift(pack, -far), from_shift(pack, far)]
    hidden, *unfinished = inner
    base = inner_second_convolution(second_taps, hidden, gridded)
    smoothed = convolutions(
        column_rows, first_taps, second_taps, normed, base, *unfinished, *rims, strip, *strips
    )

    def placed(value):
        return value.reshape(CHANNELS, ROWS, BLOCK).transpose(1, 0, 2)[:, None]

    return placed(gridded_out), placed(smoothed)


def solution(mesh):
    in_specs = (
        P("tile", "groups", None, None),
        P("tile", None, None),
        P("tile"),
        P("tile"),
        P("tile", None),
        P(),
        P(),
        P(),
    )
    out_specs = (P("tile", "groups", None, None), P("tile", "groups", None, None))
    return jax.shard_map(
        per_device, mesh=mesh, in_specs=in_specs, out_specs=out_specs, check_vma=False
    )
```

```python
import functools

import jax
import jax.numpy as jnp
from jax import lax
from jax.experimental import pallas as pl
from jax.experimental.pallas import tpu as pltpu
from jax.sharding import PartitionSpec as P

BLOCK = 128
CHANNELS = 69
PADDED = 72
WIDE = 80
ROWS = 32
ROW_BITS = 5
HALF_ROWS = ROWS // 2
TILE_COLS = 8
CAP = 8
HALF = TILE_COLS // 2
GROUPS = 2 * TILE_COLS
COLUMN_ORDER = [half * HALF + at for at in range(HALF) for half in range(2)]
SLOTS = GROUPS * CAP
MARK = CHANNELS
BODY = 64
TAILS = (MARK + 1 - BODY) * CAP
MESSAGE = CAP * BODY + TAILS
SOURCE_PARTS = 3
SOURCE_ROWS = CHANNELS * ROWS // SOURCE_PARTS
EPSILON = 1e-05
VMEM_LIMIT = 40 * 1024 * 1024
REGRID_VMEM = 60 * 1024 * 1024


def vmem():
    return pl.BlockSpec(memory_space=pltpu.VMEM)


def smem():
    return pl.BlockSpec(memory_space=pltpu.SMEM)


def split(value, size):
    if size & (size - 1) == 0:
        return value >> (size.bit_length() - 1), value & (size - 1)
    return lax.div(value, size), lax.rem(value, size)


def lanes(shape):
    return lax.broadcasted_iota(jnp.int32, shape, len(shape) - 1)


def regrid_kernel(
    column_rows, target_hbm, index_hbm, source_hbm, weight_hbm, *rest
):
    same_out, next_outs = rest[0], rest[1 : 1 + TILE_COLS]
    (
        target_ref,
        index_ref,
        source,
        weight,
        wide,
        field,
        sums,
        message,
        tails,
        plan,
        plan_scalars,
        plan_sem,
        in_sems,
        out_sems,
    ) = rest[1 + TILE_COLS :]
    entries = weight.shape[0]
    tile = lax.axis_index("tile")
    column, position = split(tile, column_rows)

    target_copy = pltpu.make_async_copy(target_hbm, target_ref, in_sems.at[0])
    index_copy = pltpu.make_async_copy(index_hbm, index_ref, in_sems.at[1])
    target_copy.start()
    source_copies = []
    for part in range(SOURCE_PARTS):
        rows = pl.ds(part * SOURCE_ROWS, SOURCE_ROWS)
        source_copies.append(
            pltpu.make_async_copy(source_hbm.at[rows], source.at[rows], in_sems.at[3 + part])
        )
        source_copies[-1].start()
    index_copy.start()
    weight_copy = pltpu.make_async_copy(weight_hbm, weight, in_sems.at[2])
    weight_copy.start()

    target_copy.wait()
    target = target_ref[...]
    owner, row = split(target, ROWS)
    owner_column, owner_position = split(owner, column_rows)
    place = ((owner_column & (HALF - 1)) << 1) + (owner_column >= HALF).astype(jnp.int32)
    group = jnp.where(owner_position == position, place, TILE_COLS + (owner_column ^ column))
    key = group * ROWS + row
    square = (entries, entries)
    down = lax.broadcasted_iota(jnp.int32, square, 0)
    along = lanes(square)
    key_along = jnp.broadcast_to(key.astype(jnp.float32), square)
    key_down = jnp.broadcast_to(
        jnp.sum(jnp.where(down == along, key_along, 0.0), axis=1, keepdims=True), square
    )
    equal = key_along == key_down
    doubles = jnp.sum(jnp.where(equal & (along < down), 1.0, 0.0), axis=1, keepdims=True)
    in_group = (key_down.astype(jnp.int32) >> ROW_BITS) == (key_along.astype(jnp.int32) >> ROW_BITS)
    below = in_group & (key_down < key_along) & (jnp.broadcast_to(doubles, square) == 0.0)
    rank = jnp.sum(jnp.where(below, 1.0, 0.0), axis=0, keepdims=True)
    mentions = jnp.sum(jnp.where(equal & (down < along), 1.0, 0.0), axis=0, keepdims=True)
    slots = group * CAP + rank.astype(jnp.int32)
    plan[...] = slots + jnp.where(mentions == 0.0, SLOTS, 0) + row * (2 * SLOTS)
    plan_copy = pltpu.make_async_copy(plan, plan_scalars, plan_sem)
    plan_copy.start()

    for slot in range(SLOTS):
        tails[pl.ds(slot * 8, 8), :] = jnp.full((8, BLOCK), ROWS, jnp.float32)
    wide[pl.ds(CHANNELS * ROWS, (PADDED - CHANNELS) * ROWS), :] = jnp.zeros(
        ((PADDED - CHANNELS) * ROWS, BLOCK), jnp.float32
    )
    nothing = jnp.zeros((WIDE - PADDED, BLOCK), jnp.float32)
    for part, copy in enumerate(source_copies):
        copy.wait()
        rows = pl.ds(part * SOURCE_ROWS, SOURCE_ROWS)
        wide[rows, :] = source[rows, :].astype(jnp.float32)
    for row in range(ROWS):
        block = wide[pl.ds(row, PADDED, stride=ROWS), :]
        field[row] = jnp.concatenate([block, nothing], axis=0).astype(jnp.bfloat16)
    is_mark = lax.broadcasted_iota(jnp.int32, (8, BLOCK), 0) == MARK - BODY
    blank = jnp.zeros((WIDE, BLOCK), jnp.bfloat16)
    index_copy.wait()
    plan_copy.wait()

    weight_copy.wait()
    for entry in range(0, entries, 2):
        one = jnp.concatenate([field[index_ref[entry]], blank], axis=1)
        two = jnp.concatenate([blank, field[index_ref[entry + 1]]], axis=1)
        products = jnp.dot(
            jnp.concatenate([one, two], axis=0),
            weight[entry : entry + 2].reshape(2 * BLOCK, BLOCK),
            preferred_element_type=jnp.float32,
        )
        for at in range(2):
            code = plan_scalars[0, entry + at]
            slot = code & (SLOTS - 1)
            fresh = (code & SLOTS) != 0
            product = products[at * WIDE : at * WIDE + PADDED]
            total = jnp.where(fresh, 0.0, sums[slot]) + product
            sums[slot] = total
            group, place = split(slot, CAP)
            message[group, pl.ds(pl.multiple_of(place * BODY, BODY), BODY), :] = total[
                :BODY
            ].astype(jnp.bfloat16)
            tails[pl.ds(pl.multiple_of(slot * 8, 8), 8), :] = jnp.where(
                is_mark, split(code, 2 * SLOTS)[0].astype(jnp.float32), total[BODY:]
            )
    copies = []
    for group in range(GROUPS):
        start = group * CAP * 8
        ends = [tails[pl.ds(start + at, CAP, stride=8), :] for at in range(MARK + 1 - BODY)]
        message[group, CAP * BODY :] = jnp.concatenate(ends, axis=0).astype(jnp.bfloat16)
        out = same_out.at[group] if group < TILE_COLS else next_outs[group - TILE_COLS]
        copies.append(pltpu.make_async_copy(message.at[group], out, out_sems.at[group]))
        copies[-1].start()
    for copy in copies:
        copy.wait()


def regrid(target, source_index, field, weights, column_rows):
    piece = jax.ShapeDtypeStruct((MESSAGE, BLOCK), jnp.bfloat16)
    same = jax.ShapeDtypeStruct((TILE_COLS, MESSAGE, BLOCK), jnp.bfloat16)
    hbm = pl.BlockSpec(memory_space=pl.ANY)
    entries = weights.shape[0]
    return pl.pallas_call(
        functools.partial(regrid_kernel, column_rows),
        in_specs=[hbm] * 4,
        out_specs=[hbm] * (1 + TILE_COLS),
        out_shape=[same] + [piece] * TILE_COLS,
        scratch_shapes=[
            pltpu.VMEM((1, entries), jnp.int32),
            pltpu.SMEM(source_index.shape, jnp.int32),
            pltpu.VMEM(field.shape, jnp.bfloat16),
            pltpu.VMEM(weights.shape, jnp.bfloat16),
            pltpu.VMEM((PADDED * ROWS, BLOCK), jnp.float32),
            pltpu.VMEM((ROWS, WIDE, BLOCK), jnp.bfloat16),
            pltpu.VMEM((SLOTS, PADDED, BLOCK), jnp.float32),
            pltpu.VMEM((GROUPS, MESSAGE, BLOCK), jnp.bfloat16),
            pltpu.VMEM((SLOTS * 8, BLOCK), jnp.float32),
            pltpu.VMEM((1, entries), jnp.int32),
            pltpu.SMEM((1, entries), jnp.int32),
            pltpu.SemaphoreType.DMA,
            pltpu.SemaphoreType.DMA((3 + SOURCE_PARTS,)),
            pltpu.SemaphoreType.DMA((GROUPS,)),
        ],
        compiler_params=pltpu.CompilerParams(vmem_limit_bytes=REGRID_VMEM),
        name="regrid",
    )(target.reshape(1, -1), source_index, field, weights)


def normalized(rounded, gain):
    value = rounded.astype(jnp.float32)
    real = lax.broadcasted_iota(jnp.int32, (PADDED - BODY, BLOCK), 0) < CHANNELS - BODY
    value = jnp.concatenate([value[:BODY], jnp.where(real, value[BODY:], 0.0)], axis=0)
    square = jnp.sum(value * value, axis=0, keepdims=True) * (1.0 / CHANNELS)
    scaled = value * lax.rsqrt(square + EPSILON) * gain
    nothing = jnp.zeros((WIDE - PADDED, BLOCK), jnp.float32)
    return jnp.concatenate([scaled, nothing], axis=0).astype(jnp.bfloat16)


def gather_kernel(column_rows, flip_ref, gain_ref, same, *rest):
    nexts = rest[:TILE_COLS]
    summed, upward, downward, strip_out, tails = rest[TILE_COLS:]
    position = lax.rem(lax.axis_index("tile"), column_rows)
    summed[...] = jnp.zeros_like(summed)

    def add(group, piece):
        ends = piece[CAP * BODY :].astype(jnp.float32)
        tails[group, :TAILS] = ends
        rows = ends[TAILS - CAP :].astype(jnp.int32)
        for place in range(CAP):
            row = rows[place, 0]
            body = piece[place * BODY : (place + 1) * BODY].astype(jnp.float32)
            summed[row, :BODY] = summed[row, :BODY] + body
            tail = tails[group, pl.ds(place, 8, stride=CAP), :]
            summed[row, BODY:] = summed[row, BODY:] + tail

    tails[:, TAILS:] = jnp.zeros((GROUPS, 8 * CAP - TAILS, BLOCK), jnp.float32)
    for group in range(TILE_COLS):
        add(group, same.at[group])

    @pl.when(position > 0)
    def _():
        for group in range(TILE_COLS):
            add(TILE_COLS + group, nexts[group])

    gain = gain_ref[...]
    for at in range(2):
        upward[at] = normalized(summed[at].astype(jnp.bfloat16), gain)
        downward[at] = normalized(summed[ROWS - 2 + at].astype(jnp.bfloat16), gain)
    lane = lanes((PADDED, BLOCK))
    strip = jnp.zeros((PADDED, BLOCK), jnp.bfloat16)
    for row in range(ROWS):
        rounded = summed[row].astype(jnp.bfloat16)
        strip = jnp.where((lane >> 2) == row, pltpu.roll(rounded, 4 * row + 2, 1), strip)
    to_lane = lanes((BLOCK, BLOCK))
    from_lane = 4 * (to_lane & (ROWS - 1)) + (((to_lane >> ROW_BITS) + 2) & 3)
    order = lax.broadcasted_iota(jnp.int32, (BLOCK, BLOCK), 0) == from_lane
    strip = jnp.dot(
        normalized(strip, gain), order.astype(jnp.bfloat16), preferred_element_type=jnp.float32
    )
    channel = lax.broadcasted_iota(jnp.int32, (WIDE, BLOCK), 0)
    for side in range(2):
        strip = jnp.where(channel == CHANNELS + side, flip_ref[0, side].astype(jnp.float32), strip)
    strip = strip.astype(jnp.bfloat16)
    upward[2] = strip
    downward[2] = strip
    strip_out[...] = strip


def normalize_kernel(gain_ref, summed, gridded, normed):
    gain = gain_ref[...]
    for row in range(ROWS):
        rounded = summed[row].astype(jnp.bfloat16)
        gridded[row] = rounded
        normed[row] = normalized(rounded, gain)


def normalize_rows(gain, summed):
    return pl.pallas_call(
        normalize_kernel,
        in_specs=[vmem()] * 2,
        out_specs=[vmem()] * 2,
        out_shape=[GRIDDED, FIELD],
        compiler_params=pltpu.CompilerParams(vmem_limit_bytes=VMEM_LIMIT),
        cost_estimate=pl.CostEstimate(
            flops=10 * ROWS * PADDED * BLOCK, bytes_accessed=2 << 20, transcendentals=0
        ),
        name="normalize_rows",
    )(gain, summed)


SUMMED = jax.ShapeDtypeStruct((ROWS + 1, PADDED, BLOCK), jnp.float32)
GRIDDED = jax.ShapeDtypeStruct((ROWS, PADDED, BLOCK), jnp.bfloat16)
FIELD = jax.ShapeDtypeStruct((ROWS, WIDE, BLOCK), jnp.bfloat16)
RIM = jax.ShapeDtypeStruct((3, WIDE, BLOCK), jnp.bfloat16)
STRIP_COLUMNS = (0, 1, BLOCK - 2, BLOCK - 1)
STRIP = jax.ShapeDtypeStruct((WIDE, BLOCK), jnp.bfloat16)


def gather_rows(column_rows, edge_flip, gain, same, nexts):
    return pl.pallas_call(
        functools.partial(gather_kernel, column_rows),
        in_specs=[smem()] + [vmem()] * (2 + TILE_COLS),
        out_specs=[vmem()] * 4,
        out_shape=[SUMMED, RIM, RIM, STRIP],
        scratch_shapes=[pltpu.VMEM((GROUPS, 8 * CAP, BLOCK), jnp.float32)],
        compiler_params=pltpu.CompilerParams(vmem_limit_bytes=VMEM_LIMIT),
        name="gather_rows",
    )(edge_flip, gain, same, *nexts)


def turn_kernel(field, out, turned):
    for row in range(ROWS):
        turned[pl.ds(row, PADDED, stride=ROWS), :] = field[row].astype(jnp.float32)
    out[...] = turned[pl.ds(0, CHANNELS * ROWS), :].astype(jnp.bfloat16)


def channels_first(field):
    return pl.pallas_call(
        turn_kernel,
        in_specs=[vmem()],
        out_specs=vmem(),
        out_shape=jax.ShapeDtypeStruct((CHANNELS * ROWS, BLOCK), jnp.bfloat16),
        scratch_shapes=[pltpu.VMEM((PADDED * ROWS, BLOCK), jnp.float32)],
        compiler_params=pltpu.CompilerParams(vmem_limit_bytes=VMEM_LIMIT),
        name="channels_first",
    )(field)


def shifted_columns(value, left_end, right_end):
    lane = lanes((WIDE, BLOCK))
    left = jnp.where(lane == 0, left_end, pltpu.roll(value, 1, 1))
    right = jnp.where(lane == BLOCK - 1, right_end, pltpu.roll(value, BLOCK - 1, 1))
    return jnp.concatenate([left, value, right], axis=0)


def tap_sums(taps, one, two):
    both = jnp.concatenate([one, two], axis=1)
    result = jnp.dot(taps, both, preferred_element_type=jnp.float32)
    return result[:, :BLOCK], result[:, BLOCK:]


def row_tap(sums, at):
    return sums[at * WIDE : (at + 1) * WIDE]


def activated(value):
    return jax.nn.gelu(value).astype(jnp.bfloat16)


def inner_kernel(taps_ref, field, hidden, ends, sides, partial):
    taps = taps_ref[...]
    blank = jnp.zeros((WIDE, BLOCK), jnp.bfloat16)
    for row in range(0, ROWS, 2):
        partial[row], partial[row + 1] = tap_sums(
            taps,
            shifted_columns(field[row], blank, blank),
            shifted_columns(field[row + 1], blank, blank),
        )
    lane = lanes((WIDE, BLOCK))
    west = jnp.zeros((WIDE, BLOCK), jnp.float32)
    east = jnp.zeros((WIDE, BLOCK), jnp.float32)
    for row in range(ROWS):
        value = partial[row, WIDE : 2 * WIDE]
        if row > 0:
            value = value + partial[row - 1, :WIDE]
        if row < ROWS - 1:
            value = value + partial[row + 1, 2 * WIDE :]
        if row == 0:
            ends[0] = value
        elif row == ROWS - 1:
            ends[1] = value
        else:
            hidden[row] = jnp.where((lane == 0) | (lane == BLOCK - 1), blank, activated(value))
        west = jnp.where(lane == row, pltpu.roll(value, row, 1), west)
        east = jnp.where(lane == row, pltpu.roll(value, row + 1, 1), east)
    hidden[0] = blank
    hidden[ROWS - 1] = blank
    sides[0] = west
    sides[1] = east


def inner_convolution(taps, field):
    pair = jax.ShapeDtypeStruct((2, WIDE, BLOCK), jnp.float32)
    return pl.pallas_call(
        inner_kernel,
        in_specs=[vmem()] * 2,
        out_specs=[vmem()] * 3,
        out_shape=[FIELD, pair, pair],
        scratch_shapes=[pltpu.VMEM((ROWS, 3 * WIDE, BLOCK), jnp.float32)],
        compiler_params=pltpu.CompilerParams(vmem_limit_bytes=VMEM_LIMIT),
        cost_estimate=pl.CostEstimate(
            flops=2 * 9 * WIDE * WIDE * ROWS * BLOCK, bytes_accessed=2 << 20, transcendentals=0
        ),
        name="inner_convolution",
    )(taps, field)


def second_kernel_inner(taps_ref, hidden, gridded, base, partial):
    taps = taps_ref[...]
    blank = jnp.zeros((WIDE, BLOCK), jnp.bfloat16)
    for row in range(0, ROWS, 2):
        partial[row], partial[row + 1] = tap_sums(
            taps,
            shifted_columns(hidden[row], blank, blank),
            shifted_columns(hidden[row + 1], blank, blank),
        )
    for row in range(ROWS):
        value = gridded[row].astype(jnp.float32) + partial[row, WIDE : WIDE + PADDED]
        if row > 0:
            value = value + partial[row - 1, :PADDED]
        if row < ROWS - 1:
            value = value + partial[row + 1, 2 * WIDE : 2 * WIDE + PADDED]
        base[row] = value


def inner_second_convolution(taps, hidden, gridded):
    return pl.pallas_call(
        second_kernel_inner,
        in_specs=[vmem()] * 3,
        out_specs=vmem(),
        out_shape=jax.ShapeDtypeStruct((ROWS, PADDED, BLOCK), jnp.float32),
        scratch_shapes=[pltpu.VMEM((ROWS, 3 * WIDE, BLOCK), jnp.float32)],
        compiler_params=pltpu.CompilerParams(vmem_limit_bytes=VMEM_LIMIT),
        cost_estimate=pl.CostEstimate(
            flops=2 * 9 * WIDE * WIDE * ROWS * BLOCK, bytes_accessed=2 << 20, transcendentals=0
        ),
        name="inner_second_convolution",
    )(taps, hidden, gridded)


def strip_plan(column_rows):
    if column_rows == 2:
        return [], 3, 1
    return [-2, 2], column_rows, 2


def conv_kernel(
    column_rows,
    first_taps_ref,
    second_taps_ref,
    field,
    base,
    ends_ref,
    sides_ref,
    above,
    below,
    own_strip,
    *rest,
):
    near, far, reach = strip_plan(column_rows)
    near_strips, (west_pack, east_pack) = rest[: len(near)], rest[len(near) : len(near) + 2]
    smoothed, turned, halves, sems = rest[len(near) + 2 :]
    count = lax.axis_size("tile")
    tile = lax.axis_index("tile")
    lane = lanes((WIDE, BLOCK))
    last = ROWS + 1
    R = column_rows
    blank = jnp.zeros((WIDE, BLOCK), jnp.bfloat16)

    strips = {-1: above[2], 0: own_strip[...], 1: below[2]}
    strips.update((shift, ref[...]) for shift, ref in zip(near, near_strips))
    for at in range(-reach, reach + 1):
        strips[at - far], strips[at + far] = west_pack[at + reach], east_pack[at + reach]

    def place(shift):
        return lax.rem(tile + shift + count, count)

    def ends(shift, before, after, middle):
        before = jnp.where(place(shift) > 0, before, blank)
        after = jnp.where(place(shift) < count - 1, after, blank)
        return jnp.where(lane == 0, before, jnp.where(lane == last, after, middle))

    memo = {}

    def padded_column(shift, which):
        if (shift, which) not in memo:
            base = which * ROWS
            memo[shift, which] = ends(
                shift,
                pltpu.roll(strips[shift - 1], (1 - base - ROWS) % BLOCK, 1),
                pltpu.roll(strips[shift + 1], (last - base) % BLOCK, 1),
                pltpu.roll(strips[shift], (1 - base) % BLOCK, 1),
            )
        return memo[shift, which]

    row_id = lax.broadcasted_iota(jnp.int32, (BLOCK, BLOCK), 0)
    reversal = (row_id + lanes((BLOCK, BLOCK)) == last).astype(jnp.bfloat16)

    def reversed_lanes(planes):
        stacked = jnp.concatenate(planes, axis=0)
        turned_round = jnp.dot(stacked, reversal, preferred_element_type=jnp.float32)
        return [row_tap(turned_round, at) for at in range(len(planes))]

    def choose(shift, which, turned_round, plain):
        flips = strips[shift].astype(jnp.float32)[CHANNELS + which : CHANNELS + which + 1]
        return jnp.where(flips > 0.5, turned_round, plain.astype(jnp.float32)).astype(jnp.bfloat16)

    west_of = {shift: (shift - R, 3) for shift in {-1, 0, 1, R - 1, R, R + 1}}
    east_of = {shift: (shift + R, 0) for shift in {-1, 0, 1, -R - 1, -R, -R + 1}}
    keys = sorted(set(west_of.values()) | set(east_of.values()))
    flipped = dict(zip(keys, reversed_lanes([padded_column(*key) for key in keys])))
    west = {
        shift: choose(shift, 0, flipped[west_of[shift]], padded_column(*west_of[shift]))
        for shift in sorted(west_of)
    }
    east = {
        shift: choose(shift, 1, flipped[east_of[shift]], padded_column(*east_of[shift]))
        for shift in sorted(east_of)
    }

    def columns(value, west_plane, west_row, east_plane, east_row):
        return shifted_columns(
            value,
            pltpu.roll(west_plane, (BLOCK - west_row) % BLOCK, 1),
            pltpu.roll(east_plane, BLOCK - 1 - east_row, 1),
        )

    def along(result):
        return (
            row_tap(result, 0)
            + pltpu.roll(row_tap(result, 1), BLOCK - 1, 1)
            + pltpu.roll(row_tap(result, 2), BLOCK - 2, 1)
        )

    first_taps = first_taps_ref[...]
    up = [jnp.where(tile > 0, above[at], blank) for at in range(2)]
    down = [jnp.where(tile < count - 1, below[at], blank) for at in range(2)]
    from_up, from_down = tap_sums(
        first_taps, shifted_columns(up[1], blank, blank), shifted_columns(down[0], blank, blank)
    )
    from_up, from_down = row_tap(from_up, 0), row_tap(from_down, 2)
    from_west, from_east = tap_sums(
        first_taps,
        jnp.concatenate([west[0], blank, blank], axis=0),
        jnp.concatenate([blank, blank, east[0]], axis=0),
    )
    from_west, from_east = along(from_west), along(from_east)
    first = ends_ref[0] + from_up
    first = first + jnp.where(lane == 0, from_west, 0.0)
    first = first + jnp.where(lane == BLOCK - 1, pltpu.roll(from_east, BLOCK - 1, 1), 0.0)
    final = ends_ref[1] + from_down
    final = final + jnp.where(lane == 0, pltpu.roll(from_west, BLOCK - ROWS + 1, 1), 0.0)
    final = final + jnp.where(lane == BLOCK - 1, pltpu.roll(from_east, BLOCK - ROWS, 1), 0.0)
    first, final = activated(first), activated(final)
    first_column = activated(sides_ref[0] + from_west)
    last_column = activated(sides_ref[1] + from_east)

    upper = jnp.zeros((WIDE, BLOCK), jnp.float32)
    lower = jnp.zeros((WIDE, BLOCK), jnp.float32)
    for at, (high, low) in enumerate(
        [(up[0], field[ROWS - 1]), (up[1], down[0]), (field[0], down[1])]
    ):
        from_row = ROWS - 1 + at
        one, two = tap_sums(
            row_tap(first_taps, at),
            columns(high, west[-1], from_row, east[-1], from_row),
            columns(low, west[1], at, east[1], at),
        )
        upper += one
        lower += two
    top = jnp.where(tile > 0, activated(upper), blank)
    bottom = jnp.where(tile < count - 1, activated(lower), blank)

    west_hidden, east_hidden = {}, {}
    for at in (-1, 0, 1):
        q = at - R
        one = jnp.concatenate([padded_column(q, 2), padded_column(q, 3), east[q]], axis=0)
        q = at + R
        two = jnp.concatenate([west[q], padded_column(q, 0), padded_column(q, 1)], axis=0)
        one, two = tap_sums(first_taps, one, two)
        west_hidden[at], east_hidden[at] = activated(along(one)), activated(along(two))

    def hidden_side(shift, values):
        return ends(
            shift,
            pltpu.roll(values[-1], BLOCK - ROWS + 1, 1),
            pltpu.roll(values[1], last, 1),
            pltpu.roll(values[0], 1, 1),
        )

    plain = [hidden_side(-R, west_hidden), hidden_side(R, east_hidden)]
    west_side, east_side = [
        choose(0, which, turned_side, plain[which])
        for which, turned_side in enumerate(reversed_lanes(plain))
    ]

    second_taps = second_taps_ref[...]
    from_top, from_first = tap_sums(
        second_taps,
        columns(top, west_side, 0, east_side, 0),
        columns(first, west_side, 1, east_side, 1),
    )
    from_final, from_bottom = tap_sums(
        second_taps,
        columns(final, west_side, ROWS, east_side, ROWS),
        columns(bottom, west_side, last, east_side, last),
    )
    rim_rows = {
        0: row_tap(from_top, 0) + row_tap(from_first, 1),
        1: row_tap(from_first, 0),
        ROWS - 2: row_tap(from_final, 2),
        ROWS - 1: row_tap(from_final, 1) + row_tap(from_bottom, 2),
    }

    other = (lane >= 2) & (lane < ROWS)

    def other_rows(plane):
        return jnp.where(other, plane, blank)

    near_west, near_east = other_rows(west_side), other_rows(east_side)
    first_column = other_rows(pltpu.roll(first_column, 1, 1))
    last_column = other_rows(pltpu.roll(last_column, 1, 1))
    to_0, to_1 = tap_sums(
        second_taps,
        jnp.concatenate([near_west, first_column, blank], axis=0),
        jnp.concatenate([first_column, blank, blank], axis=0),
    )
    to_127, to_126 = tap_sums(
        second_taps,
        jnp.concatenate([blank, last_column, near_east], axis=0),
        jnp.concatenate([blank, blank, last_column], axis=0),
    )
    spread = jnp.zeros((WIDE, BLOCK), jnp.float32)
    for at, sums in enumerate((to_126, to_127, to_0, to_1)):
        sums = along(sums)
        high = sums.astype(jnp.bfloat16)
        sums = sums - high.astype(jnp.float32)
        middle = sums.astype(jnp.bfloat16)
        low = (sums - middle.astype(jnp.float32)).astype(jnp.bfloat16)
        to_lane = (lanes((BLOCK, BLOCK)) == 4 * row_id + at).astype(jnp.bfloat16)
        parts = jnp.dot(
            jnp.concatenate([high, middle, low], axis=0),
            to_lane,
            preferred_element_type=jnp.float32,
        )
        spread = spread + (row_tap(parts, 0) + (row_tap(parts, 1) + row_tap(parts, 2)))

    rim_lanes = lanes((PADDED, BLOCK))
    rim_lanes = (rim_lanes < 2) | (rim_lanes >= BLOCK - 2)
    spread = spread[:PADDED]
    copies = []
    for half in range(2):
        for row in range(half * HALF_ROWS, (half + 1) * HALF_ROWS):
            value = base[row] + jnp.where(
                rim_lanes, pltpu.roll(spread, (BLOCK - 4 * row - 2) % BLOCK, 1), 0.0
            )
            if row in rim_rows:
                value = value + rim_rows[row][:PADDED]
            turned[half, pl.ds(row - half * HALF_ROWS, PADDED, stride=HALF_ROWS), :] = value
        rounded = turned[half, pl.ds(0, CHANNELS * HALF_ROWS), :].astype(jnp.bfloat16)
        halves[half] = rounded.reshape(CHANNELS, HALF_ROWS, BLOCK)
        rows = pl.ds(half * HALF_ROWS, HALF_ROWS)
        copies.append(pltpu.make_async_copy(halves.at[half], smoothed.at[:, rows], sems.at[half]))
        copies[-1].start()
    for copy in copies:
        copy.wait()


def convolutions(column_rows, *operands):
    return pl.pallas_call(
        functools.partial(conv_kernel, column_rows),
        in_specs=[vmem()] * len(operands),
        out_specs=pl.BlockSpec(memory_space=pl.ANY),
        out_shape=jax.ShapeDtypeStruct((CHANNELS, ROWS, BLOCK), jnp.bfloat16),
        scratch_shapes=[
            pltpu.VMEM((2, PADDED * HALF_ROWS, BLOCK), jnp.float32),
            pltpu.VMEM((2, CHANNELS, HALF_ROWS, BLOCK), jnp.bfloat16),
            pltpu.SemaphoreType.DMA((2,)),
        ],
        compiler_params=pltpu.CompilerParams(vmem_limit_bytes=VMEM_LIMIT),
        name="convolutions",
    )(*operands)


def tap_matrix(kernel):
    pad = WIDE - CHANNELS
    taps = jnp.pad(kernel, ((0, 0), (0, pad), (0, pad))).reshape(3, 3, WIDE, WIDE)
    return taps.transpose(0, 2, 1, 3).reshape(3 * WIDE, 3 * WIDE)


def from_shift(value, shift):
    count = lax.axis_size("tile")
    return lax.ppermute(value, "tile", [(i, (i - shift) % count) for i in range(count)])


def per_device(
    source, weights, block_source, block_target, edge_flip, norm_gain, first_kernel, second_kernel
):
    count = lax.axis_size("tile")
    column_rows = count // TILE_COLS
    field = source.reshape(ROWS, CHANNELS, BLOCK).transpose(1, 0, 2).reshape(-1, BLOCK)
    same, *nexts = regrid(block_target, block_source, field, weights, column_rows)

    for across in range(TILE_COLS):
        pairs = [
            (c * column_rows + p, (c ^ across) * column_rows + p + 1)
            for c in range(TILE_COLS)
            for p in range(column_rows - 1)
        ]
        nexts[across] = lax.ppermute(nexts[across], "tile", pairs)
    nexts = [nexts[across] for across in (0, 1, 2, 4, 5, 6, 7, 3)]
    same = lax.all_to_all(
        same,
        "tile",
        0,
        0,
        axis_index_groups=[
            [c * column_rows + p for c in COLUMN_ORDER] for p in range(column_rows)
        ],
        tiled=True,
    )

    gain = jnp.broadcast_to(
        jnp.pad(norm_gain, (0, PADDED - CHANNELS))[:, None], (PADDED, BLOCK)
    )
    first_taps, second_taps = tap_matrix(first_kernel), tap_matrix(second_kernel)
    same, nexts, gain, first_taps, second_taps = lax.optimization_barrier(
        (same, nexts, gain, first_taps, second_taps)
    )
    summed, upward, downward, strip = gather_rows(column_rows, edge_flip, gain, same, nexts)
    rims = [from_shift(downward, -1), from_shift(upward, 1)]
    near, far, reach = strip_plan(column_rows)
    strips = [from_shift(strip, shift) for shift in near]
    gridded, normed = normalize_rows(gain, summed)
    inner = inner_convolution(first_taps, normed)
    held = {-1: rims[0][2], 0: strip, 1: rims[1][2], **dict(zip(near, strips))}
    pack = jnp.stack([held[at] for at in range(-reach, reach + 1)])
    pack, inner = lax.optimization_barrier((pack, inner))
    strips += [from_shift(pack, -far), from_shift(pack, far)]
    gridded_out = channels_first(gridded)
    hidden, *unfinished = inner
    base = inner_second_convolution(second_taps, hidden, gridded)
    smoothed = convolutions(
        column_rows, first_taps, second_taps, normed, base, *unfinished, *rims, strip, *strips
    )

    def placed(value):
        return value.reshape(CHANNELS, ROWS, BLOCK).transpose(1, 0, 2)[:, None]

    return placed(gridded_out), placed(smoothed)


def solution(mesh):
    in_specs = (
        P("tile", "groups", None, None),
        P("tile", None, None),
        P("tile"),
        P("tile"),
        P("tile", None),
        P(),
        P(),
        P(),
    )
    out_specs = (P("tile", "groups", None, None), P("tile", "groups", None, None))
    return jax.shard_map(
        per_device, mesh=mesh, in_specs=in_specs, out_specs=out_specs, check_vma=False
    )
```

```python
import functools

import jax
import jax.numpy as jnp
from jax import lax
from jax.experimental import pallas as pl
from jax.experimental.pallas import tpu as pltpu
from jax.sharding import PartitionSpec as P

BLOCK = 128
CHANNELS = 69
PADDED = 72
WIDE = 80
ROWS = 32
ROW_BITS = 5
HALF_ROWS = ROWS // 2
TILE_COLS = 8
CAP = 8
HALF = TILE_COLS // 2
GROUPS = 2 * TILE_COLS
COLUMN_ORDER = [half * HALF + at for at in range(HALF) for half in range(2)]
SLOTS = GROUPS * CAP
MARK = CHANNELS
BODY = 64
TAILS = (MARK + 1 - BODY) * CAP
MESSAGE = CAP * BODY + TAILS
CHUNK = 96
EPSILON = 1e-05
VMEM_LIMIT = 40 * 1024 * 1024
REGRID_VMEM = 60 * 1024 * 1024


def vmem():
    return pl.BlockSpec(memory_space=pltpu.VMEM)


def smem():
    return pl.BlockSpec(memory_space=pltpu.SMEM)


def split(value, size):
    if size & (size - 1) == 0:
        return value >> (size.bit_length() - 1), value & (size - 1)
    return lax.div(value, size), lax.rem(value, size)


def lanes(shape):
    return lax.broadcasted_iota(jnp.int32, shape, len(shape) - 1)


def regrid_kernel(
    column_rows, target_hbm, target_row_hbm, index_hbm, source_hbm, weight_hbm, *rest
):
    same_out, next_outs = rest[0], rest[1 : 1 + TILE_COLS]
    (
        target_ref,
        target_row_ref,
        index_ref,
        source,
        weight,
        wide,
        field,
        sums,
        message,
        tails,
        plan,
        plan_scalars,
        plan_sem,
        in_sems,
        weight_sems,
        out_sems,
    ) = rest[1 + TILE_COLS :]
    entries = weight.shape[0]
    chunks = entries // CHUNK
    tile = lax.axis_index("tile")
    column, position = split(tile, column_rows)

    small_copies = [
        pltpu.make_async_copy(target_row_hbm, target_row_ref, in_sems.at[0]),
        pltpu.make_async_copy(target_hbm, target_ref, in_sems.at[1]),
        pltpu.make_async_copy(index_hbm, index_ref, in_sems.at[2]),
    ]
    source_copy = pltpu.make_async_copy(source_hbm, source, in_sems.at[3])
    for copy in small_copies:
        copy.start()
    source_copy.start()

    def chunk_copy(chunk):
        part = pl.ds(chunk * CHUNK, CHUNK)
        return pltpu.make_async_copy(weight_hbm.at[part], weight.at[part], weight_sems.at[chunk])

    for chunk in range(chunks):
        chunk_copy(chunk).start()

    small_copies[0].wait()
    target = target_row_ref[...]
    owner, row = split(target, ROWS)
    owner_column, owner_position = split(owner, column_rows)
    place = ((owner_column & (HALF - 1)) << 1) + (owner_column >= HALF).astype(jnp.int32)
    group = jnp.where(owner_position == position, place, TILE_COLS + (owner_column ^ column))
    key = group * ROWS + row
    square = (entries, entries)
    down = lax.broadcasted_iota(jnp.int32, square, 0)
    along = lanes(square)
    key_along = jnp.broadcast_to(key.astype(jnp.float32), square)
    key_down = jnp.broadcast_to(
        jnp.sum(jnp.where(down == along, key_along, 0.0), axis=1, keepdims=True), square
    )
    equal = key_along == key_down
    doubles = jnp.sum(jnp.where(equal & (along < down), 1.0, 0.0), axis=1, keepdims=True)
    in_group = (key_down.astype(jnp.int32) >> ROW_BITS) == (key_along.astype(jnp.int32) >> ROW_BITS)
    below = in_group & (key_down < key_along) & (jnp.broadcast_to(doubles, square) == 0.0)
    rank = jnp.sum(jnp.where(below, 1.0, 0.0), axis=0, keepdims=True)
    mentions = jnp.sum(jnp.where(equal & (down < along), 1.0, 0.0), axis=0, keepdims=True)
    slots = group * CAP + rank.astype(jnp.int32)
    plan[...] = slots + jnp.where(mentions == 0.0, SLOTS, 0)
    plan_copy = pltpu.make_async_copy(plan, plan_scalars, plan_sem)
    plan_copy.start()

    for slot in range(SLOTS):
        tails[pl.ds(slot * 8, 8), :] = jnp.full((8, BLOCK), ROWS, jnp.float32)
    wide[pl.ds(CHANNELS * ROWS, (PADDED - CHANNELS) * ROWS), :] = jnp.zeros(
        ((PADDED - CHANNELS) * ROWS, BLOCK), jnp.float32
    )
    nothing = jnp.zeros((WIDE - PADDED, BLOCK), jnp.float32)
    source_copy.wait()
    wide[pl.ds(0, CHANNELS * ROWS), :] = source[...].astype(jnp.float32)
    for row in range(ROWS):
        block = wide[pl.ds(row, PADDED, stride=ROWS), :]
        field[row] = jnp.concatenate([block, nothing], axis=0).astype(jnp.bfloat16)
    is_mark = lax.broadcasted_iota(jnp.int32, (8, BLOCK), 0) == MARK - BODY
    blank = jnp.zeros((WIDE, BLOCK), jnp.bfloat16)
    small_copies[1].wait()
    small_copies[2].wait()
    plan_copy.wait()

    for chunk in range(chunks):
        chunk_copy(chunk).wait()
        for entry in range(chunk * CHUNK, (chunk + 1) * CHUNK, 2):
            one = jnp.concatenate([field[index_ref[entry]], blank], axis=1)
            two = jnp.concatenate([blank, field[index_ref[entry + 1]]], axis=1)
            products = jnp.dot(
                jnp.concatenate([one, two], axis=0),
                weight[entry : entry + 2].reshape(2 * BLOCK, BLOCK),
                preferred_element_type=jnp.float32,
            )
            for at in range(2):
                code = plan_scalars[0, entry + at]
                slot = code & (SLOTS - 1)
                row = split(target_ref[entry + at], ROWS)[1]
                product = products[at * WIDE : at * WIDE + PADDED]
                total = jnp.where(code >= SLOTS, 0.0, sums[slot]) + product
                sums[slot] = total
                group, place = split(slot, CAP)
                message[group, pl.ds(pl.multiple_of(place * BODY, BODY), BODY), :] = total[
                    :BODY
                ].astype(jnp.bfloat16)
                tails[pl.ds(pl.multiple_of(slot * 8, 8), 8), :] = jnp.where(
                    is_mark, row.astype(jnp.float32), total[BODY:]
                )
    copies = []
    for group in range(GROUPS):
        start = group * CAP * 8
        ends = [tails[pl.ds(start + at, CAP, stride=8), :] for at in range(MARK + 1 - BODY)]
        message[group, CAP * BODY :] = jnp.concatenate(ends, axis=0).astype(jnp.bfloat16)
        if group < TILE_COLS:
            out = same_out.at[pl.ds(group * MESSAGE, MESSAGE)]
        else:
            out = next_outs[group - TILE_COLS]
        copies.append(pltpu.make_async_copy(message.at[group], out, out_sems.at[group]))
        copies[-1].start()
    for copy in copies:
        copy.wait()


def regrid(target, source_index, field, weights, column_rows):
    piece = jax.ShapeDtypeStruct((MESSAGE, BLOCK), jnp.bfloat16)
    same = jax.ShapeDtypeStruct((TILE_COLS * MESSAGE, BLOCK), jnp.bfloat16)
    hbm = pl.BlockSpec(memory_space=pl.ANY)
    entries = weights.shape[0]
    return pl.pallas_call(
        functools.partial(regrid_kernel, column_rows),
        in_specs=[hbm] * 5,
        out_specs=[hbm] * (1 + TILE_COLS),
        out_shape=[same] + [piece] * TILE_COLS,
        scratch_shapes=[
            pltpu.SMEM(target.shape, jnp.int32),
            pltpu.VMEM((1, entries), jnp.int32),
            pltpu.SMEM(source_index.shape, jnp.int32),
            pltpu.VMEM(field.shape, jnp.bfloat16),
            pltpu.VMEM(weights.shape, jnp.bfloat16),
            pltpu.VMEM((PADDED * ROWS, BLOCK), jnp.float32),
            pltpu.VMEM((ROWS, WIDE, BLOCK), jnp.bfloat16),
            pltpu.VMEM((SLOTS, PADDED, BLOCK), jnp.float32),
            pltpu.VMEM((GROUPS, MESSAGE, BLOCK), jnp.bfloat16),
            pltpu.VMEM((SLOTS * 8, BLOCK), jnp.float32),
            pltpu.VMEM((1, entries), jnp.int32),
            pltpu.SMEM((1, entries), jnp.int32),
            pltpu.SemaphoreType.DMA,
            pltpu.SemaphoreType.DMA((4,)),
            pltpu.SemaphoreType.DMA((entries // CHUNK,)),
            pltpu.SemaphoreType.DMA((GROUPS,)),
        ],
        compiler_params=pltpu.CompilerParams(vmem_limit_bytes=REGRID_VMEM),
        name="regrid",
    )(target, target.reshape(1, -1), source_index, field, weights)


def normalized(rounded, gain):
    value = rounded.astype(jnp.float32)
    real = lax.broadcasted_iota(jnp.int32, (PADDED - BODY, BLOCK), 0) < CHANNELS - BODY
    value = jnp.concatenate([value[:BODY], jnp.where(real, value[BODY:], 0.0)], axis=0)
    square = jnp.sum(value * value, axis=0, keepdims=True) * (1.0 / CHANNELS)
    scaled = value * lax.rsqrt(square + EPSILON) * gain
    nothing = jnp.zeros((WIDE - PADDED, BLOCK), jnp.float32)
    return jnp.concatenate([scaled, nothing], axis=0).astype(jnp.bfloat16)


def gather_kernel(column_rows, flip_ref, gain_ref, same, *rest):
    nexts = rest[:TILE_COLS]
    summed, upward, downward, strip_out, tails = rest[TILE_COLS:]
    position = lax.rem(lax.axis_index("tile"), column_rows)
    summed[...] = jnp.zeros_like(summed)

    def add(group, piece):
        ends = piece[CAP * BODY :].astype(jnp.float32)
        tails[group, :TAILS] = ends
        rows = ends[TAILS - CAP :].astype(jnp.int32)
        for place in range(CAP):
            row = rows[place, 0]
            body = piece[place * BODY : (place + 1) * BODY].astype(jnp.float32)
            summed[row, :BODY] = summed[row, :BODY] + body
            tail = tails[group, pl.ds(place, 8, stride=CAP), :]
            summed[row, BODY:] = summed[row, BODY:] + tail

    tails[:, TAILS:] = jnp.zeros((GROUPS, 8 * CAP - TAILS, BLOCK), jnp.float32)
    for group in range(TILE_COLS):
        add(group, same.at[pl.ds(group * MESSAGE, MESSAGE)])

    @pl.when(position > 0)
    def _():
        for group in range(TILE_COLS):
            add(TILE_COLS + group, nexts[group])

    gain = gain_ref[...]
    for at in range(2):
        upward[at] = normalized(summed[at].astype(jnp.bfloat16), gain)
        downward[at] = normalized(summed[ROWS - 2 + at].astype(jnp.bfloat16), gain)
    lane = lanes((PADDED, BLOCK))
    strip = jnp.zeros((PADDED, BLOCK), jnp.bfloat16)
    for row in range(ROWS):
        rounded = summed[row].astype(jnp.bfloat16)
        strip = jnp.where((lane >> 2) == row, pltpu.roll(rounded, 4 * row + 2, 1), strip)
    to_lane = lanes((BLOCK, BLOCK))
    from_lane = 4 * (to_lane & (ROWS - 1)) + (((to_lane >> ROW_BITS) + 2) & 3)
    order = lax.broadcasted_iota(jnp.int32, (BLOCK, BLOCK), 0) == from_lane
    strip = jnp.dot(
        normalized(strip, gain), order.astype(jnp.bfloat16), preferred_element_type=jnp.float32
    )
    channel = lax.broadcasted_iota(jnp.int32, (WIDE, BLOCK), 0)
    for side in range(2):
        strip = jnp.where(channel == CHANNELS + side, flip_ref[0, side].astype(jnp.float32), strip)
    strip = strip.astype(jnp.bfloat16)
    upward[2] = strip
    downward[2] = strip
    strip_out[...] = strip


def normalize_kernel(gain_ref, summed, gridded, normed):
    gain = gain_ref[...]
    for row in range(ROWS):
        rounded = summed[row].astype(jnp.bfloat16)
        gridded[row] = rounded
        normed[row] = normalized(rounded, gain)


def normalize_rows(gain, summed):
    return pl.pallas_call(
        normalize_kernel,
        in_specs=[vmem()] * 2,
        out_specs=[vmem()] * 2,
        out_shape=[GRIDDED, FIELD],
        compiler_params=pltpu.CompilerParams(vmem_limit_bytes=VMEM_LIMIT),
        cost_estimate=pl.CostEstimate(
            flops=10 * ROWS * PADDED * BLOCK, bytes_accessed=2 << 20, transcendentals=0
        ),
        name="normalize_rows",
    )(gain, summed)


SUMMED = jax.ShapeDtypeStruct((ROWS + 1, PADDED, BLOCK), jnp.float32)
GRIDDED = jax.ShapeDtypeStruct((ROWS, PADDED, BLOCK), jnp.bfloat16)
FIELD = jax.ShapeDtypeStruct((ROWS, WIDE, BLOCK), jnp.bfloat16)
RIM = jax.ShapeDtypeStruct((3, WIDE, BLOCK), jnp.bfloat16)
STRIP_COLUMNS = (0, 1, BLOCK - 2, BLOCK - 1)
STRIP = jax.ShapeDtypeStruct((WIDE, BLOCK), jnp.bfloat16)


def gather_rows(column_rows, edge_flip, gain, same, nexts):
    return pl.pallas_call(
        functools.partial(gather_kernel, column_rows),
        in_specs=[smem()] + [vmem()] * (2 + TILE_COLS),
        out_specs=[vmem()] * 4,
        out_shape=[SUMMED, RIM, RIM, STRIP],
        scratch_shapes=[pltpu.VMEM((GROUPS, 8 * CAP, BLOCK), jnp.float32)],
        compiler_params=pltpu.CompilerParams(vmem_limit_bytes=VMEM_LIMIT),
        name="gather_rows",
    )(edge_flip, gain, same, *nexts)


def turn_kernel(field, out, turned):
    for row in range(ROWS):
        turned[pl.ds(row, PADDED, stride=ROWS), :] = field[row].astype(jnp.float32)
    out[...] = turned[pl.ds(0, CHANNELS * ROWS), :].astype(jnp.bfloat16)


def channels_first(field):
    return pl.pallas_call(
        turn_kernel,
        in_specs=[vmem()],
        out_specs=vmem(),
        out_shape=jax.ShapeDtypeStruct((CHANNELS * ROWS, BLOCK), jnp.bfloat16),
        scratch_shapes=[pltpu.VMEM((PADDED * ROWS, BLOCK), jnp.float32)],
        compiler_params=pltpu.CompilerParams(vmem_limit_bytes=VMEM_LIMIT),
        name="channels_first",
    )(field)


def shifted_columns(value, left_end, right_end):
    lane = lanes((WIDE, BLOCK))
    left = jnp.where(lane == 0, left_end, pltpu.roll(value, 1, 1))
    right = jnp.where(lane == BLOCK - 1, right_end, pltpu.roll(value, BLOCK - 1, 1))
    return jnp.concatenate([left, value, right], axis=0)


def tap_sums(taps, one, two):
    both = jnp.concatenate([one, two], axis=1)
    result = jnp.dot(taps, both, preferred_element_type=jnp.float32)
    return result[:, :BLOCK], result[:, BLOCK:]


def row_tap(sums, at):
    return sums[at * WIDE : (at + 1) * WIDE]


def activated(value):
    return jax.nn.gelu(value).astype(jnp.bfloat16)


def inner_kernel(taps_ref, field, hidden, ends, sides, partial):
    taps = taps_ref[...]
    blank = jnp.zeros((WIDE, BLOCK), jnp.bfloat16)
    for row in range(0, ROWS, 2):
        partial[row], partial[row + 1] = tap_sums(
            taps,
            shifted_columns(field[row], blank, blank),
            shifted_columns(field[row + 1], blank, blank),
        )
    lane = lanes((WIDE, BLOCK))
    west = jnp.zeros((WIDE, BLOCK), jnp.float32)
    east = jnp.zeros((WIDE, BLOCK), jnp.float32)
    for row in range(ROWS):
        value = partial[row, WIDE : 2 * WIDE]
        if row > 0:
            value = value + partial[row - 1, :WIDE]
        if row < ROWS - 1:
            value = value + partial[row + 1, 2 * WIDE :]
        if row == 0:
            ends[0] = value
        elif row == ROWS - 1:
            ends[1] = value
        else:
            hidden[row] = jnp.where((lane == 0) | (lane == BLOCK - 1), blank, activated(value))
        west = jnp.where(lane == row, pltpu.roll(value, row, 1), west)
        east = jnp.where(lane == row, pltpu.roll(value, row + 1, 1), east)
    hidden[0] = blank
    hidden[ROWS - 1] = blank
    sides[0] = west
    sides[1] = east


def inner_convolution(taps, field):
    pair = jax.ShapeDtypeStruct((2, WIDE, BLOCK), jnp.float32)
    return pl.pallas_call(
        inner_kernel,
        in_specs=[vmem()] * 2,
        out_specs=[vmem()] * 3,
        out_shape=[FIELD, pair, pair],
        scratch_shapes=[pltpu.VMEM((ROWS, 3 * WIDE, BLOCK), jnp.float32)],
        compiler_params=pltpu.CompilerParams(vmem_limit_bytes=VMEM_LIMIT),
        cost_estimate=pl.CostEstimate(
            flops=2 * 9 * WIDE * WIDE * ROWS * BLOCK, bytes_accessed=2 << 20, transcendentals=0
        ),
        name="inner_convolution",
    )(taps, field)


def second_kernel_inner(taps_ref, hidden, gridded, base, partial):
    taps = taps_ref[...]
    blank = jnp.zeros((WIDE, BLOCK), jnp.bfloat16)
    for row in range(0, ROWS, 2):
        partial[row], partial[row + 1] = tap_sums(
            taps,
            shifted_columns(hidden[row], blank, blank),
            shifted_columns(hidden[row + 1], blank, blank),
        )
    for row in range(ROWS):
        value = gridded[row].astype(jnp.float32) + partial[row, WIDE : WIDE + PADDED]
        if row > 0:
            value = value + partial[row - 1, :PADDED]
        if row < ROWS - 1:
            value = value + partial[row + 1, 2 * WIDE : 2 * WIDE + PADDED]
        base[row] = value


def inner_second_convolution(taps, hidden, gridded):
    return pl.pallas_call(
        second_kernel_inner,
        in_specs=[vmem()] * 3,
        out_specs=vmem(),
        out_shape=jax.ShapeDtypeStruct((ROWS, PADDED, BLOCK), jnp.float32),
        scratch_shapes=[pltpu.VMEM((ROWS, 3 * WIDE, BLOCK), jnp.float32)],
        compiler_params=pltpu.CompilerParams(vmem_limit_bytes=VMEM_LIMIT),
        cost_estimate=pl.CostEstimate(
            flops=2 * 9 * WIDE * WIDE * ROWS * BLOCK, bytes_accessed=2 << 20, transcendentals=0
        ),
        name="inner_second_convolution",
    )(taps, hidden, gridded)


def pack_kernel(above, below, own, to_west, to_east):
    low = lanes((WIDE, BLOCK)) < BLOCK // 2
    before, strip, after = above[2], own[...], below[2]

    def other_half(plane):
        return pltpu.roll(plane, BLOCK // 2, 1)

    outer = jnp.where(low, after, before)
    to_east[0] = jnp.where(low, other_half(strip), after)
    to_east[1] = outer
    to_west[0] = jnp.where(low, strip, other_half(before))
    to_west[1] = outer


def half_strip_packs(above, below, own):
    pack = jax.ShapeDtypeStruct((2, WIDE, BLOCK), jnp.bfloat16)
    return pl.pallas_call(
        pack_kernel,
        in_specs=[vmem()] * 3,
        out_specs=[vmem()] * 2,
        out_shape=[pack, pack],
        compiler_params=pltpu.CompilerParams(vmem_limit_bytes=VMEM_LIMIT),
        name="half_strip_packs",
    )(above, below, own)


def half_strips(west_pack, east_pack):
    low = lanes((WIDE, BLOCK)) < BLOCK // 2

    def other_half(plane):
        return pltpu.roll(plane, BLOCK // 2, 1)

    def both_halves(plane):
        return jnp.where(low, plane, other_half(plane))

    return {
        -4: west_pack[1],
        -3: both_halves(west_pack[0]),
        -2: jnp.where(low, west_pack[1], west_pack[0]),
        2: jnp.where(low, other_half(east_pack[0]), east_pack[1]),
        3: both_halves(east_pack[0]),
        4: east_pack[1],
    }


def strip_plan(column_rows):
    if column_rows == 2:
        return [], 3, 1
    return [-2, 2], column_rows, 2


def conv_kernel(
    column_rows,
    first_taps_ref,
    second_taps_ref,
    field,
    base,
    ends_ref,
    sides_ref,
    above,
    below,
    own_strip,
    *rest,
):
    near, far, reach = strip_plan(column_rows)
    near_strips, (west_pack, east_pack) = rest[: len(near)], rest[len(near) : len(near) + 2]
    smoothed, turned, halves, sems = rest[len(near) + 2 :]
    count = lax.axis_size("tile")
    tile = lax.axis_index("tile")
    lane = lanes((WIDE, BLOCK))
    last = ROWS + 1
    R = column_rows
    blank = jnp.zeros((WIDE, BLOCK), jnp.bfloat16)

    strips = {-1: above[2], 0: own_strip[...], 1: below[2]}
    strips.update((shift, ref[...]) for shift, ref in zip(near, near_strips))
    if R == 2:
        strips.update(half_strips(west_pack, east_pack))
    else:
        for at in range(-reach, reach + 1):
            strips[at - far], strips[at + far] = west_pack[at + reach], east_pack[at + reach]

    def place(shift):
        return lax.rem(tile + shift + count, count)

    def ends(shift, before, after, middle):
        before = jnp.where(place(shift) > 0, before, blank)
        after = jnp.where(place(shift) < count - 1, after, blank)
        return jnp.where(lane == 0, before, jnp.where(lane == last, after, middle))

    memo = {}

    def padded_column(shift, which):
        if (shift, which) not in memo:
            base = which * ROWS
            memo[shift, which] = ends(
                shift,
                pltpu.roll(strips[shift - 1], (1 - base - ROWS) % BLOCK, 1),
                pltpu.roll(strips[shift + 1], (last - base) % BLOCK, 1),
                pltpu.roll(strips[shift], (1 - base) % BLOCK, 1),
            )
        return memo[shift, which]

    row_id = lax.broadcasted_iota(jnp.int32, (BLOCK, BLOCK), 0)
    reversal = (row_id + lanes((BLOCK, BLOCK)) == last).astype(jnp.bfloat16)

    def reversed_lanes(planes):
        stacked = jnp.concatenate(planes, axis=0)
        turned_round = jnp.dot(stacked, reversal, preferred_element_type=jnp.float32)
        return [row_tap(turned_round, at) for at in range(len(planes))]

    def choose(shift, which, turned_round, plain):
        flips = strips[shift].astype(jnp.float32)[CHANNELS + which : CHANNELS + which + 1]
        return jnp.where(flips > 0.5, turned_round, plain.astype(jnp.float32)).astype(jnp.bfloat16)

    west_of = {shift: (shift - R, 3) for shift in {-1, 0, 1, R - 1, R, R + 1}}
    east_of = {shift: (shift + R, 0) for shift in {-1, 0, 1, -R - 1, -R, -R + 1}}
    keys = sorted(set(west_of.values()) | set(east_of.values()))
    flipped = dict(zip(keys, reversed_lanes([padded_column(*key) for key in keys])))
    west = {
        shift: choose(shift, 0, flipped[west_of[shift]], padded_column(*west_of[shift]))
        for shift in sorted(west_of)
    }
    east = {
        shift: choose(shift, 1, flipped[east_of[shift]], padded_column(*east_of[shift]))
        for shift in sorted(east_of)
    }

    def columns(value, west_plane, west_row, east_plane, east_row):
        return shifted_columns(
            value,
            pltpu.roll(west_plane, (BLOCK - west_row) % BLOCK, 1),
            pltpu.roll(east_plane, BLOCK - 1 - east_row, 1),
        )

    def along(result):
        return (
            row_tap(result, 0)
            + pltpu.roll(row_tap(result, 1), BLOCK - 1, 1)
            + pltpu.roll(row_tap(result, 2), BLOCK - 2, 1)
        )

    first_taps = first_taps_ref[...]
    up = [jnp.where(tile > 0, above[at], blank) for at in range(2)]
    down = [jnp.where(tile < count - 1, below[at], blank) for at in range(2)]
    from_up, from_down = tap_sums(
        first_taps, shifted_columns(up[1], blank, blank), shifted_columns(down[0], blank, blank)
    )
    from_up, from_down = row_tap(from_up, 0), row_tap(from_down, 2)
    from_west, from_east = tap_sums(
        first_taps,
        jnp.concatenate([west[0], blank, blank], axis=0),
        jnp.concatenate([blank, blank, east[0]], axis=0),
    )
    from_west, from_east = along(from_west), along(from_east)
    first = ends_ref[0] + from_up
    first = first + jnp.where(lane == 0, from_west, 0.0)
    first = first + jnp.where(lane == BLOCK - 1, pltpu.roll(from_east, BLOCK - 1, 1), 0.0)
    final = ends_ref[1] + from_down
    final = final + jnp.where(lane == 0, pltpu.roll(from_west, BLOCK - ROWS + 1, 1), 0.0)
    final = final + jnp.where(lane == BLOCK - 1, pltpu.roll(from_east, BLOCK - ROWS, 1), 0.0)
    first, final = activated(first), activated(final)
    first_column = activated(sides_ref[0] + from_west)
    last_column = activated(sides_ref[1] + from_east)

    upper = jnp.zeros((WIDE, BLOCK), jnp.float32)
    lower = jnp.zeros((WIDE, BLOCK), jnp.float32)
    for at, (high, low) in enumerate(
        [(up[0], field[ROWS - 1]), (up[1], down[0]), (field[0], down[1])]
    ):
        from_row = ROWS - 1 + at
        one, two = tap_sums(
            row_tap(first_taps, at),
            columns(high, west[-1], from_row, east[-1], from_row),
            columns(low, west[1], at, east[1], at),
        )
        upper += one
        lower += two
    top = jnp.where(tile > 0, activated(upper), blank)
    bottom = jnp.where(tile < count - 1, activated(lower), blank)

    west_hidden, east_hidden = {}, {}
    for at in (-1, 0, 1):
        q = at - R
        one = jnp.concatenate([padded_column(q, 2), padded_column(q, 3), east[q]], axis=0)
        q = at + R
        two = jnp.concatenate([west[q], padded_column(q, 0), padded_column(q, 1)], axis=0)
        one, two = tap_sums(first_taps, one, two)
        west_hidden[at], east_hidden[at] = activated(along(one)), activated(along(two))

    def hidden_side(shift, values):
        return ends(
            shift,
            pltpu.roll(values[-1], BLOCK - ROWS + 1, 1),
            pltpu.roll(values[1], last, 1),
            pltpu.roll(values[0], 1, 1),
        )

    plain = [hidden_side(-R, west_hidden), hidden_side(R, east_hidden)]
    west_side, east_side = [
        choose(0, which, turned_side, plain[which])
        for which, turned_side in enumerate(reversed_lanes(plain))
    ]

    second_taps = second_taps_ref[...]
    from_top, from_first = tap_sums(
        second_taps,
        columns(top, west_side, 0, east_side, 0),
        columns(first, west_side, 1, east_side, 1),
    )
    from_final, from_bottom = tap_sums(
        second_taps,
        columns(final, west_side, ROWS, east_side, ROWS),
        columns(bottom, west_side, last, east_side, last),
    )
    rim_rows = {
        0: row_tap(from_top, 0) + row_tap(from_first, 1),
        1: row_tap(from_first, 0),
        ROWS - 2: row_tap(from_final, 2),
        ROWS - 1: row_tap(from_final, 1) + row_tap(from_bottom, 2),
    }

    other = (lane >= 2) & (lane < ROWS)

    def other_rows(plane):
        return jnp.where(other, plane, blank)

    near_west, near_east = other_rows(west_side), other_rows(east_side)
    first_column = other_rows(pltpu.roll(first_column, 1, 1))
    last_column = other_rows(pltpu.roll(last_column, 1, 1))
    to_0, to_1 = tap_sums(
        second_taps,
        jnp.concatenate([near_west, first_column, blank], axis=0),
        jnp.concatenate([first_column, blank, blank], axis=0),
    )
    to_127, to_126 = tap_sums(
        second_taps,
        jnp.concatenate([blank, last_column, near_east], axis=0),
        jnp.concatenate([blank, blank, last_column], axis=0),
    )
    spread = jnp.zeros((WIDE, BLOCK), jnp.float32)
    for at, sums in enumerate((to_126, to_127, to_0, to_1)):
        sums = along(sums)
        high = sums.astype(jnp.bfloat16)
        sums = sums - high.astype(jnp.float32)
        middle = sums.astype(jnp.bfloat16)
        low = (sums - middle.astype(jnp.float32)).astype(jnp.bfloat16)
        to_lane = (lanes((BLOCK, BLOCK)) == 4 * row_id + at).astype(jnp.bfloat16)
        parts = jnp.dot(
            jnp.concatenate([high, middle, low], axis=0),
            to_lane,
            preferred_element_type=jnp.float32,
        )
        spread = spread + (row_tap(parts, 0) + (row_tap(parts, 1) + row_tap(parts, 2)))

    rim_lanes = lanes((PADDED, BLOCK))
    rim_lanes = (rim_lanes < 2) | (rim_lanes >= BLOCK - 2)
    spread = spread[:PADDED]
    copies = []
    for half in range(2):
        for row in range(half * HALF_ROWS, (half + 1) * HALF_ROWS):
            value = base[row] + jnp.where(
                rim_lanes, pltpu.roll(spread, (BLOCK - 4 * row - 2) % BLOCK, 1), 0.0
            )
            if row in rim_rows:
                value = value + rim_rows[row][:PADDED]
            turned[half, pl.ds(row - half * HALF_ROWS, PADDED, stride=HALF_ROWS), :] = value
        rounded = turned[half, pl.ds(0, CHANNELS * HALF_ROWS), :].astype(jnp.bfloat16)
        halves[half] = rounded.reshape(CHANNELS, HALF_ROWS, BLOCK)
        rows = pl.ds(half * HALF_ROWS, HALF_ROWS)
        copies.append(pltpu.make_async_copy(halves.at[half], smoothed.at[:, rows], sems.at[half]))
        copies[-1].start()
    for copy in copies:
        copy.wait()


def convolutions(column_rows, *operands):
    return pl.pallas_call(
        functools.partial(conv_kernel, column_rows),
        in_specs=[vmem()] * len(operands),
        out_specs=pl.BlockSpec(memory_space=pl.ANY),
        out_shape=jax.ShapeDtypeStruct((CHANNELS, ROWS, BLOCK), jnp.bfloat16),
        scratch_shapes=[
            pltpu.VMEM((2, PADDED * HALF_ROWS, BLOCK), jnp.float32),
            pltpu.VMEM((2, CHANNELS, HALF_ROWS, BLOCK), jnp.bfloat16),
            pltpu.SemaphoreType.DMA((2,)),
        ],
        compiler_params=pltpu.CompilerParams(vmem_limit_bytes=VMEM_LIMIT),
        name="convolutions",
    )(*operands)


def tap_matrix(kernel):
    pad = WIDE - CHANNELS
    taps = jnp.pad(kernel, ((0, 0), (0, pad), (0, pad))).reshape(3, 3, WIDE, WIDE)
    return taps.transpose(0, 2, 1, 3).reshape(3 * WIDE, 3 * WIDE)


def from_shift(value, shift):
    count = lax.axis_size("tile")
    return lax.ppermute(value, "tile", [(i, (i - shift) % count) for i in range(count)])


def per_device(
    source, weights, block_source, block_target, edge_flip, norm_gain, first_kernel, second_kernel
):
    count = lax.axis_size("tile")
    column_rows = count // TILE_COLS
    field = source.reshape(ROWS, CHANNELS, BLOCK).transpose(1, 0, 2).reshape(-1, BLOCK)
    same, *nexts = regrid(block_target, block_source, field, weights, column_rows)

    for across in range(TILE_COLS):
        pairs = [
            (c * column_rows + p, (c ^ across) * column_rows + p + 1)
            for c in range(TILE_COLS)
            for p in range(column_rows - 1)
        ]
        nexts[across] = lax.ppermute(nexts[across], "tile", pairs)
    nexts = [nexts[across] for across in (0, 1, 2, 4, 5, 6, 7, 3)]
    same = lax.all_to_all(
        same,
        "tile",
        0,
        0,
        axis_index_groups=[
            [c * column_rows + p for c in COLUMN_ORDER] for p in range(column_rows)
        ],
        tiled=True,
    )

    gain = jnp.broadcast_to(
        jnp.pad(norm_gain, (0, PADDED - CHANNELS))[:, None], (PADDED, BLOCK)
    )
    first_taps, second_taps = tap_matrix(first_kernel), tap_matrix(second_kernel)
    same, nexts, gain, first_taps, second_taps = lax.optimization_barrier(
        (same, nexts, gain, first_taps, second_taps)
    )
    summed, upward, downward, strip = gather_rows(column_rows, edge_flip, gain, same, nexts)
    rims = [from_shift(downward, -1), from_shift(upward, 1)]
    near, far, reach = strip_plan(column_rows)
    strips = [from_shift(strip, shift) for shift in near]
    gridded, normed = normalize_rows(gain, summed)
    inner = inner_convolution(first_taps, normed)
    if column_rows == 2:
        to_west, to_east = half_strip_packs(*rims, strip)
    else:
        held = {-1: rims[0][2], 0: strip, 1: rims[1][2], **dict(zip(near, strips))}
        to_west = to_east = jnp.stack([held[at] for at in range(-reach, reach + 1)])
    to_west, to_east, inner = lax.optimization_barrier((to_west, to_east, inner))
    strips += [from_shift(to_east, -far), from_shift(to_west, far)]
    gridded_out = channels_first(gridded)
    hidden, *unfinished = inner
    base = inner_second_convolution(second_taps, hidden, gridded)
    smoothed = convolutions(
        column_rows, first_taps, second_taps, normed, base, *unfinished, *rims, strip, *strips
    )

    def placed(value):
        return value.reshape(CHANNELS, ROWS, BLOCK).transpose(1, 0, 2)[:, None]

    return placed(gridded_out), placed(smoothed)


def solution(mesh):
    in_specs = (
        P("tile", "groups", None, None),
        P("tile", None, None),
        P("tile"),
        P("tile"),
        P("tile", None),
        P(),
        P(),
        P(),
    )
    out_specs = (P("tile", "groups", None, None), P("tile", "groups", None, None))
    return jax.shard_map(
        per_device, mesh=mesh, in_specs=in_specs, out_specs=out_specs, check_vma=False
    )
```

```python
import functools

import jax
import jax.numpy as jnp
from jax import lax
from jax.experimental import pallas as pl
from jax.experimental.pallas import tpu as pltpu
from jax.sharding import PartitionSpec as P

BLOCK = 128
CHANNELS = 69
PADDED = 72
WIDE = 80
ROWS = 32
ROW_BITS = 5
HALF_ROWS = ROWS // 2
TILE_COLS = 8
CAP = 8
HALF = TILE_COLS // 2
GROUPS = 2 * TILE_COLS
COLUMN_ORDER = [half * HALF + at for at in range(HALF) for half in range(2)]
SLOTS = GROUPS * CAP
MARK = CHANNELS
BODY = 64
TAILS = (MARK + 1 - BODY) * CAP
MESSAGE = CAP * BODY + TAILS
CHUNK = 96
EPSILON = 1e-05
VMEM_LIMIT = 40 * 1024 * 1024
REGRID_VMEM = 60 * 1024 * 1024


def vmem():
    return pl.BlockSpec(memory_space=pltpu.VMEM)


def smem():
    return pl.BlockSpec(memory_space=pltpu.SMEM)


def split(value, size):
    if size & (size - 1) == 0:
        return value >> (size.bit_length() - 1), value & (size - 1)
    return lax.div(value, size), lax.rem(value, size)


def lanes(shape):
    return lax.broadcasted_iota(jnp.int32, shape, len(shape) - 1)


def regrid_kernel(
    column_rows, target_hbm, target_row_hbm, index_hbm, source_hbm, weight_hbm, *rest
):
    same_out, next_outs = rest[0], rest[1 : 1 + TILE_COLS]
    (
        target_ref,
        target_row_ref,
        index_ref,
        source,
        weight,
        wide,
        field,
        sums,
        message,
        tails,
        plan,
        plan_scalars,
        plan_sem,
        in_sems,
        weight_sems,
        out_sems,
    ) = rest[1 + TILE_COLS :]
    entries = weight.shape[0]
    chunks = entries // CHUNK
    tile = lax.axis_index("tile")
    column, position = split(tile, column_rows)

    small_copies = [
        pltpu.make_async_copy(target_row_hbm, target_row_ref, in_sems.at[0]),
        pltpu.make_async_copy(target_hbm, target_ref, in_sems.at[1]),
        pltpu.make_async_copy(index_hbm, index_ref, in_sems.at[2]),
    ]
    source_copy = pltpu.make_async_copy(source_hbm, source, in_sems.at[3])
    for copy in small_copies:
        copy.start()
    source_copy.start()

    def chunk_copy(chunk):
        part = pl.ds(chunk * CHUNK, CHUNK)
        return pltpu.make_async_copy(weight_hbm.at[part], weight.at[part], weight_sems.at[chunk])

    for chunk in range(chunks):
        chunk_copy(chunk).start()

    small_copies[0].wait()
    target = target_row_ref[...]
    owner, row = split(target, ROWS)
    owner_column, owner_position = split(owner, column_rows)
    place = ((owner_column & (HALF - 1)) << 1) + (owner_column >= HALF).astype(jnp.int32)
    group = jnp.where(owner_position == position, place, TILE_COLS + (owner_column ^ column))
    key = group * ROWS + row
    square = (entries, entries)
    down = lax.broadcasted_iota(jnp.int32, square, 0)
    along = lanes(square)
    key_along = jnp.broadcast_to(key.astype(jnp.float32), square)
    key_down = jnp.broadcast_to(
        jnp.sum(jnp.where(down == along, key_along, 0.0), axis=1, keepdims=True), square
    )
    equal = key_along == key_down
    doubles = jnp.sum(jnp.where(equal & (along < down), 1.0, 0.0), axis=1, keepdims=True)
    in_group = (key_down.astype(jnp.int32) >> ROW_BITS) == (key_along.astype(jnp.int32) >> ROW_BITS)
    below = in_group & (key_down < key_along) & (jnp.broadcast_to(doubles, square) == 0.0)
    rank = jnp.sum(jnp.where(below, 1.0, 0.0), axis=0, keepdims=True)
    mentions = jnp.sum(jnp.where(equal & (down < along), 1.0, 0.0), axis=0, keepdims=True)
    slots = group * CAP + rank.astype(jnp.int32)
    plan[...] = slots + jnp.where(mentions == 0.0, SLOTS, 0)
    plan_copy = pltpu.make_async_copy(plan, plan_scalars, plan_sem)
    plan_copy.start()

    for slot in range(SLOTS):
        tails[pl.ds(slot * 8, 8), :] = jnp.full((8, BLOCK), ROWS, jnp.float32)
    wide[pl.ds(CHANNELS * ROWS, (PADDED - CHANNELS) * ROWS), :] = jnp.zeros(
        ((PADDED - CHANNELS) * ROWS, BLOCK), jnp.float32
    )
    nothing = jnp.zeros((WIDE - PADDED, BLOCK), jnp.float32)
    source_copy.wait()
    wide[pl.ds(0, CHANNELS * ROWS), :] = source[...].astype(jnp.float32)
    turned = jnp.transpose(wide[...].reshape(PADDED, ROWS, BLOCK), (1, 0, 2))
    for row in range(ROWS):
        field[row] = jnp.concatenate([turned[row], nothing], axis=0).astype(jnp.bfloat16)
    is_mark = lax.broadcasted_iota(jnp.int32, (8, BLOCK), 0) == MARK - BODY
    blank = jnp.zeros((WIDE, BLOCK), jnp.bfloat16)
    small_copies[1].wait()
    small_copies[2].wait()
    plan_copy.wait()

    for chunk in range(chunks):
        chunk_copy(chunk).wait()
        for entry in range(chunk * CHUNK, (chunk + 1) * CHUNK, 2):
            one = jnp.concatenate([field[index_ref[entry]], blank], axis=1)
            two = jnp.concatenate([blank, field[index_ref[entry + 1]]], axis=1)
            products = jnp.dot(
                jnp.concatenate([one, two], axis=0),
                weight[entry : entry + 2].reshape(2 * BLOCK, BLOCK),
                preferred_element_type=jnp.float32,
            )
            for at in range(2):
                code = plan_scalars[0, entry + at]
                slot = code & (SLOTS - 1)
                row = split(target_ref[entry + at], ROWS)[1]
                product = products[at * WIDE : at * WIDE + PADDED]
                total = jnp.where(code >= SLOTS, 0.0, sums[slot]) + product
                sums[slot] = total
                group, place = split(slot, CAP)
                message[group, pl.ds(pl.multiple_of(place * BODY, BODY), BODY), :] = total[
                    :BODY
                ].astype(jnp.bfloat16)
                tails[pl.ds(pl.multiple_of(slot * 8, 8), 8), :] = jnp.where(
                    is_mark, row.astype(jnp.float32), total[BODY:]
                )
    copies = []
    for group in range(GROUPS):
        start = group * CAP * 8
        ends = [tails[pl.ds(start + at, CAP, stride=8), :] for at in range(MARK + 1 - BODY)]
        message[group, CAP * BODY :] = jnp.concatenate(ends, axis=0).astype(jnp.bfloat16)
        if group < TILE_COLS:
            out = same_out.at[pl.ds(group * MESSAGE, MESSAGE)]
        else:
            out = next_outs[group - TILE_COLS]
        copies.append(pltpu.make_async_copy(message.at[group], out, out_sems.at[group]))
        copies[-1].start()
    for copy in copies:
        copy.wait()


def regrid(target, source_index, field, weights, column_rows):
    piece = jax.ShapeDtypeStruct((MESSAGE, BLOCK), jnp.bfloat16)
    same = jax.ShapeDtypeStruct((TILE_COLS * MESSAGE, BLOCK), jnp.bfloat16)
    hbm = pl.BlockSpec(memory_space=pl.ANY)
    entries = weights.shape[0]
    return pl.pallas_call(
        functools.partial(regrid_kernel, column_rows),
        in_specs=[hbm] * 5,
        out_specs=[hbm] * (1 + TILE_COLS),
        out_shape=[same] + [piece] * TILE_COLS,
        scratch_shapes=[
            pltpu.SMEM(target.shape, jnp.int32),
            pltpu.VMEM((1, entries), jnp.int32),
            pltpu.SMEM(source_index.shape, jnp.int32),
            pltpu.VMEM(field.shape, jnp.bfloat16),
            pltpu.VMEM(weights.shape, jnp.bfloat16),
            pltpu.VMEM((PADDED * ROWS, BLOCK), jnp.float32),
            pltpu.VMEM((ROWS, WIDE, BLOCK), jnp.bfloat16),
            pltpu.VMEM((SLOTS, PADDED, BLOCK), jnp.float32),
            pltpu.VMEM((GROUPS, MESSAGE, BLOCK), jnp.bfloat16),
            pltpu.VMEM((SLOTS * 8, BLOCK), jnp.float32),
            pltpu.VMEM((1, entries), jnp.int32),
            pltpu.SMEM((1, entries), jnp.int32),
            pltpu.SemaphoreType.DMA,
            pltpu.SemaphoreType.DMA((4,)),
            pltpu.SemaphoreType.DMA((entries // CHUNK,)),
            pltpu.SemaphoreType.DMA((GROUPS,)),
        ],
        compiler_params=pltpu.CompilerParams(vmem_limit_bytes=REGRID_VMEM),
        name="regrid",
    )(target, target.reshape(1, -1), source_index, field, weights)


def normalized(rounded, gain):
    value = rounded.astype(jnp.float32)
    real = lax.broadcasted_iota(jnp.int32, (PADDED - BODY, BLOCK), 0) < CHANNELS - BODY
    value = jnp.concatenate([value[:BODY], jnp.where(real, value[BODY:], 0.0)], axis=0)
    square = jnp.sum(value * value, axis=0, keepdims=True) * (1.0 / CHANNELS)
    scaled = value * lax.rsqrt(square + EPSILON) * gain
    nothing = jnp.zeros((WIDE - PADDED, BLOCK), jnp.float32)
    return jnp.concatenate([scaled, nothing], axis=0).astype(jnp.bfloat16)


def gather_kernel(column_rows, flip_ref, gain_ref, same, *rest):
    nexts = rest[:TILE_COLS]
    summed, upward, downward, strip_out, tails = rest[TILE_COLS:]
    position = lax.rem(lax.axis_index("tile"), column_rows)
    summed[...] = jnp.zeros_like(summed)

    def add(group, piece):
        ends = piece[CAP * BODY :].astype(jnp.float32)
        tails[group, :TAILS] = ends
        rows = ends[TAILS - CAP :].astype(jnp.int32)
        for place in range(CAP):
            row = rows[place, 0]
            body = piece[place * BODY : (place + 1) * BODY].astype(jnp.float32)
            summed[row, :BODY] = summed[row, :BODY] + body
            tail = tails[group, pl.ds(place, 8, stride=CAP), :]
            summed[row, BODY:] = summed[row, BODY:] + tail

    tails[:, TAILS:] = jnp.zeros((GROUPS, 8 * CAP - TAILS, BLOCK), jnp.float32)
    for group in range(TILE_COLS):
        add(group, same.at[pl.ds(group * MESSAGE, MESSAGE)])

    @pl.when(position > 0)
    def _():
        for group in range(TILE_COLS):
            add(TILE_COLS + group, nexts[group])

    gain = gain_ref[...]
    for at in range(2):
        upward[at] = normalized(summed[at].astype(jnp.bfloat16), gain)
        downward[at] = normalized(summed[ROWS - 2 + at].astype(jnp.bfloat16), gain)
    lane = lanes((PADDED, BLOCK))
    strip = jnp.zeros((PADDED, BLOCK), jnp.bfloat16)
    for row in range(ROWS):
        rounded = summed[row].astype(jnp.bfloat16)
        strip = jnp.where((lane >> 2) == row, pltpu.roll(rounded, 4 * row + 2, 1), strip)
    to_lane = lanes((BLOCK, BLOCK))
    from_lane = 4 * (to_lane & (ROWS - 1)) + (((to_lane >> ROW_BITS) + 2) & 3)
    order = lax.broadcasted_iota(jnp.int32, (BLOCK, BLOCK), 0) == from_lane
    strip = jnp.dot(
        normalized(strip, gain), order.astype(jnp.bfloat16), preferred_element_type=jnp.float32
    )
    channel = lax.broadcasted_iota(jnp.int32, (WIDE, BLOCK), 0)
    for side in range(2):
        strip = jnp.where(channel == CHANNELS + side, flip_ref[0, side].astype(jnp.float32), strip)
    strip = strip.astype(jnp.bfloat16)
    upward[2] = strip
    downward[2] = strip
    strip_out[...] = strip


def normalize_kernel(gain_ref, summed, gridded, normed):
    gain = gain_ref[...]
    for row in range(ROWS):
        rounded = summed[row].astype(jnp.bfloat16)
        gridded[row] = rounded
        normed[row] = normalized(rounded, gain)


def normalize_rows(gain, summed):
    return pl.pallas_call(
        normalize_kernel,
        in_specs=[vmem()] * 2,
        out_specs=[vmem()] * 2,
        out_shape=[GRIDDED, FIELD],
        compiler_params=pltpu.CompilerParams(vmem_limit_bytes=VMEM_LIMIT),
        cost_estimate=pl.CostEstimate(
            flops=10 * ROWS * PADDED * BLOCK, bytes_accessed=2 << 20, transcendentals=0
        ),
        name="normalize_rows",
    )(gain, summed)


SUMMED = jax.ShapeDtypeStruct((ROWS + 1, PADDED, BLOCK), jnp.float32)
GRIDDED = jax.ShapeDtypeStruct((ROWS, PADDED, BLOCK), jnp.bfloat16)
FIELD = jax.ShapeDtypeStruct((ROWS, WIDE, BLOCK), jnp.bfloat16)
RIM = jax.ShapeDtypeStruct((3, WIDE, BLOCK), jnp.bfloat16)
STRIP_COLUMNS = (0, 1, BLOCK - 2, BLOCK - 1)
STRIP = jax.ShapeDtypeStruct((WIDE, BLOCK), jnp.bfloat16)


def gather_rows(column_rows, edge_flip, gain, same, nexts):
    return pl.pallas_call(
        functools.partial(gather_kernel, column_rows),
        in_specs=[smem()] + [vmem()] * (2 + TILE_COLS),
        out_specs=[vmem()] * 4,
        out_shape=[SUMMED, RIM, RIM, STRIP],
        scratch_shapes=[pltpu.VMEM((GROUPS, 8 * CAP, BLOCK), jnp.float32)],
        compiler_params=pltpu.CompilerParams(vmem_limit_bytes=VMEM_LIMIT),
        name="gather_rows",
    )(edge_flip, gain, same, *nexts)


def turn_kernel(field, out):
    turned = jnp.transpose(field[...].astype(jnp.float32), (1, 0, 2))
    out[...] = turned[:CHANNELS].reshape(CHANNELS * ROWS, BLOCK).astype(jnp.bfloat16)


def channels_first(field):
    return pl.pallas_call(
        turn_kernel,
        in_specs=[vmem()],
        out_specs=vmem(),
        out_shape=jax.ShapeDtypeStruct((CHANNELS * ROWS, BLOCK), jnp.bfloat16),
        compiler_params=pltpu.CompilerParams(vmem_limit_bytes=VMEM_LIMIT),
        name="channels_first",
    )(field)


def shifted_columns(value, left_end, right_end):
    lane = lanes((WIDE, BLOCK))
    left = jnp.where(lane == 0, left_end, pltpu.roll(value, 1, 1))
    right = jnp.where(lane == BLOCK - 1, right_end, pltpu.roll(value, BLOCK - 1, 1))
    return jnp.concatenate([left, value, right], axis=0)


def tap_sums(taps, one, two):
    both = jnp.concatenate([one, two], axis=1)
    result = jnp.dot(taps, both, preferred_element_type=jnp.float32)
    return result[:, :BLOCK], result[:, BLOCK:]


def row_tap(sums, at):
    return sums[at * WIDE : (at + 1) * WIDE]


def activated(value):
    return jax.nn.gelu(value).astype(jnp.bfloat16)


def inner_kernel(taps_ref, field, hidden, ends, sides, partial):
    taps = taps_ref[...]
    blank = jnp.zeros((WIDE, BLOCK), jnp.bfloat16)
    for row in range(0, ROWS, 2):
        partial[row], partial[row + 1] = tap_sums(
            taps,
            shifted_columns(field[row], blank, blank),
            shifted_columns(field[row + 1], blank, blank),
        )
    lane = lanes((WIDE, BLOCK))
    west = jnp.zeros((WIDE, BLOCK), jnp.float32)
    east = jnp.zeros((WIDE, BLOCK), jnp.float32)
    for row in range(ROWS):
        value = partial[row, WIDE : 2 * WIDE]
        if row > 0:
            value = value + partial[row - 1, :WIDE]
        if row < ROWS - 1:
            value = value + partial[row + 1, 2 * WIDE :]
        if row == 0:
            ends[0] = value
        elif row == ROWS - 1:
            ends[1] = value
        else:
            hidden[row] = jnp.where((lane == 0) | (lane == BLOCK - 1), blank, activated(value))
        west = jnp.where(lane == row, pltpu.roll(value, row, 1), west)
        east = jnp.where(lane == row, pltpu.roll(value, row + 1, 1), east)
    hidden[0] = blank
    hidden[ROWS - 1] = blank
    sides[0] = west
    sides[1] = east


def inner_convolution(taps, field):
    pair = jax.ShapeDtypeStruct((2, WIDE, BLOCK), jnp.float32)
    return pl.pallas_call(
        inner_kernel,
        in_specs=[vmem()] * 2,
        out_specs=[vmem()] * 3,
        out_shape=[FIELD, pair, pair],
        scratch_shapes=[pltpu.VMEM((ROWS, 3 * WIDE, BLOCK), jnp.float32)],
        compiler_params=pltpu.CompilerParams(vmem_limit_bytes=VMEM_LIMIT),
        cost_estimate=pl.CostEstimate(
            flops=2 * 9 * WIDE * WIDE * ROWS * BLOCK, bytes_accessed=2 << 20, transcendentals=0
        ),
        name="inner_convolution",
    )(taps, field)


def second_kernel_inner(taps_ref, hidden, gridded, base, partial):
    taps = taps_ref[...]
    blank = jnp.zeros((WIDE, BLOCK), jnp.bfloat16)
    for row in range(0, ROWS, 2):
        partial[row], partial[row + 1] = tap_sums(
            taps,
            shifted_columns(hidden[row], blank, blank),
            shifted_columns(hidden[row + 1], blank, blank),
        )
    for row in range(ROWS):
        value = gridded[row].astype(jnp.float32) + partial[row, WIDE : WIDE + PADDED]
        if row > 0:
            value = value + partial[row - 1, :PADDED]
        if row < ROWS - 1:
            value = value + partial[row + 1, 2 * WIDE : 2 * WIDE + PADDED]
        base[row] = value


def inner_second_convolution(taps, hidden, gridded):
    return pl.pallas_call(
        second_kernel_inner,
        in_specs=[vmem()] * 3,
        out_specs=vmem(),
        out_shape=jax.ShapeDtypeStruct((ROWS, PADDED, BLOCK), jnp.float32),
        scratch_shapes=[pltpu.VMEM((ROWS, 3 * WIDE, BLOCK), jnp.float32)],
        compiler_params=pltpu.CompilerParams(vmem_limit_bytes=VMEM_LIMIT),
        cost_estimate=pl.CostEstimate(
            flops=2 * 9 * WIDE * WIDE * ROWS * BLOCK, bytes_accessed=2 << 20, transcendentals=0
        ),
        name="inner_second_convolution",
    )(taps, hidden, gridded)


def pack_kernel(above, below, own, to_west, to_east):
    low = lanes((WIDE, BLOCK)) < BLOCK // 2
    before, strip, after = above[2], own[...], below[2]

    def other_half(plane):
        return pltpu.roll(plane, BLOCK // 2, 1)

    outer = jnp.where(low, after, before)
    to_east[0] = jnp.where(low, other_half(strip), after)
    to_east[1] = outer
    to_west[0] = jnp.where(low, strip, other_half(before))
    to_west[1] = outer


def half_strip_packs(above, below, own):
    pack = jax.ShapeDtypeStruct((2, WIDE, BLOCK), jnp.bfloat16)
    return pl.pallas_call(
        pack_kernel,
        in_specs=[vmem()] * 3,
        out_specs=[vmem()] * 2,
        out_shape=[pack, pack],
        compiler_params=pltpu.CompilerParams(vmem_limit_bytes=VMEM_LIMIT),
        name="half_strip_packs",
    )(above, below, own)


def half_strips(west_pack, east_pack):
    low = lanes((WIDE, BLOCK)) < BLOCK // 2

    def other_half(plane):
        return pltpu.roll(plane, BLOCK // 2, 1)

    def both_halves(plane):
        return jnp.where(low, plane, other_half(plane))

    return {
        -4: west_pack[1],
        -3: both_halves(west_pack[0]),
        -2: jnp.where(low, west_pack[1], west_pack[0]),
        2: jnp.where(low, other_half(east_pack[0]), east_pack[1]),
        3: both_halves(east_pack[0]),
        4: east_pack[1],
    }


def strip_plan(column_rows):
    if column_rows == 2:
        return [], 3, 1
    return [-2, 2], column_rows, 2


def conv_kernel(
    column_rows,
    first_taps_ref,
    second_taps_ref,
    field,
    base,
    ends_ref,
    sides_ref,
    above,
    below,
    own_strip,
    *rest,
):
    near, far, reach = strip_plan(column_rows)
    near_strips, (west_pack, east_pack) = rest[: len(near)], rest[len(near) : len(near) + 2]
    smoothed, unturned, halves, sems = rest[len(near) + 2 :]
    count = lax.axis_size("tile")
    tile = lax.axis_index("tile")
    lane = lanes((WIDE, BLOCK))
    last = ROWS + 1
    R = column_rows
    blank = jnp.zeros((WIDE, BLOCK), jnp.bfloat16)

    strips = {-1: above[2], 0: own_strip[...], 1: below[2]}
    strips.update((shift, ref[...]) for shift, ref in zip(near, near_strips))
    if R == 2:
        strips.update(half_strips(west_pack, east_pack))
    else:
        for at in range(-reach, reach + 1):
            strips[at - far], strips[at + far] = west_pack[at + reach], east_pack[at + reach]

    def place(shift):
        return lax.rem(tile + shift + count, count)

    def ends(shift, before, after, middle):
        before = jnp.where(place(shift) > 0, before, blank)
        after = jnp.where(place(shift) < count - 1, after, blank)
        return jnp.where(lane == 0, before, jnp.where(lane == last, after, middle))

    memo = {}

    def padded_column(shift, which):
        if (shift, which) not in memo:
            base = which * ROWS
            memo[shift, which] = ends(
                shift,
                pltpu.roll(strips[shift - 1], (1 - base - ROWS) % BLOCK, 1),
                pltpu.roll(strips[shift + 1], (last - base) % BLOCK, 1),
                pltpu.roll(strips[shift], (1 - base) % BLOCK, 1),
            )
        return memo[shift, which]

    row_id = lax.broadcasted_iota(jnp.int32, (BLOCK, BLOCK), 0)
    reversal = (row_id + lanes((BLOCK, BLOCK)) == last).astype(jnp.bfloat16)

    def reversed_lanes(planes):
        stacked = jnp.concatenate(planes, axis=0)
        turned_round = jnp.dot(stacked, reversal, preferred_element_type=jnp.float32)
        return [row_tap(turned_round, at) for at in range(len(planes))]

    def choose(shift, which, turned_round, plain):
        flips = strips[shift].astype(jnp.float32)[CHANNELS + which : CHANNELS + which + 1]
        return jnp.where(flips > 0.5, turned_round, plain.astype(jnp.float32)).astype(jnp.bfloat16)

    west_of = {shift: (shift - R, 3) for shift in {-1, 0, 1, R - 1, R, R + 1}}
    east_of = {shift: (shift + R, 0) for shift in {-1, 0, 1, -R - 1, -R, -R + 1}}
    keys = sorted(set(west_of.values()) | set(east_of.values()))
    flipped = dict(zip(keys, reversed_lanes([padded_column(*key) for key in keys])))
    west = {
        shift: choose(shift, 0, flipped[west_of[shift]], padded_column(*west_of[shift]))
        for shift in sorted(west_of)
    }
    east = {
        shift: choose(shift, 1, flipped[east_of[shift]], padded_column(*east_of[shift]))
        for shift in sorted(east_of)
    }

    def columns(value, west_plane, west_row, east_plane, east_row):
        return shifted_columns(
            value,
            pltpu.roll(west_plane, (BLOCK - west_row) % BLOCK, 1),
            pltpu.roll(east_plane, BLOCK - 1 - east_row, 1),
        )

    def along(result):
        return (
            row_tap(result, 0)
            + pltpu.roll(row_tap(result, 1), BLOCK - 1, 1)
            + pltpu.roll(row_tap(result, 2), BLOCK - 2, 1)
        )

    first_taps = first_taps_ref[...]
    up = [jnp.where(tile > 0, above[at], blank) for at in range(2)]
    down = [jnp.where(tile < count - 1, below[at], blank) for at in range(2)]
    from_up, from_down = tap_sums(
        first_taps, shifted_columns(up[1], blank, blank), shifted_columns(down[0], blank, blank)
    )
    from_up, from_down = row_tap(from_up, 0), row_tap(from_down, 2)
    from_west, from_east = tap_sums(
        first_taps,
        jnp.concatenate([west[0], blank, blank], axis=0),
        jnp.concatenate([blank, blank, east[0]], axis=0),
    )
    from_west, from_east = along(from_west), along(from_east)
    first = ends_ref[0] + from_up
    first = first + jnp.where(lane == 0, from_west, 0.0)
    first = first + jnp.where(lane == BLOCK - 1, pltpu.roll(from_east, BLOCK - 1, 1), 0.0)
    final = ends_ref[1] + from_down
    final = final + jnp.where(lane == 0, pltpu.roll(from_west, BLOCK - ROWS + 1, 1), 0.0)
    final = final + jnp.where(lane == BLOCK - 1, pltpu.roll(from_east, BLOCK - ROWS, 1), 0.0)
    first, final = activated(first), activated(final)
    first_column = activated(sides_ref[0] + from_west)
    last_column = activated(sides_ref[1] + from_east)

    upper = jnp.zeros((WIDE, BLOCK), jnp.float32)
    lower = jnp.zeros((WIDE, BLOCK), jnp.float32)
    for at, (high, low) in enumerate(
        [(up[0], field[ROWS - 1]), (up[1], down[0]), (field[0], down[1])]
    ):
        from_row = ROWS - 1 + at
        one, two = tap_sums(
            row_tap(first_taps, at),
            columns(high, west[-1], from_row, east[-1], from_row),
            columns(low, west[1], at, east[1], at),
        )
        upper += one
        lower += two
    top = jnp.where(tile > 0, activated(upper), blank)
    bottom = jnp.where(tile < count - 1, activated(lower), blank)

    west_hidden, east_hidden = {}, {}
    for at in (-1, 0, 1):
        q = at - R
        one = jnp.concatenate([padded_column(q, 2), padded_column(q, 3), east[q]], axis=0)
        q = at + R
        two = jnp.concatenate([west[q], padded_column(q, 0), padded_column(q, 1)], axis=0)
        one, two = tap_sums(first_taps, one, two)
        west_hidden[at], east_hidden[at] = activated(along(one)), activated(along(two))

    def hidden_side(shift, values):
        return ends(
            shift,
            pltpu.roll(values[-1], BLOCK - ROWS + 1, 1),
            pltpu.roll(values[1], last, 1),
            pltpu.roll(values[0], 1, 1),
        )

    plain = [hidden_side(-R, west_hidden), hidden_side(R, east_hidden)]
    west_side, east_side = [
        choose(0, which, turned_side, plain[which])
        for which, turned_side in enumerate(reversed_lanes(plain))
    ]

    second_taps = second_taps_ref[...]
    from_top, from_first = tap_sums(
        second_taps,
        columns(top, west_side, 0, east_side, 0),
        columns(first, west_side, 1, east_side, 1),
    )
    from_final, from_bottom = tap_sums(
        second_taps,
        columns(final, west_side, ROWS, east_side, ROWS),
        columns(bottom, west_side, last, east_side, last),
    )
    rim_rows = {
        0: row_tap(from_top, 0) + row_tap(from_first, 1),
        1: row_tap(from_first, 0),
        ROWS - 2: row_tap(from_final, 2),
        ROWS - 1: row_tap(from_final, 1) + row_tap(from_bottom, 2),
    }

    other = (lane >= 2) & (lane < ROWS)

    def other_rows(plane):
        return jnp.where(other, plane, blank)

    near_west, near_east = other_rows(west_side), other_rows(east_side)
    first_column = other_rows(pltpu.roll(first_column, 1, 1))
    last_column = other_rows(pltpu.roll(last_column, 1, 1))
    to_0, to_1 = tap_sums(
        second_taps,
        jnp.concatenate([near_west, first_column, blank], axis=0),
        jnp.concatenate([first_column, blank, blank], axis=0),
    )
    to_127, to_126 = tap_sums(
        second_taps,
        jnp.concatenate([blank, last_column, near_east], axis=0),
        jnp.concatenate([blank, blank, last_column], axis=0),
    )
    spread = jnp.zeros((WIDE, BLOCK), jnp.float32)
    for at, sums in enumerate((to_126, to_127, to_0, to_1)):
        sums = along(sums)
        high = sums.astype(jnp.bfloat16)
        sums = sums - high.astype(jnp.float32)
        middle = sums.astype(jnp.bfloat16)
        low = (sums - middle.astype(jnp.float32)).astype(jnp.bfloat16)
        to_lane = (lanes((BLOCK, BLOCK)) == 4 * row_id + at).astype(jnp.bfloat16)
        parts = jnp.dot(
            jnp.concatenate([high, middle, low], axis=0),
            to_lane,
            preferred_element_type=jnp.float32,
        )
        spread = spread + (row_tap(parts, 0) + (row_tap(parts, 1) + row_tap(parts, 2)))

    rim_lanes = lanes((PADDED, BLOCK))
    rim_lanes = (rim_lanes < 2) | (rim_lanes >= BLOCK - 2)
    spread = spread[:PADDED]
    copies = []
    for half in range(2):
        for row in range(half * HALF_ROWS, (half + 1) * HALF_ROWS):
            value = base[row] + jnp.where(
                rim_lanes, pltpu.roll(spread, (BLOCK - 4 * row - 2) % BLOCK, 1), 0.0
            )
            if row in rim_rows:
                value = value + rim_rows[row][:PADDED]
            unturned[half, row - half * HALF_ROWS] = value
        halves[half] = jnp.transpose(unturned[half], (1, 0, 2))[:CHANNELS].astype(jnp.bfloat16)
        rows = pl.ds(half * HALF_ROWS, HALF_ROWS)
        copies.append(pltpu.make_async_copy(halves.at[half], smoothed.at[:, rows], sems.at[half]))
        copies[-1].start()
    for copy in copies:
        copy.wait()


def convolutions(column_rows, *operands):
    return pl.pallas_call(
        functools.partial(conv_kernel, column_rows),
        in_specs=[vmem()] * len(operands),
        out_specs=pl.BlockSpec(memory_space=pl.ANY),
        out_shape=jax.ShapeDtypeStruct((CHANNELS, ROWS, BLOCK), jnp.bfloat16),
        scratch_shapes=[
            pltpu.VMEM((2, HALF_ROWS, PADDED, BLOCK), jnp.float32),
            pltpu.VMEM((2, CHANNELS, HALF_ROWS, BLOCK), jnp.bfloat16),
            pltpu.SemaphoreType.DMA((2,)),
        ],
        compiler_params=pltpu.CompilerParams(vmem_limit_bytes=VMEM_LIMIT),
        name="convolutions",
    )(*operands)


def tap_matrix(kernel):
    pad = WIDE - CHANNELS
    taps = jnp.pad(kernel, ((0, 0), (0, pad), (0, pad))).reshape(3, 3, WIDE, WIDE)
    return taps.transpose(0, 2, 1, 3).reshape(3 * WIDE, 3 * WIDE)


def from_shift(value, shift):
    count = lax.axis_size("tile")
    return lax.ppermute(value, "tile", [(i, (i - shift) % count) for i in range(count)])


def per_device(
    source, weights, block_source, block_target, edge_flip, norm_gain, first_kernel, second_kernel
):
    count = lax.axis_size("tile")
    column_rows = count // TILE_COLS
    field = source.reshape(ROWS, CHANNELS, BLOCK).transpose(1, 0, 2).reshape(-1, BLOCK)
    same, *nexts = regrid(block_target, block_source, field, weights, column_rows)

    for across in range(TILE_COLS):
        pairs = [
            (c * column_rows + p, (c ^ across) * column_rows + p + 1)
            for c in range(TILE_COLS)
            for p in range(column_rows - 1)
        ]
        nexts[across] = lax.ppermute(nexts[across], "tile", pairs)
    nexts = [nexts[across] for across in (0, 1, 2, 4, 5, 6, 7, 3)]
    same = lax.all_to_all(
        same,
        "tile",
        0,
        0,
        axis_index_groups=[
            [c * column_rows + p for c in COLUMN_ORDER] for p in range(column_rows)
        ],
        tiled=True,
    )

    gain = jnp.broadcast_to(
        jnp.pad(norm_gain, (0, PADDED - CHANNELS))[:, None], (PADDED, BLOCK)
    )
    first_taps, second_taps = tap_matrix(first_kernel), tap_matrix(second_kernel)
    same, nexts, gain, first_taps, second_taps = lax.optimization_barrier(
        (same, nexts, gain, first_taps, second_taps)
    )
    summed, upward, downward, strip = gather_rows(column_rows, edge_flip, gain, same, nexts)
    rims = [from_shift(downward, -1), from_shift(upward, 1)]
    near, far, reach = strip_plan(column_rows)
    strips = [from_shift(strip, shift) for shift in near]
    gridded, normed = normalize_rows(gain, summed)
    inner = inner_convolution(first_taps, normed)
    if column_rows == 2:
        to_west, to_east = half_strip_packs(*rims, strip)
    else:
        held = {-1: rims[0][2], 0: strip, 1: rims[1][2], **dict(zip(near, strips))}
        to_west = to_east = jnp.stack([held[at] for at in range(-reach, reach + 1)])
    to_west, to_east, inner = lax.optimization_barrier((to_west, to_east, inner))
    strips += [from_shift(to_east, -far), from_shift(to_west, far)]
    gridded_out = channels_first(gridded)
    hidden, *unfinished = inner
    base = inner_second_convolution(second_taps, hidden, gridded)
    smoothed = convolutions(
        column_rows, first_taps, second_taps, normed, base, *unfinished, *rims, strip, *strips
    )

    def placed(value):
        return value.reshape(CHANNELS, ROWS, BLOCK).transpose(1, 0, 2)[:, None]

    return placed(gridded_out), placed(smoothed)


def solution(mesh):
    in_specs = (
        P("tile", "groups", None, None),
        P("tile", None, None),
        P("tile"),
        P("tile"),
        P("tile", None),
        P(),
        P(),
        P(),
    )
    out_specs = (P("tile", "groups", None, None), P("tile", "groups", None, None))
    return jax.shard_map(
        per_device, mesh=mesh, in_specs=in_specs, out_specs=out_specs, check_vma=False
    )
```

```python
import functools

import jax
import jax.numpy as jnp
from jax import lax
from jax.experimental import pallas as pl
from jax.experimental.pallas import tpu as pltpu
from jax.sharding import PartitionSpec as P

BLOCK = 128
CHANNELS = 69
PADDED = 72
WIDE = 80
ROWS = 32
ROW_BITS = 5
HALF_ROWS = ROWS // 2
TILE_COLS = 8
CAP = 8
HALF = TILE_COLS // 2
GROUPS = 2 * TILE_COLS
COLUMN_ORDER = [half * HALF + at for at in range(HALF) for half in range(2)]
SLOTS = GROUPS * CAP
MARK = CHANNELS
BODY = 64
TAILS = (MARK + 1 - BODY) * CAP
MESSAGE = CAP * BODY + TAILS
CHUNK = 96
EPSILON = 1e-05
VMEM_LIMIT = 40 * 1024 * 1024
REGRID_VMEM = 60 * 1024 * 1024


def vmem():
    return pl.BlockSpec(memory_space=pltpu.VMEM)


def smem():
    return pl.BlockSpec(memory_space=pltpu.SMEM)


def split(value, size):
    if size & (size - 1) == 0:
        return value >> (size.bit_length() - 1), value & (size - 1)
    return lax.div(value, size), lax.rem(value, size)


def lanes(shape):
    return lax.broadcasted_iota(jnp.int32, shape, len(shape) - 1)


def regrid_kernel(
    column_rows, target_hbm, target_row_hbm, index_hbm, source_hbm, weight_hbm, *rest
):
    same_out, next_outs = rest[0], rest[1 : 1 + TILE_COLS]
    (
        target_ref,
        target_row_ref,
        index_ref,
        source,
        weight,
        wide,
        field,
        sums,
        message,
        tails,
        plan,
        plan_scalars,
        plan_sem,
        in_sems,
        weight_sems,
        out_sems,
    ) = rest[1 + TILE_COLS :]
    entries = weight.shape[0]
    chunks = entries // CHUNK
    tile = lax.axis_index("tile")
    column, position = split(tile, column_rows)

    small_copies = [
        pltpu.make_async_copy(target_row_hbm, target_row_ref, in_sems.at[0]),
        pltpu.make_async_copy(target_hbm, target_ref, in_sems.at[1]),
        pltpu.make_async_copy(index_hbm, index_ref, in_sems.at[2]),
    ]
    source_copy = pltpu.make_async_copy(source_hbm, source, in_sems.at[3])
    for copy in small_copies:
        copy.start()
    source_copy.start()

    def chunk_copy(chunk):
        part = pl.ds(chunk * CHUNK, CHUNK)
        return pltpu.make_async_copy(weight_hbm.at[part], weight.at[part], weight_sems.at[chunk])

    for chunk in range(chunks):
        chunk_copy(chunk).start()

    small_copies[0].wait()
    target = target_row_ref[...]
    owner, row = split(target, ROWS)
    owner_column, owner_position = split(owner, column_rows)
    place = ((owner_column & (HALF - 1)) << 1) + (owner_column >= HALF).astype(jnp.int32)
    group = jnp.where(owner_position == position, place, TILE_COLS + (owner_column ^ column))
    key = group * ROWS + row
    square = (entries, entries)
    down = lax.broadcasted_iota(jnp.int32, square, 0)
    along = lanes(square)
    key_along = jnp.broadcast_to(key.astype(jnp.float32), square)
    key_down = jnp.broadcast_to(
        jnp.sum(jnp.where(down == along, key_along, 0.0), axis=1, keepdims=True), square
    )
    equal = key_along == key_down
    doubles = jnp.sum(jnp.where(equal & (along < down), 1.0, 0.0), axis=1, keepdims=True)
    in_group = (key_down.astype(jnp.int32) >> ROW_BITS) == (key_along.astype(jnp.int32) >> ROW_BITS)
    below = in_group & (key_down < key_along) & (jnp.broadcast_to(doubles, square) == 0.0)
    rank = jnp.sum(jnp.where(below, 1.0, 0.0), axis=0, keepdims=True)
    mentions = jnp.sum(jnp.where(equal & (down < along), 1.0, 0.0), axis=0, keepdims=True)
    slots = group * CAP + rank.astype(jnp.int32)
    plan[...] = slots + jnp.where(mentions == 0.0, SLOTS, 0)
    plan_copy = pltpu.make_async_copy(plan, plan_scalars, plan_sem)
    plan_copy.start()

    for slot in range(SLOTS):
        tails[pl.ds(slot * 8, 8), :] = jnp.full((8, BLOCK), ROWS, jnp.float32)
    wide[pl.ds(CHANNELS * ROWS, (PADDED - CHANNELS) * ROWS), :] = jnp.zeros(
        ((PADDED - CHANNELS) * ROWS, BLOCK), jnp.float32
    )
    nothing = jnp.zeros((WIDE - PADDED, BLOCK), jnp.float32)
    source_copy.wait()
    wide[pl.ds(0, CHANNELS * ROWS), :] = source[...].astype(jnp.float32)
    turned = jnp.transpose(wide[...].reshape(PADDED, ROWS, BLOCK), (1, 0, 2))
    for row in range(ROWS):
        field[row] = jnp.concatenate([turned[row], nothing], axis=0).astype(jnp.bfloat16)
    is_mark = lax.broadcasted_iota(jnp.int32, (8, BLOCK), 0) == MARK - BODY
    blank = jnp.zeros((WIDE, BLOCK), jnp.bfloat16)
    small_copies[1].wait()
    small_copies[2].wait()
    plan_copy.wait()

    for chunk in range(chunks):
        chunk_copy(chunk).wait()
        for entry in range(chunk * CHUNK, (chunk + 1) * CHUNK, 2):
            one = jnp.concatenate([field[index_ref[entry]], blank], axis=1)
            two = jnp.concatenate([blank, field[index_ref[entry + 1]]], axis=1)
            products = jnp.dot(
                jnp.concatenate([one, two], axis=0),
                weight[entry : entry + 2].reshape(2 * BLOCK, BLOCK),
                preferred_element_type=jnp.float32,
            )
            for at in range(2):
                code = plan_scalars[0, entry + at]
                slot = code & (SLOTS - 1)
                row = split(target_ref[entry + at], ROWS)[1]
                product = products[at * WIDE : at * WIDE + PADDED]
                total = jnp.where(code >= SLOTS, 0.0, sums[slot]) + product
                sums[slot] = total
                group, place = split(slot, CAP)
                message[group, pl.ds(pl.multiple_of(place * BODY, BODY), BODY), :] = total[
                    :BODY
                ].astype(jnp.bfloat16)
                tails[pl.ds(pl.multiple_of(slot * 8, 8), 8), :] = jnp.where(
                    is_mark, row.astype(jnp.float32), total[BODY:]
                )
    copies = []
    for group in range(GROUPS):
        start = group * CAP * 8
        ends = [tails[pl.ds(start + at, CAP, stride=8), :] for at in range(MARK + 1 - BODY)]
        message[group, CAP * BODY :] = jnp.concatenate(ends, axis=0).astype(jnp.bfloat16)
        if group < TILE_COLS:
            out = same_out.at[pl.ds(group * MESSAGE, MESSAGE)]
        else:
            out = next_outs[group - TILE_COLS]
        copies.append(pltpu.make_async_copy(message.at[group], out, out_sems.at[group]))
        copies[-1].start()
    for copy in copies:
        copy.wait()


def regrid(target, source_index, field, weights, column_rows):
    piece = jax.ShapeDtypeStruct((MESSAGE, BLOCK), jnp.bfloat16)
    same = jax.ShapeDtypeStruct((TILE_COLS * MESSAGE, BLOCK), jnp.bfloat16)
    hbm = pl.BlockSpec(memory_space=pl.ANY)
    entries = weights.shape[0]
    return pl.pallas_call(
        functools.partial(regrid_kernel, column_rows),
        in_specs=[hbm] * 5,
        out_specs=[hbm] * (1 + TILE_COLS),
        out_shape=[same] + [piece] * TILE_COLS,
        scratch_shapes=[
            pltpu.SMEM(target.shape, jnp.int32),
            pltpu.VMEM((1, entries), jnp.int32),
            pltpu.SMEM(source_index.shape, jnp.int32),
            pltpu.VMEM(field.shape, jnp.bfloat16),
            pltpu.VMEM(weights.shape, jnp.bfloat16),
            pltpu.VMEM((PADDED * ROWS, BLOCK), jnp.float32),
            pltpu.VMEM((ROWS, WIDE, BLOCK), jnp.bfloat16),
            pltpu.VMEM((SLOTS, PADDED, BLOCK), jnp.float32),
            pltpu.VMEM((GROUPS, MESSAGE, BLOCK), jnp.bfloat16),
            pltpu.VMEM((SLOTS * 8, BLOCK), jnp.float32),
            pltpu.VMEM((1, entries), jnp.int32),
            pltpu.SMEM((1, entries), jnp.int32),
            pltpu.SemaphoreType.DMA,
            pltpu.SemaphoreType.DMA((4,)),
            pltpu.SemaphoreType.DMA((entries // CHUNK,)),
            pltpu.SemaphoreType.DMA((GROUPS,)),
        ],
        compiler_params=pltpu.CompilerParams(vmem_limit_bytes=REGRID_VMEM),
        name="regrid",
    )(target, target.reshape(1, -1), source_index, field, weights)


def normalized(rounded, gain):
    value = rounded.astype(jnp.float32)
    real = lax.broadcasted_iota(jnp.int32, (PADDED - BODY, BLOCK), 0) < CHANNELS - BODY
    value = jnp.concatenate([value[:BODY], jnp.where(real, value[BODY:], 0.0)], axis=0)
    square = jnp.sum(value * value, axis=0, keepdims=True) * (1.0 / CHANNELS)
    scaled = value * lax.rsqrt(square + EPSILON) * gain
    nothing = jnp.zeros((WIDE - PADDED, BLOCK), jnp.float32)
    return jnp.concatenate([scaled, nothing], axis=0).astype(jnp.bfloat16)


def gather_kernel(column_rows, flip_ref, gain_ref, same, *rest):
    nexts = rest[:TILE_COLS]
    summed, upward, downward, strip_out, tails = rest[TILE_COLS:]
    position = lax.rem(lax.axis_index("tile"), column_rows)
    summed[...] = jnp.zeros_like(summed)

    def add(group, piece):
        ends = piece[CAP * BODY :].astype(jnp.float32)
        tails[group, :TAILS] = ends
        rows = ends[TAILS - CAP :].astype(jnp.int32)
        for place in range(CAP):
            row = rows[place, 0]
            body = piece[place * BODY : (place + 1) * BODY].astype(jnp.float32)
            summed[row, :BODY] = summed[row, :BODY] + body
            tail = tails[group, pl.ds(place, 8, stride=CAP), :]
            summed[row, BODY:] = summed[row, BODY:] + tail

    tails[:, TAILS:] = jnp.zeros((GROUPS, 8 * CAP - TAILS, BLOCK), jnp.float32)
    for group in range(TILE_COLS):
        add(group, same.at[pl.ds(group * MESSAGE, MESSAGE)])

    @pl.when(position > 0)
    def _():
        for group in range(TILE_COLS):
            add(TILE_COLS + group, nexts[group])

    gain = gain_ref[...]
    for at in range(2):
        upward[at] = normalized(summed[at].astype(jnp.bfloat16), gain)
        downward[at] = normalized(summed[ROWS - 2 + at].astype(jnp.bfloat16), gain)
    lane = lanes((PADDED, BLOCK))
    strip = jnp.zeros((PADDED, BLOCK), jnp.bfloat16)
    for row in range(ROWS):
        rounded = summed[row].astype(jnp.bfloat16)
        strip = jnp.where((lane >> 2) == row, pltpu.roll(rounded, 4 * row + 2, 1), strip)
    to_lane = lanes((BLOCK, BLOCK))
    from_lane = 4 * (to_lane & (ROWS - 1)) + (((to_lane >> ROW_BITS) + 2) & 3)
    order = lax.broadcasted_iota(jnp.int32, (BLOCK, BLOCK), 0) == from_lane
    strip = jnp.dot(
        normalized(strip, gain), order.astype(jnp.bfloat16), preferred_element_type=jnp.float32
    )
    channel = lax.broadcasted_iota(jnp.int32, (WIDE, BLOCK), 0)
    for side in range(2):
        strip = jnp.where(channel == CHANNELS + side, flip_ref[0, side].astype(jnp.float32), strip)
    strip = strip.astype(jnp.bfloat16)
    upward[2] = strip
    downward[2] = strip
    strip_out[...] = strip


def normalize_kernel(gain_ref, summed, gridded, normed):
    gain = gain_ref[...]
    for row in range(ROWS):
        rounded = summed[row].astype(jnp.bfloat16)
        gridded[row] = rounded
        normed[row] = normalized(rounded, gain)


def normalize_rows(gain, summed):
    return pl.pallas_call(
        normalize_kernel,
        in_specs=[vmem()] * 2,
        out_specs=[vmem()] * 2,
        out_shape=[GRIDDED, FIELD],
        compiler_params=pltpu.CompilerParams(vmem_limit_bytes=VMEM_LIMIT),
        cost_estimate=pl.CostEstimate(
            flops=10 * ROWS * PADDED * BLOCK, bytes_accessed=2 << 20, transcendentals=0
        ),
        name="normalize_rows",
    )(gain, summed)


SUMMED = jax.ShapeDtypeStruct((ROWS + 1, PADDED, BLOCK), jnp.float32)
GRIDDED = jax.ShapeDtypeStruct((ROWS, PADDED, BLOCK), jnp.bfloat16)
FIELD = jax.ShapeDtypeStruct((ROWS, WIDE, BLOCK), jnp.bfloat16)
RIM = jax.ShapeDtypeStruct((3, WIDE, BLOCK), jnp.bfloat16)
STRIP_COLUMNS = (0, 1, BLOCK - 2, BLOCK - 1)
STRIP = jax.ShapeDtypeStruct((WIDE, BLOCK), jnp.bfloat16)


def gather_rows(column_rows, edge_flip, gain, same, nexts):
    return pl.pallas_call(
        functools.partial(gather_kernel, column_rows),
        in_specs=[smem()] + [vmem()] * (2 + TILE_COLS),
        out_specs=[vmem()] * 4,
        out_shape=[SUMMED, RIM, RIM, STRIP],
        scratch_shapes=[pltpu.VMEM((GROUPS, 8 * CAP, BLOCK), jnp.float32)],
        compiler_params=pltpu.CompilerParams(vmem_limit_bytes=VMEM_LIMIT),
        name="gather_rows",
    )(edge_flip, gain, same, *nexts)


def turn_kernel(field, out):
    turned = jnp.transpose(field[...].astype(jnp.float32), (1, 0, 2))
    out[...] = turned[:CHANNELS].reshape(CHANNELS * ROWS, BLOCK).astype(jnp.bfloat16)


def channels_first(field):
    return pl.pallas_call(
        turn_kernel,
        in_specs=[vmem()],
        out_specs=vmem(),
        out_shape=jax.ShapeDtypeStruct((CHANNELS * ROWS, BLOCK), jnp.bfloat16),
        compiler_params=pltpu.CompilerParams(vmem_limit_bytes=VMEM_LIMIT),
        name="channels_first",
    )(field)


def shifted_columns(value, left_end, right_end):
    lane = lanes((WIDE, BLOCK))
    left = jnp.where(lane == 0, left_end, pltpu.roll(value, 1, 1))
    right = jnp.where(lane == BLOCK - 1, right_end, pltpu.roll(value, BLOCK - 1, 1))
    return jnp.concatenate([left, value, right], axis=0)


def tap_sums(taps, one, two):
    both = jnp.concatenate([one, two], axis=1)
    result = jnp.dot(taps, both, preferred_element_type=jnp.float32)
    return result[:, :BLOCK], result[:, BLOCK:]


def row_tap(sums, at):
    return sums[at * WIDE : (at + 1) * WIDE]


def activated(value):
    return jax.nn.gelu(value).astype(jnp.bfloat16)


def inner_kernel(taps_ref, field, hidden, ends, sides, partial):
    taps = taps_ref[...]
    blank = jnp.zeros((WIDE, BLOCK), jnp.bfloat16)
    for row in range(0, ROWS, 2):
        partial[row], partial[row + 1] = tap_sums(
            taps,
            shifted_columns(field[row], blank, blank),
            shifted_columns(field[row + 1], blank, blank),
        )
    lane = lanes((WIDE, BLOCK))
    west = jnp.zeros((WIDE, BLOCK), jnp.float32)
    east = jnp.zeros((WIDE, BLOCK), jnp.float32)
    for row in range(ROWS):
        value = partial[row, WIDE : 2 * WIDE]
        if row > 0:
            value = value + partial[row - 1, :WIDE]
        if row < ROWS - 1:
            value = value + partial[row + 1, 2 * WIDE :]
        if row == 0:
            ends[0] = value
        elif row == ROWS - 1:
            ends[1] = value
        else:
            hidden[row] = jnp.where((lane == 0) | (lane == BLOCK - 1), blank, activated(value))
        west = jnp.where(lane == row, pltpu.roll(value, row, 1), west)
        east = jnp.where(lane == row, pltpu.roll(value, row + 1, 1), east)
    hidden[0] = blank
    hidden[ROWS - 1] = blank
    sides[0] = west
    sides[1] = east


def inner_convolution(taps, field):
    pair = jax.ShapeDtypeStruct((2, WIDE, BLOCK), jnp.float32)
    return pl.pallas_call(
        inner_kernel,
        in_specs=[vmem()] * 2,
        out_specs=[vmem()] * 3,
        out_shape=[FIELD, pair, pair],
        scratch_shapes=[pltpu.VMEM((ROWS, 3 * WIDE, BLOCK), jnp.float32)],
        compiler_params=pltpu.CompilerParams(vmem_limit_bytes=VMEM_LIMIT),
        cost_estimate=pl.CostEstimate(
            flops=2 * 9 * WIDE * WIDE * ROWS * BLOCK, bytes_accessed=2 << 20, transcendentals=0
        ),
        name="inner_convolution",
    )(taps, field)


def second_kernel_inner(taps_ref, hidden, gridded, base, partial):
    taps = taps_ref[...]
    blank = jnp.zeros((WIDE, BLOCK), jnp.bfloat16)
    for row in range(0, ROWS, 2):
        partial[row], partial[row + 1] = tap_sums(
            taps,
            shifted_columns(hidden[row], blank, blank),
            shifted_columns(hidden[row + 1], blank, blank),
        )
    for row in range(ROWS):
        value = gridded[row].astype(jnp.float32) + partial[row, WIDE : WIDE + PADDED]
        if row > 0:
            value = value + partial[row - 1, :PADDED]
        if row < ROWS - 1:
            value = value + partial[row + 1, 2 * WIDE : 2 * WIDE + PADDED]
        base[row] = value


def inner_second_convolution(taps, hidden, gridded):
    return pl.pallas_call(
        second_kernel_inner,
        in_specs=[vmem()] * 3,
        out_specs=vmem(),
        out_shape=jax.ShapeDtypeStruct((ROWS, PADDED, BLOCK), jnp.float32),
        scratch_shapes=[pltpu.VMEM((ROWS, 3 * WIDE, BLOCK), jnp.float32)],
        compiler_params=pltpu.CompilerParams(vmem_limit_bytes=VMEM_LIMIT),
        cost_estimate=pl.CostEstimate(
            flops=2 * 9 * WIDE * WIDE * ROWS * BLOCK, bytes_accessed=2 << 20, transcendentals=0
        ),
        name="inner_second_convolution",
    )(taps, hidden, gridded)


def pack_kernel(above, below, own, to_west, to_east):
    low = lanes((WIDE, BLOCK)) < BLOCK // 2
    before, strip, after = above[2], own[...], below[2]

    def other_half(plane):
        return pltpu.roll(plane, BLOCK // 2, 1)

    outer = jnp.where(low, after, before)
    to_east[0] = jnp.where(low, other_half(strip), after)
    to_east[1] = outer
    to_west[0] = jnp.where(low, strip, other_half(before))
    to_west[1] = outer


def half_strip_packs(above, below, own):
    pack = jax.ShapeDtypeStruct((2, WIDE, BLOCK), jnp.bfloat16)
    return pl.pallas_call(
        pack_kernel,
        in_specs=[vmem()] * 3,
        out_specs=[vmem()] * 2,
        out_shape=[pack, pack],
        compiler_params=pltpu.CompilerParams(vmem_limit_bytes=VMEM_LIMIT),
        name="half_strip_packs",
    )(above, below, own)


def half_strips(west_pack, east_pack):
    low = lanes((WIDE, BLOCK)) < BLOCK // 2

    def other_half(plane):
        return pltpu.roll(plane, BLOCK // 2, 1)

    def both_halves(plane):
        return jnp.where(low, plane, other_half(plane))

    return {
        -4: west_pack[1],
        -3: both_halves(west_pack[0]),
        -2: jnp.where(low, west_pack[1], west_pack[0]),
        2: jnp.where(low, other_half(east_pack[0]), east_pack[1]),
        3: both_halves(east_pack[0]),
        4: east_pack[1],
    }


def strip_plan(column_rows):
    if column_rows == 2:
        return [], 3, 1
    return [-2, 2], column_rows, 2


def conv_kernel(
    column_rows,
    first_taps_ref,
    second_taps_ref,
    field,
    base,
    ends_ref,
    sides_ref,
    above,
    below,
    own_strip,
    *rest,
):
    near, far, reach = strip_plan(column_rows)
    near_strips, (west_pack, east_pack) = rest[: len(near)], rest[len(near) : len(near) + 2]
    smoothed, unturned, halves, sems = rest[len(near) + 2 :]
    count = lax.axis_size("tile")
    tile = lax.axis_index("tile")
    lane = lanes((WIDE, BLOCK))
    last = ROWS + 1
    R = column_rows
    blank = jnp.zeros((WIDE, BLOCK), jnp.bfloat16)

    strips = {-1: above[2], 0: own_strip[...], 1: below[2]}
    strips.update((shift, ref[...]) for shift, ref in zip(near, near_strips))
    if R == 2:
        strips.update(half_strips(west_pack, east_pack))
    else:
        for at in range(-reach, reach + 1):
            strips[at - far], strips[at + far] = west_pack[at + reach], east_pack[at + reach]

    def place(shift):
        return lax.rem(tile + shift + count, count)

    def ends(shift, before, after, middle):
        before = jnp.where(place(shift) > 0, before, blank)
        after = jnp.where(place(shift) < count - 1, after, blank)
        return jnp.where(lane == 0, before, jnp.where(lane == last, after, middle))

    memo = {}

    def padded_column(shift, which):
        if (shift, which) not in memo:
            base = which * ROWS
            memo[shift, which] = ends(
                shift,
                pltpu.roll(strips[shift - 1], (1 - base - ROWS) % BLOCK, 1),
                pltpu.roll(strips[shift + 1], (last - base) % BLOCK, 1),
                pltpu.roll(strips[shift], (1 - base) % BLOCK, 1),
            )
        return memo[shift, which]

    row_id = lax.broadcasted_iota(jnp.int32, (BLOCK, BLOCK), 0)
    reversal = (row_id + lanes((BLOCK, BLOCK)) == last).astype(jnp.bfloat16)

    def reversed_lanes(planes):
        stacked = jnp.concatenate(planes, axis=0)
        turned_round = jnp.dot(stacked, reversal, preferred_element_type=jnp.float32)
        return [row_tap(turned_round, at) for at in range(len(planes))]

    def choose(shift, which, turned_round, plain):
        flips = strips[shift].astype(jnp.float32)[CHANNELS + which : CHANNELS + which + 1]
        return jnp.where(flips > 0.5, turned_round, plain.astype(jnp.float32)).astype(jnp.bfloat16)

    west_of = {shift: (shift - R, 3) for shift in {-1, 0, 1, R - 1, R, R + 1}}
    east_of = {shift: (shift + R, 0) for shift in {-1, 0, 1, -R - 1, -R, -R + 1}}
    keys = sorted(set(west_of.values()) | set(east_of.values()))
    flipped = dict(zip(keys, reversed_lanes([padded_column(*key) for key in keys])))
    west = {
        shift: choose(shift, 0, flipped[west_of[shift]], padded_column(*west_of[shift]))
        for shift in sorted(west_of)
    }
    east = {
        shift: choose(shift, 1, flipped[east_of[shift]], padded_column(*east_of[shift]))
        for shift in sorted(east_of)
    }

    def columns(value, west_plane, west_row, east_plane, east_row):
        return shifted_columns(
            value,
            pltpu.roll(west_plane, (BLOCK - west_row) % BLOCK, 1),
            pltpu.roll(east_plane, BLOCK - 1 - east_row, 1),
        )

    def along(result):
        return (
            row_tap(result, 0)
            + pltpu.roll(row_tap(result, 1), BLOCK - 1, 1)
            + pltpu.roll(row_tap(result, 2), BLOCK - 2, 1)
        )

    first_taps = first_taps_ref[...]
    up = [jnp.where(tile > 0, above[at], blank) for at in range(2)]
    down = [jnp.where(tile < count - 1, below[at], blank) for at in range(2)]
    from_up, from_down = tap_sums(
        first_taps, shifted_columns(up[1], blank, blank), shifted_columns(down[0], blank, blank)
    )
    from_up, from_down = row_tap(from_up, 0), row_tap(from_down, 2)
    from_west, from_east = tap_sums(
        first_taps,
        jnp.concatenate([west[0], blank, blank], axis=0),
        jnp.concatenate([blank, blank, east[0]], axis=0),
    )
    from_west, from_east = along(from_west), along(from_east)
    first = ends_ref[0] + from_up
    first = first + jnp.where(lane == 0, from_west, 0.0)
    first = first + jnp.where(lane == BLOCK - 1, pltpu.roll(from_east, BLOCK - 1, 1), 0.0)
    final = ends_ref[1] + from_down
    final = final + jnp.where(lane == 0, pltpu.roll(from_west, BLOCK - ROWS + 1, 1), 0.0)
    final = final + jnp.where(lane == BLOCK - 1, pltpu.roll(from_east, BLOCK - ROWS, 1), 0.0)
    first, final = activated(first), activated(final)
    first_column = activated(sides_ref[0] + from_west)
    last_column = activated(sides_ref[1] + from_east)

    upper = jnp.zeros((WIDE, BLOCK), jnp.float32)
    lower = jnp.zeros((WIDE, BLOCK), jnp.float32)
    for at, (high, low) in enumerate(
        [(up[0], field[ROWS - 1]), (up[1], down[0]), (field[0], down[1])]
    ):
        from_row = ROWS - 1 + at
        one, two = tap_sums(
            row_tap(first_taps, at),
            columns(high, west[-1], from_row, east[-1], from_row),
            columns(low, west[1], at, east[1], at),
        )
        upper += one
        lower += two
    top = jnp.where(tile > 0, activated(upper), blank)
    bottom = jnp.where(tile < count - 1, activated(lower), blank)

    west_hidden, east_hidden = {}, {}
    for at in (-1, 0, 1):
        q = at - R
        one = jnp.concatenate([padded_column(q, 2), padded_column(q, 3), east[q]], axis=0)
        q = at + R
        two = jnp.concatenate([west[q], padded_column(q, 0), padded_column(q, 1)], axis=0)
        one, two = tap_sums(first_taps, one, two)
        west_hidden[at], east_hidden[at] = activated(along(one)), activated(along(two))

    def hidden_side(shift, values):
        return ends(
            shift,
            pltpu.roll(values[-1], BLOCK - ROWS + 1, 1),
            pltpu.roll(values[1], last, 1),
            pltpu.roll(values[0], 1, 1),
        )

    plain = [hidden_side(-R, west_hidden), hidden_side(R, east_hidden)]
    west_side, east_side = [
        choose(0, which, turned_side, plain[which])
        for which, turned_side in enumerate(reversed_lanes(plain))
    ]

    second_taps = second_taps_ref[...]
    from_top, from_first = tap_sums(
        second_taps,
        columns(top, west_side, 0, east_side, 0),
        columns(first, west_side, 1, east_side, 1),
    )
    from_final, from_bottom = tap_sums(
        second_taps,
        columns(final, west_side, ROWS, east_side, ROWS),
        columns(bottom, west_side, last, east_side, last),
    )
    rim_rows = {
        0: row_tap(from_top, 0) + row_tap(from_first, 1),
        1: row_tap(from_first, 0),
        ROWS - 2: row_tap(from_final, 2),
        ROWS - 1: row_tap(from_final, 1) + row_tap(from_bottom, 2),
    }

    other = (lane >= 2) & (lane < ROWS)

    def other_rows(plane):
        return jnp.where(other, plane, blank)

    near_west, near_east = other_rows(west_side), other_rows(east_side)
    first_column = other_rows(pltpu.roll(first_column, 1, 1))
    last_column = other_rows(pltpu.roll(last_column, 1, 1))
    to_0, to_1 = tap_sums(
        second_taps,
        jnp.concatenate([near_west, first_column, blank], axis=0),
        jnp.concatenate([first_column, blank, blank], axis=0),
    )
    to_127, to_126 = tap_sums(
        second_taps,
        jnp.concatenate([blank, last_column, near_east], axis=0),
        jnp.concatenate([blank, blank, last_column], axis=0),
    )
    parts, to_lanes = [], []
    for at, sums in enumerate((to_126, to_127, to_0, to_1)):
        sums = along(sums)
        high = sums.astype(jnp.bfloat16)
        sums = sums - high.astype(jnp.float32)
        middle = sums.astype(jnp.bfloat16)
        low = (sums - middle.astype(jnp.float32)).astype(jnp.bfloat16)
        parts.append(jnp.concatenate([high, middle, low], axis=0))
        to_lanes.append((lanes((BLOCK, BLOCK)) == 4 * row_id + at).astype(jnp.bfloat16))
    spread = jnp.dot(
        jnp.concatenate(parts, axis=1),
        jnp.concatenate(to_lanes, axis=0),
        preferred_element_type=jnp.float32,
    )
    spread = row_tap(spread, 0) + (row_tap(spread, 1) + row_tap(spread, 2))

    rim_lanes = lanes((PADDED, BLOCK))
    rim_lanes = (rim_lanes < 2) | (rim_lanes >= BLOCK - 2)
    spread = spread[:PADDED]
    copies = []
    for half in range(2):
        for row in range(half * HALF_ROWS, (half + 1) * HALF_ROWS):
            value = base[row] + jnp.where(
                rim_lanes, pltpu.roll(spread, (BLOCK - 4 * row - 2) % BLOCK, 1), 0.0
            )
            if row in rim_rows:
                value = value + rim_rows[row][:PADDED]
            unturned[half, row - half * HALF_ROWS] = value
        halves[half] = jnp.transpose(unturned[half], (1, 0, 2))[:CHANNELS].astype(jnp.bfloat16)
        rows = pl.ds(half * HALF_ROWS, HALF_ROWS)
        copies.append(pltpu.make_async_copy(halves.at[half], smoothed.at[:, rows], sems.at[half]))
        copies[-1].start()
    for copy in copies:
        copy.wait()


def convolutions(column_rows, *operands):
    return pl.pallas_call(
        functools.partial(conv_kernel, column_rows),
        in_specs=[vmem()] * len(operands),
        out_specs=pl.BlockSpec(memory_space=pl.ANY),
        out_shape=jax.ShapeDtypeStruct((CHANNELS, ROWS, BLOCK), jnp.bfloat16),
        scratch_shapes=[
            pltpu.VMEM((2, HALF_ROWS, PADDED, BLOCK), jnp.float32),
            pltpu.VMEM((2, CHANNELS, HALF_ROWS, BLOCK), jnp.bfloat16),
            pltpu.SemaphoreType.DMA((2,)),
        ],
        compiler_params=pltpu.CompilerParams(vmem_limit_bytes=VMEM_LIMIT),
        name="convolutions",
    )(*operands)


def tap_matrix(kernel):
    pad = WIDE - CHANNELS
    taps = jnp.pad(kernel, ((0, 0), (0, pad), (0, pad))).reshape(3, 3, WIDE, WIDE)
    return taps.transpose(0, 2, 1, 3).reshape(3 * WIDE, 3 * WIDE)


def from_shift(value, shift):
    count = lax.axis_size("tile")
    return lax.ppermute(value, "tile", [(i, (i - shift) % count) for i in range(count)])


def per_device(
    source, weights, block_source, block_target, edge_flip, norm_gain, first_kernel, second_kernel
):
    count = lax.axis_size("tile")
    column_rows = count // TILE_COLS
    field = source.reshape(ROWS, CHANNELS, BLOCK).transpose(1, 0, 2).reshape(-1, BLOCK)
    same, *nexts = regrid(block_target, block_source, field, weights, column_rows)

    for across in range(TILE_COLS):
        pairs = [
            (c * column_rows + p, (c ^ across) * column_rows + p + 1)
            for c in range(TILE_COLS)
            for p in range(column_rows - 1)
        ]
        nexts[across] = lax.ppermute(nexts[across], "tile", pairs)
    nexts = [nexts[across] for across in (0, 1, 2, 7, 6, 5, 4, 3)]
    same = lax.all_to_all(
        same,
        "tile",
        0,
        0,
        axis_index_groups=[
            [c * column_rows + p for c in COLUMN_ORDER] for p in range(column_rows)
        ],
        tiled=True,
    )

    gain = jnp.broadcast_to(
        jnp.pad(norm_gain, (0, PADDED - CHANNELS))[:, None], (PADDED, BLOCK)
    )
    first_taps, second_taps = tap_matrix(first_kernel), tap_matrix(second_kernel)
    same, nexts, gain, first_taps, second_taps = lax.optimization_barrier(
        (same, nexts, gain, first_taps, second_taps)
    )
    summed, upward, downward, strip = gather_rows(column_rows, edge_flip, gain, same, nexts)
    rims = [from_shift(downward, -1), from_shift(upward, 1)]
    near, far, reach = strip_plan(column_rows)
    strips = [from_shift(strip, shift) for shift in near]
    gridded, normed = normalize_rows(gain, summed)
    inner = inner_convolution(first_taps, normed)
    if column_rows == 2:
        to_west, to_east = half_strip_packs(*rims, strip)
    else:
        held = {-1: rims[0][2], 0: strip, 1: rims[1][2], **dict(zip(near, strips))}
        to_west = to_east = jnp.stack([held[at] for at in range(-reach, reach + 1)])
    to_west, to_east, inner = lax.optimization_barrier((to_west, to_east, inner))
    strips += [from_shift(to_east, -far), from_shift(to_west, far)]
    gridded_out = channels_first(gridded)
    hidden, *unfinished = inner
    base = inner_second_convolution(second_taps, hidden, gridded)
    smoothed = convolutions(
        column_rows, first_taps, second_taps, normed, base, *unfinished, *rims, strip, *strips
    )

    def placed(value):
        return value.reshape(CHANNELS, ROWS, BLOCK).transpose(1, 0, 2)[:, None]

    return placed(gridded_out), placed(smoothed)


def solution(mesh):
    in_specs = (
        P("tile", "groups", None, None),
        P("tile", None, None),
        P("tile"),
        P("tile"),
        P("tile", None),
        P(),
        P(),
        P(),
    )
    out_specs = (P("tile", "groups", None, None), P("tile", "groups", None, None))
    return jax.shard_map(
        per_device, mesh=mesh, in_specs=in_specs, out_specs=out_specs, check_vma=False
    )
```

```python
import functools

import jax
import jax.numpy as jnp
from jax import lax
from jax.experimental import pallas as pl
from jax.experimental.pallas import tpu as pltpu
from jax.sharding import PartitionSpec as P

BLOCK = 128
CHANNELS = 69
PADDED = 72
WIDE = 80
ROWS = 32
ROW_BITS = 5
HALF_ROWS = ROWS // 2
TILE_COLS = 8
CAP = 8
HALF = TILE_COLS // 2
GROUPS = 2 * TILE_COLS
COLUMN_ORDER = [half * HALF + at for at in range(HALF) for half in range(2)]
SLOTS = GROUPS * CAP
MARK = CHANNELS
BODY = 64
TAILS = (MARK + 1 - BODY) * CAP
MESSAGE = CAP * BODY + TAILS
CHUNK = 96
EPSILON = 1e-05
VMEM_LIMIT = 40 * 1024 * 1024
REGRID_VMEM = 60 * 1024 * 1024


def vmem():
    return pl.BlockSpec(memory_space=pltpu.VMEM)


def smem():
    return pl.BlockSpec(memory_space=pltpu.SMEM)


def split(value, size):
    if size & (size - 1) == 0:
        return value >> (size.bit_length() - 1), value & (size - 1)
    return lax.div(value, size), lax.rem(value, size)


def lanes(shape):
    return lax.broadcasted_iota(jnp.int32, shape, len(shape) - 1)


def regrid_kernel(
    column_rows, target_hbm, target_row_hbm, index_hbm, source_hbm, weight_hbm, *rest
):
    same_out, next_outs = rest[0], rest[1 : 1 + TILE_COLS]
    (
        target_ref,
        target_row_ref,
        index_ref,
        source,
        weight,
        wide,
        field,
        sums,
        message,
        tails,
        plan,
        plan_scalars,
        plan_sem,
        in_sems,
        weight_sems,
        out_sems,
    ) = rest[1 + TILE_COLS :]
    entries = weight.shape[0]
    chunks = entries // CHUNK
    tile = lax.axis_index("tile")
    column, position = split(tile, column_rows)

    small_copies = [
        pltpu.make_async_copy(target_row_hbm, target_row_ref, in_sems.at[0]),
        pltpu.make_async_copy(target_hbm, target_ref, in_sems.at[1]),
        pltpu.make_async_copy(index_hbm, index_ref, in_sems.at[2]),
    ]
    source_copy = pltpu.make_async_copy(source_hbm, source, in_sems.at[3])
    for copy in small_copies:
        copy.start()
    source_copy.start()

    def chunk_copy(chunk):
        part = pl.ds(chunk * CHUNK, CHUNK)
        return pltpu.make_async_copy(weight_hbm.at[part], weight.at[part], weight_sems.at[chunk])

    for chunk in range(chunks):
        chunk_copy(chunk).start()

    small_copies[0].wait()
    target = target_row_ref[...]
    owner, row = split(target, ROWS)
    owner_column, owner_position = split(owner, column_rows)
    place = ((owner_column & (HALF - 1)) << 1) + (owner_column >= HALF).astype(jnp.int32)
    group = jnp.where(owner_position == position, place, TILE_COLS + (owner_column ^ column))
    key = group * ROWS + row
    square = (entries, entries)
    down = lax.broadcasted_iota(jnp.int32, square, 0)
    along = lanes(square)
    key_along = jnp.broadcast_to(key.astype(jnp.float32), square)
    key_down = jnp.broadcast_to(
        jnp.sum(jnp.where(down == along, key_along, 0.0), axis=1, keepdims=True), square
    )
    equal = key_along == key_down
    doubles = jnp.sum(jnp.where(equal & (along < down), 1.0, 0.0), axis=1, keepdims=True)
    in_group = (key_down.astype(jnp.int32) >> ROW_BITS) == (key_along.astype(jnp.int32) >> ROW_BITS)
    below = in_group & (key_down < key_along) & (jnp.broadcast_to(doubles, square) == 0.0)
    rank = jnp.sum(jnp.where(below, 1.0, 0.0), axis=0, keepdims=True)
    mentions = jnp.sum(jnp.where(equal & (down < along), 1.0, 0.0), axis=0, keepdims=True)
    slots = group * CAP + rank.astype(jnp.int32)
    plan[...] = slots + jnp.where(mentions == 0.0, SLOTS, 0)
    plan_copy = pltpu.make_async_copy(plan, plan_scalars, plan_sem)
    plan_copy.start()

    for slot in range(SLOTS):
        tails[pl.ds(slot * 8, 8), :] = jnp.full((8, BLOCK), ROWS, jnp.float32)
    wide[pl.ds(CHANNELS * ROWS, (PADDED - CHANNELS) * ROWS), :] = jnp.zeros(
        ((PADDED - CHANNELS) * ROWS, BLOCK), jnp.float32
    )
    nothing = jnp.zeros((WIDE - PADDED, BLOCK), jnp.float32)
    source_copy.wait()
    wide[pl.ds(0, CHANNELS * ROWS), :] = source[...].astype(jnp.float32)
    turned = jnp.transpose(wide[...].reshape(PADDED, ROWS, BLOCK), (1, 0, 2))
    for row in range(ROWS):
        field[row] = jnp.concatenate([turned[row], nothing], axis=0).astype(jnp.bfloat16)
    is_mark = lax.broadcasted_iota(jnp.int32, (8, BLOCK), 0) == MARK - BODY
    blank = jnp.zeros((WIDE, BLOCK), jnp.bfloat16)
    small_copies[1].wait()
    small_copies[2].wait()
    plan_copy.wait()

    for chunk in range(chunks):
        chunk_copy(chunk).wait()
        for entry in range(chunk * CHUNK, (chunk + 1) * CHUNK, 2):
            one = jnp.concatenate([field[index_ref[entry]], blank], axis=1)
            two = jnp.concatenate([blank, field[index_ref[entry + 1]]], axis=1)
            products = jnp.dot(
                jnp.concatenate([one, two], axis=0),
                weight[entry : entry + 2].reshape(2 * BLOCK, BLOCK),
                preferred_element_type=jnp.float32,
            )
            for at in range(2):
                code = plan_scalars[0, entry + at]
                slot = code & (SLOTS - 1)
                row = split(target_ref[entry + at], ROWS)[1]
                product = products[at * WIDE : at * WIDE + PADDED]
                total = jnp.where(code >= SLOTS, 0.0, sums[slot]) + product
                sums[slot] = total
                group, place = split(slot, CAP)
                message[group, pl.ds(pl.multiple_of(place * BODY, BODY), BODY), :] = total[
                    :BODY
                ].astype(jnp.bfloat16)
                tails[pl.ds(pl.multiple_of(slot * 8, 8), 8), :] = jnp.where(
                    is_mark, row.astype(jnp.float32), total[BODY:]
                )
    copies = []
    for group in range(GROUPS):
        start = group * CAP * 8
        ends = [tails[pl.ds(start + at, CAP, stride=8), :] for at in range(MARK + 1 - BODY)]
        message[group, CAP * BODY :] = jnp.concatenate(ends, axis=0).astype(jnp.bfloat16)
        if group < TILE_COLS:
            out = same_out.at[pl.ds(group * MESSAGE, MESSAGE)]
        else:
            out = next_outs[group - TILE_COLS]
        copies.append(pltpu.make_async_copy(message.at[group], out, out_sems.at[group]))
        copies[-1].start()
    for copy in copies:
        copy.wait()


def regrid(target, source_index, field, weights, column_rows):
    piece = jax.ShapeDtypeStruct((MESSAGE, BLOCK), jnp.bfloat16)
    same = jax.ShapeDtypeStruct((TILE_COLS * MESSAGE, BLOCK), jnp.bfloat16)
    hbm = pl.BlockSpec(memory_space=pl.ANY)
    entries = weights.shape[0]
    return pl.pallas_call(
        functools.partial(regrid_kernel, column_rows),
        in_specs=[hbm] * 5,
        out_specs=[hbm] * (1 + TILE_COLS),
        out_shape=[same] + [piece] * TILE_COLS,
        scratch_shapes=[
            pltpu.SMEM(target.shape, jnp.int32),
            pltpu.VMEM((1, entries), jnp.int32),
            pltpu.SMEM(source_index.shape, jnp.int32),
            pltpu.VMEM(field.shape, jnp.bfloat16),
            pltpu.VMEM(weights.shape, jnp.bfloat16),
            pltpu.VMEM((PADDED * ROWS, BLOCK), jnp.float32),
            pltpu.VMEM((ROWS, WIDE, BLOCK), jnp.bfloat16),
            pltpu.VMEM((SLOTS, PADDED, BLOCK), jnp.float32),
            pltpu.VMEM((GROUPS, MESSAGE, BLOCK), jnp.bfloat16),
            pltpu.VMEM((SLOTS * 8, BLOCK), jnp.float32),
            pltpu.VMEM((1, entries), jnp.int32),
            pltpu.SMEM((1, entries), jnp.int32),
            pltpu.SemaphoreType.DMA,
            pltpu.SemaphoreType.DMA((4,)),
            pltpu.SemaphoreType.DMA((entries // CHUNK,)),
            pltpu.SemaphoreType.DMA((GROUPS,)),
        ],
        compiler_params=pltpu.CompilerParams(vmem_limit_bytes=REGRID_VMEM),
        name="regrid",
    )(target, target.reshape(1, -1), source_index, field, weights)


def normalized(rounded, gain):
    value = rounded.astype(jnp.float32)
    real = lax.broadcasted_iota(jnp.int32, (PADDED - BODY, BLOCK), 0) < CHANNELS - BODY
    value = jnp.concatenate([value[:BODY], jnp.where(real, value[BODY:], 0.0)], axis=0)
    square = jnp.sum(value * value, axis=0, keepdims=True) * (1.0 / CHANNELS)
    scaled = value * lax.rsqrt(square + EPSILON) * gain
    nothing = jnp.zeros((WIDE - PADDED, BLOCK), jnp.float32)
    return jnp.concatenate([scaled, nothing], axis=0).astype(jnp.bfloat16)


def gather_kernel(column_rows, flip_ref, gain_ref, same, *rest):
    nexts = rest[:TILE_COLS]
    summed, upward, downward, strip_out, tails = rest[TILE_COLS:]
    position = lax.rem(lax.axis_index("tile"), column_rows)
    summed[...] = jnp.zeros_like(summed)

    def add(group, piece):
        ends = piece[CAP * BODY :].astype(jnp.float32)
        tails[group, :TAILS] = ends
        rows = ends[TAILS - CAP :].astype(jnp.int32)
        for place in range(CAP):
            row = rows[place, 0]
            body = piece[place * BODY : (place + 1) * BODY].astype(jnp.float32)
            summed[row, :BODY] = summed[row, :BODY] + body
            tail = tails[group, pl.ds(place, 8, stride=CAP), :]
            summed[row, BODY:] = summed[row, BODY:] + tail

    tails[:, TAILS:] = jnp.zeros((GROUPS, 8 * CAP - TAILS, BLOCK), jnp.float32)
    for group in range(TILE_COLS):
        add(group, same.at[pl.ds(group * MESSAGE, MESSAGE)])

    @pl.when(position > 0)
    def _():
        for group in range(TILE_COLS):
            add(TILE_COLS + group, nexts[group])

    gain = gain_ref[...]
    for at in range(2):
        upward[at] = normalized(summed[at].astype(jnp.bfloat16), gain)
        downward[at] = normalized(summed[ROWS - 2 + at].astype(jnp.bfloat16), gain)
    lane = lanes((PADDED, BLOCK))
    strip = jnp.zeros((PADDED, BLOCK), jnp.bfloat16)
    for row in range(ROWS):
        rounded = summed[row].astype(jnp.bfloat16)
        strip = jnp.where((lane >> 2) == row, pltpu.roll(rounded, 4 * row + 2, 1), strip)
    to_lane = lanes((BLOCK, BLOCK))
    from_lane = 4 * (to_lane & (ROWS - 1)) + (((to_lane >> ROW_BITS) + 2) & 3)
    order = lax.broadcasted_iota(jnp.int32, (BLOCK, BLOCK), 0) == from_lane
    strip = jnp.dot(
        normalized(strip, gain), order.astype(jnp.bfloat16), preferred_element_type=jnp.float32
    )
    channel = lax.broadcasted_iota(jnp.int32, (WIDE, BLOCK), 0)
    for side in range(2):
        strip = jnp.where(channel == CHANNELS + side, flip_ref[0, side].astype(jnp.float32), strip)
    strip = strip.astype(jnp.bfloat16)
    upward[2] = strip
    downward[2] = strip
    strip_out[...] = strip


def normalize_kernel(gain_ref, summed, gridded, normed):
    gain = gain_ref[...]
    for row in range(ROWS):
        rounded = summed[row].astype(jnp.bfloat16)
        gridded[row] = rounded
        normed[row] = normalized(rounded, gain)


def normalize_rows(gain, summed):
    return pl.pallas_call(
        normalize_kernel,
        in_specs=[vmem()] * 2,
        out_specs=[vmem()] * 2,
        out_shape=[GRIDDED, FIELD],
        compiler_params=pltpu.CompilerParams(vmem_limit_bytes=VMEM_LIMIT),
        cost_estimate=pl.CostEstimate(
            flops=10 * ROWS * PADDED * BLOCK, bytes_accessed=2 << 20, transcendentals=0
        ),
        name="normalize_rows",
    )(gain, summed)


SUMMED = jax.ShapeDtypeStruct((ROWS + 1, PADDED, BLOCK), jnp.float32)
GRIDDED = jax.ShapeDtypeStruct((ROWS, PADDED, BLOCK), jnp.bfloat16)
FIELD = jax.ShapeDtypeStruct((ROWS, WIDE, BLOCK), jnp.bfloat16)
RIM = jax.ShapeDtypeStruct((3, WIDE, BLOCK), jnp.bfloat16)
STRIP_COLUMNS = (0, 1, BLOCK - 2, BLOCK - 1)
STRIP = jax.ShapeDtypeStruct((WIDE, BLOCK), jnp.bfloat16)


def gather_rows(column_rows, edge_flip, gain, same, nexts):
    return pl.pallas_call(
        functools.partial(gather_kernel, column_rows),
        in_specs=[smem()] + [vmem()] * (2 + TILE_COLS),
        out_specs=[vmem()] * 4,
        out_shape=[SUMMED, RIM, RIM, STRIP],
        scratch_shapes=[pltpu.VMEM((GROUPS, 8 * CAP, BLOCK), jnp.float32)],
        compiler_params=pltpu.CompilerParams(vmem_limit_bytes=VMEM_LIMIT),
        name="gather_rows",
    )(edge_flip, gain, same, *nexts)


def turn_kernel(field, out):
    turned = jnp.transpose(field[...].astype(jnp.float32), (1, 0, 2))
    out[...] = turned[:CHANNELS].reshape(CHANNELS * ROWS, BLOCK).astype(jnp.bfloat16)


def channels_first(field):
    return pl.pallas_call(
        turn_kernel,
        in_specs=[vmem()],
        out_specs=vmem(),
        out_shape=jax.ShapeDtypeStruct((CHANNELS * ROWS, BLOCK), jnp.bfloat16),
        compiler_params=pltpu.CompilerParams(vmem_limit_bytes=VMEM_LIMIT),
        name="channels_first",
    )(field)


def shifted_columns(value, left_end, right_end):
    lane = lanes((WIDE, BLOCK))
    left = jnp.where(lane == 0, left_end, pltpu.roll(value, 1, 1))
    right = jnp.where(lane == BLOCK - 1, right_end, pltpu.roll(value, BLOCK - 1, 1))
    return jnp.concatenate([left, value, right], axis=0)


def tap_sums(taps, one, two):
    both = jnp.concatenate([one, two], axis=1)
    result = jnp.dot(taps, both, preferred_element_type=jnp.float32)
    return result[:, :BLOCK], result[:, BLOCK:]


def row_tap(sums, at):
    return sums[at * WIDE : (at + 1) * WIDE]


def activated(value):
    return jax.nn.gelu(value).astype(jnp.bfloat16)


def inner_kernel(taps_ref, field, hidden, ends, sides, partial):
    taps = taps_ref[...]
    blank = jnp.zeros((WIDE, BLOCK), jnp.bfloat16)
    for row in range(0, ROWS, 2):
        partial[row], partial[row + 1] = tap_sums(
            taps,
            shifted_columns(field[row], blank, blank),
            shifted_columns(field[row + 1], blank, blank),
        )
    lane = lanes((WIDE, BLOCK))
    west = jnp.zeros((WIDE, BLOCK), jnp.float32)
    east = jnp.zeros((WIDE, BLOCK), jnp.float32)
    for row in range(ROWS):
        value = partial[row, WIDE : 2 * WIDE]
        if row > 0:
            value = value + partial[row - 1, :WIDE]
        if row < ROWS - 1:
            value = value + partial[row + 1, 2 * WIDE :]
        if row == 0:
            ends[0] = value
        elif row == ROWS - 1:
            ends[1] = value
        else:
            hidden[row] = jnp.where((lane == 0) | (lane == BLOCK - 1), blank, activated(value))
        west = jnp.where(lane == row, pltpu.roll(value, row, 1), west)
        east = jnp.where(lane == row, pltpu.roll(value, row + 1, 1), east)
    hidden[0] = blank
    hidden[ROWS - 1] = blank
    sides[0] = west
    sides[1] = east


def inner_convolution(taps, field):
    pair = jax.ShapeDtypeStruct((2, WIDE, BLOCK), jnp.float32)
    return pl.pallas_call(
        inner_kernel,
        in_specs=[vmem()] * 2,
        out_specs=[vmem()] * 3,
        out_shape=[FIELD, pair, pair],
        scratch_shapes=[pltpu.VMEM((ROWS, 3 * WIDE, BLOCK), jnp.float32)],
        compiler_params=pltpu.CompilerParams(vmem_limit_bytes=VMEM_LIMIT),
        cost_estimate=pl.CostEstimate(
            flops=2 * 9 * WIDE * WIDE * ROWS * BLOCK, bytes_accessed=2 << 20, transcendentals=0
        ),
        name="inner_convolution",
    )(taps, field)


def second_kernel_inner(taps_ref, hidden, gridded, base, partial):
    taps = taps_ref[...]
    blank = jnp.zeros((WIDE, BLOCK), jnp.bfloat16)
    for row in range(0, ROWS, 2):
        partial[row], partial[row + 1] = tap_sums(
            taps,
            shifted_columns(hidden[row], blank, blank),
            shifted_columns(hidden[row + 1], blank, blank),
        )
    for row in range(ROWS):
        value = gridded[row].astype(jnp.float32) + partial[row, WIDE : WIDE + PADDED]
        if row > 0:
            value = value + partial[row - 1, :PADDED]
        if row < ROWS - 1:
            value = value + partial[row + 1, 2 * WIDE : 2 * WIDE + PADDED]
        base[row] = value


def inner_second_convolution(taps, hidden, gridded):
    return pl.pallas_call(
        second_kernel_inner,
        in_specs=[vmem()] * 3,
        out_specs=vmem(),
        out_shape=jax.ShapeDtypeStruct((ROWS, PADDED, BLOCK), jnp.float32),
        scratch_shapes=[pltpu.VMEM((ROWS, 3 * WIDE, BLOCK), jnp.float32)],
        compiler_params=pltpu.CompilerParams(vmem_limit_bytes=VMEM_LIMIT),
        cost_estimate=pl.CostEstimate(
            flops=2 * 9 * WIDE * WIDE * ROWS * BLOCK, bytes_accessed=2 << 20, transcendentals=0
        ),
        name="inner_second_convolution",
    )(taps, hidden, gridded)


def pack_kernel(above, below, own, to_west, to_east):
    low = lanes((WIDE, BLOCK)) < BLOCK // 2
    before, strip, after = above[2], own[...], below[2]

    def other_half(plane):
        return pltpu.roll(plane, BLOCK // 2, 1)

    outer = jnp.where(low, after, before)
    to_east[0] = jnp.where(low, other_half(strip), after)
    to_east[1] = outer
    to_west[0] = jnp.where(low, strip, other_half(before))
    to_west[1] = outer


def half_strip_packs(above, below, own):
    pack = jax.ShapeDtypeStruct((2, WIDE, BLOCK), jnp.bfloat16)
    return pl.pallas_call(
        pack_kernel,
        in_specs=[vmem()] * 3,
        out_specs=[vmem()] * 2,
        out_shape=[pack, pack],
        compiler_params=pltpu.CompilerParams(vmem_limit_bytes=VMEM_LIMIT),
        name="half_strip_packs",
    )(above, below, own)


def half_strips(west_pack, east_pack):
    low = lanes((WIDE, BLOCK)) < BLOCK // 2

    def other_half(plane):
        return pltpu.roll(plane, BLOCK // 2, 1)

    def both_halves(plane):
        return jnp.where(low, plane, other_half(plane))

    return {
        -4: west_pack[1],
        -3: both_halves(west_pack[0]),
        -2: jnp.where(low, west_pack[1], west_pack[0]),
        2: jnp.where(low, other_half(east_pack[0]), east_pack[1]),
        3: both_halves(east_pack[0]),
        4: east_pack[1],
    }


def strip_plan(column_rows):
    if column_rows == 2:
        return [], 3, 1
    return [-2, 2], column_rows, 2


def conv_kernel(
    column_rows,
    first_taps_ref,
    second_taps_ref,
    field,
    base,
    ends_ref,
    sides_ref,
    above,
    below,
    own_strip,
    *rest,
):
    near, far, reach = strip_plan(column_rows)
    near_strips, (west_pack, east_pack) = rest[: len(near)], rest[len(near) : len(near) + 2]
    smoothed, unturned, halves, sems = rest[len(near) + 2 :]
    count = lax.axis_size("tile")
    tile = lax.axis_index("tile")
    lane = lanes((WIDE, BLOCK))
    last = ROWS + 1
    R = column_rows
    blank = jnp.zeros((WIDE, BLOCK), jnp.bfloat16)

    strips = {-1: above[2], 0: own_strip[...], 1: below[2]}
    strips.update((shift, ref[...]) for shift, ref in zip(near, near_strips))
    if R == 2:
        strips.update(half_strips(west_pack, east_pack))
    else:
        for at in range(-reach, reach + 1):
            strips[at - far], strips[at + far] = west_pack[at + reach], east_pack[at + reach]

    def place(shift):
        return lax.rem(tile + shift + count, count)

    def ends(shift, before, after, middle):
        before = jnp.where(place(shift) > 0, before, blank)
        after = jnp.where(place(shift) < count - 1, after, blank)
        return jnp.where(lane == 0, before, jnp.where(lane == last, after, middle))

    memo = {}

    def padded_column(shift, which):
        if (shift, which) not in memo:
            base = which * ROWS
            memo[shift, which] = ends(
                shift,
                pltpu.roll(strips[shift - 1], (1 - base - ROWS) % BLOCK, 1),
                pltpu.roll(strips[shift + 1], (last - base) % BLOCK, 1),
                pltpu.roll(strips[shift], (1 - base) % BLOCK, 1),
            )
        return memo[shift, which]

    row_id = lax.broadcasted_iota(jnp.int32, (BLOCK, BLOCK), 0)
    reversal = (row_id + lanes((BLOCK, BLOCK)) == last).astype(jnp.bfloat16)

    def reversed_lanes(planes):
        stacked = jnp.concatenate(planes, axis=0)
        turned_round = jnp.dot(stacked, reversal, preferred_element_type=jnp.float32)
        return [row_tap(turned_round, at) for at in range(len(planes))]

    def choose(shift, which, turned_round, plain):
        flips = strips[shift].astype(jnp.float32)[CHANNELS + which : CHANNELS + which + 1]
        return jnp.where(flips > 0.5, turned_round, plain.astype(jnp.float32)).astype(jnp.bfloat16)

    west_of = {shift: (shift - R, 3) for shift in {-1, 0, 1, R - 1, R, R + 1}}
    east_of = {shift: (shift + R, 0) for shift in {-1, 0, 1, -R - 1, -R, -R + 1}}
    keys = sorted(set(west_of.values()) | set(east_of.values()))
    flipped = dict(zip(keys, reversed_lanes([padded_column(*key) for key in keys])))
    west = {
        shift: choose(shift, 0, flipped[west_of[shift]], padded_column(*west_of[shift]))
        for shift in sorted(west_of)
    }
    east = {
        shift: choose(shift, 1, flipped[east_of[shift]], padded_column(*east_of[shift]))
        for shift in sorted(east_of)
    }

    def columns(value, west_plane, west_row, east_plane, east_row):
        return shifted_columns(
            value,
            pltpu.roll(west_plane, (BLOCK - west_row) % BLOCK, 1),
            pltpu.roll(east_plane, BLOCK - 1 - east_row, 1),
        )

    def along(result):
        return (
            row_tap(result, 0)
            + pltpu.roll(row_tap(result, 1), BLOCK - 1, 1)
            + pltpu.roll(row_tap(result, 2), BLOCK - 2, 1)
        )

    first_taps = first_taps_ref[...]
    up = [jnp.where(tile > 0, above[at], blank) for at in range(2)]
    down = [jnp.where(tile < count - 1, below[at], blank) for at in range(2)]
    from_up, from_down = tap_sums(
        first_taps, shifted_columns(up[1], blank, blank), shifted_columns(down[0], blank, blank)
    )
    from_up, from_down = row_tap(from_up, 0), row_tap(from_down, 2)
    from_west, from_east = tap_sums(
        first_taps,
        jnp.concatenate([west[0], blank, blank], axis=0),
        jnp.concatenate([blank, blank, east[0]], axis=0),
    )
    from_west, from_east = along(from_west), along(from_east)
    first = ends_ref[0] + from_up
    first = first + jnp.where(lane == 0, from_west, 0.0)
    first = first + jnp.where(lane == BLOCK - 1, pltpu.roll(from_east, BLOCK - 1, 1), 0.0)
    final = ends_ref[1] + from_down
    final = final + jnp.where(lane == 0, pltpu.roll(from_west, BLOCK - ROWS + 1, 1), 0.0)
    final = final + jnp.where(lane == BLOCK - 1, pltpu.roll(from_east, BLOCK - ROWS, 1), 0.0)
    first, final = activated(first), activated(final)
    first_column = activated(sides_ref[0] + from_west)
    last_column = activated(sides_ref[1] + from_east)

    upper = jnp.zeros((WIDE, BLOCK), jnp.float32)
    lower = jnp.zeros((WIDE, BLOCK), jnp.float32)
    for at, (high, low) in enumerate(
        [(up[0], field[ROWS - 1]), (up[1], down[0]), (field[0], down[1])]
    ):
        from_row = ROWS - 1 + at
        one, two = tap_sums(
            row_tap(first_taps, at),
            columns(high, west[-1], from_row, east[-1], from_row),
            columns(low, west[1], at, east[1], at),
        )
        upper += one
        lower += two
    top = jnp.where(tile > 0, activated(upper), blank)
    bottom = jnp.where(tile < count - 1, activated(lower), blank)

    west_hidden, east_hidden = {}, {}
    for at in (-1, 0, 1):
        q = at - R
        one = jnp.concatenate([padded_column(q, 2), padded_column(q, 3), east[q]], axis=0)
        q = at + R
        two = jnp.concatenate([west[q], padded_column(q, 0), padded_column(q, 1)], axis=0)
        one, two = tap_sums(first_taps, one, two)
        west_hidden[at], east_hidden[at] = activated(along(one)), activated(along(two))

    def hidden_side(shift, values):
        return ends(
            shift,
            pltpu.roll(values[-1], BLOCK - ROWS + 1, 1),
            pltpu.roll(values[1], last, 1),
            pltpu.roll(values[0], 1, 1),
        )

    plain = [hidden_side(-R, west_hidden), hidden_side(R, east_hidden)]
    west_side, east_side = [
        choose(0, which, turned_side, plain[which])
        for which, turned_side in enumerate(reversed_lanes(plain))
    ]

    second_taps = second_taps_ref[...]
    from_top, from_first = tap_sums(
        second_taps,
        columns(top, west_side, 0, east_side, 0),
        columns(first, west_side, 1, east_side, 1),
    )
    from_final, from_bottom = tap_sums(
        second_taps,
        columns(final, west_side, ROWS, east_side, ROWS),
        columns(bottom, west_side, last, east_side, last),
    )
    rim_rows = {
        0: row_tap(from_top, 0) + row_tap(from_first, 1),
        1: row_tap(from_first, 0),
        ROWS - 2: row_tap(from_final, 2),
        ROWS - 1: row_tap(from_final, 1) + row_tap(from_bottom, 2),
    }

    other = (lane >= 2) & (lane < ROWS)

    def other_rows(plane):
        return jnp.where(other, plane, blank)

    near_west, near_east = other_rows(west_side), other_rows(east_side)
    first_column = other_rows(pltpu.roll(first_column, 1, 1))
    last_column = other_rows(pltpu.roll(last_column, 1, 1))
    to_0, to_1 = tap_sums(
        second_taps,
        jnp.concatenate([near_west, first_column, blank], axis=0),
        jnp.concatenate([first_column, blank, blank], axis=0),
    )
    to_127, to_126 = tap_sums(
        second_taps,
        jnp.concatenate([blank, last_column, near_east], axis=0),
        jnp.concatenate([blank, blank, last_column], axis=0),
    )
    parts, to_lanes = [], []
    for at, sums in enumerate((to_126, to_127, to_0, to_1)):
        sums = along(sums)
        high = sums.astype(jnp.bfloat16)
        sums = sums - high.astype(jnp.float32)
        middle = sums.astype(jnp.bfloat16)
        low = (sums - middle.astype(jnp.float32)).astype(jnp.bfloat16)
        parts.append(jnp.concatenate([high, middle, low], axis=0))
        to_lanes.append((lanes((BLOCK, BLOCK)) == 4 * row_id + at).astype(jnp.bfloat16))
    spread = jnp.dot(
        jnp.concatenate(parts, axis=1),
        jnp.concatenate(to_lanes, axis=0),
        preferred_element_type=jnp.float32,
    )
    spread = row_tap(spread, 0) + (row_tap(spread, 1) + row_tap(spread, 2))

    rim_lanes = lanes((PADDED, BLOCK))
    rim_lanes = (rim_lanes < 2) | (rim_lanes >= BLOCK - 2)
    spread = spread[:PADDED]
    copies = []
    for half in range(2):
        for row in range(half * HALF_ROWS, (half + 1) * HALF_ROWS):
            value = base[row] + jnp.where(
                rim_lanes, pltpu.roll(spread, (BLOCK - 4 * row - 2) % BLOCK, 1), 0.0
            )
            if row in rim_rows:
                value = value + rim_rows[row][:PADDED]
            unturned[half, row - half * HALF_ROWS] = value
        halves[half] = jnp.transpose(unturned[half], (1, 0, 2))[:CHANNELS].astype(jnp.bfloat16)
        rows = pl.ds(half * HALF_ROWS, HALF_ROWS)
        copies.append(pltpu.make_async_copy(halves.at[half], smoothed.at[:, rows], sems.at[half]))
        copies[-1].start()
    for copy in copies:
        copy.wait()


def convolutions(column_rows, *operands):
    return pl.pallas_call(
        functools.partial(conv_kernel, column_rows),
        in_specs=[vmem()] * len(operands),
        out_specs=pl.BlockSpec(memory_space=pl.ANY),
        out_shape=jax.ShapeDtypeStruct((CHANNELS, ROWS, BLOCK), jnp.bfloat16),
        scratch_shapes=[
            pltpu.VMEM((2, HALF_ROWS, PADDED, BLOCK), jnp.float32),
            pltpu.VMEM((2, CHANNELS, HALF_ROWS, BLOCK), jnp.bfloat16),
            pltpu.SemaphoreType.DMA((2,)),
        ],
        compiler_params=pltpu.CompilerParams(vmem_limit_bytes=VMEM_LIMIT),
        name="convolutions",
    )(*operands)


def tap_matrix(kernel):
    pad = WIDE - CHANNELS
    taps = jnp.pad(kernel, ((0, 0), (0, pad), (0, pad))).reshape(3, 3, WIDE, WIDE)
    return taps.transpose(0, 2, 1, 3).reshape(3 * WIDE, 3 * WIDE)


def from_shift(value, shift):
    count = lax.axis_size("tile")
    return lax.ppermute(value, "tile", [(i, (i - shift) % count) for i in range(count)])


def per_device(
    source, weights, block_source, block_target, edge_flip, norm_gain, first_kernel, second_kernel
):
    count = lax.axis_size("tile")
    column_rows = count // TILE_COLS
    field = source.reshape(ROWS, CHANNELS, BLOCK).transpose(1, 0, 2).reshape(-1, BLOCK)
    same, *nexts = regrid(block_target, block_source, field, weights, column_rows)

    for across in range(TILE_COLS):
        pairs = [
            (c * column_rows + p, (c ^ across) * column_rows + p + 1)
            for c in range(TILE_COLS)
            for p in range(column_rows - 1)
        ]
        nexts[across] = lax.ppermute(nexts[across], "tile", pairs)
    nexts = [nexts[across] for across in (0, 1, 2, 4, 7, 5, 6, 3)]
    same = lax.all_to_all(
        same,
        "tile",
        0,
        0,
        axis_index_groups=[
            [c * column_rows + p for c in COLUMN_ORDER] for p in range(column_rows)
        ],
        tiled=True,
    )

    gain = jnp.broadcast_to(
        jnp.pad(norm_gain, (0, PADDED - CHANNELS))[:, None], (PADDED, BLOCK)
    )
    first_taps, second_taps = tap_matrix(first_kernel), tap_matrix(second_kernel)
    same, nexts, gain, first_taps, second_taps = lax.optimization_barrier(
        (same, nexts, gain, first_taps, second_taps)
    )
    summed, upward, downward, strip = gather_rows(column_rows, edge_flip, gain, same, nexts)
    rims = [from_shift(downward, -1), from_shift(upward, 1)]
    near, far, reach = strip_plan(column_rows)
    strips = [from_shift(strip, shift) for shift in near]
    gridded, normed = normalize_rows(gain, summed)
    inner = inner_convolution(first_taps, normed)
    if column_rows == 2:
        to_west, to_east = half_strip_packs(*rims, strip)
    else:
        held = {-1: rims[0][2], 0: strip, 1: rims[1][2], **dict(zip(near, strips))}
        to_west = to_east = jnp.stack([held[at] for at in range(-reach, reach + 1)])
    to_west, to_east, inner = lax.optimization_barrier((to_west, to_east, inner))
    strips += [from_shift(to_east, -far), from_shift(to_west, far)]
    gridded_out = channels_first(gridded)
    hidden, *unfinished = inner
    base = inner_second_convolution(second_taps, hidden, gridded)
    smoothed = convolutions(
        column_rows, first_taps, second_taps, normed, base, *unfinished, *rims, strip, *strips
    )

    def placed(value):
        return value.reshape(CHANNELS, ROWS, BLOCK).transpose(1, 0, 2)[:, None]

    return placed(gridded_out), placed(smoothed)


def solution(mesh):
    in_specs = (
        P("tile", "groups", None, None),
        P("tile", None, None),
        P("tile"),
        P("tile"),
        P("tile", None),
        P(),
        P(),
        P(),
    )
    out_specs = (P("tile", "groups", None, None), P("tile", "groups", None, None))
    return jax.shard_map(
        per_device, mesh=mesh, in_specs=in_specs, out_specs=out_specs, check_vma=False
    )
```

```python
import functools

import jax
import jax.numpy as jnp
from jax import lax
from jax.experimental import pallas as pl
from jax.experimental.pallas import tpu as pltpu
from jax.sharding import PartitionSpec as P

BLOCK = 128
CHANNELS = 69
PADDED = 72
WIDE = 80
ROWS = 32
ROW_BITS = 5
HALF_ROWS = ROWS // 2
TILE_COLS = 8
CAP = 8
HALF = TILE_COLS // 2
GROUPS = 2 * TILE_COLS
COLUMN_ORDER = [half * HALF + at for at in range(HALF) for half in range(2)]
SLOTS = GROUPS * CAP
MARK = CHANNELS
BODY = 64
TAILS = (MARK + 1 - BODY) * CAP
MESSAGE = CAP * BODY + TAILS
CHUNK = 96
EPSILON = 1e-05
VMEM_LIMIT = 40 * 1024 * 1024
REGRID_VMEM = 60 * 1024 * 1024


def vmem():
    return pl.BlockSpec(memory_space=pltpu.VMEM)


def smem():
    return pl.BlockSpec(memory_space=pltpu.SMEM)


def split(value, size):
    if size & (size - 1) == 0:
        return value >> (size.bit_length() - 1), value & (size - 1)
    return lax.div(value, size), lax.rem(value, size)


def lanes(shape):
    return lax.broadcasted_iota(jnp.int32, shape, len(shape) - 1)


def regrid_kernel(
    column_rows, target_hbm, target_row_hbm, index_hbm, source_hbm, weight_hbm, *rest
):
    same_out, next_outs = rest[0], rest[1 : 1 + TILE_COLS]
    (
        target_ref,
        target_row_ref,
        index_ref,
        source,
        weight,
        wide,
        field,
        sums,
        message,
        tails,
        plan,
        plan_scalars,
        plan_sem,
        in_sems,
        weight_sems,
        out_sems,
    ) = rest[1 + TILE_COLS :]
    entries = weight.shape[0]
    chunks = entries // CHUNK
    tile = lax.axis_index("tile")
    column, position = split(tile, column_rows)

    small_copies = [
        pltpu.make_async_copy(target_row_hbm, target_row_ref, in_sems.at[0]),
        pltpu.make_async_copy(target_hbm, target_ref, in_sems.at[1]),
        pltpu.make_async_copy(index_hbm, index_ref, in_sems.at[2]),
    ]
    source_copy = pltpu.make_async_copy(source_hbm, source, in_sems.at[3])
    for copy in small_copies:
        copy.start()
    source_copy.start()

    def chunk_copy(chunk):
        part = pl.ds(chunk * CHUNK, CHUNK)
        return pltpu.make_async_copy(weight_hbm.at[part], weight.at[part], weight_sems.at[chunk])

    for chunk in range(chunks):
        chunk_copy(chunk).start()

    small_copies[0].wait()
    target = target_row_ref[...]
    owner, row = split(target, ROWS)
    owner_column, owner_position = split(owner, column_rows)
    place = ((owner_column & (HALF - 1)) << 1) + (owner_column >= HALF).astype(jnp.int32)
    group = jnp.where(owner_position == position, place, TILE_COLS + (owner_column ^ column))
    key = group * ROWS + row
    square = (entries, entries)
    down = lax.broadcasted_iota(jnp.int32, square, 0)
    along = lanes(square)
    key_along = jnp.broadcast_to(key.astype(jnp.float32), square)
    key_down = jnp.broadcast_to(
        jnp.sum(jnp.where(down == along, key_along, 0.0), axis=1, keepdims=True), square
    )
    equal = key_along == key_down
    doubles = jnp.sum(jnp.where(equal & (along < down), 1.0, 0.0), axis=1, keepdims=True)
    in_group = (key_down.astype(jnp.int32) >> ROW_BITS) == (key_along.astype(jnp.int32) >> ROW_BITS)
    below = in_group & (key_down < key_along) & (jnp.broadcast_to(doubles, square) == 0.0)
    rank = jnp.sum(jnp.where(below, 1.0, 0.0), axis=0, keepdims=True)
    mentions = jnp.sum(jnp.where(equal & (down < along), 1.0, 0.0), axis=0, keepdims=True)
    slots = group * CAP + rank.astype(jnp.int32)
    plan[...] = slots + jnp.where(mentions == 0.0, SLOTS, 0)
    plan_copy = pltpu.make_async_copy(plan, plan_scalars, plan_sem)
    plan_copy.start()

    for slot in range(SLOTS):
        tails[pl.ds(slot * 8, 8), :] = jnp.full((8, BLOCK), ROWS, jnp.float32)
    wide[pl.ds(CHANNELS * ROWS, (PADDED - CHANNELS) * ROWS), :] = jnp.zeros(
        ((PADDED - CHANNELS) * ROWS, BLOCK), jnp.float32
    )
    nothing = jnp.zeros((WIDE - PADDED, BLOCK), jnp.float32)
    source_copy.wait()
    wide[pl.ds(0, CHANNELS * ROWS), :] = source[...].astype(jnp.float32)
    turned = jnp.transpose(wide[...].reshape(PADDED, ROWS, BLOCK), (1, 0, 2))
    for row in range(ROWS):
        field[row] = jnp.concatenate([turned[row], nothing], axis=0).astype(jnp.bfloat16)
    is_mark = lax.broadcasted_iota(jnp.int32, (8, BLOCK), 0) == MARK - BODY
    blank = jnp.zeros((WIDE, BLOCK), jnp.bfloat16)
    small_copies[1].wait()
    small_copies[2].wait()
    plan_copy.wait()

    for chunk in range(chunks):
        chunk_copy(chunk).wait()
        for entry in range(chunk * CHUNK, (chunk + 1) * CHUNK, 2):
            one = jnp.concatenate([field[index_ref[entry]], blank], axis=1)
            two = jnp.concatenate([blank, field[index_ref[entry + 1]]], axis=1)
            products = jnp.dot(
                jnp.concatenate([one, two], axis=0),
                weight[entry : entry + 2].reshape(2 * BLOCK, BLOCK),
                preferred_element_type=jnp.float32,
            )
            for at in range(2):
                code = plan_scalars[0, entry + at]
                slot = code & (SLOTS - 1)
                row = split(target_ref[entry + at], ROWS)[1]
                product = products[at * WIDE : at * WIDE + PADDED]
                total = jnp.where(code >= SLOTS, 0.0, sums[slot]) + product
                sums[slot] = total
                group, place = split(slot, CAP)
                message[group, pl.ds(pl.multiple_of(place * BODY, BODY), BODY), :] = total[
                    :BODY
                ].astype(jnp.bfloat16)
                tails[pl.ds(pl.multiple_of(slot * 8, 8), 8), :] = jnp.where(
                    is_mark, row.astype(jnp.float32), total[BODY:]
                )
    copies = []
    for group in range(GROUPS):
        start = group * CAP * 8
        ends = [tails[pl.ds(start + at, CAP, stride=8), :] for at in range(MARK + 1 - BODY)]
        message[group, CAP * BODY :] = jnp.concatenate(ends, axis=0).astype(jnp.bfloat16)
        if group < TILE_COLS:
            out = same_out.at[pl.ds(group * MESSAGE, MESSAGE)]
        else:
            out = next_outs[group - TILE_COLS]
        copies.append(pltpu.make_async_copy(message.at[group], out, out_sems.at[group]))
        copies[-1].start()
    for copy in copies:
        copy.wait()


def regrid(target, source_index, field, weights, column_rows):
    piece = jax.ShapeDtypeStruct((MESSAGE, BLOCK), jnp.bfloat16)
    same = jax.ShapeDtypeStruct((TILE_COLS * MESSAGE, BLOCK), jnp.bfloat16)
    hbm = pl.BlockSpec(memory_space=pl.ANY)
    entries = weights.shape[0]
    return pl.pallas_call(
        functools.partial(regrid_kernel, column_rows),
        in_specs=[hbm] * 5,
        out_specs=[hbm] * (1 + TILE_COLS),
        out_shape=[same] + [piece] * TILE_COLS,
        scratch_shapes=[
            pltpu.SMEM(target.shape, jnp.int32),
            pltpu.VMEM((1, entries), jnp.int32),
            pltpu.SMEM(source_index.shape, jnp.int32),
            pltpu.VMEM(field.shape, jnp.bfloat16),
            pltpu.VMEM(weights.shape, jnp.bfloat16),
            pltpu.VMEM((PADDED * ROWS, BLOCK), jnp.float32),
            pltpu.VMEM((ROWS, WIDE, BLOCK), jnp.bfloat16),
            pltpu.VMEM((SLOTS, PADDED, BLOCK), jnp.float32),
            pltpu.VMEM((GROUPS, MESSAGE, BLOCK), jnp.bfloat16),
            pltpu.VMEM((SLOTS * 8, BLOCK), jnp.float32),
            pltpu.VMEM((1, entries), jnp.int32),
            pltpu.SMEM((1, entries), jnp.int32),
            pltpu.SemaphoreType.DMA,
            pltpu.SemaphoreType.DMA((4,)),
            pltpu.SemaphoreType.DMA((entries // CHUNK,)),
            pltpu.SemaphoreType.DMA((GROUPS,)),
        ],
        compiler_params=pltpu.CompilerParams(vmem_limit_bytes=REGRID_VMEM),
        name="regrid",
    )(target, target.reshape(1, -1), source_index, field, weights)


def normalized(rounded, gain):
    value = rounded.astype(jnp.float32)
    real = lax.broadcasted_iota(jnp.int32, (PADDED - BODY, BLOCK), 0) < CHANNELS - BODY
    value = jnp.concatenate([value[:BODY], jnp.where(real, value[BODY:], 0.0)], axis=0)
    square = jnp.sum(value * value, axis=0, keepdims=True) * (1.0 / CHANNELS)
    scaled = value * lax.rsqrt(square + EPSILON) * gain
    nothing = jnp.zeros((WIDE - PADDED, BLOCK), jnp.float32)
    return jnp.concatenate([scaled, nothing], axis=0).astype(jnp.bfloat16)


def gather_kernel(column_rows, flip_ref, gain_ref, same, *rest):
    nexts = rest[:TILE_COLS]
    summed, upward, downward, strip_out, tails = rest[TILE_COLS:]
    position = lax.rem(lax.axis_index("tile"), column_rows)
    summed[...] = jnp.zeros_like(summed)

    def add(group, piece):
        ends = piece[CAP * BODY :].astype(jnp.float32)
        tails[group, :TAILS] = ends
        rows = ends[TAILS - CAP :].astype(jnp.int32)
        for place in range(CAP):
            row = rows[place, 0]
            body = piece[place * BODY : (place + 1) * BODY].astype(jnp.float32)
            summed[row, :BODY] = summed[row, :BODY] + body
            tail = tails[group, pl.ds(place, 8, stride=CAP), :]
            summed[row, BODY:] = summed[row, BODY:] + tail

    tails[:, TAILS:] = jnp.zeros((GROUPS, 8 * CAP - TAILS, BLOCK), jnp.float32)
    for group in range(TILE_COLS):
        add(group, same.at[pl.ds(group * MESSAGE, MESSAGE)])

    @pl.when(position > 0)
    def _():
        for group in range(TILE_COLS):
            add(TILE_COLS + group, nexts[group])

    gain = gain_ref[...]
    for at in range(2):
        upward[at] = normalized(summed[at].astype(jnp.bfloat16), gain)
        downward[at] = normalized(summed[ROWS - 2 + at].astype(jnp.bfloat16), gain)
    lane = lanes((PADDED, BLOCK))
    strip = jnp.zeros((PADDED, BLOCK), jnp.bfloat16)
    for row in range(ROWS):
        rounded = summed[row].astype(jnp.bfloat16)
        strip = jnp.where((lane >> 2) == row, pltpu.roll(rounded, 4 * row + 2, 1), strip)
    to_lane = lanes((BLOCK, BLOCK))
    from_lane = 4 * (to_lane & (ROWS - 1)) + (((to_lane >> ROW_BITS) + 2) & 3)
    order = lax.broadcasted_iota(jnp.int32, (BLOCK, BLOCK), 0) == from_lane
    strip = jnp.dot(
        normalized(strip, gain), order.astype(jnp.bfloat16), preferred_element_type=jnp.float32
    )
    channel = lax.broadcasted_iota(jnp.int32, (WIDE, BLOCK), 0)
    for side in range(2):
        strip = jnp.where(channel == CHANNELS + side, flip_ref[0, side].astype(jnp.float32), strip)
    strip = strip.astype(jnp.bfloat16)
    upward[2] = strip
    downward[2] = strip
    strip_out[...] = strip


def normalize_kernel(gain_ref, summed, gridded, normed):
    gain = gain_ref[...]
    for row in range(ROWS):
        rounded = summed[row].astype(jnp.bfloat16)
        gridded[row] = rounded
        normed[row] = normalized(rounded, gain)


def normalize_rows(gain, summed):
    return pl.pallas_call(
        normalize_kernel,
        in_specs=[vmem()] * 2,
        out_specs=[vmem()] * 2,
        out_shape=[GRIDDED, FIELD],
        compiler_params=pltpu.CompilerParams(vmem_limit_bytes=VMEM_LIMIT),
        cost_estimate=pl.CostEstimate(
            flops=10 * ROWS * PADDED * BLOCK, bytes_accessed=2 << 20, transcendentals=0
        ),
        name="normalize_rows",
    )(gain, summed)


SUMMED = jax.ShapeDtypeStruct((ROWS + 1, PADDED, BLOCK), jnp.float32)
GRIDDED = jax.ShapeDtypeStruct((ROWS, PADDED, BLOCK), jnp.bfloat16)
FIELD = jax.ShapeDtypeStruct((ROWS, WIDE, BLOCK), jnp.bfloat16)
RIM = jax.ShapeDtypeStruct((3, WIDE, BLOCK), jnp.bfloat16)
STRIP_COLUMNS = (0, 1, BLOCK - 2, BLOCK - 1)
STRIP = jax.ShapeDtypeStruct((WIDE, BLOCK), jnp.bfloat16)


def gather_rows(column_rows, edge_flip, gain, same, nexts):
    return pl.pallas_call(
        functools.partial(gather_kernel, column_rows),
        in_specs=[smem()] + [vmem()] * (2 + TILE_COLS),
        out_specs=[vmem()] * 4,
        out_shape=[SUMMED, RIM, RIM, STRIP],
        scratch_shapes=[pltpu.VMEM((GROUPS, 8 * CAP, BLOCK), jnp.float32)],
        compiler_params=pltpu.CompilerParams(vmem_limit_bytes=VMEM_LIMIT),
        name="gather_rows",
    )(edge_flip, gain, same, *nexts)


def turn_kernel(field, out):
    turned = jnp.transpose(field[...].astype(jnp.float32), (1, 0, 2))
    out[...] = turned[:CHANNELS].reshape(CHANNELS * ROWS, BLOCK).astype(jnp.bfloat16)


def channels_first(field):
    return pl.pallas_call(
        turn_kernel,
        in_specs=[vmem()],
        out_specs=vmem(),
        out_shape=jax.ShapeDtypeStruct((CHANNELS * ROWS, BLOCK), jnp.bfloat16),
        compiler_params=pltpu.CompilerParams(vmem_limit_bytes=VMEM_LIMIT),
        name="channels_first",
    )(field)


def shifted_columns(value, left_end, right_end):
    lane = lanes((WIDE, BLOCK))
    left = jnp.where(lane == 0, left_end, pltpu.roll(value, 1, 1))
    right = jnp.where(lane == BLOCK - 1, right_end, pltpu.roll(value, BLOCK - 1, 1))
    return jnp.concatenate([left, value, right], axis=0)


def tap_sums(taps, one, two):
    both = jnp.concatenate([one, two], axis=1)
    result = jnp.dot(taps, both, preferred_element_type=jnp.float32)
    return result[:, :BLOCK], result[:, BLOCK:]


def row_tap(sums, at):
    return sums[at * WIDE : (at + 1) * WIDE]


def activated(value):
    return jax.nn.gelu(value).astype(jnp.bfloat16)


def inner_kernel(taps_ref, field, hidden, ends, sides, partial):
    taps = taps_ref[...]
    blank = jnp.zeros((WIDE, BLOCK), jnp.bfloat16)
    for row in range(0, ROWS, 2):
        partial[row], partial[row + 1] = tap_sums(
            taps,
            shifted_columns(field[row], blank, blank),
            shifted_columns(field[row + 1], blank, blank),
        )
    lane = lanes((WIDE, BLOCK))
    west = jnp.zeros((WIDE, BLOCK), jnp.float32)
    east = jnp.zeros((WIDE, BLOCK), jnp.float32)
    for row in range(ROWS):
        value = partial[row, WIDE : 2 * WIDE]
        if row > 0:
            value = value + partial[row - 1, :WIDE]
        if row < ROWS - 1:
            value = value + partial[row + 1, 2 * WIDE :]
        if row == 0:
            ends[0] = value
        elif row == ROWS - 1:
            ends[1] = value
        else:
            hidden[row] = jnp.where((lane == 0) | (lane == BLOCK - 1), blank, activated(value))
        west = jnp.where(lane == row, pltpu.roll(value, row, 1), west)
        east = jnp.where(lane == row, pltpu.roll(value, row + 1, 1), east)
    hidden[0] = blank
    hidden[ROWS - 1] = blank
    sides[0] = west
    sides[1] = east


def inner_convolution(taps, field):
    pair = jax.ShapeDtypeStruct((2, WIDE, BLOCK), jnp.float32)
    return pl.pallas_call(
        inner_kernel,
        in_specs=[vmem()] * 2,
        out_specs=[vmem()] * 3,
        out_shape=[FIELD, pair, pair],
        scratch_shapes=[pltpu.VMEM((ROWS, 3 * WIDE, BLOCK), jnp.float32)],
        compiler_params=pltpu.CompilerParams(vmem_limit_bytes=VMEM_LIMIT),
        cost_estimate=pl.CostEstimate(
            flops=2 * 9 * WIDE * WIDE * ROWS * BLOCK, bytes_accessed=2 << 20, transcendentals=0
        ),
        name="inner_convolution",
    )(taps, field)


def second_kernel_inner(taps_ref, hidden, gridded, base, partial):
    taps = taps_ref[...]
    blank = jnp.zeros((WIDE, BLOCK), jnp.bfloat16)
    for row in range(0, ROWS, 2):
        partial[row], partial[row + 1] = tap_sums(
            taps,
            shifted_columns(hidden[row], blank, blank),
            shifted_columns(hidden[row + 1], blank, blank),
        )
    for row in range(ROWS):
        value = gridded[row].astype(jnp.float32) + partial[row, WIDE : WIDE + PADDED]
        if row > 0:
            value = value + partial[row - 1, :PADDED]
        if row < ROWS - 1:
            value = value + partial[row + 1, 2 * WIDE : 2 * WIDE + PADDED]
        base[row] = value


def inner_second_convolution(taps, hidden, gridded):
    return pl.pallas_call(
        second_kernel_inner,
        in_specs=[vmem()] * 3,
        out_specs=vmem(),
        out_shape=jax.ShapeDtypeStruct((ROWS, PADDED, BLOCK), jnp.float32),
        scratch_shapes=[pltpu.VMEM((ROWS, 3 * WIDE, BLOCK), jnp.float32)],
        compiler_params=pltpu.CompilerParams(vmem_limit_bytes=VMEM_LIMIT),
        cost_estimate=pl.CostEstimate(
            flops=2 * 9 * WIDE * WIDE * ROWS * BLOCK, bytes_accessed=2 << 20, transcendentals=0
        ),
        name="inner_second_convolution",
    )(taps, hidden, gridded)


def pack_kernel(above, below, own, to_west, to_east):
    low = lanes((WIDE, BLOCK)) < BLOCK // 2
    before, strip, after = above[2], own[...], below[2]

    def other_half(plane):
        return pltpu.roll(plane, BLOCK // 2, 1)

    outer = jnp.where(low, after, before)
    to_east[0] = jnp.where(low, other_half(strip), after)
    to_east[1] = outer
    to_west[0] = jnp.where(low, strip, other_half(before))
    to_west[1] = outer


def half_strip_packs(above, below, own):
    pack = jax.ShapeDtypeStruct((2, WIDE, BLOCK), jnp.bfloat16)
    return pl.pallas_call(
        pack_kernel,
        in_specs=[vmem()] * 3,
        out_specs=[vmem()] * 2,
        out_shape=[pack, pack],
        compiler_params=pltpu.CompilerParams(vmem_limit_bytes=VMEM_LIMIT),
        name="half_strip_packs",
    )(above, below, own)


def half_strips(west_pack, east_pack):
    low = lanes((WIDE, BLOCK)) < BLOCK // 2

    def other_half(plane):
        return pltpu.roll(plane, BLOCK // 2, 1)

    def both_halves(plane):
        return jnp.where(low, plane, other_half(plane))

    return {
        -4: west_pack[1],
        -3: both_halves(west_pack[0]),
        -2: jnp.where(low, west_pack[1], west_pack[0]),
        2: jnp.where(low, other_half(east_pack[0]), east_pack[1]),
        3: both_halves(east_pack[0]),
        4: east_pack[1],
    }


def strip_plan(column_rows):
    if column_rows == 2:
        return [], 3, 1
    return [-2, 2], column_rows, 2


def conv_kernel(
    column_rows,
    first_taps_ref,
    second_taps_ref,
    field,
    base,
    ends_ref,
    sides_ref,
    above,
    below,
    own_strip,
    *rest,
):
    near, far, reach = strip_plan(column_rows)
    near_strips, (west_pack, east_pack) = rest[: len(near)], rest[len(near) : len(near) + 2]
    smoothed, unturned, halves, sems = rest[len(near) + 2 :]
    count = lax.axis_size("tile")
    tile = lax.axis_index("tile")
    lane = lanes((WIDE, BLOCK))
    last = ROWS + 1
    R = column_rows
    blank = jnp.zeros((WIDE, BLOCK), jnp.bfloat16)

    strips = {-1: above[2], 0: own_strip[...], 1: below[2]}
    strips.update((shift, ref[...]) for shift, ref in zip(near, near_strips))
    if R == 2:
        strips.update(half_strips(west_pack, east_pack))
    else:
        for at in range(-reach, reach + 1):
            strips[at - far], strips[at + far] = west_pack[at + reach], east_pack[at + reach]

    def place(shift):
        return lax.rem(tile + shift + count, count)

    def ends(shift, before, after, middle):
        before = jnp.where(place(shift) > 0, before, blank)
        after = jnp.where(place(shift) < count - 1, after, blank)
        return jnp.where(lane == 0, before, jnp.where(lane == last, after, middle))

    memo = {}

    def padded_column(shift, which):
        if (shift, which) not in memo:
            base = which * ROWS
            memo[shift, which] = ends(
                shift,
                pltpu.roll(strips[shift - 1], (1 - base - ROWS) % BLOCK, 1),
                pltpu.roll(strips[shift + 1], (last - base) % BLOCK, 1),
                pltpu.roll(strips[shift], (1 - base) % BLOCK, 1),
            )
        return memo[shift, which]

    row_id = lax.broadcasted_iota(jnp.int32, (BLOCK, BLOCK), 0)
    reversal = (row_id + lanes((BLOCK, BLOCK)) == last).astype(jnp.bfloat16)

    def reversed_lanes(planes):
        stacked = jnp.concatenate(planes, axis=0)
        turned_round = jnp.dot(stacked, reversal, preferred_element_type=jnp.float32)
        return [row_tap(turned_round, at) for at in range(len(planes))]

    def choose(shift, which, turned_round, plain):
        flips = strips[shift].astype(jnp.float32)[CHANNELS + which : CHANNELS + which + 1]
        return jnp.where(flips > 0.5, turned_round, plain.astype(jnp.float32)).astype(jnp.bfloat16)

    west_of = {shift: (shift - R, 3) for shift in {-1, 0, 1, R - 1, R, R + 1}}
    east_of = {shift: (shift + R, 0) for shift in {-1, 0, 1, -R - 1, -R, -R + 1}}
    keys = sorted(set(west_of.values()) | set(east_of.values()))
    flipped = dict(zip(keys, reversed_lanes([padded_column(*key) for key in keys])))
    west = {
        shift: choose(shift, 0, flipped[west_of[shift]], padded_column(*west_of[shift]))
        for shift in sorted(west_of)
    }
    east = {
        shift: choose(shift, 1, flipped[east_of[shift]], padded_column(*east_of[shift]))
        for shift in sorted(east_of)
    }

    def columns(value, west_plane, west_row, east_plane, east_row):
        return shifted_columns(
            value,
            pltpu.roll(west_plane, (BLOCK - west_row) % BLOCK, 1),
            pltpu.roll(east_plane, BLOCK - 1 - east_row, 1),
        )

    def along(result):
        return (
            row_tap(result, 0)
            + pltpu.roll(row_tap(result, 1), BLOCK - 1, 1)
            + pltpu.roll(row_tap(result, 2), BLOCK - 2, 1)
        )

    first_taps = first_taps_ref[...]
    up = [jnp.where(tile > 0, above[at], blank) for at in range(2)]
    down = [jnp.where(tile < count - 1, below[at], blank) for at in range(2)]
    from_up, from_down = tap_sums(
        first_taps, shifted_columns(up[1], blank, blank), shifted_columns(down[0], blank, blank)
    )
    from_up, from_down = row_tap(from_up, 0), row_tap(from_down, 2)
    from_west, from_east = tap_sums(
        first_taps,
        jnp.concatenate([west[0], blank, blank], axis=0),
        jnp.concatenate([blank, blank, east[0]], axis=0),
    )
    from_west, from_east = along(from_west), along(from_east)
    first = ends_ref[0] + from_up
    first = first + jnp.where(lane == 0, from_west, 0.0)
    first = first + jnp.where(lane == BLOCK - 1, pltpu.roll(from_east, BLOCK - 1, 1), 0.0)
    final = ends_ref[1] + from_down
    final = final + jnp.where(lane == 0, pltpu.roll(from_west, BLOCK - ROWS + 1, 1), 0.0)
    final = final + jnp.where(lane == BLOCK - 1, pltpu.roll(from_east, BLOCK - ROWS, 1), 0.0)
    first, final = activated(first), activated(final)
    first_column = activated(sides_ref[0] + from_west)
    last_column = activated(sides_ref[1] + from_east)

    upper = jnp.zeros((WIDE, BLOCK), jnp.float32)
    lower = jnp.zeros((WIDE, BLOCK), jnp.float32)
    for at, (high, low) in enumerate(
        [(up[0], field[ROWS - 1]), (up[1], down[0]), (field[0], down[1])]
    ):
        from_row = ROWS - 1 + at
        one, two = tap_sums(
            row_tap(first_taps, at),
            columns(high, west[-1], from_row, east[-1], from_row),
            columns(low, west[1], at, east[1], at),
        )
        upper += one
        lower += two
    top = jnp.where(tile > 0, activated(upper), blank)
    bottom = jnp.where(tile < count - 1, activated(lower), blank)

    west_hidden, east_hidden = {}, {}
    for at in (-1, 0, 1):
        q = at - R
        one = jnp.concatenate([padded_column(q, 2), padded_column(q, 3), east[q]], axis=0)
        q = at + R
        two = jnp.concatenate([west[q], padded_column(q, 0), padded_column(q, 1)], axis=0)
        one, two = tap_sums(first_taps, one, two)
        west_hidden[at], east_hidden[at] = activated(along(one)), activated(along(two))

    def hidden_side(shift, values):
        return ends(
            shift,
            pltpu.roll(values[-1], BLOCK - ROWS + 1, 1),
            pltpu.roll(values[1], last, 1),
            pltpu.roll(values[0], 1, 1),
        )

    plain = [hidden_side(-R, west_hidden), hidden_side(R, east_hidden)]
    west_side, east_side = [
        choose(0, which, turned_side, plain[which])
        for which, turned_side in enumerate(reversed_lanes(plain))
    ]

    second_taps = second_taps_ref[...]
    from_top, from_first = tap_sums(
        second_taps,
        columns(top, west_side, 0, east_side, 0),
        columns(first, west_side, 1, east_side, 1),
    )
    from_final, from_bottom = tap_sums(
        second_taps,
        columns(final, west_side, ROWS, east_side, ROWS),
        columns(bottom, west_side, last, east_side, last),
    )
    rim_rows = {
        0: row_tap(from_top, 0) + row_tap(from_first, 1),
        1: row_tap(from_first, 0),
        ROWS - 2: row_tap(from_final, 2),
        ROWS - 1: row_tap(from_final, 1) + row_tap(from_bottom, 2),
    }

    other = (lane >= 2) & (lane < ROWS)

    def other_rows(plane):
        return jnp.where(other, plane, blank)

    near_west, near_east = other_rows(west_side), other_rows(east_side)
    first_column = other_rows(pltpu.roll(first_column, 1, 1))
    last_column = other_rows(pltpu.roll(last_column, 1, 1))
    to_0, to_1 = tap_sums(
        second_taps,
        jnp.concatenate([near_west, first_column, blank], axis=0),
        jnp.concatenate([first_column, blank, blank], axis=0),
    )
    to_127, to_126 = tap_sums(
        second_taps,
        jnp.concatenate([blank, last_column, near_east], axis=0),
        jnp.concatenate([blank, blank, last_column], axis=0),
    )
    parts, to_lanes = [], []
    for at, sums in enumerate((to_126, to_127, to_0, to_1)):
        sums = along(sums)
        high = sums.astype(jnp.bfloat16)
        sums = sums - high.astype(jnp.float32)
        middle = sums.astype(jnp.bfloat16)
        low = (sums - middle.astype(jnp.float32)).astype(jnp.bfloat16)
        parts.append(jnp.concatenate([high, middle, low], axis=0))
        to_lanes.append((lanes((BLOCK, BLOCK)) == 4 * row_id + at).astype(jnp.bfloat16))
    spread = jnp.dot(
        jnp.concatenate(parts, axis=1),
        jnp.concatenate(to_lanes, axis=0),
        preferred_element_type=jnp.float32,
    )
    spread = row_tap(spread, 0) + (row_tap(spread, 1) + row_tap(spread, 2))

    rim_lanes = lanes((PADDED, BLOCK))
    rim_lanes = (rim_lanes < 2) | (rim_lanes >= BLOCK - 2)
    spread = spread[:PADDED]
    copies = []
    for half in range(2):
        for row in range(half * HALF_ROWS, (half + 1) * HALF_ROWS):
            value = base[row] + jnp.where(
                rim_lanes, pltpu.roll(spread, (BLOCK - 4 * row - 2) % BLOCK, 1), 0.0
            )
            if row in rim_rows:
                value = value + rim_rows[row][:PADDED]
            unturned[half, row - half * HALF_ROWS] = value
        halves[half] = jnp.transpose(unturned[half], (1, 0, 2))[:CHANNELS].astype(jnp.bfloat16)
        rows = pl.ds(half * HALF_ROWS, HALF_ROWS)
        copies.append(pltpu.make_async_copy(halves.at[half], smoothed.at[:, rows], sems.at[half]))
        copies[-1].start()
    for copy in copies:
        copy.wait()


def convolutions(column_rows, *operands):
    return pl.pallas_call(
        functools.partial(conv_kernel, column_rows),
        in_specs=[vmem()] * len(operands),
        out_specs=pl.BlockSpec(memory_space=pl.ANY),
        out_shape=jax.ShapeDtypeStruct((CHANNELS, ROWS, BLOCK), jnp.bfloat16),
        scratch_shapes=[
            pltpu.VMEM((2, HALF_ROWS, PADDED, BLOCK), jnp.float32),
            pltpu.VMEM((2, CHANNELS, HALF_ROWS, BLOCK), jnp.bfloat16),
            pltpu.SemaphoreType.DMA((2,)),
        ],
        compiler_params=pltpu.CompilerParams(vmem_limit_bytes=VMEM_LIMIT),
        name="convolutions",
    )(*operands)


def tap_matrix(kernel):
    pad = WIDE - CHANNELS
    taps = jnp.pad(kernel, ((0, 0), (0, pad), (0, pad))).reshape(3, 3, WIDE, WIDE)
    return taps.transpose(0, 2, 1, 3).reshape(3 * WIDE, 3 * WIDE)


def from_shift(value, shift):
    count = lax.axis_size("tile")
    return lax.ppermute(value, "tile", [(i, (i - shift) % count) for i in range(count)])


def per_device(
    source, weights, block_source, block_target, edge_flip, norm_gain, first_kernel, second_kernel
):
    count = lax.axis_size("tile")
    column_rows = count // TILE_COLS
    field = source.reshape(ROWS, CHANNELS, BLOCK).transpose(1, 0, 2).reshape(-1, BLOCK)
    same, *nexts = regrid(block_target, block_source, field, weights, column_rows)

    for across in range(TILE_COLS):
        pairs = [
            (c * column_rows + p, (c ^ across) * column_rows + p + 1)
            for c in range(TILE_COLS)
            for p in range(column_rows - 1)
        ]
        nexts[across] = lax.ppermute(nexts[across], "tile", pairs)
    nexts = [nexts[across] for across in (0, 1, 2, 4, 5, 6, 7, 3)]
    same = lax.all_to_all(
        same,
        "tile",
        0,
        0,
        axis_index_groups=[
            [c * column_rows + p for c in COLUMN_ORDER] for p in range(column_rows)
        ],
        tiled=True,
    )

    gain = jnp.broadcast_to(
        jnp.pad(norm_gain, (0, PADDED - CHANNELS))[:, None], (PADDED, BLOCK)
    )
    first_taps, second_taps = tap_matrix(first_kernel), tap_matrix(second_kernel)
    same, nexts, gain, first_taps, second_taps = lax.optimization_barrier(
        (same, nexts, gain, first_taps, second_taps)
    )
    summed, upward, downward, strip = gather_rows(column_rows, edge_flip, gain, same, nexts)
    rims = [from_shift(downward, -1), from_shift(upward, 1)]
    near, far, reach = strip_plan(column_rows)
    strips = [from_shift(strip, shift) for shift in near]
    gridded, normed = normalize_rows(gain, summed)
    inner = inner_convolution(first_taps, normed)
    if column_rows == 2:
        to_west, to_east = half_strip_packs(*rims, strip)
    else:
        held = {-1: rims[0][2], 0: strip, 1: rims[1][2], **dict(zip(near, strips))}
        to_west = to_east = jnp.stack([held[at] for at in range(-reach, reach + 1)])
    to_west, to_east, inner = lax.optimization_barrier((to_west, to_east, inner))
    strips += [from_shift(to_east, -far), from_shift(to_west, far)]
    gridded_out = channels_first(gridded)
    hidden, *unfinished = inner
    base = inner_second_convolution(second_taps, hidden, gridded)
    smoothed = convolutions(
        column_rows, first_taps, second_taps, normed, base, *unfinished, *rims, strip, *strips
    )

    def placed(value):
        return value.reshape(CHANNELS, ROWS, BLOCK).transpose(1, 0, 2)[:, None]

    return placed(gridded_out), placed(smoothed)


def solution(mesh):
    in_specs = (
        P("tile", "groups", None, None),
        P("tile", None, None),
        P("tile"),
        P("tile"),
        P("tile", None),
        P(),
        P(),
        P(),
    )
    out_specs = (P("tile", "groups", None, None), P("tile", "groups", None, None))
    return jax.shard_map(
        per_device, mesh=mesh, in_specs=in_specs, out_specs=out_specs, check_vma=False
    )
```
